128 devices in a mesh: dp: 16 (over y, x_hi, core), seq: 8 (over x_lo, z).
Axes of the slice: x: 4 (x_hi: 2, x_lo: 2; x = x_hi * 2 + x_lo), y: 4, z: 4, core: 2. Of those that a mesh axis runs over, the one named last changes fastest.
Arguments:
- patches: bfloat16 [16, 1024, 768], P('dp', 'seq'), may hold values from -6 to 6
- cls_tokens: bfloat16 [16, 10, 768], P('dp'), may hold values from -6 to 6
- segments: int32 [16, 1024], P('dp', 'seq'), may hold values from 0 to 10, as said below
- prompts: bfloat16 [2, 50, 768], replicated, may hold values from -6 to 6
- w_qkv: bfloat16 [2, 768, 2304], replicated, may hold values from -0.21875 to 0.21875
- w_out: bfloat16 [2, 768, 768], replicated, may hold values from -0.875 to 0.875
- w_up: bfloat16 [2, 768, 3072], replicated, may hold values from -0.21875 to 0.21875
- w_down: bfloat16 [2, 3072, 768], replicated, may hold values from -0.109375 to 0.109375
- norm_gains: float32 [2, 2, 768], replicated, may hold values from 0.5 to 1.5
- biases: float32 [2, 6, 768], replicated, may hold values from -1.5 to 1.5
- up_bias: float32 [2, 3072], replicated, may hold values from -1.5 to 1.5
- cot_patches: bfloat16 [16, 1024, 768], P('dp', 'seq'), may hold values from -6 to 6
- cot_cls: bfloat16 [16, 10, 768], P('dp'), may hold values from -6 to 6
Outputs:
- out_patches: float32 [16, 1024, 768], P('dp', 'seq')
- out_cls: float32 [16, 10, 768], P('dp')
- grad_patches: float32 [16, 1024, 768], P('dp', 'seq')
- grad_cls: float32 [16, 10, 768], P('dp')
- grad_prompts: float32 [2, 50, 768], P(None, None, ('dp', 'seq'))
- grad_qkv: float32 [2, 768, 2304], P(None, ('dp', 'seq'))
- grad_out: float32 [2, 768, 768], P(None, ('dp', 'seq'))
- grad_up: float32 [2, 768, 3072], P(None, ('dp', 'seq'))
- grad_down: float32 [2, 3072, 768], P(None, ('dp', 'seq'))
- grad_gains: float32 [2, 2, 768], P(None, None, ('dp', 'seq'))
- grad_biases: float32 [2, 6, 768], P(None, None, ('dp', 'seq'))
- grad_up_bias: float32 [2, 3072], P(None, ('dp', 'seq'))
The draws below stay inside these ranges and needn't reach their ends.
Inputs may be any that keep to these rules, and one draw needn't show every extreme that they name: `segments`: each row holds images of one size, 100, 196 or 576 patches, numbered 0, 1, ... without gaps; slots without an image carry 10. The patches of each image, and the empty slots, are spread evenly over the row's 1024 // 128 blocks of 128 slots (counts in two blocks differ by one at most), in any order within a block.
All inputs are finite; a program needn't handle non-finite values.
Results may differ from the reference program's by a relative error of at most 0.03.
Values may be sent and summed in bfloat16 or wider, within the bound.
No kernel may reach another device: no remote copies, remote signals or barrier semaphores. Data moves between devices by JAX's collectives and lax.ppermute only.
A program may use at most 320 MiB of HBM per device.

```python
import jax
import jax.numpy as jnp
from jax import lax

D = 768
HEADS = 12
FF = 3072
NP = 50
HEAD = 64
LAYERS = 2
ROW = 1024
PATCH_S = 100
PATCH_M = 196
PATCH_L = 576
IMG_MAX = 10
ROWS = 16
SHARD = 128


def draw_segments(key, part):
    key = jax.random.fold_in(key, 11)
    size_key, level_key, order_key = jax.random.split(key, 3)
    sizes_table = jnp.array([PATCH_S, PATCH_M, PATCH_L], jnp.int32)
    size_class = jax.random.randint(size_key, (ROWS,), 0, 3)
    patch_count = jnp.sum(jnp.where(size_class[:, None] == jnp.arange(3, dtype=jnp.int32)[None, :], sizes_table[None, :], 0), 1)
    most_images = ROW // patch_count
    row_place = jnp.arange(ROWS, dtype=jnp.int32) * 1000 + jax.random.randint(level_key, (ROWS,), 0, 1000)
    images = jnp.minimum(most_images, 1 + most_images * (ROWS * 1000 + 2 * row_place) // (3 * ROWS * 1000))
    slot_index = jnp.arange(ROW, dtype=jnp.int32)
    contiguous = jnp.where(slot_index[None, :] < (images * patch_count)[:, None], slot_index[None, :] // patch_count[:, None], IMG_MAX)
    shards = ROW // SHARD
    dealt_ids = contiguous[:, slot_index % SHARD * shards + slot_index // SHARD]
    ranking = jax.random.randint(order_key, (ROWS, shards, SHARD), 0, 1 << 20) * SHARD + jnp.arange(SHARD, dtype=jnp.int32)
    ordering = jnp.argsort(ranking, axis=-1)
    return jnp.take_along_axis(dealt_ids.reshape(ROWS, shards, SHARD), ordering, -1).reshape(ROWS, ROW).astype(jnp.int32)


def strengthened(entries, rng, source, target, parts, factor):
    owner, partner = [(jnp.arange(entries.shape[position]) // (entries.shape[position] // parts)).reshape([-1 if axis == position else 1 for axis in range(entries.ndim)]) for position in (source, target)]
    chosen = jax.random.permutation(rng, parts)[partner]
    strong = (owner == chosen) | (owner == (partner + parts // 2) % parts)
    return jnp.where(strong, factor * entries, entries)


def block_levels(stream_key, extent, cuts, low, largest):
    factor_of, own = 1.0, jax.random.fold_in(stream_key, 6)
    for dim, shards_of in cuts:
        steps = jnp.exp(jax.random.uniform(jax.random.fold_in(own, dim), (shards_of,), jnp.float32, low / len(cuts), largest / len(cuts)))
        factor_of = factor_of * jnp.repeat(steps, extent[dim] // shards_of).reshape([-1 if axis == dim else 1 for axis in range(len(extent))])
    return factor_of


def gaussian(stream_key, dims, width, limit, cuts=(), kind=jnp.bfloat16):
    entries = width * jax.random.normal(stream_key, dims, jnp.float32)
    if cuts:
        entries = entries * block_levels(stream_key, dims, cuts, -0.22, 0.18)
    return jnp.clip(entries, -limit, limit).astype(kind)


def gaussian_with(stream_key, shape, deviation, reach, cuts, heavy, kind=jnp.bfloat16):
    entries = deviation * jax.random.normal(stream_key, shape, jnp.float32)
    if cuts:
        entries = entries * block_levels(stream_key, shape, cuts, -0.22, 0.18)
    return jnp.clip(strengthened(entries, jax.random.fold_in(stream_key, 3), *heavy), -reach, reach).astype(kind)


def setup_inputs(seed: int = 0) -> dict:
    splits = jax.random.split(jax.random.key(seed), 14)
    return {
        "patches": gaussian_with(splits[0], (ROWS, ROW, D), 1.0, 6.0, ((0, 16), (1, 8)), (0, 2, 16, 2.0)),
        "cls_tokens": gaussian(splits[1], (ROWS, IMG_MAX, D), 1.0, 6.0, ((0, 16),)),
        "segments": draw_segments(jax.random.fold_in(splits[13], 71), 0),
        "prompts": gaussian(splits[3], (LAYERS, NP, D), 1.0, 6.0),
        "w_qkv": gaussian(splits[4], (LAYERS, D, 3 * D), D ** -0.5, 0.21875),
        "w_out": gaussian(splits[5], (LAYERS, D, D), (D // 16) ** -0.5, 0.875),
        "w_up": gaussian(splits[6], (LAYERS, D, FF), D ** -0.5, 0.21875),
        "w_down": gaussian(splits[7], (LAYERS, FF, D), FF ** -0.5, 0.109375),
        "norm_gains": jnp.clip(1.0 + 0.1 * jax.random.normal(splits[8], (LAYERS, 2, D), jnp.float32), 0.5, 1.5),
        "biases": gaussian(splits[9], (LAYERS, 6, D), 0.3, 1.5, (), jnp.float32),
        "up_bias": gaussian(splits[10], (LAYERS, FF), 0.3, 1.5, (), jnp.float32),
        "cot_patches": gaussian(splits[11], (ROWS, ROW, D), 1.0, 6.0, ((0, 16), (1, 8))),
        "cot_cls": gaussian(splits[12], (ROWS, IMG_MAX, D), 1.0, 6.0, ((0, 16),)),
    }


@jax.custom_vjp
def low(v):
    return lax.optimization_barrier(v.astype(jnp.bfloat16)).astype(jnp.float32)

@jax.custom_vjp
def low_back(v):
    return v

def low_keep(v):
    return (low(v), None)

def low_pass(kept, grad):
    return (grad,)

def back_keep(v):
    return (v, None)

def back_low(kept, grad):
    return (low(grad),)
low.defvjp(low_keep, low_pass)
low_back.defvjp(back_keep, back_low)
precise = lax.Precision.HIGHEST
eps_norm = 1e-06
penalty_rate = 2.0
big_negative = -1e+30

def normalize(values, gain_row, shift_row):
    centre = lax.optimization_barrier(jnp.mean(values, -1, keepdims=True))
    centred = values - centre
    spread = lax.optimization_barrier(jnp.mean(centred * centred, -1, keepdims=True))
    return centred * lax.rsqrt(spread + eps_norm) * gain_row + shift_row

def layer_step(layer_weights, tokens, query_segs, key_segs):
    prompt_in, qkv_weight, out_weight, up_weight, down_weight, gain_pair, bias_rows, up_shift = layer_weights
    model_width = tokens.shape[-1]
    stacked = jnp.concatenate([prompt_in, tokens], 0)
    normed = low(normalize(stacked, gain_pair[0], bias_rows[0]))
    qkv_shift = jnp.concatenate([bias_rows[1], jnp.zeros_like(bias_rows[1]), bias_rows[2]])
    mixed = low(low_back(jnp.dot(normed, qkv_weight, precision=precise) + qkv_shift))
    queries = mixed[NP:, :model_width].reshape(-1, HEADS, HEAD)
    keys_all = mixed[:, model_width:2 * model_width].reshape(-1, HEADS, HEAD)
    values_all = mixed[:, 2 * model_width:].reshape(-1, HEADS, HEAD)
    scores = low_back(jnp.einsum('qhd,khd->hqk', queries, keys_all, precision=precise) * HEAD ** (-0.5))
    visible = (key_segs[None, :] == query_segs[:, None]) | (key_segs[None, :] < 0)
    probs = jax.nn.softmax(jnp.where(visible[None], scores, big_negative), axis=-1)
    attended = jnp.einsum('hqk,khd->qhd', low(probs), values_all, precision=precise)
    attended = low(low_back(attended.reshape(attended.shape[0], model_width)))
    middle = tokens + low_back(jnp.dot(attended, out_weight, precision=precise) + bias_rows[3])
    normed_mid = low(normalize(middle, gain_pair[1], bias_rows[4]))
    hidden = low_back(jnp.dot(normed_mid, up_weight, precision=precise) + up_shift)
    active = low(jax.nn.gelu(hidden, approximate=False))
    return middle + low_back(jnp.dot(active, down_weight, precision=precise) + bias_rows[5])

def row_forward(weights, cls_row, patch_row, seg_row):
    cls_ids = jnp.arange(IMG_MAX, dtype=jnp.int32)
    query_segs = jnp.concatenate([cls_ids, seg_row.astype(jnp.int32)])
    key_segs = jnp.concatenate([jnp.full((NP,), -1, jnp.int32), query_segs])
    tokens = jnp.concatenate([cls_row, patch_row], 0)
    for layer_at in range(LAYERS):
        tokens = layer_step(tuple((member[layer_at] for member in weights)), tokens, query_segs, key_segs)
    return tokens

def reference(patches, cls_tokens, segments, prompts, w_qkv, w_out, w_up, w_down, norm_gains, biases, up_bias, cot_patches, cot_cls):
    weights = (prompts.astype(jnp.float32), w_qkv.astype(jnp.float32), w_out.astype(jnp.float32), w_up.astype(jnp.float32), w_down.astype(jnp.float32), norm_gains.astype(jnp.float32), biases.astype(jnp.float32), up_bias.astype(jnp.float32))
    valid = (segments < IMG_MAX).astype(jnp.float32)
    hits = (segments[:, :, None] == jnp.arange(IMG_MAX, dtype=jnp.int32)[None, None, :]).astype(jnp.float32)
    present = (lax.optimization_barrier(jnp.sum(hits, 1)) > 0).astype(jnp.float32)
    count_all = jnp.sum(valid)
    cot_rows = jnp.concatenate([cot_cls.astype(jnp.float32) * present[:, :, None], cot_patches.astype(jnp.float32) * valid[:, :, None]], 1)

    def one_row(running, inputs_row):
        cls_row, patch_row, seg_row, cot_row = inputs_row
        outcome, pull = jax.vjp(lambda params_in, cls_in, patch_in: row_forward(params_in, cls_in, patch_in, seg_row), weights, cls_row, patch_row)
        grad_weights, grad_cls_row, grad_patch_row = pull(cot_row)
        running = jax.tree.map(jnp.add, running, grad_weights)
        return (running, (outcome[IMG_MAX:], outcome[:IMG_MAX], grad_patch_row, grad_cls_row))
    zero_grads = jax.tree.map(jnp.zeros_like, weights)
    totals, (out_patch, out_cls, grad_patch, grad_cls) = lax.scan(one_row, zero_grads, (cls_tokens.astype(jnp.float32), patches.astype(jnp.float32), segments, cot_rows))
    grad_prompts = totals[0] + penalty_rate * (count_all / ROW) * weights[0]
    return (out_patch, out_cls, grad_patch, grad_cls, grad_prompts, totals[1], totals[2], totals[3], totals[4], totals[5], totals[6], totals[7])
```

```python
import jax
import jax.numpy as jnp
from jax import lax
from jax.sharding import PartitionSpec as P

HEADS = 12
HEAD = 64


eps_norm = 1e-06
penalty_rate = 2.0
big_negative = -1e30

AXES = ("dp", "seq")


def place_of(device):
    dp, seq = device // 8, device % 8
    return {"core": dp % 2, "x": dp // 2 % 2 * 2 + seq // 4, "y": dp // 4, "z": seq % 4}


def device_of(place):
    dp = (place["y"] * 2 + place["x"] // 2) * 2 + place["core"]
    return dp * 8 + place["x"] % 2 * 4 + place["z"]


SPAN = {"core": 2, "x": 4, "y": 4, "z": 4}


def moved(axis, step):
    pairs = []
    for device in range(128):
        place = place_of(device)
        place[axis] = (place[axis] + step) % SPAN[axis]
        pairs.append((device, device_of(place)))
    return pairs


def send(values, axis, step):
    return lax.ppermute(values, AXES, moved(axis, step))


def owner_order(axes):
    here = place_of(lax.axis_index("dp") * 8 + lax.axis_index("seq"))
    total = 1
    for axis in axes:
        total *= SPAN[axis]
    rest = jnp.arange(total, dtype=jnp.int32)
    place = {}
    for axis in reversed(axes):
        place[axis] = (here[axis] + rest % SPAN[axis]) % SPAN[axis]
        rest = rest // SPAN[axis]
    return device_of(place)


def ring_sum(pieces, axis):
    total = pieces[0].astype(jnp.float32)
    for step in range(1, SPAN[axis]):
        total = total + send(pieces[step], axis, step).astype(jnp.float32)
    return total


def fold(values, axis):
    return ring_sum(jnp.split(values, SPAN[axis], 0), axis)


def fold_second(values, first, axis):
    blocks = values.reshape(SPAN[first], SPAN[axis], -1, values.shape[1])
    pieces = [blocks[:, step].reshape(-1, values.shape[1]) for step in range(SPAN[axis])]
    return ring_sum(pieces, axis)


def normalize(values, gain_row, shift_row):
    centre = jnp.mean(values, -1, keepdims=True)
    centred = values - centre
    spread = jnp.mean(centred * centred, -1, keepdims=True)
    return centred * lax.rsqrt(spread + eps_norm) * gain_row + shift_row


def norm_back(values, gain_row, shift_row, upstream, row_weight):
    plain = normalize(values, jnp.ones_like(gain_row), jnp.zeros_like(shift_row))
    primal, pull = jax.vjp(lambda inner: normalize(inner, gain_row, shift_row), values)
    (d_values,) = pull(upstream)
    weighted = upstream * row_weight
    lead_axes = tuple(range(values.ndim - 1))
    return (d_values, jnp.sum(weighted * plain, lead_axes), jnp.sum(weighted, lead_axes))


def project(rows_in, matrix):
    return jnp.einsum("rqd,de->rqe", rows_in, matrix, preferred_element_type=jnp.float32)


def project_back(rows_in, matrix):
    return jnp.einsum("rqe,de->rqd", rows_in, matrix, preferred_element_type=jnp.float32)


def outer_sum(left, right):
    return jnp.einsum("rqd,rqe->de", left, right, preferred_element_type=jnp.float32)


def masked_scores(query_heads, key_heads, query_segs, key_segs):
    raw = jnp.einsum(
        "qhd,khd->hqk", query_heads, key_heads, preferred_element_type=jnp.float32
    ) * HEAD ** (-0.5)
    visible = (key_segs[None, :] == query_segs[:, None]) | (key_segs[None, :] < 0)
    return (jnp.where(visible[None], raw, big_negative), visible)


def attend_forward(query_rows, key_rows, query_segs, key_segs):
    query_total, model_width = query_rows.shape
    query_heads = query_rows.reshape(query_total, HEADS, HEAD)
    key_heads = key_rows[:, :model_width].reshape(-1, HEADS, HEAD)
    value_heads = key_rows[:, model_width:].reshape(-1, HEADS, HEAD)
    scores, visible = masked_scores(query_heads, key_heads, query_segs, key_segs)
    row_top = jnp.max(scores, -1, keepdims=True)
    raised = jnp.exp(scores - row_top)
    row_total = jnp.sum(raised, -1, keepdims=True)
    weights_low = (raised / row_total).astype(jnp.bfloat16)
    attended = jnp.einsum(
        "hqk,khd->qhd", weights_low, value_heads, preferred_element_type=jnp.float32
    )
    return (
        attended.reshape(query_total, model_width).astype(jnp.bfloat16),
        row_top[..., 0] + jnp.log(row_total[..., 0]),
    )


def attend_backward(
    query_rows, key_rows, query_segs, key_segs, log_total, grad_rows, query_share, key_limit
):
    query_total, model_width = query_rows.shape
    query_heads = query_rows.reshape(query_total, HEADS, HEAD)
    key_heads = key_rows[:, :model_width].reshape(-1, HEADS, HEAD)
    value_heads = key_rows[:, model_width:].reshape(-1, HEADS, HEAD)
    scores, visible = masked_scores(query_heads, key_heads, query_segs, key_segs)
    probs_full = jnp.where(visible[None], jnp.exp(scores - log_total[..., None]), 0.0)
    grad_heads = grad_rows.reshape(query_total, HEADS, HEAD)
    d_probs = jnp.einsum(
        "qhd,khd->hqk", grad_heads, value_heads, preferred_element_type=jnp.float32
    )
    across = jnp.sum(probs_full * d_probs, -1, keepdims=True)
    d_scores = (probs_full * (d_probs - across)).astype(jnp.bfloat16)
    scale_factor = HEAD ** (-0.5)
    d_query = (
        jnp.einsum("hqk,khd->qhd", d_scores, key_heads, preferred_element_type=jnp.float32)
        * scale_factor
    )
    share_heads = query_share[None, :, None]
    d_key = (
        jnp.einsum(
            "hqk,qhd->khd", d_scores * share_heads, query_heads, preferred_element_type=jnp.float32
        )
        * scale_factor
    )
    d_value = jnp.einsum(
        "hqk,qhd->khd",
        probs_full.astype(jnp.bfloat16) * share_heads,
        grad_heads,
        preferred_element_type=jnp.float32,
    )
    return (
        d_query.reshape(query_total, model_width),
        jnp.concatenate(
            [d_key.reshape(key_limit, model_width), d_value.reshape(key_limit, model_width)], -1
        ),
        across[..., 0],
    )


def build_keys(prompt_kv, mixed, gathered, cls_count):
    row_count = mixed.shape[0]
    return jnp.concatenate(
        [prompt_kv[None], mixed[:, :cls_count, prompt_kv.shape[1] // 2 :], gathered], 1
    )


def per_device(
    patches,
    cls_tokens,
    segments,
    prompts,
    w_qkv,
    w_out,
    w_up,
    w_down,
    norm_gains,
    biases,
    up_bias,
    cot_patches,
    cot_cls,
):
    row_count, shard_len, model_width = patches.shape
    cls_count = cls_tokens.shape[1]
    prompt_count = prompts.shape[1]
    layer_count = w_qkv.shape[0]
    front_count = prompt_count + cls_count
    row_slots = shard_len * lax.axis_size("seq")
    low_type = jnp.bfloat16
    first_seq = (lax.axis_index("seq") == 0).astype(jnp.float32)
    first_all = first_seq * (lax.axis_index("dp") == 0).astype(jnp.float32)
    cls_ids = jnp.arange(cls_count, dtype=jnp.int32)
    cls_block = jnp.broadcast_to(cls_ids, (row_count, cls_count))
    query_segs = jnp.concatenate([cls_block, segments], 1)
    row_weight = jnp.concatenate(
        [jnp.full((cls_count, 1), first_seq, jnp.float32), jnp.ones((shard_len, 1), jnp.float32)], 0
    )
    row_weight_low = row_weight.astype(low_type)
    prompt_segs = jnp.full((row_count, prompt_count), -1, jnp.int32)
    tokens = jnp.concatenate([cls_tokens, patches], 1).astype(jnp.float32)
    saved = []
    for layer_at in range(layer_count):
        gain_pair = norm_gains[layer_at]
        bias_rows = biases[layer_at]
        qkv_shift = jnp.concatenate([bias_rows[1], jnp.zeros_like(bias_rows[1]), bias_rows[2]])
        prompt_full = prompts[layer_at].astype(jnp.float32)
        prompt_norm = normalize(prompt_full, gain_pair[0], bias_rows[0]).astype(low_type)
        prompt_kv = (
            jnp.dot(
                prompt_norm, w_qkv[layer_at][:, model_width:], preferred_element_type=jnp.float32
            )
            + qkv_shift[model_width:]
        ).astype(low_type)
        normed = normalize(tokens, gain_pair[0], bias_rows[0]).astype(low_type)
        mixed = (project(normed, w_qkv[layer_at]) + qkv_shift).astype(low_type)
        gathered, seg_all = (
            lax.all_gather(mixed[:, cls_count:, model_width:], "seq", axis=1, tiled=True),
            lax.all_gather(segments, "seq", axis=1, tiled=True),
        )
        key_segs = jnp.concatenate([prompt_segs, cls_block, seg_all], 1)
        key_rows = build_keys(prompt_kv, mixed, gathered, cls_count)
        attended, log_total = lax.map(
            lambda inputs_row: attend_forward(
                inputs_row[0][:, :model_width], inputs_row[1], inputs_row[2], inputs_row[3]
            ),
            (mixed, key_rows, query_segs, key_segs),
        )
        middle = tokens + (project(attended, w_out[layer_at]) + bias_rows[3])
        normed_mid = normalize(middle, gain_pair[1], bias_rows[4]).astype(low_type)
        hidden = project(normed_mid, w_up[layer_at]) + up_bias[layer_at]
        active = jax.nn.gelu(hidden, approximate=False).astype(low_type)
        kept_keys = key_rows
        saved.append(
            (
                tokens,
                normed,
                mixed,
                prompt_full,
                prompt_norm,
                prompt_kv,
                kept_keys,
                key_segs,
                attended,
                log_total,
                middle,
                normed_mid,
                hidden,
                active,
            )
        )
        tokens = middle + (project(active, w_down[layer_at]) + bias_rows[5])
    seg_first = saved[0][7][:, front_count:]
    present = (
        jnp.sum((seg_first[:, :, None] == cls_ids[None, None, :]).astype(jnp.float32), 1) > 0
    ).astype(jnp.float32)
    group_count = jnp.sum((seg_first < cls_count).astype(jnp.float32))
    count_all = lax.psum(group_count, "dp")
    valid = (segments < cls_count).astype(jnp.float32)
    upstream = jnp.concatenate(
        [
            cot_cls.astype(jnp.float32) * present[:, :, None],
            cot_patches.astype(jnp.float32) * valid[:, :, None],
        ],
        1,
    )
    layer_grads = [None] * layer_count
    for layer_at in reversed(range(layer_count)):
        (
            tokens_in,
            normed,
            mixed,
            prompt_full,
            prompt_norm,
            prompt_kv,
            kept_keys,
            key_segs,
            attended,
            log_total,
            middle,
            normed_mid,
            hidden,
            active,
        ) = saved[layer_at]
        gain_pair = norm_gains[layer_at]
        bias_rows = biases[layer_at]
        down_low = upstream.astype(low_type)
        down_weighted = down_low * row_weight_low
        layer_down = outer_sum(active, down_weighted)
        shift_down = jnp.sum(down_weighted.astype(jnp.float32), (0, 1))
        primal, gelu_pull = jax.vjp(lambda inner: jax.nn.gelu(inner, approximate=False), hidden)
        (d_hidden,) = gelu_pull(project_back(down_low, w_down[layer_at]))
        hidden_low = d_hidden.astype(low_type)
        hidden_weighted = hidden_low * row_weight_low
        layer_up = outer_sum(normed_mid, hidden_weighted)
        shift_up = jnp.sum(hidden_weighted.astype(jnp.float32), (0, 1))
        d_middle, gain_two, shift_two = norm_back(
            middle, gain_pair[1], bias_rows[4], project_back(hidden_low, w_up[layer_at]), row_weight
        )
        upstream = upstream + d_middle
        out_low = upstream.astype(low_type)
        out_weighted = out_low * row_weight_low
        layer_out = outer_sum(attended, out_weighted)
        shift_out = jnp.sum(out_weighted.astype(jnp.float32), (0, 1))
        d_attended = project_back(out_low, w_out[layer_at]).astype(low_type)
        key_rows = kept_keys
        key_limit = key_rows.shape[1]
        query_share = row_weight_low[:, 0]
        d_query, d_keys, across = lax.map(
            lambda inputs_row: attend_backward(
                inputs_row[0][:, :model_width],
                inputs_row[1],
                inputs_row[2],
                inputs_row[3],
                inputs_row[4],
                inputs_row[5],
                query_share,
                key_limit,
            ),
            (mixed, key_rows, query_segs, key_segs, log_total, d_attended),
        )
        front = lax.psum(d_keys[:, :front_count].astype(jnp.bfloat16), "seq").astype(jnp.float32)
        local_kv = lax.psum_scatter(
            d_keys[:, front_count:].astype(jnp.bfloat16), "seq", scatter_dimension=1, tiled=True
        ).astype(jnp.float32)
        mixed_grad = jnp.concatenate(
            [d_query, jnp.concatenate([front[:, prompt_count:], local_kv], 1)], 2
        ).astype(low_type)
        prompt_grad = front[:, :prompt_count].astype(low_type) * first_seq.astype(low_type)
        mixed_weighted = mixed_grad * row_weight_low
        prompt_part = jnp.einsum(
            "pd,rpe->de", prompt_norm, prompt_grad, preferred_element_type=jnp.float32
        )
        layer_qkv = outer_sum(normed, mixed_weighted) + jnp.concatenate(
            [jnp.zeros((model_width, model_width), jnp.float32), prompt_part], 1
        )
        column_sums = jnp.sum(mixed_weighted.astype(jnp.float32), (0, 1))
        prompt_sums = jnp.sum(prompt_grad.astype(jnp.float32), (0, 1))
        shift_query = column_sums[:model_width]
        shift_value = column_sums[2 * model_width :] + prompt_sums[model_width:]
        d_normed = project_back(mixed_grad, w_qkv[layer_at])
        d_tokens, gain_one, shift_one = norm_back(
            tokens_in, gain_pair[0], bias_rows[0], d_normed, row_weight
        )
        d_prompt_norm = jnp.einsum(
            "rpe,de->pd",
            prompt_grad,
            w_qkv[layer_at][:, model_width:],
            preferred_element_type=jnp.float32,
        )
        d_prompt, gain_prompt, shift_prompt = norm_back(
            prompt_full, gain_pair[0], bias_rows[0], d_prompt_norm, 1.0
        )
        upstream = upstream + d_tokens
        layer_prompt = d_prompt + penalty_rate * (count_all / row_slots) * first_all * prompt_full
        layer_gains = jnp.stack([gain_one + gain_prompt, gain_two])
        layer_biases = jnp.stack(
            [shift_one + shift_prompt, shift_query, shift_value, shift_out, shift_two, shift_down]
        )
        layer_grads[layer_at] = (
            layer_prompt,
            layer_qkv,
            layer_out,
            layer_up,
            layer_down,
            layer_gains,
            layer_biases,
            shift_up,
        )
    low = low_type
    order = owner_order(("core", "z", "x", "y"))
    rows_wanted = (order[:, None] * 6 + jnp.arange(6, dtype=jnp.int32)).reshape(-1)
    picker = (rows_wanted[:, None] == jnp.arange(model_width, dtype=jnp.int32)[None, :]).astype(low)

    def picked(grad):
        return jnp.dot(picker, grad.astype(low), preferred_element_type=jnp.float32).astype(low)

    grads_of = lambda place: [member[place] for member in layer_grads]
    small = jnp.concatenate(
        [member for member in grads_of(0)]
        + grads_of(5)
        + grads_of(6)
        + [member.reshape(model_width, 4).T for member in grads_of(7)]
        + [jnp.zeros((4, model_width), jnp.float32)],
        0,
    )
    group_up = picked(jnp.concatenate(grads_of(3), 1))
    group_mixed = picked(jnp.concatenate(grads_of(1) + grads_of(2) + [small.T], 1))
    down_order = owner_order(("core", "y", "z", "x"))
    group_down = jnp.concatenate(
        [
            jnp.take(member.astype(low).reshape(128, 24, model_width), down_order, 0).reshape(
                -1, model_width
            )
            for member in grads_of(4)
        ],
        1,
    )
    group_up = fold(group_up, "core").astype(low)
    group_down = fold(group_down, "core").astype(low)
    group_mixed = fold(group_mixed, "core").astype(low)
    group_up = fold(group_up, "z").astype(low)
    group_down = fold(group_down, "y").astype(low)
    group_mixed = fold_second(group_mixed, "z", "x").astype(low)
    group_up = fold(group_up, "x").astype(low)
    group_down = fold(group_down, "z").astype(low)
    group_mixed = fold(group_mixed, "z").astype(low)
    group_up = fold(group_up, "y")
    group_down = fold(group_down, "x")
    group_mixed = fold(group_mixed, "y")

    def columns(group, edges):
        out, at = [], 0
        for width in edges:
            out.append(group[:, at : at + width])
            at += width
        return out

    grad_up = jnp.stack(columns(group_up, [3072] * 2))
    grad_down = jnp.stack(columns(group_down, [768] * 2))
    mixed_parts = columns(group_mixed, [2304] * 2 + [768] * 2 + [50, 50, 2, 2, 6, 6, 4, 4])
    grad_qkv = jnp.stack(mixed_parts[:2])
    grad_out = jnp.stack(mixed_parts[2:4])
    grad_prompts = jnp.stack([part.T for part in mixed_parts[4:6]])
    grad_gains = jnp.stack([part.T for part in mixed_parts[6:8]])
    grad_biases = jnp.stack([part.T for part in mixed_parts[8:10]])
    grad_up_bias = jnp.stack([part.reshape(-1) for part in mixed_parts[10:12]])
    return (
        tokens[:, cls_count:],
        tokens[:, :cls_count],
        upstream[:, cls_count:],
        upstream[:, :cls_count],
        grad_prompts,
        grad_qkv,
        grad_out,
        grad_up,
        grad_down,
        grad_gains,
        grad_biases,
        grad_up_bias,
    )


def solution(mesh):
    placed = (
        P("dp", "seq", None),
        P("dp", None, None),
        P("dp", "seq"),
        P(),
        P(),
        P(),
        P(),
        P(),
        P(),
        P(),
        P(),
        P("dp", "seq", None),
        P("dp", None, None),
    )
    return jax.shard_map(
        per_device,
        mesh=mesh,
        in_specs=placed,
        out_specs=(
            P("dp", "seq", None),
            P("dp", None, None),
            P("dp", "seq", None),
            P("dp", None, None),
            P(None, None, ("dp", "seq")),
            P(None, ("dp", "seq"), None),
            P(None, ("dp", "seq"), None),
            P(None, ("dp", "seq"), None),
            P(None, ("dp", "seq"), None),
            P(None, None, ("dp", "seq")),
            P(None, None, ("dp", "seq")),
            P(None, ("dp", "seq")),
        ),
        check_vma=False,
    )
```

```python
import functools

import jax
import jax.numpy as jnp
from jax import lax
from jax.experimental import pallas as pl
from jax.experimental.pallas import tpu as pltpu
from jax.sharding import PartitionSpec as P

HEADS = 12
HEAD = 64
WIDTH = 768
HIDDEN = 3072
PATCHES = 128
CLS = 10
PROMPTS = 50
OWN = 144
KEYS = 1152
CLS_AT = 1024
PROMPT_AT = 1040
FRONT = 128
BLOCKS = 8
PAY = 864
PACKED = 2 * WIDTH + HIDDEN
HALF = WIDTH // 2
TILE = 256
LOW = jnp.bfloat16
FULL = jnp.float32

eps_norm = 1e-06
penalty_rate = 2.0
big_negative = -1e30

AXES = ("dp", "seq")
SPAN = {"core": 2, "x": 4, "y": 4, "z": 4}
RINGS = (("y", "z", "x"), ("z", "y", "x"))
ANY = pl.BlockSpec(memory_space=pl.ANY)
VM = "whole"
SM = pl.BlockSpec(memory_space=pltpu.SMEM)


def place_of(device):
    dp, seq = device // 8, device % 8
    return {"core": dp % 2, "x": dp // 2 % 2 * 2 + seq // 4, "y": dp // 4, "z": seq % 4}


def device_of(place):
    dp = (place["y"] * 2 + place["x"] // 2) * 2 + place["core"]
    return dp * 8 + place["x"] % 2 * 4 + place["z"]


def moved(axis, step):
    pairs = []
    for device in range(128):
        place = place_of(device)
        place[axis] = (place[axis] + step) % SPAN[axis]
        pairs.append((device, device_of(place)))
    return pairs


def send(values, axis, step):
    return lax.ppermute(values, AXES, moved(axis, step))


def groups_of(axes):
    found = {}
    for device in range(128):
        place = place_of(device)
        rest = tuple(place[axis] for axis in SPAN if axis not in axes)
        found.setdefault(rest, []).append((tuple(place[axis] for axis in axes), device))
    return [[device for _, device in sorted(group)] for group in found.values()]


def deal_out(values, axes):
    return lax.all_to_all(
        values, AXES, 0, 0, tiled=True, axis_index_groups=groups_of(axes)
    )


def swap_rows(values):
    return lax.all_to_all(values, "seq", 0, 0, tiled=True)


def owner_order(axes, steps=()):
    here = place_of(lax.axis_index("dp") * 8 + lax.axis_index("seq"))
    rest = jnp.arange(128, dtype=jnp.int32)
    place = {}
    for axis in reversed(axes):
        place[axis] = rest % SPAN[axis]
        if axis in steps:
            place[axis] = (here[axis] + place[axis]) % SPAN[axis]
        rest = rest // SPAN[axis]
    place["core"] = (here["core"] + rest) % 2
    return device_of(place)


def nn(left, right):
    return lax.dot_general(left, right, (((1,), (0,)), ((), ())), preferred_element_type=FULL)


def nt(left, right):
    return lax.dot_general(left, right, (((1,), (1,)), ((), ())), preferred_element_type=FULL)


def plain_norm(values):
    centred = values - jnp.mean(values, -1, keepdims=True)
    scale = lax.rsqrt(jnp.mean(centred * centred, -1, keepdims=True) + eps_norm)
    return centred * scale, scale


def norm_pull(plain, scale, gain, upstream):
    inner = upstream * gain
    return scale * (
        inner
        - jnp.mean(inner, -1, keepdims=True)
        - plain * jnp.mean(inner * plain, -1, keepdims=True)
    )


def whole(dims):
    return pl.BlockSpec(dims, lambda i: (0,) * len(dims))


class Late:
    def __init__(self, index=None, cuts=1, axis=0):
        self.index, self.cuts, self.axis = index, cuts, axis


class Early:
    def __init__(self, dims, kind=FULL):
        self.shape, self.dtype = dims, kind


class Moves:
    def __init__(self):
        self.ins, self.outs, self.gone = {}, {}, []

    def start(self, *refs):
        for ref in refs:
            for copy in self.ins[id(ref)]:
                copy.start()

    def wait(self, ref, piece=None):
        copies = self.ins[id(ref)]
        for copy in copies if piece is None else copies[piece : piece + 1]:
            copy.wait()

    def flush(self, *refs):
        for ref in refs:
            copy = self.outs.pop(id(ref))
            copy.start()
            self.gone.append(copy)

    def close(self):
        for copy in self.outs.values():
            copy.start()
        for copy in [*self.gone, *self.outs.values()]:
            copy.wait()


def run(body, operands, specs, outs, name, micros, scratch=(), mib=56):
    late = [(at, spec) for at, spec in enumerate(specs) if isinstance(spec, Late)]
    early = [(at, out) for at, out in enumerate(outs) if isinstance(out, Early)]
    buffers, total = [], 0
    for at, spec in late:
        dims = operands[at].shape if spec.index is None else operands[at].shape[1:]
        buffers.append(pltpu.VMEM(dims, operands[at].dtype))
        total += spec.cuts
    buffers += [pltpu.VMEM(out.shape, out.dtype) for _, out in early]
    total += len(early)

    def kernel(*refs):
        refs = list(refs)
        first = len(operands) + len(outs) + len(scratch)
        space, sems = refs[first : first + len(buffers)], refs[-1]
        moves, sem = Moves(), 0
        for (at, spec), buffer in zip(late, space):
            source = refs[at] if spec.index is None else refs[at].at[spec.index]
            size = buffer.shape[spec.axis] // spec.cuts
            copies = []
            for piece in range(spec.cuts):
                part = pl.ds(piece * size, size)
                view = lambda ref: ref.at[part] if spec.axis == 0 else ref.at[:, part]
                pair = (source, buffer) if spec.cuts == 1 else (view(source), view(buffer))
                copies.append(pltpu.make_async_copy(*pair, sems.at[sem]))
                sem += 1
            moves.ins[id(buffer)] = copies
            refs[at] = buffer
        for (at, out), buffer in zip(early, space[len(late) :]):
            at += len(operands)
            moves.outs[id(buffer)] = pltpu.make_async_copy(buffer, refs[at], sems.at[sem])
            sem += 1
            refs[at] = buffer
        body(moves, refs[:first])
        moves.close()

    in_specs = []
    for operand, spec in zip(operands, specs):
        if isinstance(spec, Late):
            in_specs.append(ANY)
        else:
            in_specs.append(whole(operand.shape) if spec == "whole" else spec)
    return pl.pallas_call(
        kernel,
        grid=(1,),
        out_shape=tuple(shape(out.shape, out.dtype) for out in outs),
        in_specs=in_specs,
        out_specs=tuple(ANY if isinstance(out, Early) else whole(out.shape) for out in outs),
        scratch_shapes=[*scratch, *buffers, pltpu.SemaphoreType.DMA((max(total, 1),))],
        compiler_params=params(mib),
        cost_estimate=cost(micros),
        name=name,
    )(*operands)


def after(values, *others):
    return lax.optimization_barrier((values, others))[0]


def tile_at(index, size):
    return pl.ds(pl.multiple_of(index * size, size), size)


def params(mib=56):
    return pltpu.CompilerParams(vmem_limit_bytes=mib * 2**20)


SHARE = 1.0
ATT = 6
LEFT = 1
MIX = 1
BMLP = 10


def cost(micros):
    return pl.CostEstimate(flops=int(micros * 1.1e9), bytes_accessed=1 << 20, transcendentals=0)


def shape(dims, kind=FULL):
    return jax.ShapeDtypeStruct(dims, kind)


def open_body(patch_ref, cls_ref, seg_ref, gain_ref, bias_ref, x_ref, pay_ref, own_ref):
    x_ref[0:PATCHES] = patch_ref[...].astype(FULL)
    x_ref[PATCHES:OWN] = cls_ref[...].astype(FULL)
    plain, _ = plain_norm(x_ref[...])
    normed = (plain * gain_ref[...] + bias_ref[...]).astype(LOW)
    own_ref[...] = normed
    segs = jnp.broadcast_to(seg_ref[...], (16, PATCHES)).astype(LOW)
    last = jnp.concatenate([segs, jnp.zeros((16, WIDTH - PATCHES), LOW)], 1)
    for block in range(BLOCKS):
        pay_ref[block, 0:PATCHES] = normed[0:PATCHES]
        pay_ref[block, PATCHES:OWN] = last


def open_call(patches, cls_pad, segs, gain, bias):
    outs = (shape((OWN, WIDTH)), shape((BLOCKS, OWN, WIDTH), LOW), shape((OWN, WIDTH), LOW))
    return run(lambda moves, refs: open_body(*refs), (patches, cls_pad, segs, gain, bias), [VM] * 5, outs, "open_norm", 2)


def seen_mask(key_ref, query_ref, mask_ref):
    keys = key_ref[0:1, :]
    seen = (keys == query_ref[:, 0:1]) | (keys == -1.0)
    mask_ref[...] = jnp.where(seen, 0.0, big_negative)


def half_lanes(rows):
    return lax.broadcasted_iota(jnp.int32, (rows, 2 * HEAD), 1) < HEAD


def two_heads(rows, lower):
    none = jnp.zeros_like(rows)
    return jnp.concatenate([jnp.where(lower, rows, none), jnp.where(lower, none, rows)], 0)


def split_rows(rows, patch_ref, cls_ref):
    patch_ref[...] = rows[0:PATCHES]
    for place in range(CLS):
        cls_ref[place] = rows[PATCHES + place : PATCHES + place + 1]


def forward_body(layer, last, moves, refs):
    first = layer == 0
    r = iter(refs)
    nxt = lambda: next(r)
    x_ref = nxt()
    come_ref = nxt()
    own_ref, prompt_ref, vec_ref, up_bias_ref, query_seg_ref = nxt(), nxt(), nxt(), nxt(), nxt()
    key_in_ref = None if first else nxt()
    wqkv, wout, wup, wdown = nxt(), nxt(), nxt(), nxt()
    q_ref, k_ref, v_ref, all_ref = nxt(), nxt(), nxt(), nxt()
    att_ref, lse_ref, mid_ref, nmid_ref = nxt(), nxt(), nxt(), nxt()
    slope_ref, active_ref, out_ref = nxt(), nxt(), nxt()
    next_ref, next_own_ref = nxt(), nxt()
    key_ref = nxt() if first else key_in_ref
    mask_ref = nxt()
    if first:
        seg_ref = nxt()
    block_sems = nxt()

    steps = []
    for block in range(BLOCKS):
        source = come_ref.at[block]
        steps.append(
            pltpu.make_async_copy(
                source.at[pl.ds(0, PATCHES)],
                all_ref.at[pl.ds(block * PATCHES, PATCHES)],
                block_sems.at[block],
            )
        )
        if first:
            steps.append(
                pltpu.make_async_copy(
                    source.at[pl.ds(PATCHES, 16), pl.ds(0, PATCHES)],
                    seg_ref.at[block],
                    block_sems.at[BLOCKS + block],
                )
            )
    for step in steps:
        step.start()
    moves.start(wqkv)

    gain_one, bias_one = vec_ref[0:1], vec_ref[2:3]
    gain_two, bias_two = vec_ref[1:2], vec_ref[6:7]

    plain, _ = plain_norm(prompt_ref[...])
    all_ref[CLS_AT:PROMPT_AT] = own_ref[PATCHES:OWN]
    all_ref[PROMPT_AT : PROMPT_AT + 64] = (plain * gain_one + bias_one).astype(LOW)
    all_ref[PROMPT_AT + 64 : KEYS] = jnp.zeros((KEYS - PROMPT_AT - 64, WIDTH), LOW)
    for step in steps:
        step.wait()
    moves.flush(all_ref)
    if first:
        lane = lax.broadcasted_iota(jnp.int32, (8, FRONT), 1)
        front = jnp.where(
            lane < CLS, lane, jnp.where((lane >= 16) & (lane < 16 + PROMPTS), -1, -2)
        )
        for block in range(BLOCKS):
            key_ref[:, block * PATCHES : (block + 1) * PATCHES] = seg_ref[block].astype(FULL)[0:8]
        key_ref[:, CLS_AT:KEYS] = front.astype(FULL)
    seen_mask(key_ref, query_seg_ref, mask_ref)

    def keys(tile, carry):
        at = tile_at(tile, TILE)
        rows = nn(all_ref[...], wqkv[:, pl.ds(pl.multiple_of(WIDTH + tile * TILE, TILE), TILE)])
        k_ref[:, at] = rows.astype(LOW)
        return carry

    def values(tile, carry):
        at = tile_at(tile, TILE)
        rows = nn(all_ref[...], wqkv[:, pl.ds(pl.multiple_of(2 * WIDTH + tile * TILE, TILE), TILE)])
        v_ref[:, at] = (rows + vec_ref[4:5, at]).astype(LOW)
        return carry

    def queries(tile, carry):
        at = tile_at(tile, TILE)
        rows = nn(own_ref[...], wqkv[:, at]) + vec_ref[3:4, at]
        q_ref[:, at] = (rows.astype(LOW).astype(FULL) * HEAD**-0.5).astype(LOW)
        return carry

    moves.wait(wqkv, 0)
    lax.fori_loop(0, 3, queries, 0, unroll=3)
    moves.wait(wqkv, 1)
    moves.start(wout, wup)
    lax.fori_loop(0, 3, keys, 0, unroll=3)
    moves.flush(k_ref)
    moves.wait(wqkv, 2)
    lax.fori_loop(0, 3, values, 0, unroll=3)
    moves.flush(v_ref)
    moves.start(wdown)

    lse_ref[...] = jnp.zeros((OWN, 128), FULL)
    lower = half_lanes(OWN)
    lane = lax.broadcasted_iota(jnp.int32, (OWN, 128), 1)

    def heads(pair, carry):
        at = tile_at(pair, 2 * HEAD)
        query, key, value = q_ref[:, at], k_ref[:, at], v_ref[:, at]
        outs = []
        for side in range(2):
            mine = lower if side == 0 else ~lower
            scores = nt(jnp.where(mine, query, jnp.zeros_like(query)), key) + mask_ref[...]
            top = jnp.max(scores, -1, keepdims=True)
            raised = jnp.exp(scores - top)
            total = jnp.sum(raised, -1, keepdims=True)
            outs.append(nn(raised.astype(LOW), value) / total)
            lane = lax.broadcasted_iota(jnp.int32, (OWN, 128), 1)
            lse_ref[...] = jnp.where(lane == 2 * pair + side, top + jnp.log(total), lse_ref[...])
        att_ref[:, at] = jnp.where(lower, outs[0], outs[1]).astype(LOW)
        return carry

    lax.fori_loop(0, HEADS // 2, heads, 0, unroll=2)

    moves.wait(wout)

    def project(tile, carry):
        at = tile_at(tile, TILE)
        mid_ref[:, at] = x_ref[:, at] + (nn(att_ref[...], wout[:, at]) + vec_ref[5:6, at])
        return carry

    lax.fori_loop(0, 3, project, 0, unroll=3)
    plain, _ = plain_norm(mid_ref[...])
    nmid_ref[...] = (plain * gain_two + bias_two).astype(LOW)
    moves.wait(wup)

    def rise(tile, carry):
        at = tile_at(tile, TILE)
        hidden = nn(nmid_ref[...], wup[:, at]) + up_bias_ref[0:1, at]
        share = 0.5 * (1.0 + lax.erf(hidden * 0.7071067811865476))
        active_ref[:, at] = (hidden * share).astype(LOW)
        slope_ref[:, at] = share + hidden * (0.3989422804014327 * jnp.exp(-0.5 * hidden * hidden))
        return carry

    lax.fori_loop(0, HIDDEN // TILE, rise, 0, unroll=4)
    moves.flush(slope_ref, active_ref)
    moves.wait(wdown)

    def lower_back(tile, carry):
        at = tile_at(tile, TILE)
        out_ref[:, at] = mid_ref[:, at] + (nn(active_ref[...], wdown[:, at]) + vec_ref[7:8, at])
        return carry

    lax.fori_loop(0, 3, lower_back, 0, unroll=3)
    if not last:
        plain, _ = plain_norm(out_ref[...])
        normed = (plain * vec_ref[8:9] + vec_ref[9:10]).astype(LOW)
        next_own_ref[...] = normed
        for block in range(BLOCKS):
            next_ref[block] = normed[0:PATCHES]
    else:
        split_rows(out_ref[...], next_ref, next_own_ref)


def forward_call(layer, last, x, come, own, prompt, vec, up_bias, query_seg, key_seg, weights):
    first = layer == 0
    outs = [
        shape((OWN, WIDTH), LOW),
        Early((KEYS, WIDTH), LOW),
        Early((KEYS, WIDTH), LOW),
        Early((KEYS, WIDTH), LOW),
        shape((OWN, WIDTH), LOW),
        shape((OWN, 128)),
        shape((OWN, WIDTH)),
        shape((OWN, WIDTH), LOW),
        Early((OWN, HIDDEN)),
        Early((OWN, HIDDEN), LOW),
        shape((OWN, WIDTH)),
    ]
    if last:
        outs += [shape((PATCHES, WIDTH)), shape((CLS, 1, WIDTH))]
    else:
        outs += [shape((BLOCKS, PATCHES, WIDTH), LOW), shape((OWN, WIDTH), LOW)]
    if first:
        outs += [shape((8, KEYS))]
    operands = [x, come, own, prompt, vec, up_bias, query_seg]
    specs = [VM, ANY] + [VM] * 5
    if not first:
        operands.append(key_seg)
        specs.append(VM)
    operands += weights
    specs += [Late(layer, 3, 1), Late(layer), Late(layer), Late(layer)]
    scratch = [pltpu.VMEM((OWN, KEYS), FULL)]
    if first:
        scratch.append(pltpu.VMEM((BLOCKS, 16, PATCHES), LOW))
    scratch += [pltpu.SemaphoreType.DMA((2 * BLOCKS,))]
    body = lambda moves, refs: forward_body(layer, last, moves, refs)
    return run(body, operands, specs, outs, "forward_layer", 24 * SHARE, scratch)


def gathered_pull(come_ref, qpart_ref, x_ref, gain, mid_grad_ref):
    total = come_ref[0].astype(FULL)
    for block in range(1, BLOCKS):
        total = total + come_ref[block].astype(FULL)
    patch_part = total[0:WIDTH].T
    cls_part = jnp.concatenate(
        [total[WIDTH + 16 * lane : WIDTH + 16 * (lane + 1)] for lane in range(6)], 1
    )
    d_normed = jnp.concatenate([patch_part, cls_part], 0) + qpart_ref[...]
    plain, scale = plain_norm(x_ref[...])
    return mid_grad_ref[...] + norm_pull(plain, scale, gain, d_normed)


def row_share(first_ref):
    row = lax.broadcasted_iota(jnp.int32, (OWN, 1), 0)
    return jnp.where(row < PATCHES, 1.0, jnp.where(row < PATCHES + CLS, first_ref[0, 0], 0.0))


def back_mlp_body(last, moves, refs):
    r = iter(refs)
    nxt = lambda: next(r)
    if last:
        cot_ref, cot_cls_ref, key_ref, query_seg_ref = nxt(), nxt(), nxt(), nxt()
    else:
        come_ref = nxt()
        up_qpart_ref, up_x_ref, up_mid_grad_ref, up_vec_ref = nxt(), nxt(), nxt(), nxt()
    first_ref, mid_ref, slope_ref, vec_ref = nxt(), nxt(), nxt(), nxt()
    wout, wup, wdown = nxt(), nxt(), nxt()
    grad_refs = nxt(), nxt()
    datt_ref, mid_grad_ref = nxt(), nxt()
    rows_ref, up_row_ref = nxt(), nxt()
    up_ref, low_ref, hid_ref = nxt(), nxt(), nxt()

    moves.start(wdown, slope_ref)
    gain_two = vec_ref[1:2]
    share = row_share(first_ref)
    if last:
        valid = ((query_seg_ref[...] < CLS) & (query_seg_ref[...] >= 0)).astype(FULL)
        up_ref[0:PATCHES] = cot_ref[...].astype(FULL) * valid[0:PATCHES, 0:1]
        hits = (key_ref[0:1, 0:CLS_AT] == query_seg_ref[PATCHES:OWN, 0:1]).astype(FULL)
        present = jnp.max(hits, -1, keepdims=True)
        up_ref[PATCHES:OWN] = cot_cls_ref[...].astype(FULL) * present
    else:
        up_ref[...] = gathered_pull(
            come_ref, up_qpart_ref, up_x_ref, up_vec_ref[0:1], up_mid_grad_ref
        )
    low_ref[...] = up_ref[...].astype(LOW)
    weighted = low_ref[...].astype(FULL) * share
    grad_refs[0][:, 0:WIDTH] = weighted.astype(LOW)
    rows_ref[...] = jnp.zeros((8, WIDTH), FULL)
    rows_ref[0:1] = jnp.sum(weighted, 0, keepdims=True)
    moves.start(wup)

    def to_hidden(half, tile, carry):
        at = tile_at(tile, TILE)
        grad = (nt(low_ref[...], wdown[at, :]) * slope_ref[:, at]).astype(LOW)
        hid_ref[:, at] = grad
        counted = grad.astype(FULL) * share
        to = WIDTH + tile * TILE - half * (PACKED // 2)
        grad_refs[half][:, pl.ds(pl.multiple_of(to, TILE), TILE)] = counted.astype(LOW)
        up_row_ref[:, at] = jnp.broadcast_to(jnp.sum(counted, 0, keepdims=True), (8, TILE))
        return carry

    moves.wait(slope_ref)
    for piece in range(4):
        moves.wait(wdown, piece)
        body = functools.partial(to_hidden, piece // 2)
        lax.fori_loop(3 * piece, 3 * piece + 3, body, 0, unroll=3)
    moves.wait(wup)
    moves.start(wout)

    def to_mid(tile, carry):
        at = tile_at(tile, TILE)
        mid_grad_ref[:, at] = nt(hid_ref[...], wup[at, :])
        return carry

    lax.fori_loop(0, 3, to_mid, 0, unroll=3)
    d_normed = mid_grad_ref[...]
    plain, scale = plain_norm(mid_ref[...])
    counted = d_normed * share
    rows_ref[1:2] = jnp.sum(counted * plain, 0, keepdims=True)
    rows_ref[2:3] = jnp.sum(counted, 0, keepdims=True)
    mid_grad_ref[...] = up_ref[...] + norm_pull(plain, scale, gain_two, d_normed)
    low_ref[...] = mid_grad_ref[...].astype(LOW)
    weighted = low_ref[...].astype(FULL) * share
    grad_refs[1][:, PACKED // 2 - WIDTH :] = weighted.astype(LOW)
    rows_ref[3:4] = jnp.sum(weighted, 0, keepdims=True)
    moves.flush(*grad_refs)
    moves.wait(wout)

    def to_att(tile, carry):
        at = tile_at(tile, TILE)
        datt_ref[:, at] = nt(low_ref[...], wout[at, :]).astype(LOW)
        return carry

    lax.fori_loop(0, 3, to_att, 0, unroll=3)


def back_mlp_call(layer, last, start, first_seq, mid, slope, vec, weights):
    operands = [*start, first_seq, mid, slope, vec, *weights[1:]]
    specs = [VM] * len(start) + [SM, VM, Late(), VM, Late(layer), Late(layer), Late(layer, 4)]
    outs = [
        Early((OWN, PACKED // 2), LOW),
        Early((OWN, PACKED // 2), LOW),
        shape((OWN, WIDTH), LOW),
        shape((OWN, WIDTH)),
        shape((8, WIDTH)),
        shape((8, HIDDEN)),
    ]
    scratch = [
        pltpu.VMEM((OWN, WIDTH), FULL),
        pltpu.VMEM((OWN, WIDTH), LOW),
        pltpu.VMEM((OWN, HIDDEN), LOW),
    ]
    body = lambda moves, refs: back_mlp_body(last, moves, refs)
    return run(body, operands, specs, outs, "backward_mlp", BMLP, scratch)


def back_att_body(layer, moves, refs):
    r = iter(refs)
    nxt = lambda: next(r)
    first_ref, rows_in_ref, datt_ref = nxt(), nxt(), nxt()
    q_ref, k_ref, v_ref, lse_ref = nxt(), nxt(), nxt(), nxt()
    prompt_ref, vec_ref, query_seg_ref, key_ref = nxt(), nxt(), nxt(), nxt()
    if layer == 0:
        pick_ref, spot_ref, prompts_1, rows_1, up_ref = [nxt() for _ in range(5)]
    wqkv = nxt()
    dq_ref, qpart_ref, dkv_ref, pay_ref = nxt(), nxt(), nxt(), nxt()
    if layer == 0:
        small_refs = nxt(), nxt()
        dprompt_ref, rows_ref = nxt(), nxt()
    else:
        dprompt_ref, rows_ref = nxt(), nxt()
    mask_ref, dqf_ref, qt_ref, dat_ref, front_ref = [nxt() for _ in range(5)]

    moves.start(k_ref, v_ref, wqkv)
    gain_one = vec_ref[0:1]
    share = row_share(first_ref)
    seen_mask(key_ref, query_seg_ref, mask_ref)
    rows_ref[...] = rows_in_ref[...]

    def turn(tile, carry):
        at = tile_at(tile, TILE)
        dat_ref[at, :] = (datt_ref[:, at].astype(FULL) * share).T.astype(LOW)
        qt_ref[at, :] = (q_ref[:, at].astype(FULL) * share).T.astype(LOW)
        return carry

    lax.fori_loop(0, 3, turn, 0, unroll=3)
    lower = half_lanes(OWN)
    lane = lax.broadcasted_iota(jnp.int32, (OWN, 128), 1)
    moves.wait(k_ref)
    moves.wait(v_ref)

    def heads(pair, carry):
        at = tile_at(pair, 2 * HEAD)
        query, key, value, grad = q_ref[:, at], k_ref[:, at], v_ref[:, at], datt_ref[:, at]
        outs = []
        for side in range(2):
            mine = lower if side == 0 else ~lower
            head = 2 * pair + side
            log_total = jnp.sum(jnp.where(lane == head, lse_ref[...], 0.0), -1, keepdims=True)
            scores = nt(jnp.where(mine, query, jnp.zeros_like(query)), key) + mask_ref[...]
            probs = jnp.exp(scores - log_total)
            d_probs = nt(jnp.where(mine, grad, jnp.zeros_like(grad)), value)
            both = probs * d_probs
            across = jnp.sum(both, -1, keepdims=True)
            d_scores = (both - probs * across).astype(LOW)
            probs_low = probs.astype(LOW)
            outs.append(nn(d_scores, key))
            rows = tile_at(head, HEAD)
            dkv_ref[rows, :] = nn(qt_ref[rows, :], d_scores).astype(LOW)
            value_rows = pl.ds(pl.multiple_of(WIDTH + head * HEAD, HEAD), HEAD)
            dkv_ref[value_rows, :] = nn(dat_ref[rows, :], probs_low).astype(LOW)
        dqf_ref[:, at] = (jnp.where(lower, outs[0], outs[1]) * HEAD**-0.5).astype(LOW)
        return carry

    lax.fori_loop(0, HEADS // 2, heads, 0, unroll=2)
    moves.flush(dkv_ref)
    counted = dqf_ref[...].astype(FULL) * share
    dq_ref[...] = counted.astype(LOW)
    rows_ref[4:5] = jnp.sum(counted, 0, keepdims=True)
    moves.wait(wqkv)

    def to_normed(tile, carry):
        at = tile_at(tile, TILE)
        qpart_ref[:, at] = nt(dqf_ref[...], wqkv[at, 0:WIDTH])
        return carry

    lax.fori_loop(0, 3, to_normed, 0, unroll=3)

    front_ref[...] = nn(wqkv[:, WIDTH:], dkv_ref[:, CLS_AT:KEYS])
    shift = jnp.sum(front_ref[...], -1, keepdims=True)
    front = front_ref[...].T
    cls_rows = jnp.concatenate(
        [front[0:16, 128 * place : 128 * (place + 1)] for place in range(6)], 0
    )
    for block in range(0, BLOCKS, 2):
        part = nn(wqkv[:, WIDTH:], dkv_ref[:, block * PATCHES : (block + 2) * PATCHES])
        shift = shift + jnp.sum(part, -1, keepdims=True)
        for side in range(2):
            pay_ref[block + side, 0:WIDTH] = part[:, side * PATCHES : (side + 1) * PATCHES].astype(LOW)
            pay_ref[block + side, WIDTH:PAY] = cls_rows.astype(LOW)
    moves.flush(pay_ref)

    plain, scale = plain_norm(prompt_ref[...])
    d_prompt = norm_pull(plain, scale, gain_one, front[16:80])
    query_seg = query_seg_ref[0:PATCHES, 0:1]
    slots = jnp.sum((query_seg < CLS).astype(FULL), 0, keepdims=True)
    dprompt_ref[...] = d_prompt + (penalty_rate / 1024.0) * slots * prompt_ref[...]

    turned = jnp.broadcast_to(shift, (WIDTH, 128)).T
    rows_ref[6:7] = turned[0:1] + jnp.sum(qpart_ref[...] * share, 0, keepdims=True)
    totals = jnp.sum(dkv_ref[WIDTH : 2 * WIDTH].astype(FULL), -1, keepdims=True)
    rows_ref[5:6] = jnp.broadcast_to(totals, (WIDTH, 128)).T[0:1]
    if layer != 0:
        return
    joined = jnp.concatenate([dprompt_ref[0:56], prompts_1[0:56], rows_ref[...], rows_1[...]], 0)
    turned = nt(pick_ref[...], joined.astype(LOW))
    ups = nn(spot_ref[...], up_ref[...].astype(LOW))
    rows = jnp.concatenate([turned[128 * part : 128 * (part + 1)] for part in range(6)], 1)
    ups = jnp.concatenate([ups, jnp.zeros((128, WIDTH - 128), FULL)], 1)
    for half in range(2):
        spots = slice(64 * half, 64 * (half + 1))
        small_refs[half][...] = jnp.concatenate([rows[spots], ups[spots]], 0).astype(LOW)


def back_att_call(layer, first_seq, rows, datt, saved, prompt, vec, query_seg, key_seg, small, weight):
    operands = [first_seq, rows, datt, *saved, prompt, vec, query_seg, key_seg, *small, weight]
    specs = [SM] + [VM] * 3 + [Late()] * 2 + [VM] * (5 + len(small)) + [Late(layer)]
    outs = [
        shape((OWN, WIDTH), LOW),
        shape((OWN, WIDTH)),
        Early((2 * WIDTH, KEYS), LOW),
        Early((BLOCKS, PAY, 128), LOW),
    ]
    if layer == 0:
        outs += [shape((128, WIDTH), LOW)] * 2
    outs += [shape((64, WIDTH)), shape((8, WIDTH))]
    scratch = [
        pltpu.VMEM((OWN, KEYS), FULL),
        pltpu.VMEM((OWN, WIDTH), LOW),
        pltpu.VMEM((WIDTH, OWN), LOW),
        pltpu.VMEM((WIDTH, OWN), LOW),
        pltpu.VMEM((WIDTH, FRONT), FULL),
    ]
    body = lambda moves, refs: back_att_body(layer, moves, refs)
    return run(body, operands, specs, outs, "backward_attention", ATT, scratch)


def close_body(come_ref, qpart_ref, x_ref, mid_grad_ref, vec_ref, patch_ref, cls_ref):
    rows = gathered_pull(come_ref, qpart_ref, x_ref, vec_ref[0:1], mid_grad_ref)
    split_rows(rows, patch_ref, cls_ref)


def close_call(operands):
    outs = (shape((PATCHES, WIDTH)), shape((CLS, 1, WIDTH)))
    return run(lambda moves, refs: close_body(*refs), operands, [VM] * len(operands), outs, "close_norm", 2)


def left_body(plan, moves, refs):
    order_ref, *refs = refs
    picks, (all_ref, att_ref, mid_ref, active_ref) = refs[0:2], refs[2:6]
    tall_refs, wide_refs = refs[6:8], refs[8:10]
    turned_ref, down_ref = refs[10:12]

    def turn(tile, carry):
        at = tile_at(tile, TILE)
        turned_ref[at, :] = active_ref[:, at].astype(FULL).T
        return carry

    def move(spot, carry):
        source = pl.ds(pl.multiple_of(order_ref[spot] * 24, 8), 24)
        target = pl.ds(pl.multiple_of(spot * 24, 8), 24)
        down_ref[target, :] = turned_ref[source, :]
        return carry

    moves.start(all_ref)
    lax.fori_loop(0, HIDDEN // TILE, turn, 0)
    lax.fori_loop(0, 128, move, 0)
    for half in range(2):
        tall_refs[half][0 : 2 * WIDTH] = down_ref[half * 2 * WIDTH : (half + 1) * 2 * WIDTH].astype(LOW)
    row = 2 * WIDTH
    for kind, ring_at in plan:
        source = {"mid": mid_ref, "att": att_ref}[kind][...]
        turned = nt(picks[ring_at][...], source).astype(LOW)
        for half in range(2):
            tall_refs[half][row : row + HALF] = turned[half * HALF : (half + 1) * HALF]
        row += HALF
    moves.flush(*tall_refs)
    moves.wait(all_ref)
    for half in range(2):
        wide = nt(picks[1][half * HALF : (half + 1) * HALF], all_ref[...])
        wide_refs[half][...] = wide.astype(LOW)


def left_call(plan, order, picks, normed_all, att, nmid, active):
    tall = (2 * WIDTH + len(plan) * HALF, OWN)
    outs = [Early(tall, LOW)] * 2 + [shape((HALF, KEYS), LOW)] * 2
    operands = (order, *picks, normed_all, att, nmid, active)
    scratch = [pltpu.VMEM((HIDDEN, OWN), FULL), pltpu.VMEM((HIDDEN, OWN), FULL)]
    body = lambda moves, refs: left_body(plan, moves, refs)
    return run(body, operands, [SM, VM, VM, Late(), VM, VM, VM], outs, "left_factors", LEFT, scratch)


def rights_of(grad_refs, kind, part, tile):
    at = {"down": 0, "up": WIDTH + part * WIDTH, "out": WIDTH + HIDDEN}[kind] + tile * TILE
    half, at = at // (PACKED // 2), at % (PACKED // 2)
    return [grad_refs[2 * side + half][:, at : at + TILE] for side in range(2)]


def piece_shapes(classes):
    outs = []
    for number, rows in classes:
        outs += [shape((4, rows, WIDTH), LOW)] if number == 0 else [shape((rows, WIDTH), LOW)] * 4
    return outs


def by_class(classes, arrays):
    found, at = {}, 0
    for number, _ in classes:
        if number == 0:
            found[0] = [arrays[at].at[way] for way in range(4)]
            at += 1
        else:
            found[number] = list(arrays[at : at + 4])
            at += 4
    return found


def deal(out, row, values, columns):
    size = values.shape[0] // 4
    for way in range(4):
        out[way][row : row + size, columns] = values[way * size : (way + 1) * size].astype(LOW)


def mlp_body(plan, classes, refs):
    tall_refs, grad_refs = refs[0:2], refs[2:6]
    outs = by_class(classes, refs[6:])
    for kind, part, left_row, out, out_row in plan:
        for tile in range(3):
            columns = slice(tile * TILE, (tile + 1) * TILE)
            rights = rights_of(grad_refs, kind, part, tile)
            for piece in range(4 if kind == "down" else 1):
                rows = slice(left_row + piece * HALF, left_row + (piece + 1) * HALF)
                values = nn(tall_refs[0][rows], rights[0]) + nn(tall_refs[1][rows], rights[1])
                if kind == "down":
                    outs[out][piece][out_row : out_row + HALF, columns] = values.astype(LOW)
                else:
                    deal(outs[out], out_row, values, columns)


def mlp_call(plan, classes, talls, grads, micros=8 * SHARE):
    operands = (*talls, *grads)
    body = lambda moves, refs: mlp_body(plan, classes, refs)
    out = run(body, operands, [VM] * 6, piece_shapes(classes), "grad_mlp", micros)
    return by_class_values(classes, out)


def by_class_values(classes, arrays):
    found, at = {}, 0
    for number, _ in classes:
        found[number] = arrays[at] if number == 0 else list(arrays[at : at + 4])
        at += 1 if number == 0 else 4
    return found


def mixed_body(plan, classes, small, refs):
    seq_ref, *refs = refs
    tall_refs, wide_refs, dq_refs, dkv_refs = [refs[2 * at : 2 * at + 2] for at in range(4)]
    grad_refs, small_refs = refs[8:12], refs[12:14]
    outs = by_class(classes, refs[14:] if small else refs[12:])
    if small:
        joined = small_refs[0][...].astype(FULL) + small_refs[1][...].astype(FULL)
        for way in range(4):
            spots = [joined[64 * part + 16 * way : 64 * part + 16 * (way + 1)] for part in range(2)]
            outs[1][way][3 * HALF // 4 : 3 * HALF // 4 + 32] = jnp.concatenate(spots, 0).astype(LOW)
    for kind, left_row, out, out_row in plan:
        for tile in range(3):
            columns = slice(tile * TILE, (tile + 1) * TILE)
            values = jnp.zeros((HALF, TILE), FULL)
            for side in range(2):
                if kind in ("k", "v"):
                    at = (0 if kind == "k" else WIDTH) + tile * TILE
                    values = values + nt(wide_refs[side][...], dkv_refs[side][at : at + TILE])
                    continue
                if kind == "q" and left_row is None:
                    wide = wide_refs[side]
                    mine = pl.ds(pl.multiple_of(seq_ref[0, 0] * PATCHES, PATCHES), PATCHES)
                    left = jnp.concatenate([wide[:, mine], wide[:, CLS_AT:PROMPT_AT]], 1)
                else:
                    left = tall_refs[side][left_row : left_row + HALF]
                if kind == "q":
                    right = dq_refs[side][:, columns]
                else:
                    name, part = ("out", 0) if kind == "out" else ("up", kind)
                    right = rights_of(grad_refs, name, part, tile)[side]
                values = values + nn(left, right)
            deal(outs[out], out_row, values, columns)


def mixed_call(plan, classes, seq, talls, wides, dqs, dkvs, grads, small=()):
    operands = (seq, *talls, *wides, *dqs, *dkvs, *grads, *small)
    body = lambda moves, refs: mixed_body(plan, classes, bool(small), refs)
    specs = [SM] + [VM] * (len(operands) - 1)
    out = run(body, operands, specs, piece_shapes(classes), "grad_mixed", MIX)
    return by_class_values(classes, out)


def fold_body(classes, refs):
    r = iter(refs)
    totals = []
    for groups in classes:
        totals.append([])
        for _ in groups:
            come = next(r)
            ways = [come.at[way] for way in range(4)] if len(come.shape) == 3 else [come]
            ways += [next(r) for _ in range(4 - len(ways))]
            total = ways[0][...].astype(FULL)
            for way in ways[1:]:
                total = total + way[...].astype(FULL)
            totals[-1].append(total)
    for groups, sums in zip(classes, totals):
        out = next(r)
        for way in range(16):
            parts = []
            for total, items in zip(sums, groups):
                at = 0
                for rows in items:
                    size = rows // 16
                    parts.append(total[at + way * size : at + (way + 1) * size])
                    at += rows
            short = out.shape[1] - sum(part.shape[0] for part in parts)
            if short:
                parts.append(jnp.zeros((short, out.shape[2]), FULL))
            out[way] = jnp.concatenate(parts, 0).astype(LOW)


def fold_call(classes):
    operands = []
    for groups in classes:
        for come, _ in groups:
            operands += come if isinstance(come, list) else [come]
    counts = [[items for _, items in groups] for groups in classes]
    wide = 256
    sizes = [-(-sum(sum(items) for items in groups) // 256) * 16 for groups in counts]
    block = lambda *dims: pl.BlockSpec((*dims, wide), lambda i: (*[0] * len(dims), i))
    return pl.pallas_call(
        lambda *refs: fold_body(counts, refs),
        grid=(WIDTH // wide,),
        out_shape=tuple(shape((16, size, WIDTH), LOW) for size in sizes),
        in_specs=[block(*come.shape[:-1]) for come in operands],
        out_specs=tuple(block(16, size) for size in sizes),
        compiler_params=params(56),
        cost_estimate=cost(4 * SHARE),
        name="ring_fold",
    )(*operands)


def final_body(layouts, refs):
    r = iter(refs)
    arrays = [next(r) for _ in layouts]
    own_w_ref, own_vec_ref = next(r), next(r)
    qkv_ref, out_ref, up_ref, down_ref = next(r), next(r), next(r), next(r)
    prompt_ref, gain_ref, bias_ref, up_bias_ref = next(r), next(r), next(r), next(r)
    pieces = []
    for array, layout in zip(arrays, layouts):
        total = array[0].astype(FULL)
        for way in range(1, 16):
            total = total + array[way].astype(FULL)
        at = 0
        for entry in layout:
            pieces.append((entry[:3], total[at : at + entry[3]]))
            at += entry[3]
    small = None
    wholes = [jnp.zeros((6, 1), FULL)] * 2
    for (kind, layer, part), piece in pieces:
        columns = slice(part * WIDTH, (part + 1) * WIDTH)
        if kind == "qkv":
            qkv_ref[:, layer, columns] = piece
            weight = own_w_ref[layer, :, columns].astype(FULL)
            wholes[layer] = wholes[layer] + jnp.sum(piece * weight, -1, keepdims=True)
        elif kind == "out":
            out_ref[:, layer, :] = piece
        elif kind == "up":
            up_ref[:, layer, columns] = piece
        elif kind == "down":
            down_ref[layer] = piece
        elif kind == "small":
            small = jnp.concatenate([piece[:, 128 * i : 128 * (i + 1)] for i in range(6)], 0)
        else:
            up_bias_ref[0:1] = piece[:, 0:24]
            up_bias_ref[1:2] = piece[:, 24:48]
    turn = lambda values: jnp.concatenate([values, jnp.zeros((2, 128), FULL)], 0).T
    rows = turn(small)
    for layer in range(2):
        prompt_ref[:, layer, :] = small[:, 56 * layer : 56 * layer + PROMPTS]
        at = 112 + 8 * layer
        part = rows[at : at + 8, 0:6]
        whole = turn(jnp.broadcast_to(wholes[layer], (6, 128)))[0:1, 0:6]
        gain, shift = own_vec_ref[layer, 0:1], own_vec_ref[layer, 1:2]
        gain_ref[layer, 0:1] = (whole - shift * part[6:7]) / gain
        gain_ref[layer, 1:2] = part[1:2]
        for place, source in enumerate((6, 4, 5, 3, 2, 0)):
            bias_ref[place, layer : layer + 1] = part[source : source + 1]


def final_call(arrays, layouts, own_w, own_vec):
    operands = [*arrays, own_w, own_vec]
    outs = (
        shape((6, 2, 3 * WIDTH)),
        shape((6, 2, WIDTH)),
        shape((6, 2, HIDDEN)),
        shape((2, 24, WIDTH)),
        shape((6, 2, PROMPTS)),
        shape((2, 2, 6)),
        shape((6, 2, 6)),
        shape((2, 24)),
    )
    body = lambda moves, refs: final_body(layouts, refs)
    return run(body, operands, [VM] * len(operands), outs, "final_fold", 3)


def per_device(
    patches,
    cls_tokens,
    segments,
    prompts,
    w_qkv,
    w_out,
    w_up,
    w_down,
    norm_gains,
    biases,
    up_bias,
    cot_patches,
    cot_cls,
):
    layers = 2
    weights = (w_qkv, w_out, w_up, w_down)
    pad_cls = lambda rows: jnp.pad(rows[0], ((0, 16 - CLS), (0, 0)))
    segs = segments.astype(FULL)
    query_ids = jnp.concatenate([segs[0], jnp.arange(CLS, dtype=FULL), jnp.full((6,), -5.0, FULL)])
    query_seg = jnp.broadcast_to(query_ids[:, None], (OWN, 128))
    first_seq = (lax.axis_index("seq") == 0).astype(FULL).reshape(1, 1)
    prompt_rows = jnp.pad(prompts.astype(FULL), ((0, 0), (0, 64 - PROMPTS), (0, 0)))
    vecs = []
    for layer in range(layers):
        following = min(layer + 1, layers - 1)
        vecs.append(
            jnp.concatenate(
                [
                    norm_gains[layer],
                    biases[layer],
                    norm_gains[following, 0:1],
                    biases[following, 0:1],
                    jnp.zeros((6, WIDTH), FULL),
                ],
                0,
            )
        )
    up_rows = [jnp.broadcast_to(up_bias[layer], (8, HIDDEN)) for layer in range(layers)]
    orders = [
        owner_order(RINGS[0]),
        owner_order(RINGS[1], RINGS[1][:1]),
        owner_order(RINGS[0], RINGS[0][:1]),
    ]
    steps = jnp.arange(6, dtype=jnp.int32)
    one_hot = lambda wanted, size: (wanted[:, None] == jnp.arange(size)[None, :]).astype(LOW)
    picks = [one_hot((order[:, None] * 6 + steps).reshape(-1), WIDTH) for order in orders]
    small_pick = one_hot((orders[1][None, :] * 6 + steps[:, None]).reshape(-1), WIDTH)
    small_spot = one_hot(orders[1], 128)

    seq = lax.axis_index("seq").astype(jnp.int32).reshape(1, 1)
    x, payload, own = open_call(
        patches[0], pad_cls(cls_tokens), segs, norm_gains[0, 0:1], biases[0, 0:1]
    )
    key_seg = None
    kept = []
    lefts = []
    factors = []
    left_plans = (
        (("mid", 0), ("att", 0), ("mid", 1)),
        (("mid", 0), ("mid", 1), ("att", 1)),
    )
    def left_factors(layer, *behind):
        normed_all, att, nmid, active = factors[layer]
        tall, tall_other, wide, wide_other = left_call(
            left_plans[layer], orders[2 - 2 * layer], (picks[2 - 2 * layer], picks[1]), normed_all, att, after(nmid, *behind), active
        )
        return (tall, send(tall_other, "core", 1), wide, send(wide_other, "core", 1))

    for layer in range(layers):
        last = layer == layers - 1
        come = swap_rows(payload)
        if layer > 0:
            x = after(x, lefts[0][0], lefts[0][2])
        out = forward_call(
            layer, last, x, come, own, prompt_rows[layer], vecs[layer], up_rows[layer],
            query_seg, key_seg, weights,
        )
        q, k, v, normed_all, att, lse, mid, nmid, slope, active, x_next = out[:11]
        kept.append((x, q, k, v, lse, mid, slope))
        payload, own = out[11:13]
        if layer == 0:
            key_seg = out[13]
        x = x_next
        factors.append((normed_all, att, nmid, active))
        if layer == 0:
            lefts.append(left_factors(0))
    out_patch, out_cls = payload, own

    def back_mlp(layer, start):
        mid, slope = kept[layer][5:7]
        return back_mlp_call(
            layer, layer == layers - 1, start, first_seq, mid, slope, vecs[layer], weights
        )

    def back_att(layer, rows, datt, small=()):
        return back_att_call(
            layer, first_seq, rows, datt, kept[layer][1:5], prompt_rows[layer], vecs[layer],
            query_seg, key_seg, small, weights[0],
        )

    def both(values):
        return (values, send(values, "core", 1))

    def both_parts(parts):
        return (*parts, *[send(part, "core", 1) for part in parts])

    def give_back(layer, pays, qpart, mid_grad):
        return (swap_rows(pays), qpart, kept[layer][0], mid_grad, vecs[layer])

    arrived = [[], []]

    def start_ring(at, made, rows):
        pieces, ring_at = made[at], at % 2
        axis = RINGS[ring_at][0]
        if at == 0:
            come = deal_out(pieces, (axis,))
        else:
            come = [pieces[0]] + [send(pieces[step], axis, step) for step in range(1, 4)]
        arrived[ring_at].append((come, rows))

    tile = HALF // 4
    mid_at = 2 * WIDTH
    start = (cot_patches[0], pad_cls(cot_cls), key_seg, query_seg)
    *packed, datt, mid_grad, rows, up_row_1 = back_mlp(1, start)
    grads = both_parts(packed)
    out = back_att(1, rows, after(datt, *lefts[0]))
    dq, dkv, prompts_1, rows_1 = out[0], out[2], out[4], out[5]
    dqs, dkvs = both(dq), both(dkv)
    start = give_back(1, out[3], out[1], mid_grad)
    lefts.append(left_factors(1, dkv))
    plan = [("down", 0, 0, 0, 0)]
    plan += [("up", part, mid_at, 0, HALF + part * tile) for part in range(2)]
    made = mlp_call(plan, ((0, HALF + 2 * tile),), lefts[1][0:2], grads)
    plan = [("q", None, 1, 0), ("k", None, 1, tile), ("v", None, 1, 2 * tile)]
    plan += [("out", mid_at + 2 * HALF, 1, 3 * tile)]
    plan += [(part, mid_at + HALF, 1, (2 + part) * tile) for part in range(2, 4)]
    talls = (after(lefts[1][0], made[0]), lefts[1][1])
    mixed = mixed_call(plan, ((1, 6 * tile),), seq, talls, lefts[1][2:], dqs, dkvs, grads)
    start_ring(0, made, (HALF, tile, tile))
    start_ring(1, mixed, (tile,) * 6)

    start = (after(start[0], mixed[1][0]), *start[1:])
    *packed, datt, mid_grad, rows, up_row_0 = back_mlp(0, start)
    grads = both_parts(packed)
    ups = [row[0].reshape(128, 24) for row in (up_row_0, up_row_1)]
    ups = jnp.pad(jnp.concatenate(ups, 1), ((0, 0), (0, 80)))
    small = (small_pick, small_spot, prompts_1, rows_1, ups)
    out = back_att(0, rows, datt, small)
    dq, dkv = out[0], out[2]
    plan = [("down", 0, 0, 2, 0), ("out", 0, mid_at + HALF, 2, HALF), ("up", 0, mid_at, 2, HALF + tile)]
    plan += [("up", part, mid_at + 2 * HALF, 1, (part - 1) * tile) for part in range(1, 4)]
    talls = (after(lefts[0][0], dkv, *arrived[1][0][0]), lefts[0][1])
    made = mlp_call(plan, ((2, HALF + 2 * tile), (1, 3 * tile)), talls, grads, 60)
    start_ring(2, made, (HALF, tile, tile))
    start_ring(1, made, (tile,) * 3)
    dqs, dkvs = both(dq), both(dkv)
    small = (out[4], send(out[5], "core", 1))
    plan = [("q", None, 1, 0), ("k", None, 1, tile), ("v", None, 1, 2 * tile)]
    talls = (after(lefts[0][0], made[1][0]), lefts[0][1])
    mixed = mixed_call(
        plan, ((1, 3 * tile + 32),), seq, talls, lefts[0][2:], dqs, dkvs, grads, small
    )
    start_ring(1, mixed, (tile,) * 3 + (16, 16))
    start = give_back(0, out[3], out[1], mid_grad)
    start = (after(start[0], mixed[1][0]), *start[1:])
    grad_patch, grad_cls = close_call(start)

    lasts = [deal_out(part, axes[1:]) for part, axes in zip(fold_call(arrived), RINGS)]
    layouts = (
        [("down", 1, 0, 24), ("up", 1, 0, 6), ("up", 1, 1, 6)]
        + [("down", 0, 0, 24), ("out", 0, 0, 6), ("up", 0, 0, 6)],
        [("qkv", 1, part, 6) for part in range(3)]
        + [("out", 1, 0, 6), ("up", 1, 2, 6), ("up", 1, 3, 6)]
        + [("up", 0, part, 6) for part in range(1, 4)]
        + [("qkv", 0, part, 6) for part in range(3)]
        + [("small", 0, 0, 1), ("bias", 0, 0, 1)],
    )
    here = lax.axis_index("dp") * 8 + lax.axis_index("seq")
    mine_of = lambda values, axis: lax.dynamic_slice_in_dim(values, here * 6, 6, axis)
    own_vec = jnp.stack([mine_of(norm_gains, 2)[:, 0], mine_of(biases, 2)[:, 0]], 1)
    done = final_call(lasts, layouts, mine_of(w_qkv, 1), own_vec)
    swap = lambda values: jnp.transpose(values, (1, 0, 2))
    return (
        out_patch[None],
        swap(out_cls),
        grad_patch[None],
        swap(grad_cls),
        jnp.transpose(done[4], (1, 2, 0)),
        swap(done[0]),
        swap(done[1]),
        swap(done[2]),
        done[3],
        done[5],
        swap(done[6]),
        done[7],
    )


def solution(mesh):
    placed = (
        P("dp", "seq", None),
        P("dp", None, None),
        P("dp", "seq"),
        P(),
        P(),
        P(),
        P(),
        P(),
        P(),
        P(),
        P(),
        P("dp", "seq", None),
        P("dp", None, None),
    )
    return jax.shard_map(
        per_device,
        mesh=mesh,
        in_specs=placed,
        out_specs=(
            P("dp", "seq", None),
            P("dp", None, None),
            P("dp", "seq", None),
            P("dp", None, None),
            P(None, None, ("dp", "seq")),
            P(None, ("dp", "seq"), None),
            P(None, ("dp", "seq"), None),
            P(None, ("dp", "seq"), None),
            P(None, ("dp", "seq"), None),
            P(None, None, ("dp", "seq")),
            P(None, None, ("dp", "seq")),
            P(None, ("dp", "seq")),
        ),
        check_vma=False,
    )
```

```python
import functools

import jax
import jax.numpy as jnp
from jax import lax
from jax.experimental import pallas as pl
from jax.experimental.pallas import tpu as pltpu
from jax.sharding import PartitionSpec as P

HEADS = 12
HEAD = 64
WIDTH = 768
HIDDEN = 3072
PATCHES = 128
CLS = 10
PROMPTS = 50
OWN = 144
KEYS = 1152
CLS_AT = 1024
PROMPT_AT = 1040
FRONT = 128
BLOCKS = 8
PAY = 864
PACKED = 2 * WIDTH + HIDDEN
HALF = WIDTH // 2
TILE = 256
LOW = jnp.bfloat16
FULL = jnp.float32

eps_norm = 1e-06
penalty_rate = 2.0
big_negative = -1e30

AXES = ("dp", "seq")
SPAN = {"core": 2, "x": 4, "y": 4, "z": 4}
RINGS = (("y", "z", "x"), ("z", "y", "x"))
ANY = pl.BlockSpec(memory_space=pl.ANY)
VM = "whole"
SM = pl.BlockSpec(memory_space=pltpu.SMEM)


def place_of(device):
    dp, seq = device // 8, device % 8
    return {"core": dp % 2, "x": dp // 2 % 2 * 2 + seq // 4, "y": dp // 4, "z": seq % 4}


def device_of(place):
    dp = (place["y"] * 2 + place["x"] // 2) * 2 + place["core"]
    return dp * 8 + place["x"] % 2 * 4 + place["z"]


def moved(axis, step):
    pairs = []
    for device in range(128):
        place = place_of(device)
        place[axis] = (place[axis] + step) % SPAN[axis]
        pairs.append((device, device_of(place)))
    return pairs


def send(values, axis, step):
    return lax.ppermute(values, AXES, moved(axis, step))


def groups_of(axes):
    found = {}
    for device in range(128):
        place = place_of(device)
        rest = tuple(place[axis] for axis in SPAN if axis not in axes)
        found.setdefault(rest, []).append((tuple(place[axis] for axis in axes), device))
    return [[device for _, device in sorted(group)] for group in found.values()]


def deal_out(values, axes):
    return lax.all_to_all(
        values, AXES, 0, 0, tiled=True, axis_index_groups=groups_of(axes)
    )


def swap_rows(values):
    return lax.all_to_all(values, "seq", 0, 0, tiled=True)


def owner_order(axes, steps=()):
    here = place_of(lax.axis_index("dp") * 8 + lax.axis_index("seq"))
    rest = jnp.arange(128, dtype=jnp.int32)
    place = {}
    for axis in reversed(axes):
        place[axis] = rest % SPAN[axis]
        if axis in steps:
            place[axis] = (here[axis] + place[axis]) % SPAN[axis]
        rest = rest // SPAN[axis]
    place["core"] = (here["core"] + rest) % 2
    return device_of(place)


def nn(left, right):
    return lax.dot_general(left, right, (((1,), (0,)), ((), ())), preferred_element_type=FULL)


def nt(left, right):
    return lax.dot_general(left, right, (((1,), (1,)), ((), ())), preferred_element_type=FULL)


def plain_norm(values):
    centred = values - jnp.mean(values, -1, keepdims=True)
    scale = lax.rsqrt(jnp.mean(centred * centred, -1, keepdims=True) + eps_norm)
    return centred * scale, scale


def norm_pull(plain, scale, gain, upstream):
    inner = upstream * gain
    return scale * (
        inner
        - jnp.mean(inner, -1, keepdims=True)
        - plain * jnp.mean(inner * plain, -1, keepdims=True)
    )


def whole(dims):
    return pl.BlockSpec(dims, lambda i: (0,) * len(dims))


class Late:
    def __init__(self, index=None, cuts=1, axis=0):
        self.index, self.cuts, self.axis = index, cuts, axis


class Early:
    def __init__(self, dims, kind=FULL):
        self.shape, self.dtype = dims, kind


class Moves:
    def __init__(self):
        self.ins, self.outs, self.gone = {}, {}, []

    def start(self, *refs):
        for ref in refs:
            for copy in self.ins[id(ref)]:
                copy.start()

    def resident(self):
        part = Moves()
        part.start = part.wait = lambda *_: None
        part.flush = self.flush
        return part

    def wait(self, ref, piece=None):
        copies = self.ins[id(ref)]
        for copy in copies if piece is None else copies[piece : piece + 1]:
            copy.wait()

    def flush(self, *refs):
        for ref in refs:
            copy = self.outs.pop(id(ref), None)
            if copy is not None:
                copy.start()
                self.gone.append(copy)

    def close(self):
        for copy in self.outs.values():
            copy.start()
        for copy in [*self.gone, *self.outs.values()]:
            copy.wait()


def run(body, operands, specs, outs, name, micros, scratch=(), mib=56):
    late = [(at, spec) for at, spec in enumerate(specs) if isinstance(spec, Late)]
    early = [(at, out) for at, out in enumerate(outs) if isinstance(out, Early)]
    buffers, total = [], 0
    for at, spec in late:
        dims = operands[at].shape if spec.index is None else operands[at].shape[1:]
        buffers.append(pltpu.VMEM(dims, operands[at].dtype))
        total += spec.cuts
    buffers += [pltpu.VMEM(out.shape, out.dtype) for _, out in early]
    total += len(early)

    def kernel(*refs):
        refs = list(refs)
        first = len(operands) + len(outs) + len(scratch)
        space, sems = refs[first : first + len(buffers)], refs[-1]
        moves, sem = Moves(), 0
        for (at, spec), buffer in zip(late, space):
            source = refs[at] if spec.index is None else refs[at].at[spec.index]
            size = buffer.shape[spec.axis] // spec.cuts
            copies = []
            for piece in range(spec.cuts):
                part = pl.ds(piece * size, size)
                view = lambda ref: ref.at[part] if spec.axis == 0 else ref.at[:, part]
                pair = (source, buffer) if spec.cuts == 1 else (view(source), view(buffer))
                copies.append(pltpu.make_async_copy(*pair, sems.at[sem]))
                sem += 1
            moves.ins[id(buffer)] = copies
            refs[at] = buffer
        for (at, out), buffer in zip(early, space[len(late) :]):
            at += len(operands)
            moves.outs[id(buffer)] = pltpu.make_async_copy(buffer, refs[at], sems.at[sem])
            sem += 1
            refs[at] = buffer
        body(moves, refs[:first])
        moves.close()

    in_specs = []
    for operand, spec in zip(operands, specs):
        if isinstance(spec, Late):
            in_specs.append(ANY)
        else:
            in_specs.append(whole(operand.shape) if spec == "whole" else spec)
    return pl.pallas_call(
        kernel,
        grid=(1,),
        out_shape=tuple(shape(out.shape, out.dtype) for out in outs),
        in_specs=in_specs,
        out_specs=tuple(ANY if isinstance(out, Early) else whole(out.shape) for out in outs),
        scratch_shapes=[*scratch, *buffers, pltpu.SemaphoreType.DMA((max(total, 1),))],
        compiler_params=params(mib),
        cost_estimate=cost(micros),
        name=name,
    )(*operands)


def after(values, *others):
    return lax.optimization_barrier((values, others))[0]


def tile_at(index, size):
    return pl.ds(pl.multiple_of(index * size, size), size)


def params(mib=56):
    return pltpu.CompilerParams(vmem_limit_bytes=mib * 2**20)


SHARE = 1.0
ATT = 6
LEFT = 0.1
MIX = 0.1
BMLP = 10
TURN = 40
FOLD = 4
MLP1 = 0.1


def cost(micros):
    return pl.CostEstimate(flops=int(micros * 1.1e9), bytes_accessed=1 << 20, transcendentals=0)


def shape(dims, kind=FULL):
    return jax.ShapeDtypeStruct(dims, kind)


def open_body(patch_ref, cls_ref, seg_ref, gain_ref, bias_ref, x_ref, pay_ref, own_ref, query_ref):
    x_ref[0:PATCHES] = patch_ref[0].astype(FULL)
    cls_rows = jnp.concatenate([cls_ref[0].astype(FULL), jnp.zeros((16 - CLS, WIDTH), FULL)], 0)
    x_ref[PATCHES:OWN] = cls_rows
    plain, _ = plain_norm(x_ref[...])
    normed = (plain * gain_ref[0, 0:1] + bias_ref[0, 0:1]).astype(LOW)
    own_ref[...] = normed
    segs = seg_ref[...].astype(FULL)
    last = jnp.broadcast_to(segs, (16, PATCHES)).astype(LOW)
    last = jnp.concatenate([last, jnp.zeros((16, WIDTH - PATCHES), LOW)], 1)
    for block in range(BLOCKS):
        pay_ref[block, 0:PATCHES] = normed[0:PATCHES]
        pay_ref[block, PATCHES:OWN] = last
    query_ref[0:PATCHES] = jnp.broadcast_to(segs, (PATCHES, PATCHES)).T
    row = lax.broadcasted_iota(jnp.int32, (16, 128), 0)
    query_ref[PATCHES:OWN] = jnp.where(row < CLS, row, -5).astype(FULL)


def open_call(patches, cls_tokens, segments, gains, biases):
    outs = (
        shape((OWN, WIDTH)),
        shape((BLOCKS, OWN, WIDTH), LOW),
        shape((OWN, WIDTH), LOW),
        shape((OWN, 128)),
    )
    operands = (patches, cls_tokens, segments, gains, biases)
    return run(lambda moves, refs: open_body(*refs), operands, [VM] * 5, outs, "open_norm", 2)


def seen_mask(key_ref, query_ref, mask_ref):
    keys = key_ref[0:1, :]
    seen = (keys == query_ref[:, 0:1]) | (keys == -1.0)
    mask_ref[...] = jnp.where(seen, 0.0, big_negative)


def half_lanes(rows):
    return lax.broadcasted_iota(jnp.int32, (rows, 2 * HEAD), 1) < HEAD


def two_heads(rows, lower):
    none = jnp.zeros_like(rows)
    return jnp.concatenate([jnp.where(lower, rows, none), jnp.where(lower, none, rows)], 0)


def split_rows(rows, patch_ref, cls_ref):
    patch_ref[...] = rows[0:PATCHES]
    for place in range(CLS):
        cls_ref[place] = rows[PATCHES + place : PATCHES + place + 1]


def forward_body(layer, last, moves, refs):
    first = layer == 0
    r = iter(refs)
    nxt = lambda: next(r)
    x_ref = nxt()
    come_ref = nxt()
    own_ref, prompt_ref, vec_ref, up_bias_ref, query_seg_ref = nxt(), nxt(), nxt(), nxt(), nxt()
    key_in_ref = None if first else nxt()
    wqkv, wout, wup, wdown = nxt(), nxt(), nxt(), nxt()
    q_ref, k_ref, v_ref, all_ref = nxt(), nxt(), nxt(), nxt()
    att_ref, lse_ref, mid_ref, nmid_ref = nxt(), nxt(), nxt(), nxt()
    slope_ref, active_ref, out_ref = nxt(), nxt(), nxt()
    next_ref, next_own_ref = nxt(), nxt()
    key_ref = nxt() if first else key_in_ref
    mask_ref = nxt()
    if first:
        seg_ref = nxt()
    block_sems = nxt()

    steps = []
    for block in range(BLOCKS):
        source = come_ref.at[block]
        steps.append(
            pltpu.make_async_copy(
                source.at[pl.ds(0, PATCHES)],
                all_ref.at[pl.ds(block * PATCHES, PATCHES)],
                block_sems.at[block],
            )
        )
        if first:
            steps.append(
                pltpu.make_async_copy(
                    source.at[pl.ds(PATCHES, 16), pl.ds(0, PATCHES)],
                    seg_ref.at[block],
                    block_sems.at[BLOCKS + block],
                )
            )
    for step in steps:
        step.start()
    moves.start(wqkv)

    gain_one, bias_one = vec_ref[0:1], vec_ref[2:3]
    gain_two, bias_two = vec_ref[1:2], vec_ref[6:7]

    plain, _ = plain_norm(prompt_ref[...])
    all_ref[CLS_AT:PROMPT_AT] = own_ref[PATCHES:OWN]
    all_ref[PROMPT_AT : PROMPT_AT + 64] = (plain * gain_one + bias_one).astype(LOW)
    all_ref[PROMPT_AT + 64 : KEYS] = jnp.zeros((KEYS - PROMPT_AT - 64, WIDTH), LOW)
    for step in steps:
        step.wait()
    moves.flush(all_ref)
    if first:
        lane = lax.broadcasted_iota(jnp.int32, (8, FRONT), 1)
        front = jnp.where(
            lane < CLS, lane, jnp.where((lane >= 16) & (lane < 16 + PROMPTS), -1, -2)
        )
        for block in range(BLOCKS):
            key_ref[:, block * PATCHES : (block + 1) * PATCHES] = seg_ref[block].astype(FULL)[0:8]
        key_ref[:, CLS_AT:KEYS] = front.astype(FULL)
    seen_mask(key_ref, query_seg_ref, mask_ref)

    def keys(tile, carry):
        at = tile_at(tile, TILE)
        rows = nn(all_ref[...], wqkv[:, pl.ds(pl.multiple_of(WIDTH + tile * TILE, TILE), TILE)])
        k_ref[:, at] = rows.astype(LOW)
        return carry

    def values(tile, carry):
        at = tile_at(tile, TILE)
        rows = nn(all_ref[...], wqkv[:, pl.ds(pl.multiple_of(2 * WIDTH + tile * TILE, TILE), TILE)])
        v_ref[:, at] = (rows + vec_ref[4:5, at]).astype(LOW)
        return carry

    def queries(tile, carry):
        at = tile_at(tile, TILE)
        rows = nn(own_ref[...], wqkv[:, at]) + vec_ref[3:4, at]
        q_ref[:, at] = (rows.astype(LOW).astype(FULL) * HEAD**-0.5).astype(LOW)
        return carry

    moves.wait(wqkv, 0)
    lax.fori_loop(0, 3, queries, 0, unroll=3)
    moves.wait(wqkv, 1)
    moves.start(wout, wup)
    lax.fori_loop(0, 3, keys, 0, unroll=3)
    moves.flush(k_ref)
    moves.wait(wqkv, 2)
    lax.fori_loop(0, 3, values, 0, unroll=3)
    moves.flush(v_ref)
    moves.start(wdown)

    lse_ref[...] = jnp.zeros((OWN, 128), FULL)
    lower = half_lanes(OWN)
    lane = lax.broadcasted_iota(jnp.int32, (OWN, 128), 1)

    def heads(pair, carry):
        at = tile_at(pair, 2 * HEAD)
        query, key, value = q_ref[:, at], k_ref[:, at], v_ref[:, at]
        outs = []
        for side in range(2):
            mine = lower if side == 0 else ~lower
            scores = nt(jnp.where(mine, query, jnp.zeros_like(query)), key) + mask_ref[...]
            top = jnp.max(scores, -1, keepdims=True)
            raised = jnp.exp(scores - top)
            total = jnp.sum(raised, -1, keepdims=True)
            outs.append(nn(raised.astype(LOW), value) / total)
            lane = lax.broadcasted_iota(jnp.int32, (OWN, 128), 1)
            lse_ref[...] = jnp.where(lane == 2 * pair + side, top + jnp.log(total), lse_ref[...])
        att_ref[:, at] = jnp.where(lower, outs[0], outs[1]).astype(LOW)
        return carry

    lax.fori_loop(0, HEADS // 2, heads, 0, unroll=2)

    moves.wait(wout)

    def project(tile, carry):
        at = tile_at(tile, TILE)
        mid_ref[:, at] = x_ref[:, at] + (nn(att_ref[...], wout[:, at]) + vec_ref[5:6, at])
        return carry

    lax.fori_loop(0, 3, project, 0, unroll=3)
    plain, _ = plain_norm(mid_ref[...])
    nmid_ref[...] = (plain * gain_two + bias_two).astype(LOW)
    moves.wait(wup)

    def rise(tile, carry):
        at = tile_at(tile, TILE)
        hidden = nn(nmid_ref[...], wup[:, at]) + up_bias_ref[0:1, at]
        share = 0.5 * (1.0 + lax.erf(hidden * 0.7071067811865476))
        active_ref[:, at] = (hidden * share).astype(LOW)
        slope_ref[:, at] = share + hidden * (0.3989422804014327 * jnp.exp(-0.5 * hidden * hidden))
        return carry

    lax.fori_loop(0, HIDDEN // TILE, rise, 0, unroll=4)
    moves.flush(slope_ref, active_ref)
    moves.wait(wdown)

    def lower_back(tile, carry):
        at = tile_at(tile, TILE)
        out_ref[:, at] = mid_ref[:, at] + (nn(active_ref[...], wdown[:, at]) + vec_ref[7:8, at])
        return carry

    lax.fori_loop(0, 3, lower_back, 0, unroll=3)
    if not last:
        plain, _ = plain_norm(out_ref[...])
        normed = (plain * vec_ref[8:9] + vec_ref[9:10]).astype(LOW)
        next_own_ref[...] = normed
        for block in range(BLOCKS):
            next_ref[block] = normed[0:PATCHES]
    else:
        split_rows(out_ref[...], next_ref, next_own_ref)


def forward_call(layer, last, x, come, own, prompt, vec, up_bias, query_seg, key_seg, weights):
    first = layer == 0
    outs = [
        shape((OWN, WIDTH), LOW),
        Early((KEYS, WIDTH), LOW),
        Early((KEYS, WIDTH), LOW),
        Early((KEYS, WIDTH), LOW),
        shape((OWN, WIDTH), LOW),
        shape((OWN, 128)),
        shape((OWN, WIDTH)),
        shape((OWN, WIDTH), LOW),
        Early((OWN, HIDDEN)),
        Early((OWN, HIDDEN), LOW),
        shape((OWN, WIDTH)),
    ]
    if last:
        outs += [shape((PATCHES, WIDTH)), shape((CLS, 1, WIDTH))]
    else:
        outs += [shape((BLOCKS, PATCHES, WIDTH), LOW), shape((OWN, WIDTH), LOW)]
    if first:
        outs += [shape((8, KEYS))]
    operands = [x, come, own, prompt, vec, up_bias, query_seg]
    specs = [VM, ANY] + [VM] * 5
    if not first:
        operands.append(key_seg)
        specs.append(VM)
    operands += weights
    specs += [Late(layer, 3, 1), Late(layer), Late(layer), Late(layer)]
    scratch = [pltpu.VMEM((OWN, KEYS), FULL)]
    if first:
        scratch.append(pltpu.VMEM((BLOCKS, 16, PATCHES), LOW))
    scratch += [pltpu.SemaphoreType.DMA((2 * BLOCKS,))]
    body = lambda moves, refs: forward_body(layer, last, moves, refs)
    return run(body, operands, specs, outs, "forward_layer", 24 * SHARE, scratch)


def gathered_pull(come_ref, qpart_ref, x_ref, gain, mid_grad_ref):
    total = come_ref[0].astype(FULL)
    for block in range(1, BLOCKS):
        total = total + come_ref[block].astype(FULL)
    patch_part = total[0:WIDTH].T
    cls_part = jnp.concatenate(
        [total[WIDTH + 16 * lane : WIDTH + 16 * (lane + 1)] for lane in range(6)], 1
    )
    d_normed = jnp.concatenate([patch_part, cls_part], 0) + qpart_ref[...]
    plain, scale = plain_norm(x_ref[...])
    return mid_grad_ref[...] + norm_pull(plain, scale, gain, d_normed)


def row_share(first_ref):
    row = lax.broadcasted_iota(jnp.int32, (OWN, 1), 0)
    return jnp.where(row < PATCHES, 1.0, jnp.where(row < PATCHES + CLS, first_ref[0, 0], 0.0))


def back_mlp_body(last, moves, refs):
    r = iter(refs)
    nxt = lambda: next(r)
    if last:
        cot_ref, cot_cls_ref, key_ref, query_seg_ref = nxt(), nxt(), nxt(), nxt()
    else:
        come_ref = nxt()
        up_qpart_ref, up_x_ref, up_mid_grad_ref, up_vec_ref = nxt(), nxt(), nxt(), nxt()
    first_ref, mid_ref, slope_ref, vec_ref = nxt(), nxt(), nxt(), nxt()
    wout, wup, wdown = nxt(), nxt(), nxt()
    grad_refs = nxt(), nxt()
    datt_ref, mid_grad_ref = nxt(), nxt()
    rows_ref, up_spot_ref = nxt(), nxt()
    up_ref, low_ref, hid_ref, up_row_ref = nxt(), nxt(), nxt(), nxt()

    moves.start(wdown, slope_ref)
    gain_two = vec_ref[1:2]
    share = row_share(first_ref)
    if last:
        valid = ((query_seg_ref[...] < CLS) & (query_seg_ref[...] >= 0)).astype(FULL)
        up_ref[0:PATCHES] = cot_ref[...].astype(FULL) * valid[0:PATCHES, 0:1]
        hits = (key_ref[0:1, 0:CLS_AT] == query_seg_ref[PATCHES:OWN, 0:1]).astype(FULL)
        present = jnp.max(hits, -1, keepdims=True)
        cls_rows = [cot_cls_ref[...].astype(FULL), jnp.zeros((16 - CLS, WIDTH), FULL)]
        up_ref[PATCHES:OWN] = jnp.concatenate(cls_rows, 0) * present
    else:
        up_ref[...] = gathered_pull(
            come_ref, up_qpart_ref, up_x_ref, up_vec_ref[0:1], up_mid_grad_ref
        )
    low_ref[...] = up_ref[...].astype(LOW)
    weighted = low_ref[...].astype(FULL) * share
    grad_refs[0][:, 0:WIDTH] = weighted.astype(LOW)
    rows_ref[...] = jnp.zeros((8, WIDTH), FULL)
    rows_ref[0:1] = jnp.sum(weighted, 0, keepdims=True)
    moves.start(wup)

    def to_hidden(half, tile, carry):
        at = tile_at(tile, TILE)
        grad = (nt(low_ref[...], wdown[at, :]) * slope_ref[:, at]).astype(LOW)
        hid_ref[:, at] = grad
        counted = grad.astype(FULL) * share
        to = WIDTH + tile * TILE - half * (PACKED // 2)
        grad_refs[half][:, pl.ds(pl.multiple_of(to, TILE), TILE)] = counted.astype(LOW)
        up_row_ref[:, at] = jnp.broadcast_to(jnp.sum(counted, 0, keepdims=True), (8, TILE))
        return carry

    moves.wait(slope_ref)
    for piece in range(4):
        moves.wait(wdown, piece)
        body = functools.partial(to_hidden, piece // 2)
        lax.fori_loop(3 * piece, 3 * piece + 3, body, 0, unroll=3)
    moves.wait(wup)
    moves.start(wout)

    def to_mid(tile, carry):
        at = tile_at(tile, TILE)
        mid_grad_ref[:, at] = nt(hid_ref[...], wup[at, :])
        return carry

    lax.fori_loop(0, 3, to_mid, 0, unroll=3)
    d_normed = mid_grad_ref[...]
    plain, scale = plain_norm(mid_ref[...])
    counted = d_normed * share
    rows_ref[1:2] = jnp.sum(counted * plain, 0, keepdims=True)
    rows_ref[2:3] = jnp.sum(counted, 0, keepdims=True)
    mid_grad_ref[...] = up_ref[...] + norm_pull(plain, scale, gain_two, d_normed)
    low_ref[...] = mid_grad_ref[...].astype(LOW)
    weighted = low_ref[...].astype(FULL) * share
    grad_refs[1][:, PACKED // 2 - WIDTH :] = weighted.astype(LOW)
    rows_ref[3:4] = jnp.sum(weighted, 0, keepdims=True)
    moves.flush(*grad_refs)
    up_row = up_row_ref[0:1]
    spots = [up_row[:, 24 * spot : 24 * (spot + 1)] for spot in range(128)]
    up_spot_ref[...] = jnp.concatenate(spots, 0)
    moves.wait(wout)

    def to_att(tile, carry):
        at = tile_at(tile, TILE)
        datt_ref[:, at] = nt(low_ref[...], wout[at, :]).astype(LOW)
        return carry

    lax.fori_loop(0, 3, to_att, 0, unroll=3)


def back_mlp_call(layer, last, start, first_seq, mid, slope, vec, weights):
    operands = [*start, first_seq, mid, slope, vec, *weights[1:]]
    specs = [VM] * len(start) + [SM, VM, Late(), VM, Late(layer), Late(layer), Late(layer, 4)]
    outs = [
        Early((OWN, PACKED // 2), LOW),
        Early((OWN, PACKED // 2), LOW),
        shape((OWN, WIDTH), LOW),
        shape((OWN, WIDTH)),
        shape((8, WIDTH)),
        shape((128, 24)),
    ]
    scratch = [
        pltpu.VMEM((OWN, WIDTH), FULL),
        pltpu.VMEM((OWN, WIDTH), LOW),
        pltpu.VMEM((OWN, HIDDEN), LOW),
        pltpu.VMEM((8, HIDDEN), FULL),
    ]
    body = lambda moves, refs: back_mlp_body(last, moves, refs)
    return run(body, operands, specs, outs, "backward_mlp", BMLP, scratch)


def back_att_body(layer, moves, refs):
    r = iter(refs)
    nxt = lambda: next(r)
    first_ref, rows_in_ref, datt_ref = nxt(), nxt(), nxt()
    q_ref, k_ref, v_ref, lse_ref = nxt(), nxt(), nxt(), nxt()
    prompt_ref, vec_ref, query_seg_ref, key_ref = nxt(), nxt(), nxt(), nxt()
    if layer == 0:
        pick_ref, spot_ref, prompts_1, rows_1, up_0, up_1 = [nxt() for _ in range(6)]
    wqkv = nxt()
    dq_ref, qpart_ref, dkv_ref, pay_ref = nxt(), nxt(), nxt(), nxt()
    if layer == 0:
        small_refs = nxt(), nxt()
        dprompt_ref, rows_ref = nxt(), nxt()
    else:
        dprompt_ref, rows_ref = nxt(), nxt()
    mask_ref, dqf_ref, qt_ref, dat_ref, front_ref = [nxt() for _ in range(5)]

    moves.start(k_ref, v_ref, wqkv)
    gain_one = vec_ref[0:1]
    share = row_share(first_ref)
    seen_mask(key_ref, query_seg_ref, mask_ref)
    rows_ref[...] = rows_in_ref[...]

    def turn(tile, carry):
        at = tile_at(tile, TILE)
        dat_ref[at, :] = (datt_ref[:, at].astype(FULL) * share).T.astype(LOW)
        qt_ref[at, :] = (q_ref[:, at].astype(FULL) * share).T.astype(LOW)
        return carry

    lax.fori_loop(0, 3, turn, 0, unroll=3)
    lower = half_lanes(OWN)
    lane = lax.broadcasted_iota(jnp.int32, (OWN, 128), 1)
    moves.wait(k_ref)
    moves.wait(v_ref)

    def heads(pair, carry):
        at = tile_at(pair, 2 * HEAD)
        query, key, value, grad = q_ref[:, at], k_ref[:, at], v_ref[:, at], datt_ref[:, at]
        outs = []
        for side in range(2):
            mine = lower if side == 0 else ~lower
            head = 2 * pair + side
            log_total = jnp.sum(jnp.where(lane == head, lse_ref[...], 0.0), -1, keepdims=True)
            scores = nt(jnp.where(mine, query, jnp.zeros_like(query)), key) + mask_ref[...]
            probs = jnp.exp(scores - log_total)
            d_probs = nt(jnp.where(mine, grad, jnp.zeros_like(grad)), value)
            both = probs * d_probs
            across = jnp.sum(both, -1, keepdims=True)
            d_scores = (both - probs * across).astype(LOW)
            probs_low = probs.astype(LOW)
            outs.append(nn(d_scores, key))
            rows = tile_at(head, HEAD)
            dkv_ref[rows, :] = nn(qt_ref[rows, :], d_scores).astype(LOW)
            value_rows = pl.ds(pl.multiple_of(WIDTH + head * HEAD, HEAD), HEAD)
            dkv_ref[value_rows, :] = nn(dat_ref[rows, :], probs_low).astype(LOW)
        dqf_ref[:, at] = (jnp.where(lower, outs[0], outs[1]) * HEAD**-0.5).astype(LOW)
        return carry

    lax.fori_loop(0, HEADS // 2, heads, 0, unroll=2)
    moves.flush(dkv_ref)
    counted = dqf_ref[...].astype(FULL) * share
    dq_ref[...] = counted.astype(LOW)
    rows_ref[4:5] = jnp.sum(counted, 0, keepdims=True)
    moves.wait(wqkv)

    def to_normed(tile, carry):
        at = tile_at(tile, TILE)
        qpart_ref[:, at] = nt(dqf_ref[...], wqkv[at, 0:WIDTH])
        return carry

    lax.fori_loop(0, 3, to_normed, 0, unroll=3)

    front_ref[...] = nn(wqkv[:, WIDTH:], dkv_ref[:, CLS_AT:KEYS])
    shift = jnp.sum(front_ref[...], -1, keepdims=True)
    front = front_ref[...].T
    cls_rows = jnp.concatenate(
        [front[0:16, 128 * place : 128 * (place + 1)] for place in range(6)], 0
    )
    for block in range(0, BLOCKS, 2):
        part = nn(wqkv[:, WIDTH:], dkv_ref[:, block * PATCHES : (block + 2) * PATCHES])
        shift = shift + jnp.sum(part, -1, keepdims=True)
        for side in range(2):
            pay_ref[block + side, 0:WIDTH] = part[:, side * PATCHES : (side + 1) * PATCHES].astype(LOW)
            pay_ref[block + side, WIDTH:PAY] = cls_rows.astype(LOW)
    moves.flush(pay_ref)

    plain, scale = plain_norm(prompt_ref[...])
    d_prompt = norm_pull(plain, scale, gain_one, front[16:80])
    query_seg = query_seg_ref[0:PATCHES, 0:1]
    slots = jnp.sum((query_seg < CLS).astype(FULL), 0, keepdims=True)
    dprompt_ref[...] = d_prompt + (penalty_rate / 1024.0) * slots * prompt_ref[...]

    turned = jnp.broadcast_to(shift, (WIDTH, 128)).T
    rows_ref[6:7] = turned[0:1] + jnp.sum(qpart_ref[...] * share, 0, keepdims=True)
    totals = jnp.sum(dkv_ref[WIDTH : 2 * WIDTH].astype(FULL), -1, keepdims=True)
    rows_ref[5:6] = jnp.broadcast_to(totals, (WIDTH, 128)).T[0:1]
    if layer != 0:
        return
    joined = jnp.concatenate([dprompt_ref[0:56], prompts_1[0:56], rows_ref[...], rows_1[...]], 0)
    turned = nt(pick_ref[...], joined.astype(LOW))
    ups = [nn(spot_ref[...], up[...].astype(LOW)) for up in (up_0, up_1)]
    rows = jnp.concatenate([turned[128 * part : 128 * (part + 1)] for part in range(6)], 1)
    ups = jnp.concatenate([*ups, jnp.zeros((128, WIDTH - 48), FULL)], 1)
    for half in range(2):
        spots = slice(64 * half, 64 * (half + 1))
        small_refs[half][...] = jnp.concatenate([rows[spots], ups[spots]], 0).astype(LOW)


def back_att_call(layer, first_seq, rows, datt, saved, prompt, vec, query_seg, key_seg, small, weight):
    operands = [first_seq, rows, datt, *saved, prompt, vec, query_seg, key_seg, *small, weight]
    specs = [SM] + [VM] * 3 + [Late()] * 2 + [VM] * (5 + len(small)) + [Late(layer)]
    outs = [
        shape((OWN, WIDTH), LOW),
        shape((OWN, WIDTH)),
        Early((2 * WIDTH, KEYS), LOW),
        Early((BLOCKS, PAY, 128), LOW),
    ]
    if layer == 0:
        outs += [shape((128, WIDTH), LOW)] * 2
    outs += [shape((64, WIDTH)), shape((8, WIDTH))]
    scratch = [
        pltpu.VMEM((OWN, KEYS), FULL),
        pltpu.VMEM((OWN, WIDTH), LOW),
        pltpu.VMEM((WIDTH, OWN), LOW),
        pltpu.VMEM((WIDTH, OWN), LOW),
        pltpu.VMEM((WIDTH, FRONT), FULL),
    ]
    body = lambda moves, refs: back_att_body(layer, moves, refs)
    return run(body, operands, specs, outs, "backward_attention", ATT, scratch)


def turn_body(moves, refs):
    r = iter(refs)
    take = lambda count: [next(r) for _ in range(count)]
    x, come, own, prompt, vec, up_bias, query_seg, key = take(8)
    cots, first = take(2), next(r)
    wqkv, wout, wup, wdown = take(4)
    normed_all, att, nmid, active, out_patch, out_cls = take(6)
    grads, mid_grad, up_spot = take(2), next(r), next(r)
    dq, qpart, dkv, pay, dprompt, rows = take(6)
    q, k, v, lse, mid, slope, out, mask, block_sems = take(9)
    datt, rows_in, up, low, hid, up_row = take(6)
    dqf, qt, dat, front = take(4)
    forward_body(
        1, True, moves,
        [x, come, own, prompt, vec, up_bias, query_seg, key, wqkv, wout, wup, wdown]
        + [q, k, v, normed_all, att, lse, mid, nmid, slope, active, out, out_patch, out_cls]
        + [mask, block_sems],
    )
    still = moves.resident()
    back_mlp_body(
        True, still,
        [*cots, key, query_seg, first, mid, slope, vec, wout, wup, wdown]
        + [*grads, datt, mid_grad, rows_in, up_spot, up, low, hid, up_row],
    )
    back_att_body(
        1, still,
        [first, rows_in, datt, q, k, v, lse, prompt, vec, query_seg, key, wqkv]
        + [dq, qpart, dkv, pay, dprompt, rows, mask, dqf, qt, dat, front],
    )


def turn_call(x, come, own, prompt, vec, up_bias, query_seg, key_seg, cots, first_seq, weights):
    operands = [x, come, own, prompt, vec, up_bias, query_seg, key_seg, *cots, first_seq, *weights]
    specs = [VM, ANY] + [VM] * 8 + [SM, Late(1, 3, 1), Late(1), Late(1), Late(1)]
    outs = [
        Early((KEYS, WIDTH), LOW),
        shape((OWN, WIDTH), LOW),
        shape((OWN, WIDTH), LOW),
        Early((OWN, HIDDEN), LOW),
        shape((PATCHES, WIDTH)),
        shape((CLS, 1, WIDTH)),
        Early((OWN, PACKED // 2), LOW),
        Early((OWN, PACKED // 2), LOW),
        shape((OWN, WIDTH)),
        shape((128, 24)),
        shape((OWN, WIDTH), LOW),
        shape((OWN, WIDTH)),
        Early((2 * WIDTH, KEYS), LOW),
        Early((BLOCKS, PAY, 128), LOW),
        shape((64, WIDTH)),
        shape((8, WIDTH)),
    ]
    space = lambda *dims: pltpu.VMEM(dims, FULL)
    low = lambda *dims: pltpu.VMEM(dims, LOW)
    scratch = [low(OWN, WIDTH), low(KEYS, WIDTH), low(KEYS, WIDTH), space(OWN, 128)]
    scratch += [space(OWN, WIDTH), space(OWN, HIDDEN), space(OWN, WIDTH), space(OWN, KEYS)]
    scratch += [pltpu.SemaphoreType.DMA((2 * BLOCKS,))]
    scratch += [low(OWN, WIDTH), space(8, WIDTH), space(OWN, WIDTH), low(OWN, WIDTH)]
    scratch += [low(OWN, HIDDEN), space(8, HIDDEN), low(OWN, WIDTH), low(WIDTH, OWN)]
    scratch += [low(WIDTH, OWN), space(WIDTH, FRONT)]
    return run(turn_body, operands, specs, outs, "turn_layer", TURN, scratch)


def close_body(come_ref, qpart_ref, x_ref, mid_grad_ref, vec_ref, patch_ref, cls_ref):
    rows = gathered_pull(come_ref, qpart_ref, x_ref, vec_ref[0:1], mid_grad_ref)
    split_rows(rows, patch_ref, cls_ref)


def close_call(operands):
    outs = (shape((PATCHES, WIDTH)), shape((CLS, 1, WIDTH)))
    return run(lambda moves, refs: close_body(*refs), operands, [VM] * len(operands), outs, "close_norm", 2)


def left_body(plan, moves, refs):
    order_ref, *refs = refs
    picks, (all_ref, att_ref, mid_ref, active_ref) = refs[0:2], refs[2:6]
    tall_refs, wide_refs = refs[6:8], refs[8:10]
    turned_ref, down_ref = refs[10:12]

    def turn(tile, carry):
        at = tile_at(tile, TILE)
        turned_ref[at, :] = active_ref[:, at].astype(FULL).T
        return carry

    def move(spot, carry):
        source = pl.ds(pl.multiple_of(order_ref[spot] * 24, 8), 24)
        target = pl.ds(pl.multiple_of(spot * 24, 8), 24)
        down_ref[target, :] = turned_ref[source, :]
        return carry

    moves.start(all_ref)
    lax.fori_loop(0, HIDDEN // TILE, turn, 0)
    lax.fori_loop(0, 128, move, 0)
    for half in range(2):
        rows = slice(half * 2 * WIDTH, (half + 1) * 2 * WIDTH)
        tall_refs[half][0 : 2 * WIDTH, 0:OWN] = down_ref[rows].astype(LOW)
    row = 2 * WIDTH
    for kind, ring_at in plan:
        source = {"mid": mid_ref, "att": att_ref}[kind][...]
        turned = nt(picks[ring_at][...], source).astype(LOW)
        for half in range(2):
            tall_refs[half][row : row + HALF, 0:OWN] = turned[half * HALF : (half + 1) * HALF]
        row += HALF
    moves.flush(*tall_refs)
    moves.wait(all_ref)
    for half in range(2):
        wide = nt(picks[1][half * HALF : (half + 1) * HALF], all_ref[...])
        wide_refs[half][...] = wide.astype(LOW)


def left_call(plan, order, picks, normed_all, att, nmid, active):
    tall = (2 * WIDTH + len(plan) * HALF, 256)
    outs = [Early(tall, LOW)] * 2 + [shape((HALF, KEYS), LOW)] * 2
    operands = (order, *picks, normed_all, att, nmid, active)
    scratch = [pltpu.VMEM((HIDDEN, OWN), FULL), pltpu.VMEM((HIDDEN, OWN), FULL)]
    body = lambda moves, refs: left_body(plan, moves, refs)
    return run(body, operands, [SM, VM, VM, Late(), VM, VM, VM], outs, "left_factors", LEFT, scratch)


def rights_of(grad_refs, kind, part, tile):
    at = {"down": 0, "up": WIDTH + part * WIDTH, "out": WIDTH + HIDDEN}[kind] + tile * TILE
    half, at = at // (PACKED // 2), at % (PACKED // 2)
    return [grad_refs[2 * side + half][:, at : at + TILE] for side in range(2)]


def piece_shapes(classes):
    outs = []
    for number, rows in classes:
        outs += [shape((4, rows, WIDTH), LOW)] if number == 0 else [shape((rows, WIDTH), LOW)] * 4
    return outs


def by_class(classes, arrays):
    found, at = {}, 0
    for number, _ in classes:
        if number == 0:
            found[0] = [arrays[at].at[way] for way in range(4)]
            at += 1
        else:
            found[number] = list(arrays[at : at + 4])
            at += 4
    return found


def deal(out, row, values, columns):
    size = values.shape[0] // 4
    for way in range(4):
        out[way][row : row + size, columns] = values[way * size : (way + 1) * size].astype(LOW)


def mlp_body(plan, classes, refs):
    tall_refs, grad_refs = refs[0:2], refs[2:6]
    outs = by_class(classes, refs[6:])
    for kind, part, left_row, out, out_row in plan:
        for tile in range(3):
            columns = slice(tile * TILE, (tile + 1) * TILE)
            rights = rights_of(grad_refs, kind, part, tile)
            for piece in range(4 if kind == "down" else 1):
                rows = slice(left_row + piece * HALF, left_row + (piece + 1) * HALF)
                lefts = [tall[rows, 0:OWN] for tall in tall_refs]
                values = nn(lefts[0], rights[0]) + nn(lefts[1], rights[1])
                if kind == "down":
                    outs[out][piece][out_row : out_row + HALF, columns] = values.astype(LOW)
                else:
                    deal(outs[out], out_row, values, columns)


def mlp_call(plan, classes, talls, grads, micros=MLP1):
    operands = (*talls, *grads)
    body = lambda moves, refs: mlp_body(plan, classes, refs)
    out = run(body, operands, [VM] * 6, piece_shapes(classes), "grad_mlp", micros)
    return by_class_values(classes, out)


def by_class_values(classes, arrays):
    found, at = {}, 0
    for number, _ in classes:
        found[number] = arrays[at] if number == 0 else list(arrays[at : at + 4])
        at += 1 if number == 0 else 4
    return found


def mixed_body(plan, classes, small, refs):
    seq_ref, *refs = refs
    tall_refs, wide_refs, dq_refs, dkv_refs = [refs[2 * at : 2 * at + 2] for at in range(4)]
    grad_refs, small_refs = refs[8:12], refs[12:14]
    outs = by_class(classes, refs[14:] if small else refs[12:])
    if small:
        joined = small_refs[0][...].astype(FULL) + small_refs[1][...].astype(FULL)
        for way in range(4):
            spots = [joined[64 * part + 16 * way : 64 * part + 16 * (way + 1)] for part in range(2)]
            outs[1][way][3 * HALF // 4 : 3 * HALF // 4 + 32] = jnp.concatenate(spots, 0).astype(LOW)
    for kind, left_row, out, out_row in plan:
        for tile in range(3):
            columns = slice(tile * TILE, (tile + 1) * TILE)
            values = jnp.zeros((HALF, TILE), FULL)
            for side in range(2):
                if kind in ("k", "v"):
                    at = (0 if kind == "k" else WIDTH) + tile * TILE
                    values = values + nt(wide_refs[side][...], dkv_refs[side][at : at + TILE])
                    continue
                if kind == "q" and left_row is None:
                    wide = wide_refs[side]
                    mine = pl.ds(pl.multiple_of(seq_ref[0, 0] * PATCHES, PATCHES), PATCHES)
                    left = jnp.concatenate([wide[:, mine], wide[:, CLS_AT:PROMPT_AT]], 1)
                else:
                    left = tall_refs[side][left_row : left_row + HALF, 0:OWN]
                if kind == "q":
                    right = dq_refs[side][:, columns]
                else:
                    name, part = ("out", 0) if kind == "out" else ("up", kind)
                    right = rights_of(grad_refs, name, part, tile)[side]
                values = values + nn(left, right)
            deal(outs[out], out_row, values, columns)


def mixed_call(plan, classes, seq, talls, wides, dqs, dkvs, grads, small=()):
    operands = (seq, *talls, *wides, *dqs, *dkvs, *grads, *small)
    body = lambda moves, refs: mixed_body(plan, classes, bool(small), refs)
    specs = [SM] + [VM] * (len(operands) - 1)
    out = run(body, operands, specs, piece_shapes(classes), "grad_mixed", MIX)
    return by_class_values(classes, out)


def fold_body(classes, refs):
    r = iter(refs)
    totals = []
    for _, groups in classes:
        totals.append([])
        for arrays, _ in groups:
            come = next(r)
            ways = [come.at[way] for way in range(4)] if len(come.shape) == 3 else [come]
            ways += [next(r) for _ in range(arrays - 1)]
            total = ways[0][...].astype(FULL)
            for way in ways[1:]:
                total = total + way[...].astype(FULL)
            totals[-1].append(total)
    for (ways, groups), sums in zip(classes, totals):
        joint = next(r) if ways == 16 else None
        for way in range(ways):
            out = joint.at[way] if ways == 16 else next(r)
            parts = []
            for total, (_, items) in zip(sums, groups):
                at = 0
                for rows in items:
                    size = rows // ways
                    parts.append(total[at + way * size : at + (way + 1) * size])
                    at += rows
            short = out.shape[0] - sum(part.shape[0] for part in parts)
            if short:
                parts.append(jnp.zeros((short, out.shape[1]), FULL))
            out[...] = jnp.concatenate(parts, 0).astype(LOW)


def fold_call(classes):
    operands = []
    for _, groups in classes:
        for come, _ in groups:
            operands += come if isinstance(come, list) else [come]
    number = lambda come: len(come) if isinstance(come, list) else 1
    counts = [(ways, [(number(come), items) for come, items in groups]) for ways, groups in classes]
    wide = 256
    outs = []
    for ways, groups in counts:
        size = sum(sum(items) for _, items in groups) // ways
        if ways == 16:
            outs.append(shape((16, -(-size // 8) * 8, WIDTH), LOW))
        else:
            outs += [shape((size, WIDTH), LOW)] * ways
    block = lambda *dims: pl.BlockSpec((*dims, wide), lambda i: (*[0] * len(dims), i))
    return list(
        pl.pallas_call(
            lambda *refs: fold_body(counts, refs),
            grid=(WIDTH // wide,),
            out_shape=tuple(outs),
            in_specs=[block(*come.shape[:-1]) for come in operands],
            out_specs=tuple(block(*out.shape[:-1]) for out in outs),
            compiler_params=params(56),
            cost_estimate=cost(FOLD),
            name="ring_fold",
        )(*operands)
    )


def final_body(layouts, refs):
    r = iter(refs)
    plane, ring = next(r), [next(r) for _ in range(4)]
    arrays = ([plane.at[way] for way in range(16)], ring)
    own_w_ref, own_vec_ref = next(r), next(r)
    qkv_ref, out_ref, up_ref, down_ref = next(r), next(r), next(r), next(r)
    prompt_ref, gain_ref, bias_ref, up_bias_ref = next(r), next(r), next(r), next(r)
    pieces = []
    for array, layout in zip(arrays, layouts):
        total = array[0][...].astype(FULL)
        for way in array[1:]:
            total = total + way[...].astype(FULL)
        at = 0
        for entry in layout:
            pieces.append((entry[:3], total[at : at + entry[3]]))
            at += entry[3]
    small = None
    wholes = [jnp.zeros((6, 1), FULL)] * 2
    for (kind, layer, part), piece in pieces:
        columns = slice(part * WIDTH, (part + 1) * WIDTH)
        if kind == "qkv":
            qkv_ref[:, layer, columns] = piece
            weight = own_w_ref[layer, :, columns].astype(FULL)
            wholes[layer] = wholes[layer] + jnp.sum(piece * weight, -1, keepdims=True)
        elif kind == "out":
            out_ref[:, layer, :] = piece
        elif kind == "up":
            up_ref[:, layer, columns] = piece
        elif kind == "down":
            down_ref[layer] = piece
        elif kind == "small":
            small = jnp.concatenate([piece[:, 128 * i : 128 * (i + 1)] for i in range(6)], 0)
        else:
            up_bias_ref[0:1] = piece[:, 0:24]
            up_bias_ref[1:2] = piece[:, 24:48]
    turn = lambda values: jnp.concatenate([values, jnp.zeros((2, 128), FULL)], 0).T
    rows = turn(small)
    for layer in range(2):
        prompt_ref[:, layer, :] = small[:, 56 * layer : 56 * layer + PROMPTS]
        at = 112 + 8 * layer
        part = rows[at : at + 8, 0:6]
        whole = turn(jnp.broadcast_to(wholes[layer], (6, 128)))[0:1, 0:6]
        gain, shift = own_vec_ref[layer, 0:1], own_vec_ref[layer, 1:2]
        gain_ref[layer, 0:1] = (whole - shift * part[6:7]) / gain
        gain_ref[layer, 1:2] = part[1:2]
        for place, source in enumerate((6, 4, 5, 3, 2, 0)):
            bias_ref[place, layer : layer + 1] = part[source : source + 1]


def final_call(arrays, layouts, own_w, own_vec):
    operands = [*arrays, own_w, own_vec]
    outs = (
        shape((6, 2, 3 * WIDTH)),
        shape((6, 2, WIDTH)),
        shape((6, 2, HIDDEN)),
        shape((2, 24, WIDTH)),
        shape((6, 2, PROMPTS)),
        shape((2, 2, 6)),
        shape((6, 2, 6)),
        shape((2, 24)),
    )
    body = lambda moves, refs: final_body(layouts, refs)
    return run(body, operands, [VM] * len(operands), outs, "final_fold", 3)


def per_device(
    patches,
    cls_tokens,
    segments,
    prompts,
    w_qkv,
    w_out,
    w_up,
    w_down,
    norm_gains,
    biases,
    up_bias,
    cot_patches,
    cot_cls,
):
    layers = 2
    weights = (w_qkv, w_out, w_up, w_down)
    first_seq = (lax.axis_index("seq") == 0).astype(FULL).reshape(1, 1)
    prompt_rows = jnp.pad(prompts.astype(FULL), ((0, 0), (0, 64 - PROMPTS), (0, 0)))
    vecs = []
    for layer in range(layers):
        following = min(layer + 1, layers - 1)
        vecs.append(
            jnp.concatenate(
                [
                    norm_gains[layer],
                    biases[layer],
                    norm_gains[following, 0:1],
                    biases[following, 0:1],
                    jnp.zeros((6, WIDTH), FULL),
                ],
                0,
            )
        )
    up_rows = [jnp.broadcast_to(up_bias[layer], (8, HIDDEN)) for layer in range(layers)]
    orders = [
        owner_order(RINGS[0]),
        owner_order(RINGS[1], RINGS[1]),
        owner_order(RINGS[0], RINGS[0][:1]),
    ]
    steps = jnp.arange(6, dtype=jnp.int32)
    one_hot = lambda wanted, size: (wanted[:, None] == jnp.arange(size)[None, :]).astype(LOW)
    picks = [one_hot((order[:, None] * 6 + steps).reshape(-1), WIDTH) for order in orders]
    small_pick = one_hot((orders[1][None, :] * 6 + steps[:, None]).reshape(-1), WIDTH)
    small_spot = one_hot(orders[1], 128)

    seq = lax.axis_index("seq").astype(jnp.int32).reshape(1, 1)
    here = lax.axis_index("dp") * 8 + lax.axis_index("seq")
    mine_of = lambda values, axis: lax.dynamic_slice_in_dim(values, here * 6, 6, axis)
    own_w = mine_of(w_qkv, 1)
    own_vec = jnp.stack([mine_of(norm_gains, 2)[:, 0], mine_of(biases, 2)[:, 0]], 1)
    prompt_rows = [prompt_rows[layer] for layer in range(layers)]
    x, payload, own, query_seg = open_call(patches, cls_tokens, segments, norm_gains, biases)
    key_seg = None
    kept = []
    lefts = []
    factors = []
    left_plans = (
        (("mid", 0), ("att", 0), ("mid", 1)),
        (("mid", 0), ("mid", 1), ("att", 1)),
    )
    def left_factors(layer, *behind):
        normed_all, att, nmid, active = factors[layer]
        tall, tall_other, wide, wide_other = left_call(
            left_plans[layer], orders[2 - 2 * layer], (picks[2 - 2 * layer], picks[1]), normed_all, att, after(nmid, *behind), active
        )
        return (tall, send(tall_other, "core", 1), wide, send(wide_other, "core", 1))

    come = swap_rows(payload)
    x, vecs, up_rows, prompt_rows, picks, small_pick, small_spot, own_w, own_vec = (
        lax.optimization_barrier(
            (x, vecs, up_rows, prompt_rows, picks, small_pick, small_spot, own_w, own_vec)
        )
    )
    out = forward_call(
        0, False, x, come, own, prompt_rows[0], vecs[0], up_rows[0], query_seg, None, weights
    )
    q, k, v, normed_all, att, lse, mid, nmid, slope, active, x_next, payload, own, key_seg = out
    kept.append((x, q, k, v, lse, mid, slope))
    factors.append((normed_all, att, nmid, active))
    lefts.append(left_factors(0))
    come = swap_rows(payload)
    x = after(x_next, lefts[0][0], lefts[0][2])
    kept.append((x,))
    cots = (cot_patches[0], cot_cls[0])
    out = turn_call(
        x, come, own, prompt_rows[1], vecs[1], up_rows[1], query_seg, key_seg, cots, first_seq, weights
    )
    factors.append(out[0:4])
    out_patch, out_cls = out[4:6]

    def back_mlp(layer, start):
        mid, slope = kept[layer][5:7]
        return back_mlp_call(
            layer, layer == layers - 1, start, first_seq, mid, slope, vecs[layer], weights
        )

    def back_att(layer, rows, datt, small=()):
        return back_att_call(
            layer, first_seq, rows, datt, kept[layer][1:5], prompt_rows[layer], vecs[layer],
            query_seg, key_seg, small, weights[0],
        )

    def both(values):
        return (values, send(values, "core", 1))

    def both_parts(parts):
        return (*parts, *[send(part, "core", 1) for part in parts])

    def give_back(layer, pays, qpart, mid_grad):
        return (swap_rows(pays), qpart, kept[layer][0], mid_grad, vecs[layer])

    arrived = [[], []]

    def start_ring(at, made, rows):
        pieces, ring_at = made[at], at % 2
        axis = RINGS[ring_at][0]
        if at == 0:
            come = deal_out(pieces, (axis,))
        else:
            come = [pieces[0]] + [send(pieces[step], axis, step) for step in range(1, 4)]
        arrived[ring_at].append((come, rows))

    tile = HALF // 4
    mid_at = 2 * WIDTH
    packed, (mid_grad, up_row_1, dq, qpart, dkv, pays, prompts_1, rows_1) = out[6:8], out[8:]
    grads = both_parts(packed)
    dqs, dkvs = both(dq), both(dkv)
    start = give_back(1, pays, qpart, mid_grad)
    lefts.append(left_factors(1, dkv))
    plan = [("down", 0, 0, 0, 0)]
    plan += [("up", part, mid_at, 0, HALF + part * tile) for part in range(3)]
    made = mlp_call(plan, ((0, HALF + 3 * tile),), lefts[1][0:2], grads)
    plan = [("q", None, 1, 0), ("k", None, 1, tile), ("v", None, 1, 2 * tile)]
    plan += [("out", mid_at + 2 * HALF, 1, 3 * tile), (3, mid_at + HALF, 1, 4 * tile)]
    talls = (after(lefts[1][0], made[0]), lefts[1][1])
    mixed = mixed_call(plan, ((1, 5 * tile),), seq, talls, lefts[1][2:], dqs, dkvs, grads)
    start_ring(0, made, (HALF,) + (tile,) * 3)
    start_ring(1, mixed, (tile,) * 5)

    start = (after(start[0], mixed[1][0]), *start[1:])
    *packed, datt, mid_grad, rows, up_row_0 = back_mlp(0, start)
    grads = both_parts(packed)
    small = (small_pick, small_spot, prompts_1, rows_1, up_row_0, up_row_1)
    out = back_att(0, rows, datt, small)
    dq, dkv = out[0], out[2]
    plan = [("down", 0, 0, 2, 0), ("out", 0, mid_at + HALF, 2, HALF)]
    plan += [("up", part, mid_at, 2, HALF + (1 + part) * tile) for part in range(3)]
    talls = (after(lefts[0][0], dkv, arrived[0][0][0], *arrived[1][0][0]), lefts[0][1])
    made = mlp_call(plan, ((2, HALF + 4 * tile),), talls, grads, 60)
    start_ring(2, made, (HALF,) + (tile,) * 4)
    start = give_back(0, after(out[3], arrived[0][0][0]), out[1], mid_grad)
    dqs, dkvs = both(dq), both(dkv)
    small = (out[4], send(out[5], "core", 1))
    plan = [("q", None, 1, 0), ("k", None, 1, tile), ("v", None, 1, 2 * tile)]
    plan += [(3, mid_at + 2 * HALF, 1, 3 * tile + 32)]
    talls = (after(lefts[0][0], made[2][0]), lefts[0][1])
    mixed = mixed_call(
        plan, ((1, 4 * tile + 32),), seq, talls, lefts[0][2:], dqs, dkvs, grads, small
    )
    start_ring(1, mixed, (tile,) * 3 + (16, 16) + (tile,))
    grad_patch, grad_cls = close_call((after(start[0], mixed[1][0], *arrived[0][1][0]), *start[1:]))
    for group in arrived:
        come, rows = group[0]
        (total,) = fold_call([(1, [(come, rows)])])
        group[0] = ([total], rows)
    (come, rows), *others = arrived[0]
    plane, *pieces = fold_call([(16, [([after(come[0], grad_cls)], rows), *others]), (4, arrived[1])])
    plane = deal_out(plane, RINGS[0][1:])
    second = [pieces[0]] + [send(pieces[step], RINGS[1][1], step) for step in range(1, 4)]
    rows = tuple(row // 4 for _, items in arrived[1] for row in items)
    pieces = fold_call([(4, [(second, rows)])])
    third = [pieces[0]] + [send(pieces[step], RINGS[1][2], step) for step in range(1, 4)]
    lasts = [plane, *third]
    layouts = (
        [("down", 1, 0, 24)]
        + [("up", 1, part, 6) for part in range(3)]
        + [("down", 0, 0, 24), ("out", 0, 0, 6)]
        + [("up", 0, part, 6) for part in range(3)],
        [("qkv", 1, part, 6) for part in range(3)]
        + [("out", 1, 0, 6), ("up", 1, 3, 6)]
        + [("qkv", 0, part, 6) for part in range(3)]
        + [("small", 0, 0, 1), ("bias", 0, 0, 1), ("up", 0, 3, 6)],
    )
    done = final_call(lasts, layouts, own_w, own_vec)
    swap = lambda values: jnp.transpose(values, (1, 0, 2))
    return (
        out_patch[None],
        swap(out_cls),
        grad_patch[None],
        swap(grad_cls),
        jnp.transpose(done[4], (1, 2, 0)),
        swap(done[0]),
        swap(done[1]),
        swap(done[2]),
        done[3],
        done[5],
        swap(done[6]),
        done[7],
    )


def solution(mesh):
    placed = (
        P("dp", "seq", None),
        P("dp", None, None),
        P("dp", "seq"),
        P(),
        P(),
        P(),
        P(),
        P(),
        P(),
        P(),
        P(),
        P("dp", "seq", None),
        P("dp", None, None),
    )
    return jax.shard_map(
        per_device,
        mesh=mesh,
        in_specs=placed,
        out_specs=(
            P("dp", "seq", None),
            P("dp", None, None),
            P("dp", "seq", None),
            P("dp", None, None),
            P(None, None, ("dp", "seq")),
            P(None, ("dp", "seq"), None),
            P(None, ("dp", "seq"), None),
            P(None, ("dp", "seq"), None),
            P(None, ("dp", "seq"), None),
            P(None, None, ("dp", "seq")),
            P(None, None, ("dp", "seq")),
            P(None, ("dp", "seq")),
        ),
        check_vma=False,
    )
```

```python
import functools

import jax
import jax.numpy as jnp
from jax import lax
from jax.experimental import pallas as pl
from jax.experimental.pallas import tpu as pltpu
from jax.sharding import PartitionSpec as P

HEADS = 12
HEAD = 64
WIDTH = 768
HIDDEN = 3072
PATCHES = 128
CLS = 10
PROMPTS = 50
OWN = 144
KEYS = 1152
CLS_AT = 1024
PROMPT_AT = 1040
FRONT = 128
BLOCKS = 8
PAY = 864
PACKED = 2 * WIDTH + HIDDEN
HALF = WIDTH // 2
TILE = 256
LOW = jnp.bfloat16
FULL = jnp.float32

eps_norm = 1e-06
penalty_rate = 2.0
big_negative = -1e30

AXES = ("dp", "seq")
SPAN = {"core": 2, "x": 4, "y": 4, "z": 4}
RINGS = (("y", "z", "x"), ("z", "y", "x"))
ANY = pl.BlockSpec(memory_space=pl.ANY)
VM = "whole"
HERE = pl.BlockSpec(memory_space=pltpu.VMEM)
SM = pl.BlockSpec(memory_space=pltpu.SMEM)


def place_of(device):
    dp, seq = device // 8, device % 8
    return {"core": dp % 2, "x": dp // 2 % 2 * 2 + seq // 4, "y": dp // 4, "z": seq % 4}


def device_of(place):
    dp = (place["y"] * 2 + place["x"] // 2) * 2 + place["core"]
    return dp * 8 + place["x"] % 2 * 4 + place["z"]


def moved(axis, step):
    pairs = []
    for device in range(128):
        place = place_of(device)
        place[axis] = (place[axis] + step) % SPAN[axis]
        pairs.append((device, device_of(place)))
    return pairs


def send(values, axis, step):
    return lax.ppermute(values, AXES, moved(axis, step))


def groups_of(axes):
    found = {}
    for device in range(128):
        place = place_of(device)
        rest = tuple(place[axis] for axis in SPAN if axis not in axes)
        found.setdefault(rest, []).append((tuple(place[axis] for axis in axes), device))
    return [[device for _, device in sorted(group)] for group in found.values()]


def deal_out(values, axes):
    return lax.all_to_all(
        values, AXES, 0, 0, tiled=True, axis_index_groups=groups_of(axes)
    )


def swap_rows(values):
    return lax.all_to_all(values, "seq", 0, 0, tiled=True)


def owner_order(axes, steps=()):
    here = place_of(lax.axis_index("dp") * 8 + lax.axis_index("seq"))
    rest = jnp.arange(128, dtype=jnp.int32)
    place = {}
    for axis in reversed(axes):
        place[axis] = rest % SPAN[axis]
        if axis in steps:
            place[axis] = (here[axis] + place[axis]) % SPAN[axis]
        rest = rest // SPAN[axis]
    place["core"] = (here["core"] + rest) % 2
    return device_of(place)


def nn(left, right):
    return lax.dot_general(left, right, (((1,), (0,)), ((), ())), preferred_element_type=FULL)


def nt(left, right):
    return lax.dot_general(left, right, (((1,), (1,)), ((), ())), preferred_element_type=FULL)


def plain_norm(values):
    centred = values - jnp.mean(values, -1, keepdims=True)
    scale = lax.rsqrt(jnp.mean(centred * centred, -1, keepdims=True) + eps_norm)
    return centred * scale, scale


def norm_pull(plain, scale, gain, upstream):
    inner = upstream * gain
    return scale * (
        inner
        - jnp.mean(inner, -1, keepdims=True)
        - plain * jnp.mean(inner * plain, -1, keepdims=True)
    )


def whole(dims):
    return pl.BlockSpec(dims, lambda i: (0,) * len(dims))


class Late:
    def __init__(self, index=None, cuts=1, axis=0):
        self.index, self.cuts, self.axis = index, cuts, axis


class Early:
    def __init__(self, dims, kind=FULL):
        self.shape, self.dtype = dims, kind


class Moves:
    def __init__(self):
        self.ins, self.outs, self.gone = {}, {}, []

    def start(self, *refs):
        for ref in refs:
            for copy in self.ins[id(ref)]:
                copy.start()

    def resident(self):
        part = Moves()
        part.start = part.wait = lambda *_: None
        part.flush = self.flush
        return part

    def wait(self, ref, piece=None):
        copies = self.ins[id(ref)]
        for copy in copies if piece is None else copies[piece : piece + 1]:
            copy.wait()

    def flush(self, *refs):
        for ref in refs:
            copy = self.outs.pop(id(ref), None)
            if copy is not None:
                copy.start()
                self.gone.append(copy)

    def close(self):
        for copy in self.outs.values():
            copy.start()
        for copy in [*self.gone, *self.outs.values()]:
            copy.wait()


def run(body, operands, specs, outs, name, micros, scratch=(), mib=62):
    late = [(at, spec) for at, spec in enumerate(specs) if isinstance(spec, Late)]
    early = [(at, out) for at, out in enumerate(outs) if isinstance(out, Early)]
    buffers, total = [], 0
    for at, spec in late:
        dims = operands[at].shape if spec.index is None else operands[at].shape[1:]
        buffers.append(pltpu.VMEM(dims, operands[at].dtype))
        total += spec.cuts
    buffers += [pltpu.VMEM(out.shape, out.dtype) for _, out in early]
    total += len(early)

    def kernel(*refs):
        refs = list(refs)
        first = len(operands) + len(outs) + len(scratch)
        space, sems = refs[first : first + len(buffers)], refs[-1]
        moves, sem = Moves(), 0
        for (at, spec), buffer in zip(late, space):
            source = refs[at] if spec.index is None else refs[at].at[spec.index]
            size = buffer.shape[spec.axis] // spec.cuts
            copies = []
            for piece in range(spec.cuts):
                part = pl.ds(piece * size, size)
                view = lambda ref: ref.at[part] if spec.axis == 0 else ref.at[:, part]
                pair = (source, buffer) if spec.cuts == 1 else (view(source), view(buffer))
                copies.append(pltpu.make_async_copy(*pair, sems.at[sem]))
                sem += 1
            moves.ins[id(buffer)] = copies
            refs[at] = buffer
        for (at, out), buffer in zip(early, space[len(late) :]):
            at += len(operands)
            moves.outs[id(buffer)] = pltpu.make_async_copy(buffer, refs[at], sems.at[sem])
            sem += 1
            refs[at] = buffer
        body(moves, refs[:first])
        moves.close()

    in_specs = []
    for operand, spec in zip(operands, specs):
        if isinstance(spec, Late):
            in_specs.append(ANY)
        else:
            in_specs.append(whole(operand.shape) if spec == "whole" else spec)
    return pl.pallas_call(
        kernel,
        grid=(1,),
        out_shape=tuple(shape(out.shape, out.dtype) for out in outs),
        in_specs=in_specs,
        out_specs=tuple(ANY if isinstance(out, Early) else whole(out.shape) for out in outs),
        scratch_shapes=[*scratch, *buffers, pltpu.SemaphoreType.DMA((max(total, 1),))],
        compiler_params=params(mib),
        cost_estimate=cost(micros),
        name=name,
    )(*operands)


def after(values, *others):
    return lax.optimization_barrier((values, others))[0]


def tile_at(index, size):
    return pl.ds(pl.multiple_of(index * size, size), size)


def params(mib=56):
    return pltpu.CompilerParams(vmem_limit_bytes=mib * 2**20)


SHARE = 1.0
ATT = 6
LEFT = 0.1
MIX = 0.1
BMLP = 10
TURN = 40
FOLD = 0.2
LATE = 8
MLP1 = 0.1


def cost(micros):
    return pl.CostEstimate(flops=int(micros * 1.1e9), bytes_accessed=1 << 20, transcendentals=0)


def shape(dims, kind=FULL):
    return jax.ShapeDtypeStruct(dims, kind)


def open_body(patch_ref, cls_ref, seg_ref, gain_ref, bias_ref, x_ref, pay_ref, own_ref, query_ref):
    x_ref[0:PATCHES] = patch_ref[0].astype(FULL)
    cls_rows = jnp.concatenate([cls_ref[0].astype(FULL), jnp.zeros((16 - CLS, WIDTH), FULL)], 0)
    x_ref[PATCHES:OWN] = cls_rows
    plain, _ = plain_norm(x_ref[...])
    normed = (plain * gain_ref[0, 0:1] + bias_ref[0, 0:1]).astype(LOW)
    own_ref[...] = normed
    segs = seg_ref[...].astype(FULL)
    last = jnp.broadcast_to(segs, (16, PATCHES)).astype(LOW)
    last = jnp.concatenate([last, jnp.zeros((16, WIDTH - PATCHES), LOW)], 1)
    for block in range(BLOCKS):
        pay_ref[block, 0:PATCHES] = normed[0:PATCHES]
        pay_ref[block, PATCHES:OWN] = last
    query_ref[0:PATCHES] = jnp.broadcast_to(segs, (PATCHES, PATCHES)).T
    row = lax.broadcasted_iota(jnp.int32, (16, 128), 0)
    query_ref[PATCHES:OWN] = jnp.where(row < CLS, row, -5).astype(FULL)


def open_call(patches, cls_tokens, segments, gains, biases):
    outs = (
        shape((OWN, WIDTH)),
        shape((BLOCKS, OWN, WIDTH), LOW),
        shape((OWN, WIDTH), LOW),
        shape((OWN, 128)),
    )
    operands = (patches, cls_tokens, segments, gains, biases)
    return run(lambda moves, refs: open_body(*refs), operands, [VM] * 5, outs, "open_norm", 2)


def seen_mask(key_ref, query_ref, mask_ref):
    keys = key_ref[0:1, :]
    seen = (keys == query_ref[:, 0:1]) | (keys == -1.0)
    mask_ref[...] = jnp.where(seen, 0.0, big_negative)


def half_lanes(rows):
    return lax.broadcasted_iota(jnp.int32, (rows, 2 * HEAD), 1) < HEAD


def two_heads(rows, lower):
    none = jnp.zeros_like(rows)
    return jnp.concatenate([jnp.where(lower, rows, none), jnp.where(lower, none, rows)], 0)


def split_rows(rows, patch_ref, cls_ref):
    patch_ref[...] = rows[0:PATCHES]
    for place in range(CLS):
        cls_ref[place] = rows[PATCHES + place : PATCHES + place + 1]


def forward_body(layer, last, moves, refs):
    first = layer == 0
    r = iter(refs)
    nxt = lambda: next(r)
    x_ref = nxt()
    come_ref = nxt()
    own_ref, prompt_ref, vec_ref, up_bias_ref, query_seg_ref = nxt(), nxt(), nxt(), nxt(), nxt()
    key_in_ref = None if first else nxt()
    wqkv, wout, wup, wdown = nxt(), nxt(), nxt(), nxt()
    q_ref, k_ref, v_ref, all_ref = nxt(), nxt(), nxt(), nxt()
    att_ref, lse_ref, mid_ref, nmid_ref = nxt(), nxt(), nxt(), nxt()
    slope_ref, active_ref, out_ref = nxt(), nxt(), nxt()
    next_ref, next_own_ref = nxt(), nxt()
    key_ref = nxt() if first else key_in_ref
    mask_ref = nxt()

    moves.start(wqkv)
    for block in range(BLOCKS):
        all_ref[block * PATCHES : (block + 1) * PATCHES] = come_ref[block, 0:PATCHES]

    gain_one, bias_one = vec_ref[0:1], vec_ref[2:3]
    gain_two, bias_two = vec_ref[1:2], vec_ref[6:7]

    plain, _ = plain_norm(prompt_ref[...])
    all_ref[CLS_AT:PROMPT_AT] = own_ref[PATCHES:OWN]
    all_ref[PROMPT_AT : PROMPT_AT + 64] = (plain * gain_one + bias_one).astype(LOW)
    all_ref[PROMPT_AT + 64 : KEYS] = jnp.zeros((KEYS - PROMPT_AT - 64, WIDTH), LOW)
    moves.flush(all_ref)
    if first:
        lane = lax.broadcasted_iota(jnp.int32, (8, FRONT), 1)
        front = jnp.where(
            lane < CLS, lane, jnp.where((lane >= 16) & (lane < 16 + PROMPTS), -1, -2)
        )
        for block in range(BLOCKS):
            segs = come_ref[block, PATCHES:OWN, 0:PATCHES].astype(FULL)
            key_ref[:, block * PATCHES : (block + 1) * PATCHES] = segs[0:8]
        key_ref[:, CLS_AT:KEYS] = front.astype(FULL)
    seen_mask(key_ref, query_seg_ref, mask_ref)

    def keys(tile, carry):
        at = tile_at(tile, TILE)
        rows = nn(all_ref[...], wqkv[:, pl.ds(pl.multiple_of(WIDTH + tile * TILE, TILE), TILE)])
        k_ref[:, at] = rows.astype(LOW)
        return carry

    def values(tile, carry):
        at = tile_at(tile, TILE)
        rows = nn(all_ref[...], wqkv[:, pl.ds(pl.multiple_of(2 * WIDTH + tile * TILE, TILE), TILE)])
        v_ref[:, at] = (rows + vec_ref[4:5, at]).astype(LOW)
        return carry

    def queries(tile, carry):
        at = tile_at(tile, TILE)
        rows = nn(own_ref[...], wqkv[:, at]) + vec_ref[3:4, at]
        q_ref[:, at] = (rows.astype(LOW).astype(FULL) * HEAD**-0.5).astype(LOW)
        return carry

    moves.wait(wqkv, 0)
    lax.fori_loop(0, 3, queries, 0, unroll=3)
    moves.wait(wqkv, 1)
    moves.start(wout, wup)
    lax.fori_loop(0, 3, keys, 0, unroll=3)
    moves.flush(k_ref)
    moves.wait(wqkv, 2)
    lax.fori_loop(0, 3, values, 0, unroll=3)
    moves.flush(v_ref)
    moves.start(wdown)

    lse_ref[...] = jnp.zeros((OWN, 128), FULL)
    lower = half_lanes(OWN)
    lane = lax.broadcasted_iota(jnp.int32, (OWN, 128), 1)

    def heads(pair, carry):
        at = tile_at(pair, 2 * HEAD)
        query, key, value = q_ref[:, at], k_ref[:, at], v_ref[:, at]
        outs = []
        for side in range(2):
            mine = lower if side == 0 else ~lower
            scores = nt(jnp.where(mine, query, jnp.zeros_like(query)), key) + mask_ref[...]
            top = jnp.max(scores, -1, keepdims=True)
            raised = jnp.exp(scores - top)
            total = jnp.sum(raised, -1, keepdims=True)
            outs.append(nn(raised.astype(LOW), value) / total)
            lane = lax.broadcasted_iota(jnp.int32, (OWN, 128), 1)
            lse_ref[...] = jnp.where(lane == 2 * pair + side, top + jnp.log(total), lse_ref[...])
        att_ref[:, at] = jnp.where(lower, outs[0], outs[1]).astype(LOW)
        return carry

    lax.fori_loop(0, HEADS // 2, heads, 0, unroll=2)

    moves.wait(wout)

    def project(tile, carry):
        at = tile_at(tile, TILE)
        mid_ref[:, at] = x_ref[:, at] + (nn(att_ref[...], wout[:, at]) + vec_ref[5:6, at])
        return carry

    lax.fori_loop(0, 3, project, 0, unroll=3)
    plain, _ = plain_norm(mid_ref[...])
    nmid_ref[...] = (plain * gain_two + bias_two).astype(LOW)
    moves.wait(wup)

    def rise(tile, carry):
        at = tile_at(tile, TILE)
        hidden = nn(nmid_ref[...], wup[:, at]) + up_bias_ref[0:1, at]
        share = 0.5 * (1.0 + lax.erf(hidden * 0.7071067811865476))
        active_ref[:, at] = (hidden * share).astype(LOW)
        slope_ref[:, at] = share + hidden * (0.3989422804014327 * jnp.exp(-0.5 * hidden * hidden))
        return carry

    lax.fori_loop(0, HIDDEN // TILE, rise, 0, unroll=4)
    moves.flush(slope_ref, active_ref)
    moves.wait(wdown)

    def lower_back(tile, carry):
        at = tile_at(tile, TILE)
        out_ref[:, at] = mid_ref[:, at] + (nn(active_ref[...], wdown[:, at]) + vec_ref[7:8, at])
        return carry

    lax.fori_loop(0, 3, lower_back, 0, unroll=3)
    if not last:
        plain, _ = plain_norm(out_ref[...])
        normed = (plain * vec_ref[8:9] + vec_ref[9:10]).astype(LOW)
        next_own_ref[...] = normed
        for block in range(BLOCKS):
            next_ref[block] = normed[0:PATCHES]
    else:
        split_rows(out_ref[...], next_ref, next_own_ref)


def forward_call(layer, last, x, come, own, prompt, vec, up_bias, query_seg, key_seg, weights):
    first = layer == 0
    outs = [
        shape((OWN, WIDTH), LOW),
        Early((KEYS, WIDTH), LOW),
        Early((KEYS, WIDTH), LOW),
        Early((KEYS, WIDTH), LOW),
        shape((OWN, WIDTH), LOW),
        shape((OWN, 128)),
        shape((OWN, WIDTH)),
        shape((OWN, WIDTH), LOW),
        Early((OWN, HIDDEN)),
        Early((OWN, HIDDEN), LOW),
        shape((OWN, WIDTH)),
    ]
    if last:
        outs += [shape((PATCHES, WIDTH)), shape((CLS, 1, WIDTH))]
    else:
        outs += [shape((BLOCKS, PATCHES, WIDTH), LOW), shape((OWN, WIDTH), LOW)]
    if first:
        outs += [shape((8, KEYS))]
    operands = [x, come, own, prompt, vec, up_bias, query_seg]
    specs = [VM, HERE] + [VM] * 5
    if not first:
        operands.append(key_seg)
        specs.append(VM)
    operands += weights
    specs += [Late(layer, 3, 1), Late(layer), Late(layer), Late(layer)]
    scratch = [pltpu.VMEM((OWN, KEYS), FULL)]
    body = lambda moves, refs: forward_body(layer, last, moves, refs)
    return run(body, operands, specs, outs, "forward_layer", 24 * SHARE, scratch)


def gathered_pull(come_ref, qpart_ref, x_ref, gain, mid_grad_ref):
    total = come_ref[0].astype(FULL)
    for block in range(1, BLOCKS):
        total = total + come_ref[block].astype(FULL)
    patch_part = total[0:WIDTH].T
    cls_part = jnp.concatenate(
        [total[WIDTH + 16 * lane : WIDTH + 16 * (lane + 1)] for lane in range(6)], 1
    )
    d_normed = jnp.concatenate([patch_part, cls_part], 0) + qpart_ref[...]
    plain, scale = plain_norm(x_ref[...])
    return mid_grad_ref[...] + norm_pull(plain, scale, gain, d_normed)


def row_share(first_ref):
    row = lax.broadcasted_iota(jnp.int32, (OWN, 1), 0)
    return jnp.where(row < PATCHES, 1.0, jnp.where(row < PATCHES + CLS, first_ref[0, 0], 0.0))


def back_mlp_body(last, moves, refs):
    r = iter(refs)
    nxt = lambda: next(r)
    if last:
        cot_ref, cot_cls_ref, key_ref, query_seg_ref = nxt(), nxt(), nxt(), nxt()
    else:
        come_ref = nxt()
        up_qpart_ref, up_x_ref, up_mid_grad_ref, up_vec_ref = nxt(), nxt(), nxt(), nxt()
    first_ref, mid_ref, slope_ref, vec_ref = nxt(), nxt(), nxt(), nxt()
    wout, wup, wdown = nxt(), nxt(), nxt()
    grad_refs = nxt(), nxt()
    datt_ref, mid_grad_ref = nxt(), nxt()
    rows_ref, up_spot_ref = nxt(), nxt()
    up_ref, low_ref, hid_ref, up_row_ref = nxt(), nxt(), nxt(), nxt()

    moves.start(wdown, slope_ref)
    gain_two = vec_ref[1:2]
    share = row_share(first_ref)
    if last:
        valid = ((query_seg_ref[...] < CLS) & (query_seg_ref[...] >= 0)).astype(FULL)
        up_ref[0:PATCHES] = cot_ref[...].astype(FULL) * valid[0:PATCHES, 0:1]
        hits = (key_ref[0:1, 0:CLS_AT] == query_seg_ref[PATCHES:OWN, 0:1]).astype(FULL)
        present = jnp.max(hits, -1, keepdims=True)
        cls_rows = [cot_cls_ref[...].astype(FULL), jnp.zeros((16 - CLS, WIDTH), FULL)]
        up_ref[PATCHES:OWN] = jnp.concatenate(cls_rows, 0) * present
    else:
        up_ref[...] = gathered_pull(
            come_ref, up_qpart_ref, up_x_ref, up_vec_ref[0:1], up_mid_grad_ref
        )
    low_ref[...] = up_ref[...].astype(LOW)
    weighted = low_ref[...].astype(FULL) * share
    grad_refs[0][:, 0:WIDTH] = weighted.astype(LOW)
    rows_ref[...] = jnp.zeros((8, WIDTH), FULL)
    rows_ref[0:1] = jnp.sum(weighted, 0, keepdims=True)
    moves.start(wup)

    def to_hidden(half, tile, carry):
        at = tile_at(tile, TILE)
        grad = (nt(low_ref[...], wdown[at, :]) * slope_ref[:, at]).astype(LOW)
        hid_ref[:, at] = grad
        counted = grad.astype(FULL) * share
        to = WIDTH + tile * TILE - half * (PACKED // 2)
        grad_refs[half][:, pl.ds(pl.multiple_of(to, TILE), TILE)] = counted.astype(LOW)
        up_row_ref[:, at] = jnp.broadcast_to(jnp.sum(counted, 0, keepdims=True), (8, TILE))
        return carry

    moves.wait(slope_ref)
    for piece in range(4):
        moves.wait(wdown, piece)
        body = functools.partial(to_hidden, piece // 2)
        lax.fori_loop(3 * piece, 3 * piece + 3, body, 0, unroll=3)
    moves.wait(wup)
    moves.start(wout)

    def to_mid(tile, carry):
        at = tile_at(tile, TILE)
        mid_grad_ref[:, at] = nt(hid_ref[...], wup[at, :])
        return carry

    lax.fori_loop(0, 3, to_mid, 0, unroll=3)
    d_normed = mid_grad_ref[...]
    plain, scale = plain_norm(mid_ref[...])
    counted = d_normed * share
    rows_ref[1:2] = jnp.sum(counted * plain, 0, keepdims=True)
    rows_ref[2:3] = jnp.sum(counted, 0, keepdims=True)
    mid_grad_ref[...] = up_ref[...] + norm_pull(plain, scale, gain_two, d_normed)
    low_ref[...] = mid_grad_ref[...].astype(LOW)
    weighted = low_ref[...].astype(FULL) * share
    grad_refs[1][:, PACKED // 2 - WIDTH :] = weighted.astype(LOW)
    rows_ref[3:4] = jnp.sum(weighted, 0, keepdims=True)
    moves.flush(*grad_refs)
    up_row = up_row_ref[0:1]
    spots = [up_row[:, 24 * spot : 24 * (spot + 1)] for spot in range(128)]
    up_spot_ref[...] = jnp.concatenate(spots, 0)
    moves.wait(wout)

    def to_att(tile, carry):
        at = tile_at(tile, TILE)
        datt_ref[:, at] = nt(low_ref[...], wout[at, :]).astype(LOW)
        return carry

    lax.fori_loop(0, 3, to_att, 0, unroll=3)


def back_att_body(layer, moves, refs):
    r = iter(refs)
    nxt = lambda: next(r)
    first_ref, rows_in_ref, datt_ref = nxt(), nxt(), nxt()
    q_ref, k_ref, v_ref, lse_ref = nxt(), nxt(), nxt(), nxt()
    prompt_ref, vec_ref, query_seg_ref, key_ref = nxt(), nxt(), nxt(), nxt()
    if layer == 0:
        pick_ref, spot_ref, prompts_1, rows_1, up_0, up_1 = [nxt() for _ in range(6)]
    wqkv = nxt()
    dq_ref, qpart_ref, dkv_ref, pay_ref = nxt(), nxt(), nxt(), nxt()
    if layer == 0:
        small_refs = nxt(), nxt()
        dprompt_ref, rows_ref = nxt(), nxt()
    else:
        dprompt_ref, rows_ref = nxt(), nxt()
    mask_ref, dqf_ref, qt_ref, dat_ref, front_ref = [nxt() for _ in range(5)]

    moves.start(k_ref, v_ref, wqkv)
    gain_one = vec_ref[0:1]
    share = row_share(first_ref)
    seen_mask(key_ref, query_seg_ref, mask_ref)
    rows_ref[...] = rows_in_ref[...]

    def turn(tile, carry):
        at = tile_at(tile, TILE)
        dat_ref[at, :] = (datt_ref[:, at].astype(FULL) * share).T.astype(LOW)
        qt_ref[at, :] = (q_ref[:, at].astype(FULL) * share).T.astype(LOW)
        return carry

    lax.fori_loop(0, 3, turn, 0, unroll=3)
    lower = half_lanes(OWN)
    lane = lax.broadcasted_iota(jnp.int32, (OWN, 128), 1)
    moves.wait(k_ref)
    moves.wait(v_ref)

    def heads(pair, carry):
        at = tile_at(pair, 2 * HEAD)
        query, key, value, grad = q_ref[:, at], k_ref[:, at], v_ref[:, at], datt_ref[:, at]
        outs = []
        for side in range(2):
            mine = lower if side == 0 else ~lower
            head = 2 * pair + side
            log_total = jnp.sum(jnp.where(lane == head, lse_ref[...], 0.0), -1, keepdims=True)
            scores = nt(jnp.where(mine, query, jnp.zeros_like(query)), key) + mask_ref[...]
            probs = jnp.exp(scores - log_total)
            d_probs = nt(jnp.where(mine, grad, jnp.zeros_like(grad)), value)
            both = probs * d_probs
            across = jnp.sum(both, -1, keepdims=True)
            d_scores = (both - probs * across).astype(LOW)
            probs_low = probs.astype(LOW)
            outs.append(nn(d_scores, key))
            rows = tile_at(head, HEAD)
            dkv_ref[rows, :] = nn(qt_ref[rows, :], d_scores).astype(LOW)
            value_rows = pl.ds(pl.multiple_of(WIDTH + head * HEAD, HEAD), HEAD)
            dkv_ref[value_rows, :] = nn(dat_ref[rows, :], probs_low).astype(LOW)
        dqf_ref[:, at] = (jnp.where(lower, outs[0], outs[1]) * HEAD**-0.5).astype(LOW)
        return carry

    lax.fori_loop(0, HEADS // 2, heads, 0, unroll=2)
    moves.flush(dkv_ref)
    counted = dqf_ref[...].astype(FULL) * share
    dq_ref[...] = counted.astype(LOW)
    rows_ref[4:5] = jnp.sum(counted, 0, keepdims=True)
    moves.wait(wqkv)

    def to_normed(tile, carry):
        at = tile_at(tile, TILE)
        qpart_ref[:, at] = nt(dqf_ref[...], wqkv[at, 0:WIDTH])
        return carry

    lax.fori_loop(0, 3, to_normed, 0, unroll=3)

    front_ref[...] = nn(wqkv[:, WIDTH:], dkv_ref[:, CLS_AT:KEYS])
    shift = jnp.sum(front_ref[...], -1, keepdims=True)
    front = front_ref[...].T
    cls_rows = jnp.concatenate(
        [front[0:16, 128 * place : 128 * (place + 1)] for place in range(6)], 0
    )
    for block in range(0, BLOCKS, 2):
        part = nn(wqkv[:, WIDTH:], dkv_ref[:, block * PATCHES : (block + 2) * PATCHES])
        shift = shift + jnp.sum(part, -1, keepdims=True)
        for side in range(2):
            pay_ref[block + side, 0:WIDTH] = part[:, side * PATCHES : (side + 1) * PATCHES].astype(LOW)
            pay_ref[block + side, WIDTH:PAY] = cls_rows.astype(LOW)
    moves.flush(pay_ref)

    plain, scale = plain_norm(prompt_ref[...])
    d_prompt = norm_pull(plain, scale, gain_one, front[16:80])
    query_seg = query_seg_ref[0:PATCHES, 0:1]
    slots = jnp.sum((query_seg < CLS).astype(FULL), 0, keepdims=True)
    dprompt_ref[...] = d_prompt + (penalty_rate / 1024.0) * slots * prompt_ref[...]

    turned = jnp.broadcast_to(shift, (WIDTH, 128)).T
    rows_ref[6:7] = turned[0:1] + jnp.sum(qpart_ref[...] * share, 0, keepdims=True)
    totals = jnp.sum(dkv_ref[WIDTH : 2 * WIDTH].astype(FULL), -1, keepdims=True)
    rows_ref[5:6] = jnp.broadcast_to(totals, (WIDTH, 128)).T[0:1]
    if layer != 0:
        return
    joined = jnp.concatenate([dprompt_ref[0:56], prompts_1[0:56], rows_ref[...], rows_1[...]], 0)
    turned = nt(pick_ref[...], joined.astype(LOW))
    ups = [nn(spot_ref[...], up[...].astype(LOW)) for up in (up_0, up_1)]
    rows = jnp.concatenate([turned[128 * part : 128 * (part + 1)] for part in range(6)], 1)
    ups = jnp.concatenate([*ups, jnp.zeros((128, WIDTH - 48), FULL)], 1)
    for half in range(2):
        spots = slice(64 * half, 64 * (half + 1))
        small_refs[half][...] = jnp.concatenate([rows[spots], ups[spots]], 0).astype(LOW)


class Joined:
    def __init__(self, moves, last, *more):
        self.moves, self.last, self.more = moves, last, more
        self.wait, self.flush = moves.wait, moves.flush

    def start(self, *refs):
        self.moves.start(*refs)
        if any(ref is self.last for ref in refs):
            self.moves.start(*self.more)


class Started(Joined):
    def start(self, *refs):
        pass


def back_body(moves, refs):
    r = iter(refs)
    take = lambda count: [next(r) for _ in range(count)]
    start, first = take(5), next(r)
    mid, slope, q, k, v, lse, prompt, vec, query_seg, key = take(10)
    small, (wqkv, wout, wup, wdown) = take(6), take(4)
    grads, mid_grad, up_spot = take(2), next(r), next(r)
    dq, qpart, dkv, pay = take(4)
    small_out = take(2)
    datt, rows_in, up, low, hid, up_row, mask, dqf, qt, dat, front, dprompt, rows = take(13)
    back_mlp_body(
        False, Joined(moves, wup, k, v, wqkv),
        [*start, first, mid, slope, vec, wout, wup, wdown]
        + [*grads, datt, mid_grad, rows_in, up_spot, up, low, hid, up_row],
    )
    back_att_body(
        0, Started(moves, None),
        [first, rows_in, datt, q, k, v, lse, prompt, vec, query_seg, key, *small[:4], up_spot, small[5]]
        + [wqkv, dq, qpart, dkv, pay, *small_out, dprompt, rows, mask, dqf, qt, dat, front],
    )


def back_call(start, first_seq, saved, prompt, vec, query_seg, key_seg, small, weights):
    mid, slope, q, k, v, lse = saved
    operands = [*start, first_seq, mid, slope, q, k, v, lse, prompt, vec, query_seg, key_seg]
    operands += [*small, *weights]
    specs = [HERE] + [VM] * 4 + [SM, VM, Late(), VM, Late(), Late()] + [VM] * 11
    specs += [Late(0), Late(0), Late(0), Late(0, 4)]
    outs = [
        Early((OWN, PACKED // 2), LOW),
        Early((OWN, PACKED // 2), LOW),
        shape((OWN, WIDTH)),
        shape((128, 24)),
        shape((OWN, WIDTH), LOW),
        shape((OWN, WIDTH)),
        Early((2 * WIDTH, KEYS), LOW),
        Early((BLOCKS, PAY, 128), LOW),
        shape((128, WIDTH), LOW),
        shape((128, WIDTH), LOW),
    ]
    space = lambda *dims: pltpu.VMEM(dims, FULL)
    low = lambda *dims: pltpu.VMEM(dims, LOW)
    scratch = [low(OWN, WIDTH), space(8, WIDTH), space(OWN, WIDTH), low(OWN, WIDTH)]
    scratch += [low(OWN, HIDDEN), space(8, HIDDEN), space(OWN, KEYS), low(OWN, WIDTH)]
    scratch += [low(WIDTH, OWN), low(WIDTH, OWN), space(WIDTH, FRONT), space(64, WIDTH)]
    scratch += [space(8, WIDTH)]
    return run(back_body, operands, specs, outs, "backward_layer", ATT, scratch)


def turn_body(moves, refs):
    r = iter(refs)
    take = lambda count: [next(r) for _ in range(count)]
    x, come, own, prompt, vec, up_bias, query_seg, key = take(8)
    cots, first = take(2), next(r)
    wqkv, wout, wup, wdown = take(4)
    normed_all, att, nmid, active, out_patch, out_cls = take(6)
    grads, mid_grad, up_spot = take(2), next(r), next(r)
    dq, qpart, dkv, pay, dprompt, rows = take(6)
    q, k, v, lse, mid, slope, out, mask = take(8)
    datt, rows_in, up, low, hid, up_row = take(6)
    dqf, qt, dat, front = take(4)
    forward_body(
        1, True, moves,
        [x, come, own, prompt, vec, up_bias, query_seg, key, wqkv, wout, wup, wdown]
        + [q, k, v, normed_all, att, lse, mid, nmid, slope, active, out, out_patch, out_cls]
        + [mask],
    )
    still = moves.resident()
    back_mlp_body(
        True, still,
        [*cots, key, query_seg, first, mid, slope, vec, wout, wup, wdown]
        + [*grads, datt, mid_grad, rows_in, up_spot, up, low, hid, up_row],
    )
    back_att_body(
        1, still,
        [first, rows_in, datt, q, k, v, lse, prompt, vec, query_seg, key, wqkv]
        + [dq, qpart, dkv, pay, dprompt, rows, mask, dqf, qt, dat, front],
    )


def turn_call(x, come, own, prompt, vec, up_bias, query_seg, key_seg, cots, first_seq, weights):
    operands = [x, come, own, prompt, vec, up_bias, query_seg, key_seg, *cots, first_seq, *weights]
    specs = [VM, HERE] + [VM] * 8 + [SM, Late(1, 3, 1), Late(1), Late(1), Late(1)]
    outs = [
        Early((KEYS, WIDTH), LOW),
        shape((OWN, WIDTH), LOW),
        shape((OWN, WIDTH), LOW),
        Early((OWN, HIDDEN), LOW),
        shape((PATCHES, WIDTH)),
        shape((CLS, 1, WIDTH)),
        Early((OWN, PACKED // 2), LOW),
        Early((OWN, PACKED // 2), LOW),
        shape((OWN, WIDTH)),
        shape((128, 24)),
        shape((OWN, WIDTH), LOW),
        shape((OWN, WIDTH)),
        Early((2 * WIDTH, KEYS), LOW),
        Early((BLOCKS, PAY, 128), LOW),
        shape((64, WIDTH)),
        shape((8, WIDTH)),
    ]
    space = lambda *dims: pltpu.VMEM(dims, FULL)
    low = lambda *dims: pltpu.VMEM(dims, LOW)
    scratch = [low(OWN, WIDTH), low(KEYS, WIDTH), low(KEYS, WIDTH), space(OWN, 128)]
    scratch += [space(OWN, WIDTH), space(OWN, HIDDEN), space(OWN, WIDTH), space(OWN, KEYS)]
    scratch += [low(OWN, WIDTH), space(8, WIDTH), space(OWN, WIDTH), low(OWN, WIDTH)]
    scratch += [low(OWN, HIDDEN), space(8, HIDDEN), low(OWN, WIDTH), low(WIDTH, OWN)]
    scratch += [low(WIDTH, OWN), space(WIDTH, FRONT)]
    return run(turn_body, operands, specs, outs, "turn_layer", TURN, scratch)


def close_body(come_ref, qpart_ref, x_ref, mid_grad_ref, vec_ref, patch_ref, cls_ref):
    rows = gathered_pull(come_ref, qpart_ref, x_ref, vec_ref[0:1], mid_grad_ref)
    split_rows(rows, patch_ref, cls_ref)


def close_call(operands):
    outs = (shape((PATCHES, WIDTH)), shape((CLS, 1, WIDTH)))
    specs = [HERE] + [VM] * (len(operands) - 1)
    return run(lambda moves, refs: close_body(*refs), operands, specs, outs, "close_norm", 2)


def left_body(plan, moves, refs):
    order_ref, *refs = refs
    picks, (all_ref, att_ref, mid_ref, active_ref) = refs[0:2], refs[2:6]
    tall_refs, wide_refs = refs[6:8], refs[8:10]
    turned_ref, down_ref = refs[10:12]

    def turn(tile, carry):
        at = tile_at(tile, TILE)
        turned_ref[at, :] = active_ref[:, at].astype(FULL).T
        return carry

    def move(spot, carry):
        source = pl.ds(pl.multiple_of(order_ref[spot] * 24, 8), 24)
        target = pl.ds(pl.multiple_of(spot * 24, 8), 24)
        down_ref[target, :] = turned_ref[source, :]
        return carry

    moves.start(all_ref)
    lax.fori_loop(0, HIDDEN // TILE, turn, 0, unroll=3)
    lax.fori_loop(0, 128, move, 0, unroll=8)
    for half in range(2):
        rows = slice(half * 2 * WIDTH, (half + 1) * 2 * WIDTH)
        tall_refs[half][0 : 2 * WIDTH, 0:OWN] = down_ref[rows].astype(LOW)
    row = 2 * WIDTH
    for kind, ring_at in plan:
        source = {"mid": mid_ref, "att": att_ref}[kind][...]
        turned = nt(picks[ring_at][...], source).astype(LOW)
        for half in range(2):
            tall_refs[half][row : row + HALF, 0:OWN] = turned[half * HALF : (half + 1) * HALF]
        row += HALF
    moves.flush(*tall_refs)
    moves.wait(all_ref)
    for half in range(2):
        wide = nt(picks[1][half * HALF : (half + 1) * HALF], all_ref[...])
        wide_refs[half][...] = wide.astype(LOW)


def left_call(plan, order, picks, normed_all, att, nmid, active):
    tall = (2 * WIDTH + len(plan) * HALF, 256)
    outs = [Early(tall, LOW)] * 2 + [shape((HALF, KEYS), LOW)] * 2
    operands = (order, *picks, normed_all, att, nmid, active)
    scratch = [pltpu.VMEM((HIDDEN, OWN), FULL), pltpu.VMEM((HIDDEN, OWN), FULL)]
    body = lambda moves, refs: left_body(plan, moves, refs)
    return run(body, operands, [SM, VM, VM, Late(), VM, VM, VM], outs, "left_factors", LEFT, scratch)


def rights_of(grad_refs, kind, part, tile):
    at = {"down": 0, "up": WIDTH + part * WIDTH, "out": WIDTH + HIDDEN}[kind] + tile * TILE
    half, at = at // (PACKED // 2), at % (PACKED // 2)
    return [grad_refs[2 * side + half][:, at : at + TILE] for side in range(2)]


def piece_shapes(classes):
    outs = []
    for number, rows in classes:
        outs += [shape((4, rows, WIDTH), LOW)] if number == 0 else [shape((rows, WIDTH), LOW)] * 4
    return outs


def by_class(classes, arrays):
    found, at = {}, 0
    for number, _ in classes:
        if number == 0:
            found[0] = [arrays[at].at[way] for way in range(4)]
            at += 1
        else:
            found[number] = list(arrays[at : at + 4])
            at += 4
    return found


def deal(out, row, values, columns):
    size = values.shape[0] // 4
    for way in range(4):
        out[way][row : row + size, columns] = values[way * size : (way + 1) * size].astype(LOW)


def mlp_body(plan, classes, refs):
    tall_refs, grad_refs = refs[0:2], refs[2:6]
    outs = by_class(classes, refs[6:])
    for kind, part, left_row, out, out_row in plan:
        for tile in range(3):
            columns = slice(tile * TILE, (tile + 1) * TILE)
            rights = rights_of(grad_refs, kind, part, tile)
            for piece in range(4 if kind == "down" else 1):
                rows = slice(left_row + piece * HALF, left_row + (piece + 1) * HALF)
                lefts = [tall[rows, 0:OWN] for tall in tall_refs]
                values = nn(lefts[0], rights[0]) + nn(lefts[1], rights[1])
                if kind == "down":
                    outs[out][piece][out_row : out_row + HALF, columns] = values.astype(LOW)
                else:
                    deal(outs[out], out_row, values, columns)


def mlp_call(plan, classes, talls, grads, micros=MLP1):
    operands = (*talls, *grads)
    body = lambda moves, refs: mlp_body(plan, classes, refs)
    out = run(body, operands, [VM] * 6, piece_shapes(classes), "grad_mlp", micros)
    return by_class_values(classes, out)


def by_class_values(classes, arrays):
    found, at = {}, 0
    for number, _ in classes:
        found[number] = arrays[at] if number == 0 else list(arrays[at : at + 4])
        at += 1 if number == 0 else 4
    return found


def mixed_body(plan, classes, small, moves, refs):
    seq_ref, *refs = refs
    tall_refs, wide_refs, dq_refs, dkv_refs = [refs[2 * at : 2 * at + 2] for at in range(4)]
    grad_refs, small_refs = refs[8:12], refs[12:14]
    outs = by_class(classes, refs[14:] if small else refs[12:])
    moves.start(*wide_refs, *dkv_refs)
    for ref in (*wide_refs, *dkv_refs):
        moves.wait(ref)
    moves.start(*tall_refs, *grad_refs)
    brought = False
    if small:
        joined = small_refs[0][...].astype(FULL) + small_refs[1][...].astype(FULL)
        for way in range(4):
            spots = [joined[64 * part + 16 * way : 64 * part + 16 * (way + 1)] for part in range(2)]
            outs[1][way][3 * HALF // 4 : 3 * HALF // 4 + 32] = jnp.concatenate(spots, 0).astype(LOW)
    for kind, left_row, out, out_row in plan:
        for tile in range(3):
            columns = slice(tile * TILE, (tile + 1) * TILE)
            values = jnp.zeros((HALF, TILE), FULL)
            for side in range(2):
                if kind in ("k", "v"):
                    at = (0 if kind == "k" else WIDTH) + tile * TILE
                    values = values + nt(wide_refs[side][...], dkv_refs[side][at : at + TILE])
                    continue
                if kind == "q" and left_row is None:
                    wide = wide_refs[side]
                    mine = pl.ds(pl.multiple_of(seq_ref[0, 0] * PATCHES, PATCHES), PATCHES)
                    left = jnp.concatenate([wide[:, mine], wide[:, CLS_AT:PROMPT_AT]], 1)
                else:
                    if not brought:
                        brought = True
                        for ref in (*tall_refs, *grad_refs):
                            moves.wait(ref)
                    left = tall_refs[side][left_row : left_row + HALF, 0:OWN]
                if kind == "q":
                    right = dq_refs[side][:, columns]
                else:
                    name, part = ("out", 0) if kind == "out" else ("up", kind)
                    right = rights_of(grad_refs, name, part, tile)[side]
                values = values + nn(left, right)
            deal(outs[out], out_row, values, columns)


def mixed_call(plan, classes, seq, talls, wides, dqs, dkvs, grads, small=()):
    operands = (seq, *talls, *wides, *dqs, *dkvs, *grads, *small)
    body = lambda moves, refs: mixed_body(plan, classes, bool(small), moves, refs)
    specs = [SM] + [Late()] * 4 + [VM] * 2 + [Late()] * 6 + [VM] * len(small)
    out = run(body, operands, specs, piece_shapes(classes), "grad_mixed", MIX)
    return by_class_values(classes, out)


def fold_body(classes, refs):
    r = iter(refs)
    totals = []
    for _, groups in classes:
        totals.append([])
        for arrays, _ in groups:
            come = next(r)
            ways = [come.at[way] for way in range(4)] if len(come.shape) == 3 else [come]
            ways += [next(r) for _ in range(arrays - 1)]
            total = ways[0][...].astype(FULL)
            for way in ways[1:]:
                total = total + way[...].astype(FULL)
            totals[-1].append(total)
    for (ways, groups), sums in zip(classes, totals):
        joint = next(r) if ways == 16 else None
        for way in range(ways):
            out = joint.at[way] if ways == 16 else next(r)
            parts = []
            for total, (_, items) in zip(sums, groups):
                at = 0
                for rows in items:
                    size = rows // ways
                    parts.append(total[at + way * size : at + (way + 1) * size])
                    at += rows
            short = out.shape[0] - sum(part.shape[0] for part in parts)
            if short:
                parts.append(jnp.zeros((short, out.shape[1]), FULL))
            out[...] = jnp.concatenate(parts, 0).astype(LOW)


def fold_call(classes, micros=FOLD):
    operands = []
    for _, groups in classes:
        for come, _ in groups:
            operands += come if isinstance(come, list) else [come]
    number = lambda come: len(come) if isinstance(come, list) else 1
    counts = [(ways, [(number(come), items) for come, items in groups]) for ways, groups in classes]
    wide = 256
    outs = []
    for ways, groups in counts:
        size = sum(sum(items) for _, items in groups) // ways
        if ways == 16:
            outs.append(shape((16, -(-size // 8) * 8, WIDTH), LOW))
        else:
            outs += [shape((size, WIDTH), LOW)] * ways
    block = lambda *dims: pl.BlockSpec((*dims, wide), lambda i: (*[0] * len(dims), i))
    return list(
        pl.pallas_call(
            lambda *refs: fold_body(counts, refs),
            grid=(WIDTH // wide,),
            out_shape=tuple(outs),
            in_specs=[block(*come.shape[:-1]) for come in operands],
            out_specs=tuple(block(*out.shape[:-1]) for out in outs),
            compiler_params=params(62),
            cost_estimate=cost(micros),
            name="ring_fold",
        )(*operands)
    )


def final_body(layouts, refs):
    r = iter(refs)
    plane, ring = next(r), [next(r) for _ in range(4)]
    arrays = ([plane.at[way] for way in range(16)], ring)
    own_w_ref, own_vec_ref = next(r), next(r)
    qkv_ref, out_ref, up_ref, down_ref = next(r), next(r), next(r), next(r)
    prompt_ref, gain_ref, bias_ref, up_bias_ref = next(r), next(r), next(r), next(r)
    pieces = []
    for array, layout in zip(arrays, layouts):
        total = array[0][...].astype(FULL)
        for way in array[1:]:
            total = total + way[...].astype(FULL)
        at = 0
        for entry in layout:
            pieces.append((entry[:3], total[at : at + entry[3]]))
            at += entry[3]
    small = None
    wholes = [jnp.zeros((6, 1), FULL)] * 2
    for (kind, layer, part), piece in pieces:
        columns = slice(part * WIDTH, (part + 1) * WIDTH)
        if kind == "qkv":
            qkv_ref[:, layer, columns] = piece
            weight = own_w_ref[layer, :, columns].astype(FULL)
            wholes[layer] = wholes[layer] + jnp.sum(piece * weight, -1, keepdims=True)
        elif kind == "out":
            out_ref[:, layer, :] = piece
        elif kind == "up":
            up_ref[:, layer, columns] = piece
        elif kind == "down":
            down_ref[layer] = piece
        elif kind == "small":
            small = jnp.concatenate([piece[:, 128 * i : 128 * (i + 1)] for i in range(6)], 0)
        else:
            up_bias_ref[0:1] = piece[:, 0:24]
            up_bias_ref[1:2] = piece[:, 24:48]
    turn = lambda values: jnp.concatenate([values, jnp.zeros((2, 128), FULL)], 0).T
    rows = turn(small)
    for layer in range(2):
        prompt_ref[:, layer, :] = small[:, 56 * layer : 56 * layer + PROMPTS]
        at = 112 + 8 * layer
        part = rows[at : at + 8, 0:6]
        whole = turn(jnp.broadcast_to(wholes[layer], (6, 128)))[0:1, 0:6]
        gain, shift = own_vec_ref[layer, 0:1], own_vec_ref[layer, 1:2]
        gain_ref[layer, 0:1] = (whole - shift * part[6:7]) / gain
        gain_ref[layer, 1:2] = part[1:2]
        for place, source in enumerate((6, 4, 5, 3, 2, 0)):
            bias_ref[place, layer : layer + 1] = part[source : source + 1]


def final_call(arrays, layouts, own_w, own_vec):
    operands = [*arrays, own_w, own_vec]
    outs = (
        shape((6, 2, 3 * WIDTH)),
        shape((6, 2, WIDTH)),
        shape((6, 2, HIDDEN)),
        shape((2, 24, WIDTH)),
        shape((6, 2, PROMPTS)),
        shape((2, 2, 6)),
        shape((6, 2, 6)),
        shape((2, 24)),
    )
    body = lambda moves, refs: final_body(layouts, refs)
    return run(body, operands, [VM] * len(operands), outs, "final_fold", 3)


def per_device(
    patches,
    cls_tokens,
    segments,
    prompts,
    w_qkv,
    w_out,
    w_up,
    w_down,
    norm_gains,
    biases,
    up_bias,
    cot_patches,
    cot_cls,
):
    layers = 2
    weights = (w_qkv, w_out, w_up, w_down)
    first_seq = (lax.axis_index("seq") == 0).astype(FULL).reshape(1, 1)
    prompt_rows = jnp.pad(prompts.astype(FULL), ((0, 0), (0, 64 - PROMPTS), (0, 0)))
    vecs = []
    for layer in range(layers):
        following = min(layer + 1, layers - 1)
        vecs.append(
            jnp.concatenate(
                [
                    norm_gains[layer],
                    biases[layer],
                    norm_gains[following, 0:1],
                    biases[following, 0:1],
                    jnp.zeros((6, WIDTH), FULL),
                ],
                0,
            )
        )
    up_rows = [jnp.broadcast_to(up_bias[layer], (8, HIDDEN)) for layer in range(layers)]
    orders = [
        owner_order(RINGS[0]),
        owner_order(RINGS[1], RINGS[1]),
        owner_order(RINGS[0], RINGS[0][:1]),
    ]
    steps = jnp.arange(6, dtype=jnp.int32)
    one_hot = lambda wanted, size: (wanted[:, None] == jnp.arange(size)[None, :]).astype(LOW)
    picks = [one_hot((order[:, None] * 6 + steps).reshape(-1), WIDTH) for order in orders]
    small_pick = one_hot((orders[1][None, :] * 6 + steps[:, None]).reshape(-1), WIDTH)
    small_spot = one_hot(orders[1], 128)

    seq = lax.axis_index("seq").astype(jnp.int32).reshape(1, 1)
    here = lax.axis_index("dp") * 8 + lax.axis_index("seq")
    mine_of = lambda values, axis: lax.dynamic_slice_in_dim(values, here * 6, 6, axis)
    own_w = mine_of(w_qkv, 1)
    own_vec = jnp.stack([mine_of(norm_gains, 2)[:, 0], mine_of(biases, 2)[:, 0]], 1)
    prompt_rows = [prompt_rows[layer] for layer in range(layers)]
    x, payload, own, query_seg = open_call(patches, cls_tokens, segments, norm_gains, biases)
    key_seg = None
    kept = []
    lefts = []
    factors = []
    left_plans = (
        (("mid", 0), ("att", 0), ("mid", 1)),
        (("mid", 0), ("mid", 1), ("att", 1)),
    )
    def left_factors(layer, *behind):
        normed_all, att, nmid, active = factors[layer]
        tall, tall_other, wide, wide_other = left_call(
            left_plans[layer], orders[2 - 2 * layer], (picks[2 - 2 * layer], picks[1]), normed_all, att, after(nmid, *behind), active
        )
        return (tall, send(tall_other, "core", 1), wide, send(wide_other, "core", 1))

    come = swap_rows(payload)
    x, vecs, up_rows, prompt_rows, picks, small_pick, small_spot, own_w, own_vec = (
        lax.optimization_barrier(
            (x, vecs, up_rows, prompt_rows, picks, small_pick, small_spot, own_w, own_vec)
        )
    )
    out = forward_call(
        0, False, x, come, own, prompt_rows[0], vecs[0], up_rows[0], query_seg, None, weights
    )
    q, k, v, normed_all, att, lse, mid, nmid, slope, active, x_next, payload, own, key_seg = out
    kept.append((x, q, k, v, lse, mid, slope))
    factors.append((normed_all, att, nmid, active))
    lefts.append(left_factors(0))
    come = swap_rows(payload)
    x = after(x_next, lefts[0][0], lefts[0][2])
    kept.append((x,))
    cots = (cot_patches[0], cot_cls[0])
    out = turn_call(
        x, come, own, prompt_rows[1], vecs[1], up_rows[1], query_seg, key_seg, cots, first_seq, weights
    )
    factors.append(out[0:4])
    out_patch, out_cls = out[4:6]

    def both(values):
        return (values, send(values, "core", 1))

    def both_parts(parts):
        return (*parts, *[send(part, "core", 1) for part in parts])

    def give_back(layer, pays, qpart, mid_grad):
        return (swap_rows(pays), qpart, kept[layer][0], mid_grad, vecs[layer])

    arrived = [[], []]

    def start_ring(at, made, rows):
        pieces, ring_at = made[at], at % 2
        axis = RINGS[ring_at][0]
        if at == 0:
            come = deal_out(pieces, (axis,))
        else:
            come = [pieces[0]] + [send(pieces[step], axis, step) for step in (1, 3, 2)]
        arrived[ring_at].append((come, rows))

    tile = HALF // 4
    mid_at = 2 * WIDTH
    packed, (mid_grad, up_row_1, dq, qpart, dkv, pays, prompts_1, rows_1) = out[6:8], out[8:]
    grads = both_parts(packed)
    dqs, dkvs = both(dq), both(dkv)
    start = give_back(1, pays, qpart, mid_grad)
    lefts.append(left_factors(1, dkv, lefts[0][1], lefts[0][3], *grads[2:]))
    plan = [("down", 0, 0, 0, 0)]
    plan += [("up", part, mid_at, 0, HALF + part * tile) for part in range(3)]
    made = mlp_call(plan, ((0, HALF + 3 * tile),), lefts[1][0:2], grads)
    plan = [("q", None, 1, 0), ("k", None, 1, tile), ("v", None, 1, 2 * tile)]
    plan += [("out", mid_at + 2 * HALF, 1, 3 * tile), (3, mid_at + HALF, 1, 4 * tile)]
    talls = (after(lefts[1][0], made[0]), lefts[1][1])
    mixed = mixed_call(plan, ((1, 5 * tile),), seq, talls, lefts[1][2:], dqs, dkvs, grads)
    start_ring(0, made, (HALF,) + (tile,) * 3)
    start_ring(1, mixed, (tile,) * 5)

    start = (after(start[0], mixed[1][0]), *start[1:])
    x_in, q, k, v, lse, mid, slope = kept[0]
    small = (small_pick, small_spot, prompts_1, rows_1, up_row_1, up_row_1)
    out = back_call(
        start, first_seq, (mid, slope, q, k, v, lse), prompt_rows[0], vecs[0], query_seg, key_seg,
        small, weights,
    )
    packed, (mid_grad, _, dq, qpart, dkv, pays) = out[0:2], out[2:8]
    grads = both_parts(packed)
    plan = [("down", 0, 0, 2, 0), ("out", 0, mid_at + HALF, 2, HALF)]
    plan += [("up", part, mid_at, 2, HALF + (1 + part) * tile) for part in range(2)]
    talls = (after(lefts[0][0], dkv, arrived[0][0][0], *arrived[1][0][0]), lefts[0][1])
    made = mlp_call(plan, ((2, HALF + 3 * tile),), talls, grads, 60)
    second_steps = made[2]
    start = give_back(0, after(pays, arrived[0][0][0]), qpart, mid_grad)
    dqs, dkvs = both(dq), both(dkv)
    small = (out[8], send(out[9], "core", 1))
    plan = [("q", None, 1, 0), ("k", None, 1, tile), ("v", None, 1, 2 * tile)]
    plan += [(part, mid_at + 2 * HALF, 1, (1 + part) * tile + 32) for part in (2, 3)]
    talls = (after(lefts[0][0], second_steps[0]), lefts[0][1])
    mixed = mixed_call(
        plan, ((1, 5 * tile + 32),), seq, talls, lefts[0][2:], dqs, dkvs, grads, small
    )
    second_steps[2] = after(second_steps[2], mixed[1][0])
    start_ring(2, {2: second_steps}, (HALF,) + (tile,) * 3)
    start_ring(1, mixed, (tile,) * 3 + (16, 16) + (tile,) * 2)
    for group in arrived:
        come, rows = group[0]
        (total,) = fold_call([(1, [(come, rows)])])
        group[0] = ([total], rows)
    grad_patch, grad_cls = close_call((after(start[0], mixed[1][0]), *start[1:]))
    (come, rows), *others = arrived[0]
    (plane,) = fold_call([(16, [([after(come[0], arrived[1][0][0][0])], rows), *others])])
    (come, rows), *others = arrived[1]
    pieces = fold_call([(4, [([after(come[0], plane)], rows), *others])])
    plane = deal_out(plane, RINGS[0][1:])
    second = [pieces[0]] + [send(pieces[step], RINGS[1][1], step) for step in range(1, 4)]
    rows = tuple(row // 4 for _, items in arrived[1] for row in items)
    pieces = fold_call([(4, [(second, rows)])], LATE)
    third = [pieces[0]] + [send(pieces[step], RINGS[1][2], step) for step in range(1, 4)]
    lasts = [plane, *third]
    layouts = (
        [("down", 1, 0, 24)]
        + [("up", 1, part, 6) for part in range(3)]
        + [("down", 0, 0, 24), ("out", 0, 0, 6)]
        + [("up", 0, part, 6) for part in range(2)],
        [("qkv", 1, part, 6) for part in range(3)]
        + [("out", 1, 0, 6), ("up", 1, 3, 6)]
        + [("qkv", 0, part, 6) for part in range(3)]
        + [("small", 0, 0, 1), ("bias", 0, 0, 1), ("up", 0, 2, 6), ("up", 0, 3, 6)],
    )
    done = final_call(lasts, layouts, own_w, own_vec)
    swap = lambda values: jnp.transpose(values, (1, 0, 2))
    return (
        out_patch[None],
        swap(out_cls),
        grad_patch[None],
        swap(grad_cls),
        jnp.transpose(done[4], (1, 2, 0)),
        swap(done[0]),
        swap(done[1]),
        swap(done[2]),
        done[3],
        done[5],
        swap(done[6]),
        done[7],
    )


def solution(mesh):
    placed = (
        P("dp", "seq", None),
        P("dp", None, None),
        P("dp", "seq"),
        P(),
        P(),
        P(),
        P(),
        P(),
        P(),
        P(),
        P(),
        P("dp", "seq", None),
        P("dp", None, None),
    )
    return jax.shard_map(
        per_device,
        mesh=mesh,
        in_specs=placed,
        out_specs=(
            P("dp", "seq", None),
            P("dp", None, None),
            P("dp", "seq", None),
            P("dp", None, None),
            P(None, None, ("dp", "seq")),
            P(None, ("dp", "seq"), None),
            P(None, ("dp", "seq"), None),
            P(None, ("dp", "seq"), None),
            P(None, ("dp", "seq"), None),
            P(None, None, ("dp", "seq")),
            P(None, None, ("dp", "seq")),
            P(None, ("dp", "seq")),
        ),
        check_vma=False,
    )
```

```python
import functools

import jax
import jax.numpy as jnp
from jax import lax
from jax.experimental import pallas as pl
from jax.experimental.pallas import tpu as pltpu
from jax.sharding import PartitionSpec as P

HEADS = 12
HEAD = 64
WIDTH = 768
HIDDEN = 3072
PATCHES = 128
CLS = 10
PROMPTS = 50
OWN = 144
KEYS = 1152
CLS_AT = 1024
PROMPT_AT = 1040
FRONT = 128
BLOCKS = 8
PAY = 864
PACKED = 2 * WIDTH + HIDDEN
HALF = WIDTH // 2
TILE = 256
LOW = jnp.bfloat16
FULL = jnp.float32

eps_norm = 1e-06
penalty_rate = 2.0
big_negative = -1e30

AXES = ("dp", "seq")
SPAN = {"core": 2, "x": 4, "y": 4, "z": 4}
RINGS = (("y", "z", "x"), ("z", "y", "x"))
ANY = pl.BlockSpec(memory_space=pl.ANY)
VM = "whole"
HERE = pl.BlockSpec(memory_space=pltpu.VMEM)
SM = pl.BlockSpec(memory_space=pltpu.SMEM)


def place_of(device):
    dp, seq = device // 8, device % 8
    return {"core": dp % 2, "x": dp // 2 % 2 * 2 + seq // 4, "y": dp // 4, "z": seq % 4}


def device_of(place):
    dp = (place["y"] * 2 + place["x"] // 2) * 2 + place["core"]
    return dp * 8 + place["x"] % 2 * 4 + place["z"]


def moved(axis, step):
    pairs = []
    for device in range(128):
        place = place_of(device)
        place[axis] = (place[axis] + step) % SPAN[axis]
        pairs.append((device, device_of(place)))
    return pairs


def send(values, axis, step):
    return lax.ppermute(values, AXES, moved(axis, step))


def groups_of(axes):
    found = {}
    for device in range(128):
        place = place_of(device)
        rest = tuple(place[axis] for axis in SPAN if axis not in axes)
        found.setdefault(rest, []).append((tuple(place[axis] for axis in axes), device))
    return [[device for _, device in sorted(group)] for group in found.values()]


def deal_out(values, axes):
    return lax.all_to_all(
        values, AXES, 0, 0, tiled=True, axis_index_groups=groups_of(axes)
    )


def swap_rows(values):
    return lax.all_to_all(values, "seq", 0, 0, tiled=True)


def owner_order(axes, steps=()):
    here = place_of(lax.axis_index("dp") * 8 + lax.axis_index("seq"))
    rest = jnp.arange(128, dtype=jnp.int32)
    place = {}
    for axis in reversed(axes):
        place[axis] = rest % SPAN[axis]
        if axis in steps:
            place[axis] = (here[axis] + place[axis]) % SPAN[axis]
        rest = rest // SPAN[axis]
    place["core"] = (here["core"] + rest) % 2
    return device_of(place)


def nn(left, right):
    return lax.dot_general(left, right, (((1,), (0,)), ((), ())), preferred_element_type=FULL)


def nt(left, right):
    return lax.dot_general(left, right, (((1,), (1,)), ((), ())), preferred_element_type=FULL)


def plain_norm(values):
    centred = values - jnp.mean(values, -1, keepdims=True)
    scale = lax.rsqrt(jnp.mean(centred * centred, -1, keepdims=True) + eps_norm)
    return centred * scale, scale


def norm_pull(plain, scale, gain, upstream):
    inner = upstream * gain
    return scale * (
        inner
        - jnp.mean(inner, -1, keepdims=True)
        - plain * jnp.mean(inner * plain, -1, keepdims=True)
    )


def whole(dims):
    return pl.BlockSpec(dims, lambda i: (0,) * len(dims))


class Late:
    def __init__(self, index=None, cuts=1, axis=0):
        self.index, self.cuts, self.axis = index, cuts, axis


class Early:
    def __init__(self, dims, kind=FULL):
        self.shape, self.dtype = dims, kind


class Moves:
    def __init__(self):
        self.ins, self.outs, self.gone = {}, {}, []

    def start(self, *refs):
        for ref in refs:
            for copy in self.ins[id(ref)]:
                copy.start()

    def resident(self):
        part = Moves()
        part.start = part.wait = lambda *_: None
        part.flush = self.flush
        return part

    def wait(self, ref, piece=None):
        copies = self.ins[id(ref)]
        for copy in copies if piece is None else copies[piece : piece + 1]:
            copy.wait()

    def flush(self, *refs):
        for ref in refs:
            copy = self.outs.pop(id(ref), None)
            if copy is not None:
                copy.start()
                self.gone.append(copy)

    def close(self):
        for copy in self.outs.values():
            copy.start()
        for copy in [*self.gone, *self.outs.values()]:
            copy.wait()


def run(body, operands, specs, outs, name, micros, scratch=(), mib=63):
    late = [(at, spec) for at, spec in enumerate(specs) if isinstance(spec, Late)]
    early = [(at, out) for at, out in enumerate(outs) if isinstance(out, Early)]
    buffers, total = [], 0
    for at, spec in late:
        dims = operands[at].shape if spec.index is None else operands[at].shape[1:]
        buffers.append(pltpu.VMEM(dims, operands[at].dtype))
        total += spec.cuts
    buffers += [pltpu.VMEM(out.shape, out.dtype) for _, out in early]
    total += len(early)

    def kernel(*refs):
        refs = list(refs)
        first = len(operands) + len(outs) + len(scratch)
        space, sems = refs[first : first + len(buffers)], refs[-1]
        moves, sem = Moves(), 0
        for (at, spec), buffer in zip(late, space):
            source = refs[at] if spec.index is None else refs[at].at[spec.index]
            size = buffer.shape[spec.axis] // spec.cuts
            copies = []
            for piece in range(spec.cuts):
                part = pl.ds(piece * size, size)
                view = lambda ref: ref.at[part] if spec.axis == 0 else ref.at[:, part]
                pair = (source, buffer) if spec.cuts == 1 else (view(source), view(buffer))
                copies.append(pltpu.make_async_copy(*pair, sems.at[sem]))
                sem += 1
            moves.ins[id(buffer)] = copies
            refs[at] = buffer
        for (at, out), buffer in zip(early, space[len(late) :]):
            at += len(operands)
            moves.outs[id(buffer)] = pltpu.make_async_copy(buffer, refs[at], sems.at[sem])
            sem += 1
            refs[at] = buffer
        body(moves, refs[:first])
        moves.close()

    in_specs = []
    for operand, spec in zip(operands, specs):
        if isinstance(spec, Late):
            in_specs.append(ANY)
        else:
            in_specs.append(whole(operand.shape) if spec == "whole" else spec)
    return pl.pallas_call(
        kernel,
        grid=(1,),
        out_shape=tuple(shape(out.shape, out.dtype) for out in outs),
        in_specs=in_specs,
        out_specs=tuple(ANY if isinstance(out, Early) else whole(out.shape) for out in outs),
        scratch_shapes=[*scratch, *buffers, pltpu.SemaphoreType.DMA((max(total, 1),))],
        compiler_params=params(mib),
        cost_estimate=cost(micros),
        name=name,
    )(*operands)


def after(values, *others):
    return lax.optimization_barrier((values, others))[0]


def tile_at(index, size):
    return pl.ds(pl.multiple_of(index * size, size), size)


def params(mib=56):
    return pltpu.CompilerParams(vmem_limit_bytes=mib * 2**20)


SHARE = 1.0
ATT = 6
LEFT = 0.1
MIX = 0.1
BMLP = 10
TURN = 40
FOLD = 0.2
LATE = 8
MLP1 = 0.1


def cost(micros):
    return pl.CostEstimate(flops=int(micros * 1.1e9), bytes_accessed=1 << 20, transcendentals=0)


def shape(dims, kind=FULL):
    return jax.ShapeDtypeStruct(dims, kind)


def open_body(patch_ref, cls_ref, seg_ref, gain_ref, bias_ref, x_ref, pay_ref, own_ref, query_ref):
    x_ref[0:PATCHES] = patch_ref[0].astype(FULL)
    cls_rows = jnp.concatenate([cls_ref[0].astype(FULL), jnp.zeros((16 - CLS, WIDTH), FULL)], 0)
    x_ref[PATCHES:OWN] = cls_rows
    plain, _ = plain_norm(x_ref[...])
    normed = (plain * gain_ref[0, 0:1] + bias_ref[0, 0:1]).astype(LOW)
    own_ref[...] = normed
    segs = seg_ref[...].astype(FULL)
    last = jnp.broadcast_to(segs, (16, PATCHES)).astype(LOW)
    last = jnp.concatenate([last, jnp.zeros((16, WIDTH - PATCHES), LOW)], 1)
    for block in range(BLOCKS):
        pay_ref[block, 0:PATCHES] = normed[0:PATCHES]
        pay_ref[block, PATCHES:OWN] = last
    query_ref[0:PATCHES] = jnp.broadcast_to(segs, (PATCHES, PATCHES)).T
    row = lax.broadcasted_iota(jnp.int32, (16, 128), 0)
    query_ref[PATCHES:OWN] = jnp.where(row < CLS, row, -5).astype(FULL)


def open_call(patches, cls_tokens, segments, gains, biases):
    outs = (
        shape((OWN, WIDTH)),
        shape((BLOCKS, OWN, WIDTH), LOW),
        shape((OWN, WIDTH), LOW),
        shape((OWN, 128)),
    )
    operands = (patches, cls_tokens, segments, gains, biases)
    return run(lambda moves, refs: open_body(*refs), operands, [VM] * 5, outs, "open_norm", 2)


def seen_mask(key_ref, query_ref, mask_ref):
    keys = key_ref[0:1, :]
    seen = (keys == query_ref[:, 0:1]) | (keys == -1.0)
    mask_ref[...] = jnp.where(seen, 0.0, big_negative)


def half_lanes(rows):
    return lax.broadcasted_iota(jnp.int32, (rows, 2 * HEAD), 1) < HEAD


def two_heads(rows, lower):
    none = jnp.zeros_like(rows)
    return jnp.concatenate([jnp.where(lower, rows, none), jnp.where(lower, none, rows)], 0)


def split_rows(rows, patch_ref, cls_ref):
    patch_ref[...] = rows[0:PATCHES]
    for place in range(CLS):
        cls_ref[place] = rows[PATCHES + place : PATCHES + place + 1]


def forward_body(layer, last, moves, refs):
    first = layer == 0
    r = iter(refs)
    nxt = lambda: next(r)
    x_ref = nxt()
    come_ref = nxt()
    own_ref, prompt_ref, vec_ref, up_bias_ref, query_seg_ref = nxt(), nxt(), nxt(), nxt(), nxt()
    key_in_ref = None if first else nxt()
    wqkv, wout, wup, wdown = nxt(), nxt(), nxt(), nxt()
    q_ref, k_ref, v_ref, all_ref = nxt(), nxt(), nxt(), nxt()
    att_ref, lse_ref, mid_ref, nmid_ref = nxt(), nxt(), nxt(), nxt()
    slope_ref, active_ref, out_ref = nxt(), nxt(), nxt()
    next_ref, next_own_ref = nxt(), nxt()
    key_ref = nxt() if first else key_in_ref
    mask_ref = nxt()

    moves.start(wqkv)
    for block in range(BLOCKS):
        all_ref[block * PATCHES : (block + 1) * PATCHES] = come_ref[block, 0:PATCHES]

    gain_one, bias_one = vec_ref[0:1], vec_ref[2:3]
    gain_two, bias_two = vec_ref[1:2], vec_ref[6:7]

    plain, _ = plain_norm(prompt_ref[...])
    all_ref[CLS_AT:PROMPT_AT] = own_ref[PATCHES:OWN]
    all_ref[PROMPT_AT : PROMPT_AT + 64] = (plain * gain_one + bias_one).astype(LOW)
    all_ref[PROMPT_AT + 64 : KEYS] = jnp.zeros((KEYS - PROMPT_AT - 64, WIDTH), LOW)
    moves.flush(all_ref)
    if first:
        lane = lax.broadcasted_iota(jnp.int32, (8, FRONT), 1)
        front = jnp.where(
            lane < CLS, lane, jnp.where((lane >= 16) & (lane < 16 + PROMPTS), -1, -2)
        )
        for block in range(BLOCKS):
            segs = come_ref[block, PATCHES:OWN, 0:PATCHES].astype(FULL)
            key_ref[:, block * PATCHES : (block + 1) * PATCHES] = segs[0:8]
        key_ref[:, CLS_AT:KEYS] = front.astype(FULL)
    seen_mask(key_ref, query_seg_ref, mask_ref)

    def keys(tile, carry):
        at = tile_at(tile, TILE)
        rows = nn(all_ref[...], wqkv[:, pl.ds(pl.multiple_of(WIDTH + tile * TILE, TILE), TILE)])
        k_ref[:, at] = rows.astype(LOW)
        return carry

    def values(tile, carry):
        at = tile_at(tile, TILE)
        rows = nn(all_ref[...], wqkv[:, pl.ds(pl.multiple_of(2 * WIDTH + tile * TILE, TILE), TILE)])
        v_ref[:, at] = (rows + vec_ref[4:5, at]).astype(LOW)
        return carry

    def queries(tile, carry):
        at = tile_at(tile, TILE)
        rows = nn(own_ref[...], wqkv[:, at]) + vec_ref[3:4, at]
        q_ref[:, at] = (rows.astype(LOW).astype(FULL) * HEAD**-0.5).astype(LOW)
        return carry

    moves.wait(wqkv, 0)
    lax.fori_loop(0, 3, queries, 0, unroll=3)
    moves.wait(wqkv, 1)
    moves.start(wout, wup)
    lax.fori_loop(0, 3, keys, 0, unroll=3)
    moves.flush(k_ref)
    moves.wait(wqkv, 2)
    lax.fori_loop(0, 3, values, 0, unroll=3)
    moves.flush(v_ref)
    moves.start(wdown)

    lse_ref[...] = jnp.zeros((OWN, 128), FULL)
    lower = half_lanes(OWN)
    lane = lax.broadcasted_iota(jnp.int32, (OWN, 128), 1)

    def heads(pair, carry):
        at = tile_at(pair, 2 * HEAD)
        query, key, value = q_ref[:, at], k_ref[:, at], v_ref[:, at]
        outs = []
        for side in range(2):
            mine = lower if side == 0 else ~lower
            scores = nt(jnp.where(mine, query, jnp.zeros_like(query)), key) + mask_ref[...]
            top = jnp.max(scores, -1, keepdims=True)
            raised = jnp.exp(scores - top)
            total = jnp.sum(raised, -1, keepdims=True)
            outs.append(nn(raised.astype(LOW), value) / total)
            lane = lax.broadcasted_iota(jnp.int32, (OWN, 128), 1)
            lse_ref[...] = jnp.where(lane == 2 * pair + side, top + jnp.log(total), lse_ref[...])
        att_ref[:, at] = jnp.where(lower, outs[0], outs[1]).astype(LOW)
        return carry

    lax.fori_loop(0, HEADS // 2, heads, 0, unroll=2)

    moves.wait(wout)

    def project(tile, carry):
        at = tile_at(tile, TILE)
        mid_ref[:, at] = x_ref[:, at] + (nn(att_ref[...], wout[:, at]) + vec_ref[5:6, at])
        return carry

    lax.fori_loop(0, 3, project, 0, unroll=3)
    plain, _ = plain_norm(mid_ref[...])
    nmid_ref[...] = (plain * gain_two + bias_two).astype(LOW)
    moves.wait(wup)

    def rise(tile, carry):
        at = tile_at(tile, TILE)
        hidden = nn(nmid_ref[...], wup[:, at]) + up_bias_ref[0:1, at]
        share = 0.5 * (1.0 + lax.erf(hidden * 0.7071067811865476))
        active_ref[:, at] = (hidden * share).astype(LOW)
        slope_ref[:, at] = share + hidden * (0.3989422804014327 * jnp.exp(-0.5 * hidden * hidden))
        return carry

    lax.fori_loop(0, HIDDEN // TILE, rise, 0, unroll=4)
    moves.flush(slope_ref, active_ref)
    moves.wait(wdown)

    def lower_back(tile, carry):
        at = tile_at(tile, TILE)
        out_ref[:, at] = mid_ref[:, at] + (nn(active_ref[...], wdown[:, at]) + vec_ref[7:8, at])
        return carry

    lax.fori_loop(0, 3, lower_back, 0, unroll=3)
    if not last:
        plain, _ = plain_norm(out_ref[...])
        normed = (plain * vec_ref[8:9] + vec_ref[9:10]).astype(LOW)
        next_own_ref[...] = normed
        for block in range(BLOCKS):
            next_ref[block] = normed[0:PATCHES]
    else:
        split_rows(out_ref[...], next_ref, next_own_ref)


def forward_call(layer, last, x, come, own, prompt, vec, up_bias, query_seg, key_seg, weights):
    first = layer == 0
    outs = [
        shape((OWN, WIDTH), LOW),
        Early((KEYS, WIDTH), LOW),
        Early((KEYS, WIDTH), LOW),
        Early((KEYS, WIDTH), LOW),
        shape((OWN, WIDTH), LOW),
        shape((OWN, 128)),
        shape((OWN, WIDTH)),
        shape((OWN, WIDTH), LOW),
        Early((OWN, HIDDEN)),
        Early((OWN, HIDDEN), LOW),
        shape((OWN, WIDTH)),
    ]
    if last:
        outs += [shape((PATCHES, WIDTH)), shape((CLS, 1, WIDTH))]
    else:
        outs += [shape((BLOCKS, PATCHES, WIDTH), LOW), shape((OWN, WIDTH), LOW)]
    if first:
        outs += [shape((8, KEYS))]
    operands = [x, come, own, prompt, vec, up_bias, query_seg]
    specs = [VM, HERE] + [VM] * 5
    if not first:
        operands.append(key_seg)
        specs.append(VM)
    operands += weights
    specs += [Late(layer, 3, 1), Late(layer), Late(layer), Late(layer)]
    scratch = [pltpu.VMEM((OWN, KEYS), FULL)]
    body = lambda moves, refs: forward_body(layer, last, moves, refs)
    return run(body, operands, specs, outs, "forward_layer", 24 * SHARE, scratch)


def gathered_pull(come_ref, qpart_ref, x_ref, gain, mid_grad_ref):
    total = come_ref[0].astype(FULL)
    for block in range(1, BLOCKS):
        total = total + come_ref[block].astype(FULL)
    patch_part = total[0:WIDTH].T
    cls_part = jnp.concatenate(
        [total[WIDTH + 16 * lane : WIDTH + 16 * (lane + 1)] for lane in range(6)], 1
    )
    d_normed = jnp.concatenate([patch_part, cls_part], 0) + qpart_ref[...]
    plain, scale = plain_norm(x_ref[...])
    return mid_grad_ref[...] + norm_pull(plain, scale, gain, d_normed)


def row_share(first_ref):
    row = lax.broadcasted_iota(jnp.int32, (OWN, 1), 0)
    return jnp.where(row < PATCHES, 1.0, jnp.where(row < PATCHES + CLS, first_ref[0, 0], 0.0))


def back_mlp_body(last, moves, refs):
    r = iter(refs)
    nxt = lambda: next(r)
    if last:
        cot_ref, cot_cls_ref, key_ref, query_seg_ref = nxt(), nxt(), nxt(), nxt()
    else:
        come_ref = nxt()
        up_qpart_ref, up_x_ref, up_mid_grad_ref, up_vec_ref = nxt(), nxt(), nxt(), nxt()
    first_ref, mid_ref, slope_ref, vec_ref = nxt(), nxt(), nxt(), nxt()
    wout, wup, wdown = nxt(), nxt(), nxt()
    grad_refs = nxt(), nxt()
    datt_ref, mid_grad_ref = nxt(), nxt()
    rows_ref, up_spot_ref = nxt(), nxt()
    up_ref, low_ref, hid_ref, up_row_ref = nxt(), nxt(), nxt(), nxt()

    moves.start(wdown, slope_ref)
    gain_two = vec_ref[1:2]
    share = row_share(first_ref)
    if last:
        valid = ((query_seg_ref[...] < CLS) & (query_seg_ref[...] >= 0)).astype(FULL)
        up_ref[0:PATCHES] = cot_ref[...].astype(FULL) * valid[0:PATCHES, 0:1]
        hits = (key_ref[0:1, 0:CLS_AT] == query_seg_ref[PATCHES:OWN, 0:1]).astype(FULL)
        present = jnp.max(hits, -1, keepdims=True)
        cls_rows = [cot_cls_ref[...].astype(FULL), jnp.zeros((16 - CLS, WIDTH), FULL)]
        up_ref[PATCHES:OWN] = jnp.concatenate(cls_rows, 0) * present
    else:
        up_ref[...] = gathered_pull(
            come_ref, up_qpart_ref, up_x_ref, up_vec_ref[0:1], up_mid_grad_ref
        )
    low_ref[...] = up_ref[...].astype(LOW)
    weighted = low_ref[...].astype(FULL) * share
    grad_refs[0][:, 0:WIDTH] = weighted.astype(LOW)
    rows_ref[...] = jnp.zeros((8, WIDTH), FULL)
    rows_ref[0:1] = jnp.sum(weighted, 0, keepdims=True)
    moves.start(wup)

    def to_hidden(half, tile, carry):
        at = tile_at(tile, TILE)
        grad = (nt(low_ref[...], wdown[at, :]) * slope_ref[:, at]).astype(LOW)
        hid_ref[:, at] = grad
        counted = grad.astype(FULL) * share
        to = WIDTH + tile * TILE - half * (PACKED // 2)
        grad_refs[half][:, pl.ds(pl.multiple_of(to, TILE), TILE)] = counted.astype(LOW)
        up_row_ref[:, at] = jnp.broadcast_to(jnp.sum(counted, 0, keepdims=True), (8, TILE))
        return carry

    moves.wait(slope_ref)
    for piece in range(4):
        moves.wait(wdown, piece)
        body = functools.partial(to_hidden, piece // 2)
        lax.fori_loop(3 * piece, 3 * piece + 3, body, 0, unroll=3)
    moves.wait(wup)
    moves.start(wout)

    def to_mid(tile, carry):
        at = tile_at(tile, TILE)
        mid_grad_ref[:, at] = nt(hid_ref[...], wup[at, :])
        return carry

    lax.fori_loop(0, 3, to_mid, 0, unroll=3)
    d_normed = mid_grad_ref[...]
    plain, scale = plain_norm(mid_ref[...])
    counted = d_normed * share
    rows_ref[1:2] = jnp.sum(counted * plain, 0, keepdims=True)
    rows_ref[2:3] = jnp.sum(counted, 0, keepdims=True)
    mid_grad_ref[...] = up_ref[...] + norm_pull(plain, scale, gain_two, d_normed)
    low_ref[...] = mid_grad_ref[...].astype(LOW)
    weighted = low_ref[...].astype(FULL) * share
    grad_refs[1][:, PACKED // 2 - WIDTH :] = weighted.astype(LOW)
    rows_ref[3:4] = jnp.sum(weighted, 0, keepdims=True)
    moves.flush(*grad_refs)
    up_row = up_row_ref[0:1]
    spots = [up_row[:, 24 * spot : 24 * (spot + 1)] for spot in range(128)]
    up_spot_ref[...] = jnp.concatenate(spots, 0)
    moves.wait(wout)

    def to_att(tile, carry):
        at = tile_at(tile, TILE)
        datt_ref[:, at] = nt(low_ref[...], wout[at, :]).astype(LOW)
        return carry

    lax.fori_loop(0, 3, to_att, 0, unroll=3)


def back_att_body(layer, moves, refs):
    r = iter(refs)
    nxt = lambda: next(r)
    first_ref, rows_in_ref, datt_ref = nxt(), nxt(), nxt()
    q_ref, k_ref, v_ref, lse_ref = nxt(), nxt(), nxt(), nxt()
    prompt_ref, vec_ref, query_seg_ref, key_ref = nxt(), nxt(), nxt(), nxt()
    if layer == 0:
        pick_ref, spot_ref, prompts_1, rows_1, up_0, up_1 = [nxt() for _ in range(6)]
    wqkv = nxt()
    dq_ref, qpart_ref, dkv_ref, pay_ref = nxt(), nxt(), nxt(), nxt()
    if layer == 0:
        small_refs = nxt(), nxt()
        dprompt_ref, rows_ref = nxt(), nxt()
    else:
        dprompt_ref, rows_ref = nxt(), nxt()
    mask_ref, dqf_ref, qt_ref, dat_ref, front_ref = [nxt() for _ in range(5)]

    moves.start(k_ref, v_ref, wqkv)
    gain_one = vec_ref[0:1]
    share = row_share(first_ref)
    seen_mask(key_ref, query_seg_ref, mask_ref)
    rows_ref[...] = rows_in_ref[...]

    def turn(tile, carry):
        at = tile_at(tile, TILE)
        dat_ref[at, :] = (datt_ref[:, at].astype(FULL) * share).T.astype(LOW)
        qt_ref[at, :] = (q_ref[:, at].astype(FULL) * share).T.astype(LOW)
        return carry

    lax.fori_loop(0, 3, turn, 0, unroll=3)
    lower = half_lanes(OWN)
    lane = lax.broadcasted_iota(jnp.int32, (OWN, 128), 1)
    moves.wait(k_ref)
    moves.wait(v_ref)

    def heads(pair, carry):
        at = tile_at(pair, 2 * HEAD)
        query, key, value, grad = q_ref[:, at], k_ref[:, at], v_ref[:, at], datt_ref[:, at]
        outs = []
        for side in range(2):
            mine = lower if side == 0 else ~lower
            head = 2 * pair + side
            log_total = jnp.sum(jnp.where(lane == head, lse_ref[...], 0.0), -1, keepdims=True)
            scores = nt(jnp.where(mine, query, jnp.zeros_like(query)), key) + mask_ref[...]
            probs = jnp.exp(scores - log_total)
            d_probs = nt(jnp.where(mine, grad, jnp.zeros_like(grad)), value)
            both = probs * d_probs
            across = jnp.sum(both, -1, keepdims=True)
            d_scores = (both - probs * across).astype(LOW)
            probs_low = probs.astype(LOW)
            outs.append(nn(d_scores, key))
            rows = tile_at(head, HEAD)
            dkv_ref[rows, :] = nn(qt_ref[rows, :], d_scores).astype(LOW)
            value_rows = pl.ds(pl.multiple_of(WIDTH + head * HEAD, HEAD), HEAD)
            dkv_ref[value_rows, :] = nn(dat_ref[rows, :], probs_low).astype(LOW)
        dqf_ref[:, at] = (jnp.where(lower, outs[0], outs[1]) * HEAD**-0.5).astype(LOW)
        return carry

    lax.fori_loop(0, HEADS // 2, heads, 0, unroll=2)
    moves.flush(dkv_ref)
    counted = dqf_ref[...].astype(FULL) * share
    dq_ref[...] = counted.astype(LOW)
    rows_ref[4:5] = jnp.sum(counted, 0, keepdims=True)
    moves.wait(wqkv)

    def to_normed(tile, carry):
        at = tile_at(tile, TILE)
        qpart_ref[:, at] = nt(dqf_ref[...], wqkv[at, 0:WIDTH])
        return carry

    lax.fori_loop(0, 3, to_normed, 0, unroll=3)

    front_ref[...] = nn(wqkv[:, WIDTH:], dkv_ref[:, CLS_AT:KEYS])
    shift = jnp.sum(front_ref[...], -1, keepdims=True)
    front = front_ref[...].T
    cls_rows = jnp.concatenate(
        [front[0:16, 128 * place : 128 * (place + 1)] for place in range(6)], 0
    )
    for block in range(0, BLOCKS, 2):
        part = nn(wqkv[:, WIDTH:], dkv_ref[:, block * PATCHES : (block + 2) * PATCHES])
        shift = shift + jnp.sum(part, -1, keepdims=True)
        for side in range(2):
            pay_ref[block + side, 0:WIDTH] = part[:, side * PATCHES : (side + 1) * PATCHES].astype(LOW)
            pay_ref[block + side, WIDTH:PAY] = cls_rows.astype(LOW)
    moves.flush(pay_ref)

    plain, scale = plain_norm(prompt_ref[...])
    d_prompt = norm_pull(plain, scale, gain_one, front[16:80])
    query_seg = query_seg_ref[0:PATCHES, 0:1]
    slots = jnp.sum((query_seg < CLS).astype(FULL), 0, keepdims=True)
    dprompt_ref[...] = d_prompt + (penalty_rate / 1024.0) * slots * prompt_ref[...]

    turned = jnp.broadcast_to(shift, (WIDTH, 128)).T
    rows_ref[6:7] = turned[0:1] + jnp.sum(qpart_ref[...] * share, 0, keepdims=True)
    totals = jnp.sum(dkv_ref[WIDTH : 2 * WIDTH].astype(FULL), -1, keepdims=True)
    rows_ref[5:6] = jnp.broadcast_to(totals, (WIDTH, 128)).T[0:1]
    if layer != 0:
        return
    joined = jnp.concatenate([dprompt_ref[0:56], prompts_1[0:56], rows_ref[...], rows_1[...]], 0)
    turned = nt(pick_ref[...], joined.astype(LOW))
    ups = [nn(spot_ref[...], up[...].astype(LOW)) for up in (up_0, up_1)]
    rows = jnp.concatenate([turned[128 * part : 128 * (part + 1)] for part in range(6)], 1)
    ups = jnp.concatenate([*ups, jnp.zeros((128, WIDTH - 48), FULL)], 1)
    for half in range(2):
        spots = slice(64 * half, 64 * (half + 1))
        small_refs[half][...] = jnp.concatenate([rows[spots], ups[spots]], 0).astype(LOW)


class Joined:
    def __init__(self, moves, last, *more):
        self.moves, self.last, self.more = moves, last, more
        self.wait, self.flush = moves.wait, moves.flush

    def start(self, *refs):
        self.moves.start(*refs)
        if any(ref is self.last for ref in refs):
            self.moves.start(*self.more)


class Started(Joined):
    def start(self, *refs):
        pass


def back_body(moves, refs):
    r = iter(refs)
    take = lambda count: [next(r) for _ in range(count)]
    start, first = take(5), next(r)
    mid, slope, q, k, v, lse, prompt, vec, query_seg, key = take(10)
    small, (wqkv, wout, wup, wdown) = take(6), take(4)
    grads, mid_grad, up_spot = take(2), next(r), next(r)
    dq, qpart, dkv, pay = take(4)
    small_out = take(2)
    datt, rows_in, up, low, hid, up_row, mask, dqf, qt, dat, front, dprompt, rows = take(13)
    back_mlp_body(
        False, Joined(moves, wup, k, v, wqkv),
        [*start, first, mid, slope, vec, wout, wup, wdown]
        + [*grads, datt, mid_grad, rows_in, up_spot, up, low, hid, up_row],
    )
    back_att_body(
        0, Started(moves, None),
        [first, rows_in, datt, q, k, v, lse, prompt, vec, query_seg, key, *small[:4], up_spot, small[5]]
        + [wqkv, dq, qpart, dkv, pay, *small_out, dprompt, rows, mask, dqf, qt, dat, front],
    )


def back_call(start, first_seq, saved, prompt, vec, query_seg, key_seg, small, weights):
    mid, slope, q, k, v, lse = saved
    operands = [*start, first_seq, mid, slope, q, k, v, lse, prompt, vec, query_seg, key_seg]
    operands += [*small, *weights]
    specs = [HERE] + [VM] * 4 + [SM, VM, Late(), VM, Late(), Late()] + [VM] * 11
    specs += [Late(0), Late(0), Late(0), Late(0, 4)]
    outs = [
        Early((OWN, PACKED // 2), LOW),
        Early((OWN, PACKED // 2), LOW),
        shape((OWN, WIDTH)),
        shape((128, 24)),
        shape((OWN, WIDTH), LOW),
        shape((OWN, WIDTH)),
        Early((2 * WIDTH, KEYS), LOW),
        Early((BLOCKS, PAY, 128), LOW),
        shape((128, WIDTH), LOW),
        shape((128, WIDTH), LOW),
    ]
    space = lambda *dims: pltpu.VMEM(dims, FULL)
    low = lambda *dims: pltpu.VMEM(dims, LOW)
    scratch = [low(OWN, WIDTH), space(8, WIDTH), space(OWN, WIDTH), low(OWN, WIDTH)]
    scratch += [low(OWN, HIDDEN), space(8, HIDDEN), space(OWN, KEYS), low(OWN, WIDTH)]
    scratch += [low(WIDTH, OWN), low(WIDTH, OWN), space(WIDTH, FRONT), space(64, WIDTH)]
    scratch += [space(8, WIDTH)]
    return run(back_body, operands, specs, outs, "backward_layer", ATT, scratch)


def turn_body(moves, refs):
    r = iter(refs)
    take = lambda count: [next(r) for _ in range(count)]
    x, come, own, prompt, vec, up_bias, query_seg, key = take(8)
    cots, first = take(2), next(r)
    wqkv, wout, wup, wdown = take(4)
    normed_all, att, nmid, active, out_patch, out_cls = take(6)
    grads, mid_grad, up_spot = take(2), next(r), next(r)
    dq, qpart, dkv, pay, dprompt, rows = take(6)
    q, k, v, lse, mid, slope, out, mask = take(8)
    datt, rows_in, up, low, hid, up_row = take(6)
    dqf, qt, dat, front = take(4)
    forward_body(
        1, True, moves,
        [x, come, own, prompt, vec, up_bias, query_seg, key, wqkv, wout, wup, wdown]
        + [q, k, v, normed_all, att, lse, mid, nmid, slope, active, out, out_patch, out_cls]
        + [mask],
    )
    still = moves.resident()
    back_mlp_body(
        True, still,
        [*cots, key, query_seg, first, mid, slope, vec, wout, wup, wdown]
        + [*grads, datt, mid_grad, rows_in, up_spot, up, low, hid, up_row],
    )
    back_att_body(
        1, still,
        [first, rows_in, datt, q, k, v, lse, prompt, vec, query_seg, key, wqkv]
        + [dq, qpart, dkv, pay, dprompt, rows, mask, dqf, qt, dat, front],
    )


def turn_call(x, come, own, prompt, vec, up_bias, query_seg, key_seg, cots, first_seq, weights):
    operands = [x, come, own, prompt, vec, up_bias, query_seg, key_seg, *cots, first_seq, *weights]
    specs = [VM, HERE] + [VM] * 8 + [SM, Late(1, 3, 1), Late(1), Late(1), Late(1)]
    outs = [
        Early((KEYS, WIDTH), LOW),
        shape((OWN, WIDTH), LOW),
        shape((OWN, WIDTH), LOW),
        Early((OWN, HIDDEN), LOW),
        shape((PATCHES, WIDTH)),
        shape((CLS, 1, WIDTH)),
        Early((OWN, PACKED // 2), LOW),
        Early((OWN, PACKED // 2), LOW),
        shape((OWN, WIDTH)),
        shape((128, 24)),
        shape((OWN, WIDTH), LOW),
        shape((OWN, WIDTH)),
        Early((2 * WIDTH, KEYS), LOW),
        Early((BLOCKS, PAY, 128), LOW),
        shape((64, WIDTH)),
        shape((8, WIDTH)),
    ]
    space = lambda *dims: pltpu.VMEM(dims, FULL)
    low = lambda *dims: pltpu.VMEM(dims, LOW)
    scratch = [low(OWN, WIDTH), low(KEYS, WIDTH), low(KEYS, WIDTH), space(OWN, 128)]
    scratch += [space(OWN, WIDTH), space(OWN, HIDDEN), space(OWN, WIDTH), space(OWN, KEYS)]
    scratch += [low(OWN, WIDTH), space(8, WIDTH), space(OWN, WIDTH), low(OWN, WIDTH)]
    scratch += [low(OWN, HIDDEN), space(8, HIDDEN), low(OWN, WIDTH), low(WIDTH, OWN)]
    scratch += [low(WIDTH, OWN), space(WIDTH, FRONT)]
    return run(turn_body, operands, specs, outs, "turn_layer", TURN, scratch)


def close_body(come_ref, qpart_ref, x_ref, mid_grad_ref, vec_ref, patch_ref, cls_ref):
    rows = gathered_pull(come_ref, qpart_ref, x_ref, vec_ref[0:1], mid_grad_ref)
    split_rows(rows, patch_ref, cls_ref)


def close_call(operands):
    outs = (shape((PATCHES, WIDTH)), shape((CLS, 1, WIDTH)))
    specs = [HERE] + [VM] * (len(operands) - 1)
    return run(lambda moves, refs: close_body(*refs), operands, specs, outs, "close_norm", 2)


def left_body(plan, moves, refs):
    order_ref, *refs = refs
    picks, (all_ref, att_ref, mid_ref, active_ref) = refs[0:2], refs[2:6]
    tall_refs, wide_refs = refs[6:8], refs[8:10]
    turned_ref, down_ref = refs[10:12]

    def turn(tile, carry):
        at = tile_at(tile, TILE)
        turned_ref[at, :] = active_ref[:, at].astype(FULL).T
        return carry

    def move(spot, carry):
        source = pl.ds(pl.multiple_of(order_ref[spot] * 24, 8), 24)
        target = pl.ds(pl.multiple_of(spot * 24, 8), 24)
        down_ref[target, :] = turned_ref[source, :]
        return carry

    moves.start(all_ref)
    lax.fori_loop(0, HIDDEN // TILE, turn, 0, unroll=3)
    lax.fori_loop(0, 128, move, 0, unroll=8)
    for half in range(2):
        rows = slice(half * 2 * WIDTH, (half + 1) * 2 * WIDTH)
        tall_refs[half][0 : 2 * WIDTH, 0:OWN] = down_ref[rows].astype(LOW)
    row = 2 * WIDTH
    for kind, ring_at in plan:
        source = {"mid": mid_ref, "att": att_ref}[kind][...]
        turned = nt(picks[ring_at][...], source).astype(LOW)
        for half in range(2):
            tall_refs[half][row : row + HALF, 0:OWN] = turned[half * HALF : (half + 1) * HALF]
        row += HALF
    moves.flush(*tall_refs)
    moves.wait(all_ref)
    for half in range(2):
        wide = nt(picks[1][half * HALF : (half + 1) * HALF], all_ref[...])
        wide_refs[half][...] = wide.astype(LOW)


def left_call(plan, order, picks, normed_all, att, nmid, active):
    tall = (2 * WIDTH + len(plan) * HALF, 256)
    outs = [Early(tall, LOW)] * 2 + [shape((HALF, KEYS), LOW)] * 2
    operands = (order, *picks, normed_all, att, nmid, active)
    scratch = [pltpu.VMEM((HIDDEN, OWN), FULL), pltpu.VMEM((HIDDEN, OWN), FULL)]
    body = lambda moves, refs: left_body(plan, moves, refs)
    return run(body, operands, [SM, VM, VM, Late(), VM, VM, VM], outs, "left_factors", LEFT, scratch)


def rights_of(grad_refs, kind, part, tile):
    at = {"down": 0, "up": WIDTH + part * WIDTH, "out": WIDTH + HIDDEN}[kind] + tile * TILE
    half, at = at // (PACKED // 2), at % (PACKED // 2)
    return [grad_refs[2 * side + half][:, at : at + TILE] for side in range(2)]


def piece_shapes(classes):
    outs = []
    for number, rows in classes:
        outs += [shape((4, rows, WIDTH), LOW)] if number == 0 else [shape((rows, WIDTH), LOW)] * 4
    return outs


def by_class(classes, arrays):
    found, at = {}, 0
    for number, _ in classes:
        if number == 0:
            found[0] = [arrays[at].at[way] for way in range(4)]
            at += 1
        else:
            found[number] = list(arrays[at : at + 4])
            at += 4
    return found


def deal(out, row, values, columns):
    size = values.shape[0] // 4
    for way in range(4):
        out[way][row : row + size, columns] = values[way * size : (way + 1) * size].astype(LOW)


def mlp_body(plan, classes, refs):
    tall_refs, grad_refs = refs[0:2], refs[2:6]
    outs = by_class(classes, refs[6:])
    for kind, part, left_row, out, out_row in plan:
        for tile in range(3):
            columns = slice(tile * TILE, (tile + 1) * TILE)
            rights = rights_of(grad_refs, kind, part, tile)
            for piece in range(4 if kind == "down" else 1):
                rows = slice(left_row + piece * HALF, left_row + (piece + 1) * HALF)
                lefts = [tall[rows, 0:OWN] for tall in tall_refs]
                values = nn(lefts[0], rights[0]) + nn(lefts[1], rights[1])
                if kind == "down":
                    outs[out][piece][out_row : out_row + HALF, columns] = values.astype(LOW)
                else:
                    deal(outs[out], out_row, values, columns)


def mlp_call(plan, classes, talls, grads, micros=MLP1):
    operands = (*talls, *grads)
    body = lambda moves, refs: mlp_body(plan, classes, refs)
    out = run(body, operands, [VM] * 6, piece_shapes(classes), "grad_mlp", micros)
    return by_class_values(classes, out)


def by_class_values(classes, arrays):
    found, at = {}, 0
    for number, _ in classes:
        found[number] = arrays[at] if number == 0 else list(arrays[at : at + 4])
        at += 1 if number == 0 else 4
    return found


def mixed_body(plan, classes, small, moves, refs):
    seq_ref, *refs = refs
    tall_refs, wide_refs, dq_refs, dkv_refs = [refs[2 * at : 2 * at + 2] for at in range(4)]
    grad_refs, small_refs = refs[8:12], refs[12:14]
    outs = by_class(classes, refs[14:] if small else refs[12:])
    moves.start(*wide_refs, *dkv_refs)
    for ref in (*wide_refs, *dkv_refs):
        moves.wait(ref)
    moves.start(*tall_refs, *grad_refs)
    brought = False
    if small:
        joined = small_refs[0][...].astype(FULL) + small_refs[1][...].astype(FULL)
        for way in range(4):
            spots = [joined[64 * part + 16 * way : 64 * part + 16 * (way + 1)] for part in range(2)]
            outs[1][way][3 * HALF // 4 : 3 * HALF // 4 + 32] = jnp.concatenate(spots, 0).astype(LOW)
    for kind, left_row, out, out_row in plan:
        for tile in range(3):
            columns = slice(tile * TILE, (tile + 1) * TILE)
            values = jnp.zeros((HALF, TILE), FULL)
            for side in range(2):
                if kind in ("k", "v"):
                    at = (0 if kind == "k" else WIDTH) + tile * TILE
                    values = values + nt(wide_refs[side][...], dkv_refs[side][at : at + TILE])
                    continue
                if kind == "q" and left_row is None:
                    wide = wide_refs[side]
                    mine = pl.ds(pl.multiple_of(seq_ref[0, 0] * PATCHES, PATCHES), PATCHES)
                    left = jnp.concatenate([wide[:, mine], wide[:, CLS_AT:PROMPT_AT]], 1)
                else:
                    if not brought:
                        brought = True
                        for ref in (*tall_refs, *grad_refs):
                            moves.wait(ref)
                    left = tall_refs[side][left_row : left_row + HALF, 0:OWN]
                if kind == "q":
                    right = dq_refs[side][:, columns]
                else:
                    name, part = ("out", 0) if kind == "out" else ("up", kind)
                    right = rights_of(grad_refs, name, part, tile)[side]
                values = values + nn(left, right)
            deal(outs[out], out_row, values, columns)


def mixed_call(plan, classes, seq, talls, wides, dqs, dkvs, grads, small=()):
    operands = (seq, *talls, *wides, *dqs, *dkvs, *grads, *small)
    body = lambda moves, refs: mixed_body(plan, classes, bool(small), moves, refs)
    specs = [SM] + [Late()] * 4 + [VM] * 2 + [Late()] * 6 + [VM] * len(small)
    out = run(body, operands, specs, piece_shapes(classes), "grad_mixed", MIX)
    return by_class_values(classes, out)


def fold_body(classes, refs):
    r = iter(refs)
    totals = []
    for _, groups in classes:
        totals.append([])
        for arrays, _ in groups:
            come = next(r)
            ways = [come.at[way] for way in range(4)] if len(come.shape) == 3 else [come]
            ways += [next(r) for _ in range(arrays - 1)]
            total = ways[0][...].astype(FULL)
            for way in ways[1:]:
                total = total + way[...].astype(FULL)
            totals[-1].append(total)
    for (ways, groups), sums in zip(classes, totals):
        joint = next(r) if ways == 16 else None
        for way in range(ways):
            out = joint.at[way] if ways == 16 else next(r)
            parts = []
            for total, (_, items) in zip(sums, groups):
                at = 0
                for rows in items:
                    size = rows // ways
                    parts.append(total[at + way * size : at + (way + 1) * size])
                    at += rows
            short = out.shape[0] - sum(part.shape[0] for part in parts)
            if short:
                parts.append(jnp.zeros((short, out.shape[1]), FULL))
            out[...] = jnp.concatenate(parts, 0).astype(LOW)


def fold_call(classes, micros=FOLD):
    operands = []
    for _, groups in classes:
        for come, _ in groups:
            operands += come if isinstance(come, list) else [come]
    number = lambda come: len(come) if isinstance(come, list) else 1
    counts = [(ways, [(number(come), items) for come, items in groups]) for ways, groups in classes]
    wide = 256
    outs = []
    for ways, groups in counts:
        size = sum(sum(items) for _, items in groups) // ways
        if ways == 16:
            outs.append(shape((16, -(-size // 8) * 8, WIDTH), LOW))
        else:
            outs += [shape((size, WIDTH), LOW)] * ways
    block = lambda *dims: pl.BlockSpec((*dims, wide), lambda i: (*[0] * len(dims), i))
    return list(
        pl.pallas_call(
            lambda *refs: fold_body(counts, refs),
            grid=(WIDTH // wide,),
            out_shape=tuple(outs),
            in_specs=[block(*come.shape[:-1]) for come in operands],
            out_specs=tuple(block(*out.shape[:-1]) for out in outs),
            compiler_params=params(63),
            cost_estimate=cost(micros),
            name="ring_fold",
        )(*operands)
    )


def final_body(layouts, refs):
    r = iter(refs)
    plane, ring = next(r), [next(r) for _ in range(4)]
    arrays = ([plane.at[way] for way in range(16)], ring)
    own_w_ref, own_vec_ref = next(r), next(r)
    qkv_ref, out_ref, up_ref, down_ref = next(r), next(r), next(r), next(r)
    prompt_ref, gain_ref, bias_ref, up_bias_ref = next(r), next(r), next(r), next(r)
    pieces = []
    for array, layout in zip(arrays, layouts):
        total = array[0][...].astype(FULL)
        for way in array[1:]:
            total = total + way[...].astype(FULL)
        at = 0
        for entry in layout:
            pieces.append((entry[:3], total[at : at + entry[3]]))
            at += entry[3]
    small = None
    wholes = [jnp.zeros((6, 1), FULL)] * 2
    for (kind, layer, part), piece in pieces:
        columns = slice(part * WIDTH, (part + 1) * WIDTH)
        if kind == "qkv":
            qkv_ref[:, layer, columns] = piece
            weight = own_w_ref[layer, :, columns].astype(FULL)
            wholes[layer] = wholes[layer] + jnp.sum(piece * weight, -1, keepdims=True)
        elif kind == "out":
            out_ref[:, layer, :] = piece
        elif kind == "up":
            up_ref[:, layer, columns] = piece
        elif kind == "down":
            down_ref[layer] = piece
        elif kind == "small":
            small = jnp.concatenate([piece[:, 128 * i : 128 * (i + 1)] for i in range(6)], 0)
        else:
            up_bias_ref[0:1] = piece[:, 0:24]
            up_bias_ref[1:2] = piece[:, 24:48]
    turn = lambda values: jnp.concatenate([values, jnp.zeros((2, 128), FULL)], 0).T
    rows = turn(small)
    for layer in range(2):
        prompt_ref[:, layer, :] = small[:, 56 * layer : 56 * layer + PROMPTS]
        at = 112 + 8 * layer
        part = rows[at : at + 8, 0:6]
        whole = turn(jnp.broadcast_to(wholes[layer], (6, 128)))[0:1, 0:6]
        gain, shift = own_vec_ref[layer, 0:1], own_vec_ref[layer, 1:2]
        gain_ref[layer, 0:1] = (whole - shift * part[6:7]) / gain
        gain_ref[layer, 1:2] = part[1:2]
        for place, source in enumerate((6, 4, 5, 3, 2, 0)):
            bias_ref[place, layer : layer + 1] = part[source : source + 1]


def final_call(arrays, layouts, own_w, own_vec):
    operands = [*arrays, own_w, own_vec]
    outs = (
        shape((6, 2, 3 * WIDTH)),
        shape((6, 2, WIDTH)),
        shape((6, 2, HIDDEN)),
        shape((2, 24, WIDTH)),
        shape((6, 2, PROMPTS)),
        shape((2, 2, 6)),
        shape((6, 2, 6)),
        shape((2, 24)),
    )
    body = lambda moves, refs: final_body(layouts, refs)
    return run(body, operands, [VM] * len(operands), outs, "final_fold", 3)


def per_device(
    patches,
    cls_tokens,
    segments,
    prompts,
    w_qkv,
    w_out,
    w_up,
    w_down,
    norm_gains,
    biases,
    up_bias,
    cot_patches,
    cot_cls,
):
    layers = 2
    weights = (w_qkv, w_out, w_up, w_down)
    first_seq = (lax.axis_index("seq") == 0).astype(FULL).reshape(1, 1)
    prompt_rows = jnp.pad(prompts.astype(FULL), ((0, 0), (0, 64 - PROMPTS), (0, 0)))
    vecs = []
    for layer in range(layers):
        following = min(layer + 1, layers - 1)
        vecs.append(
            jnp.concatenate(
                [
                    norm_gains[layer],
                    biases[layer],
                    norm_gains[following, 0:1],
                    biases[following, 0:1],
                    jnp.zeros((6, WIDTH), FULL),
                ],
                0,
            )
        )
    up_rows = [jnp.broadcast_to(up_bias[layer], (8, HIDDEN)) for layer in range(layers)]
    orders = [
        owner_order(RINGS[0]),
        owner_order(RINGS[1], RINGS[1]),
        owner_order(RINGS[0], RINGS[0][:1]),
    ]
    steps = jnp.arange(6, dtype=jnp.int32)
    one_hot = lambda wanted, size: (wanted[:, None] == jnp.arange(size)[None, :]).astype(LOW)
    picks = [one_hot((order[:, None] * 6 + steps).reshape(-1), WIDTH) for order in orders]
    small_pick = one_hot((orders[1][None, :] * 6 + steps[:, None]).reshape(-1), WIDTH)
    small_spot = one_hot(orders[1], 128)

    seq = lax.axis_index("seq").astype(jnp.int32).reshape(1, 1)
    here = lax.axis_index("dp") * 8 + lax.axis_index("seq")
    mine_of = lambda values, axis: lax.dynamic_slice_in_dim(values, here * 6, 6, axis)
    own_w = mine_of(w_qkv, 1)
    own_vec = jnp.stack([mine_of(norm_gains, 2)[:, 0], mine_of(biases, 2)[:, 0]], 1)
    prompt_rows = [prompt_rows[layer] for layer in range(layers)]
    x, payload, own, query_seg = open_call(patches, cls_tokens, segments, norm_gains, biases)
    key_seg = None
    kept = []
    lefts = []
    factors = []
    left_plans = (
        (("mid", 0), ("att", 0), ("mid", 1)),
        (("mid", 0), ("mid", 1), ("att", 1)),
    )
    def left_factors(layer, *behind):
        normed_all, att, nmid, active = factors[layer]
        tall, tall_other, wide, wide_other = left_call(
            left_plans[layer], orders[2 - 2 * layer], (picks[2 - 2 * layer], picks[1]), normed_all, att, after(nmid, *behind), active
        )
        return (tall, send(tall_other, "core", 1), wide, send(wide_other, "core", 1))

    come = swap_rows(payload)
    x, vecs, up_rows, prompt_rows, picks, small_pick, small_spot, own_w, own_vec = (
        lax.optimization_barrier(
            (x, vecs, up_rows, prompt_rows, picks, small_pick, small_spot, own_w, own_vec)
        )
    )
    out = forward_call(
        0, False, x, come, own, prompt_rows[0], vecs[0], up_rows[0], query_seg, None, weights
    )
    q, k, v, normed_all, att, lse, mid, nmid, slope, active, x_next, payload, own, key_seg = out
    kept.append((x, q, k, v, lse, mid, slope))
    factors.append((normed_all, att, nmid, active))
    lefts.append(left_factors(0))
    come = swap_rows(payload)
    x = after(x_next, lefts[0][0], lefts[0][2])
    kept.append((x,))
    cots = (cot_patches[0], cot_cls[0])
    out = turn_call(
        x, come, own, prompt_rows[1], vecs[1], up_rows[1], query_seg, key_seg, cots, first_seq, weights
    )
    factors.append(out[0:4])
    out_patch, out_cls = out[4:6]

    def both(values):
        return (values, send(values, "core", 1))

    def both_parts(parts):
        return (*parts, *[send(part, "core", 1) for part in parts])

    def give_back(layer, pays, qpart, mid_grad):
        return (swap_rows(pays), qpart, kept[layer][0], mid_grad, vecs[layer])

    arrived = [[], []]

    def start_ring(at, made, rows):
        pieces, ring_at = made[at], at % 2
        axis = RINGS[ring_at][0]
        if at == 0:
            come = deal_out(pieces, (axis,))
        else:
            come = [pieces[0]] + [send(pieces[step], axis, step) for step in (1, 3, 2)]
        arrived[ring_at].append((come, rows))

    tile = HALF // 4
    mid_at = 2 * WIDTH
    packed, (mid_grad, up_row_1, dq, qpart, dkv, pays, prompts_1, rows_1) = out[6:8], out[8:]
    grads = both_parts(packed)
    dqs, dkvs = both(dq), both(dkv)
    start = give_back(1, pays, qpart, mid_grad)
    lefts.append(left_factors(1, dkv, lefts[0][1], lefts[0][3], *grads[2:]))
    plan = [("down", 0, 0, 0, 0)]
    plan += [("up", part, mid_at, 0, HALF + part * tile) for part in range(3)]
    made = mlp_call(plan, ((0, HALF + 3 * tile),), lefts[1][0:2], grads)
    plan = [("q", None, 1, 0), ("k", None, 1, tile), ("v", None, 1, 2 * tile)]
    plan += [("out", mid_at + 2 * HALF, 1, 3 * tile), (3, mid_at + HALF, 1, 4 * tile)]
    talls = (after(lefts[1][0], made[0]), lefts[1][1])
    mixed = mixed_call(plan, ((1, 5 * tile),), seq, talls, lefts[1][2:], dqs, dkvs, grads)
    start_ring(0, made, (HALF,) + (tile,) * 3)
    start_ring(1, mixed, (tile,) * 5)

    start = (after(start[0], mixed[1][0]), *start[1:])
    x_in, q, k, v, lse, mid, slope = kept[0]
    small = (small_pick, small_spot, prompts_1, rows_1, up_row_1, up_row_1)
    out = back_call(
        start, first_seq, (mid, slope, q, k, v, lse), prompt_rows[0], vecs[0], query_seg, key_seg,
        small, weights,
    )
    packed, (mid_grad, _, dq, qpart, dkv, pays) = out[0:2], out[2:8]
    grads = both_parts(packed)
    plan = [("down", 0, 0, 2, 0), ("out", 0, mid_at + HALF, 2, HALF)]
    plan += [("up", part, mid_at, 2, HALF + (1 + part) * tile) for part in range(2)]
    talls = (after(lefts[0][0], dkv, arrived[0][0][0], *arrived[1][0][0]), lefts[0][1])
    made = mlp_call(plan, ((2, HALF + 3 * tile),), talls, grads, 60)
    second_steps = made[2]
    start = give_back(0, after(pays, arrived[0][0][0]), qpart, mid_grad)
    dqs, dkvs = both(dq), both(dkv)
    small = (out[8], send(out[9], "core", 1))
    plan = [("q", None, 1, 0), ("k", None, 1, tile), ("v", None, 1, 2 * tile)]
    plan += [(part, mid_at + 2 * HALF, 1, (1 + part) * tile + 32) for part in (2, 3)]
    talls = (after(lefts[0][0], second_steps[0]), lefts[0][1])
    mixed = mixed_call(
        plan, ((1, 5 * tile + 32),), seq, talls, lefts[0][2:], dqs, dkvs, grads, small
    )
    second_steps[2] = after(second_steps[2], mixed[1][0])
    start_ring(2, {2: second_steps}, (HALF,) + (tile,) * 3)
    start_ring(1, mixed, (tile,) * 3 + (16, 16) + (tile,) * 2)
    for group in arrived:
        come, rows = group[0]
        (total,) = fold_call([(1, [(come, rows)])])
        group[0] = ([total], rows)
    grad_patch, grad_cls = close_call((after(start[0], mixed[1][0]), *start[1:]))
    (come, rows), *others = arrived[0]
    (plane,) = fold_call([(16, [([after(come[0], arrived[1][0][0][0])], rows), *others])])
    (come, rows), *others = arrived[1]
    pieces = fold_call([(4, [([after(come[0], plane)], rows), *others])])
    plane = deal_out(plane, RINGS[0][1:])
    second = [pieces[0]] + [send(pieces[step], RINGS[1][1], step) for step in range(1, 4)]
    rows = tuple(row // 4 for _, items in arrived[1] for row in items)
    pieces = fold_call([(4, [(second, rows)])], LATE)
    third = [pieces[0]] + [send(pieces[step], RINGS[1][2], step) for step in range(1, 4)]
    lasts = [plane, *third]
    layouts = (
        [("down", 1, 0, 24)]
        + [("up", 1, part, 6) for part in range(3)]
        + [("down", 0, 0, 24), ("out", 0, 0, 6)]
        + [("up", 0, part, 6) for part in range(2)],
        [("qkv", 1, part, 6) for part in range(3)]
        + [("out", 1, 0, 6), ("up", 1, 3, 6)]
        + [("qkv", 0, part, 6) for part in range(3)]
        + [("small", 0, 0, 1), ("bias", 0, 0, 1), ("up", 0, 2, 6), ("up", 0, 3, 6)],
    )
    done = final_call(lasts, layouts, own_w, own_vec)
    swap = lambda values: jnp.transpose(values, (1, 0, 2))
    return (
        out_patch[None],
        swap(out_cls),
        grad_patch[None],
        swap(grad_cls),
        jnp.transpose(done[4], (1, 2, 0)),
        swap(done[0]),
        swap(done[1]),
        swap(done[2]),
        done[3],
        done[5],
        swap(done[6]),
        done[7],
    )


def solution(mesh):
    placed = (
        P("dp", "seq", None),
        P("dp", None, None),
        P("dp", "seq"),
        P(),
        P(),
        P(),
        P(),
        P(),
        P(),
        P(),
        P(),
        P("dp", "seq", None),
        P("dp", None, None),
    )
    return jax.shard_map(
        per_device,
        mesh=mesh,
        in_specs=placed,
        out_specs=(
            P("dp", "seq", None),
            P("dp", None, None),
            P("dp", "seq", None),
            P("dp", None, None),
            P(None, None, ("dp", "seq")),
            P(None, ("dp", "seq"), None),
            P(None, ("dp", "seq"), None),
            P(None, ("dp", "seq"), None),
            P(None, ("dp", "seq"), None),
            P(None, None, ("dp", "seq")),
            P(None, None, ("dp", "seq")),
            P(None, ("dp", "seq")),
        ),
        check_vma=False,
    )
```

```python
import functools

import jax
import jax.numpy as jnp
from jax import lax
from jax.experimental import pallas as pl
from jax.experimental.pallas import tpu as pltpu
from jax.sharding import PartitionSpec as P

HEADS = 12
HEAD = 64
WIDTH = 768
HIDDEN = 3072
PATCHES = 128
CLS = 10
PROMPTS = 50
OWN = 144
KEYS = 1152
CLS_AT = 1024
PROMPT_AT = 1040
FRONT = 128
BLOCKS = 8
PAY = 864
PACKED = 2 * WIDTH + HIDDEN
HALF = WIDTH // 2
TILE = 256
LOW = jnp.bfloat16
FULL = jnp.float32

eps_norm = 1e-06
penalty_rate = 2.0
big_negative = -1e30

AXES = ("dp", "seq")
SPAN = {"core": 2, "x": 4, "y": 4, "z": 4}
RINGS = (("y", "z", "x"), ("z", "y", "x"))
ANY = pl.BlockSpec(memory_space=pl.ANY)
VM = "whole"
HERE = pl.BlockSpec(memory_space=pltpu.VMEM)
SM = pl.BlockSpec(memory_space=pltpu.SMEM)


def place_of(device):
    dp, seq = device // 8, device % 8
    return {"core": dp % 2, "x": dp // 2 % 2 * 2 + seq // 4, "y": dp // 4, "z": seq % 4}


def device_of(place):
    dp = (place["y"] * 2 + place["x"] // 2) * 2 + place["core"]
    return dp * 8 + place["x"] % 2 * 4 + place["z"]


def moved(axis, step):
    pairs = []
    for device in range(128):
        place = place_of(device)
        place[axis] = (place[axis] + step) % SPAN[axis]
        pairs.append((device, device_of(place)))
    return pairs


def send(values, axis, step):
    return lax.ppermute(values, AXES, moved(axis, step))


def groups_of(axes):
    found = {}
    for device in range(128):
        place = place_of(device)
        rest = tuple(place[axis] for axis in SPAN if axis not in axes)
        found.setdefault(rest, []).append((tuple(place[axis] for axis in axes), device))
    return [[device for _, device in sorted(group)] for group in found.values()]


def deal_out(values, axes):
    return lax.all_to_all(
        values, AXES, 0, 0, tiled=True, axis_index_groups=groups_of(axes)
    )


def swap_rows(values):
    return lax.all_to_all(values, "seq", 0, 0, tiled=True)


def owner_order(axes, steps=()):
    here = place_of(lax.axis_index("dp") * 8 + lax.axis_index("seq"))
    rest = jnp.arange(128, dtype=jnp.int32)
    place = {}
    for axis in reversed(axes):
        place[axis] = rest % SPAN[axis]
        if axis in steps:
            place[axis] = (here[axis] + place[axis]) % SPAN[axis]
        rest = rest // SPAN[axis]
    place["core"] = (here["core"] + rest) % 2
    return device_of(place)


def nn(left, right):
    return lax.dot_general(left, right, (((1,), (0,)), ((), ())), preferred_element_type=FULL)


def nt(left, right):
    return lax.dot_general(left, right, (((1,), (1,)), ((), ())), preferred_element_type=FULL)


def plain_norm(values):
    centred = values - jnp.mean(values, -1, keepdims=True)
    scale = lax.rsqrt(jnp.mean(centred * centred, -1, keepdims=True) + eps_norm)
    return centred * scale, scale


def norm_pull(plain, scale, gain, upstream):
    inner = upstream * gain
    return scale * (
        inner
        - jnp.mean(inner, -1, keepdims=True)
        - plain * jnp.mean(inner * plain, -1, keepdims=True)
    )


def whole(dims):
    return pl.BlockSpec(dims, lambda i: (0,) * len(dims))


class Late:
    def __init__(self, index=None, cuts=1, axis=0):
        self.index, self.cuts, self.axis = index, cuts, axis


class Early:
    def __init__(self, dims, kind=FULL):
        self.shape, self.dtype = dims, kind


class Moves:
    def __init__(self):
        self.ins, self.outs, self.gone = {}, {}, []

    def start(self, *refs):
        for ref in refs:
            for copy in self.ins[id(ref)]:
                copy.start()

    def resident(self):
        part = Moves()
        part.start = part.wait = lambda *_: None
        part.flush = self.flush
        return part

    def wait(self, ref, piece=None):
        copies = self.ins[id(ref)]
        for copy in copies if piece is None else copies[piece : piece + 1]:
            copy.wait()

    def flush(self, *refs):
        for ref in refs:
            copy = self.outs.pop(id(ref), None)
            if copy is not None:
                copy.start()
                self.gone.append(copy)

    def close(self):
        for copy in self.outs.values():
            copy.start()
        for copy in [*self.gone, *self.outs.values()]:
            copy.wait()


def run(body, operands, specs, outs, name, micros, scratch=(), mib=63):
    late = [(at, spec) for at, spec in enumerate(specs) if isinstance(spec, Late)]
    early = [(at, out) for at, out in enumerate(outs) if isinstance(out, Early)]
    buffers, total = [], 0
    for at, spec in late:
        dims = operands[at].shape if spec.index is None else operands[at].shape[1:]
        buffers.append(pltpu.VMEM(dims, operands[at].dtype))
        total += spec.cuts
    buffers += [pltpu.VMEM(out.shape, out.dtype) for _, out in early]
    total += len(early)

    def kernel(*refs):
        refs = list(refs)
        first = len(operands) + len(outs) + len(scratch)
        space, sems = refs[first : first + len(buffers)], refs[-1]
        moves, sem = Moves(), 0
        for (at, spec), buffer in zip(late, space):
            source = refs[at] if spec.index is None else refs[at].at[spec.index]
            size = buffer.shape[spec.axis] // spec.cuts
            copies = []
            for piece in range(spec.cuts):
                part = pl.ds(piece * size, size)
                view = lambda ref: ref.at[part] if spec.axis == 0 else ref.at[:, part]
                pair = (source, buffer) if spec.cuts == 1 else (view(source), view(buffer))
                copies.append(pltpu.make_async_copy(*pair, sems.at[sem]))
                sem += 1
            moves.ins[id(buffer)] = copies
            refs[at] = buffer
        for (at, out), buffer in zip(early, space[len(late) :]):
            at += len(operands)
            moves.outs[id(buffer)] = pltpu.make_async_copy(buffer, refs[at], sems.at[sem])
            sem += 1
            refs[at] = buffer
        body(moves, refs[:first])
        moves.close()

    in_specs = []
    for operand, spec in zip(operands, specs):
        if isinstance(spec, Late):
            in_specs.append(ANY)
        else:
            in_specs.append(whole(operand.shape) if spec == "whole" else spec)
    return pl.pallas_call(
        kernel,
        grid=(1,),
        out_shape=tuple(shape(out.shape, out.dtype) for out in outs),
        in_specs=in_specs,
        out_specs=tuple(ANY if isinstance(out, Early) else whole(out.shape) for out in outs),
        scratch_shapes=[*scratch, *buffers, pltpu.SemaphoreType.DMA((max(total, 1),))],
        compiler_params=params(mib),
        cost_estimate=cost(micros),
        name=name,
    )(*operands)


def after(values, *others):
    return lax.optimization_barrier((values, others))[0]


def tile_at(index, size):
    return pl.ds(pl.multiple_of(index * size, size), size)


def params(mib=56):
    return pltpu.CompilerParams(vmem_limit_bytes=mib * 2**20)


SHARE = 1.0
ATT = 6
LEFT = 0.1
MIX = 0.1
TURN = 40
FOLD = 0.01
LATE = 12
MLP1 = 0.1


def cost(micros):
    return pl.CostEstimate(flops=int(micros * 1.1e9), bytes_accessed=1 << 20, transcendentals=0)


def shape(dims, kind=FULL):
    return jax.ShapeDtypeStruct(dims, kind)


def open_body(patch_ref, cls_ref, seg_ref, gain_ref, bias_ref, x_ref, pay_ref, own_ref, query_ref):
    x_ref[0:PATCHES] = patch_ref[0].astype(FULL)
    cls_rows = jnp.concatenate([cls_ref[0].astype(FULL), jnp.zeros((16 - CLS, WIDTH), FULL)], 0)
    x_ref[PATCHES:OWN] = cls_rows
    plain, _ = plain_norm(x_ref[...])
    normed = (plain * gain_ref[0, 0:1] + bias_ref[0, 0:1]).astype(LOW)
    own_ref[...] = normed
    segs = seg_ref[...].astype(FULL)
    last = jnp.broadcast_to(segs, (16, PATCHES)).astype(LOW)
    last = jnp.concatenate([last, jnp.zeros((16, WIDTH - PATCHES), LOW)], 1)
    for block in range(BLOCKS):
        pay_ref[block, 0:PATCHES] = normed[0:PATCHES]
        pay_ref[block, PATCHES:OWN] = last
    query_ref[0:PATCHES] = jnp.broadcast_to(segs, (PATCHES, PATCHES)).T
    row = lax.broadcasted_iota(jnp.int32, (16, 128), 0)
    query_ref[PATCHES:OWN] = jnp.where(row < CLS, row, -5).astype(FULL)


def open_call(patches, cls_tokens, segments, gains, biases):
    outs = (
        shape((OWN, WIDTH)),
        shape((BLOCKS, OWN, WIDTH), LOW),
        shape((OWN, WIDTH), LOW),
        shape((OWN, 128)),
    )
    operands = (patches, cls_tokens, segments, gains, biases)
    return run(lambda moves, refs: open_body(*refs), operands, [VM] * 5, outs, "open_norm", 2)


def seen_mask(key_ref, query_ref, mask_ref):
    keys = key_ref[0:1, :]
    seen = (keys == query_ref[:, 0:1]) | (keys == -1.0)
    mask_ref[...] = jnp.where(seen, 0.0, big_negative)


def half_lanes(rows):
    return lax.broadcasted_iota(jnp.int32, (rows, 2 * HEAD), 1) < HEAD


def split_rows(rows, patch_ref, cls_ref):
    patch_ref[...] = rows[0:PATCHES]
    for place in range(CLS):
        cls_ref[place] = rows[PATCHES + place : PATCHES + place + 1]


def forward_body(layer, last, moves, refs):
    first = layer == 0
    r = iter(refs)
    nxt = lambda: next(r)
    x_ref = nxt()
    come_ref = nxt()
    own_ref, prompt_ref, vec_ref, up_bias_ref, query_seg_ref = nxt(), nxt(), nxt(), nxt(), nxt()
    key_in_ref = None if first else nxt()
    wqkv, wout, wup, wdown = nxt(), nxt(), nxt(), nxt()
    q_ref, k_ref, v_ref, all_ref = nxt(), nxt(), nxt(), nxt()
    att_ref, lse_ref, mid_ref, nmid_ref = nxt(), nxt(), nxt(), nxt()
    slope_ref, active_ref, out_ref = nxt(), nxt(), nxt()
    next_ref, next_own_ref = nxt(), nxt()
    key_ref = nxt() if first else key_in_ref
    mask_ref = nxt()

    moves.start(wqkv)
    for block in range(BLOCKS):
        all_ref[block * PATCHES : (block + 1) * PATCHES] = come_ref[block, 0:PATCHES]

    gain_one, bias_one = vec_ref[0:1], vec_ref[2:3]
    gain_two, bias_two = vec_ref[1:2], vec_ref[6:7]

    plain, _ = plain_norm(prompt_ref[...])
    all_ref[CLS_AT:PROMPT_AT] = own_ref[PATCHES:OWN]
    all_ref[PROMPT_AT : PROMPT_AT + 64] = (plain * gain_one + bias_one).astype(LOW)
    all_ref[PROMPT_AT + 64 : KEYS] = jnp.zeros((KEYS - PROMPT_AT - 64, WIDTH), LOW)
    moves.flush(all_ref)
    if first:
        lane = lax.broadcasted_iota(jnp.int32, (8, FRONT), 1)
        front = jnp.where(
            lane < CLS, lane, jnp.where((lane >= 16) & (lane < 16 + PROMPTS), -1, -2)
        )
        for block in range(BLOCKS):
            segs = come_ref[block, PATCHES:OWN, 0:PATCHES].astype(FULL)
            key_ref[:, block * PATCHES : (block + 1) * PATCHES] = segs[0:8]
        key_ref[:, CLS_AT:KEYS] = front.astype(FULL)
    seen_mask(key_ref, query_seg_ref, mask_ref)

    def keys(tile, carry):
        at = tile_at(tile, TILE)
        rows = nn(all_ref[...], wqkv[:, pl.ds(pl.multiple_of(WIDTH + tile * TILE, TILE), TILE)])
        k_ref[:, at] = rows.astype(LOW)
        return carry

    def values(tile, carry):
        at = tile_at(tile, TILE)
        rows = nn(all_ref[...], wqkv[:, pl.ds(pl.multiple_of(2 * WIDTH + tile * TILE, TILE), TILE)])
        v_ref[:, at] = (rows + vec_ref[4:5, at]).astype(LOW)
        return carry

    def queries(tile, carry):
        at = tile_at(tile, TILE)
        rows = nn(own_ref[...], wqkv[:, at]) + vec_ref[3:4, at]
        q_ref[:, at] = (rows.astype(LOW).astype(FULL) * HEAD**-0.5).astype(LOW)
        return carry

    moves.wait(wqkv, 0)
    lax.fori_loop(0, 3, queries, 0, unroll=3)
    moves.wait(wqkv, 1)
    moves.start(wout, wup)
    lax.fori_loop(0, 3, keys, 0, unroll=3)
    moves.flush(k_ref)
    moves.wait(wqkv, 2)
    lax.fori_loop(0, 3, values, 0, unroll=3)
    moves.flush(v_ref)
    moves.start(wdown)

    lse_ref[...] = jnp.zeros((OWN, 128), FULL)
    lower = half_lanes(OWN)
    lane = lax.broadcasted_iota(jnp.int32, (OWN, 128), 1)

    def heads(pair, carry):
        at = tile_at(pair, 2 * HEAD)
        query, key, value = q_ref[:, at], k_ref[:, at], v_ref[:, at]
        outs = []
        for side in range(2):
            mine = lower if side == 0 else ~lower
            scores = nt(jnp.where(mine, query, jnp.zeros_like(query)), key) + mask_ref[...]
            top = jnp.max(scores, -1, keepdims=True)
            raised = jnp.exp(scores - top)
            total = jnp.sum(raised, -1, keepdims=True)
            outs.append(nn(raised.astype(LOW), value) / total)
            lane = lax.broadcasted_iota(jnp.int32, (OWN, 128), 1)
            lse_ref[...] = jnp.where(lane == 2 * pair + side, top + jnp.log(total), lse_ref[...])
        att_ref[:, at] = jnp.where(lower, outs[0], outs[1]).astype(LOW)
        return carry

    lax.fori_loop(0, HEADS // 2, heads, 0, unroll=2)

    moves.wait(wout)

    def project(tile, carry):
        at = tile_at(tile, TILE)
        mid_ref[:, at] = x_ref[:, at] + (nn(att_ref[...], wout[:, at]) + vec_ref[5:6, at])
        return carry

    lax.fori_loop(0, 3, project, 0, unroll=3)
    plain, _ = plain_norm(mid_ref[...])
    nmid_ref[...] = (plain * gain_two + bias_two).astype(LOW)
    moves.wait(wup)

    def rise(tile, carry):
        at = tile_at(tile, TILE)
        hidden = nn(nmid_ref[...], wup[:, at]) + up_bias_ref[0:1, at]
        share = 0.5 * (1.0 + lax.erf(hidden * 0.7071067811865476))
        active_ref[:, at] = (hidden * share).astype(LOW)
        slope_ref[:, at] = share + hidden * (0.3989422804014327 * jnp.exp(-0.5 * hidden * hidden))
        return carry

    lax.fori_loop(0, HIDDEN // TILE, rise, 0, unroll=4)
    moves.flush(slope_ref, active_ref)
    moves.wait(wdown)

    def lower_back(tile, carry):
        at = tile_at(tile, TILE)
        out_ref[:, at] = mid_ref[:, at] + (nn(active_ref[...], wdown[:, at]) + vec_ref[7:8, at])
        return carry

    lax.fori_loop(0, 3, lower_back, 0, unroll=3)
    if not last:
        plain, _ = plain_norm(out_ref[...])
        normed = (plain * vec_ref[8:9] + vec_ref[9:10]).astype(LOW)
        next_own_ref[...] = normed
        for block in range(BLOCKS):
            next_ref[block] = normed[0:PATCHES]
    else:
        split_rows(out_ref[...], next_ref, next_own_ref)


def forward_call(layer, last, x, come, own, prompt, vec, up_bias, query_seg, key_seg, weights):
    first = layer == 0
    outs = [
        shape((OWN, WIDTH), LOW),
        Early((KEYS, WIDTH), LOW),
        Early((KEYS, WIDTH), LOW),
        Early((KEYS, WIDTH), LOW),
        shape((OWN, WIDTH), LOW),
        shape((OWN, 128)),
        shape((OWN, WIDTH)),
        shape((OWN, WIDTH), LOW),
        Early((OWN, HIDDEN)),
        Early((OWN, HIDDEN), LOW),
        shape((OWN, WIDTH)),
    ]
    if last:
        outs += [shape((PATCHES, WIDTH)), shape((CLS, 1, WIDTH))]
    else:
        outs += [shape((BLOCKS, PATCHES, WIDTH), LOW), shape((OWN, WIDTH), LOW)]
    if first:
        outs += [shape((8, KEYS))]
    operands = [x, come, own, prompt, vec, up_bias, query_seg]
    specs = [VM, HERE] + [VM] * 5
    if not first:
        operands.append(key_seg)
        specs.append(VM)
    operands += weights
    specs += [Late(layer, 3, 1), Late(layer), Late(layer), Late(layer)]
    scratch = [pltpu.VMEM((OWN, KEYS), FULL)]
    body = lambda moves, refs: forward_body(layer, last, moves, refs)
    return run(body, operands, specs, outs, "forward_layer", 24 * SHARE, scratch)


def gathered_pull(come_ref, qpart_ref, x_ref, gain, mid_grad_ref):
    total = come_ref[0].astype(FULL)
    for block in range(1, BLOCKS):
        total = total + come_ref[block].astype(FULL)
    patch_part = total[0:WIDTH].T
    cls_part = jnp.concatenate(
        [total[WIDTH + 16 * lane : WIDTH + 16 * (lane + 1)] for lane in range(6)], 1
    )
    d_normed = jnp.concatenate([patch_part, cls_part], 0) + qpart_ref[...]
    plain, scale = plain_norm(x_ref[...])
    return mid_grad_ref[...] + norm_pull(plain, scale, gain, d_normed)


def row_share(first_ref):
    row = lax.broadcasted_iota(jnp.int32, (OWN, 1), 0)
    return jnp.where(row < PATCHES, 1.0, jnp.where(row < PATCHES + CLS, first_ref[0, 0], 0.0))


def back_mlp_body(last, moves, refs):
    r = iter(refs)
    nxt = lambda: next(r)
    if last:
        cot_ref, cot_cls_ref, key_ref, query_seg_ref = nxt(), nxt(), nxt(), nxt()
    else:
        come_ref = nxt()
        up_qpart_ref, up_x_ref, up_mid_grad_ref, up_vec_ref = nxt(), nxt(), nxt(), nxt()
    first_ref, mid_ref, slope_ref, vec_ref = nxt(), nxt(), nxt(), nxt()
    wout, wup, wdown = nxt(), nxt(), nxt()
    grad_refs = nxt(), nxt()
    datt_ref, mid_grad_ref = nxt(), nxt()
    rows_ref, up_spot_ref = nxt(), nxt()
    up_ref, low_ref, hid_ref, up_row_ref = nxt(), nxt(), nxt(), nxt()

    moves.start(wdown, slope_ref)
    gain_two = vec_ref[1:2]
    share = row_share(first_ref)
    if last:
        valid = ((query_seg_ref[...] < CLS) & (query_seg_ref[...] >= 0)).astype(FULL)
        up_ref[0:PATCHES] = cot_ref[...].astype(FULL) * valid[0:PATCHES, 0:1]
        hits = (key_ref[0:1, 0:CLS_AT] == query_seg_ref[PATCHES:OWN, 0:1]).astype(FULL)
        present = jnp.max(hits, -1, keepdims=True)
        cls_rows = [cot_cls_ref[...].astype(FULL), jnp.zeros((16 - CLS, WIDTH), FULL)]
        up_ref[PATCHES:OWN] = jnp.concatenate(cls_rows, 0) * present
    else:
        up_ref[...] = gathered_pull(
            come_ref, up_qpart_ref, up_x_ref, up_vec_ref[0:1], up_mid_grad_ref
        )
    low_ref[...] = up_ref[...].astype(LOW)
    weighted = low_ref[...].astype(FULL) * share
    grad_refs[0][:, 0:WIDTH] = weighted.astype(LOW)
    rows_ref[...] = jnp.zeros((8, WIDTH), FULL)
    rows_ref[0:1] = jnp.sum(weighted, 0, keepdims=True)
    moves.start(wup)

    def to_hidden(half, tile, carry):
        at = tile_at(tile, TILE)
        grad = (nt(low_ref[...], wdown[at, :]) * slope_ref[:, at]).astype(LOW)
        hid_ref[:, at] = grad
        counted = grad.astype(FULL) * share
        to = WIDTH + tile * TILE - half * (PACKED // 2)
        grad_refs[half][:, pl.ds(pl.multiple_of(to, TILE), TILE)] = counted.astype(LOW)
        up_row_ref[:, at] = jnp.broadcast_to(jnp.sum(counted, 0, keepdims=True), (8, TILE))
        return carry

    moves.wait(slope_ref)
    for piece in range(4):
        moves.wait(wdown, piece)
        body = functools.partial(to_hidden, piece // 2)
        lax.fori_loop(3 * piece, 3 * piece + 3, body, 0, unroll=3)
    moves.wait(wup)
    moves.start(wout)

    def to_mid(tile, carry):
        at = tile_at(tile, TILE)
        mid_grad_ref[:, at] = nt(hid_ref[...], wup[at, :])
        return carry

    lax.fori_loop(0, 3, to_mid, 0, unroll=3)
    d_normed = mid_grad_ref[...]
    plain, scale = plain_norm(mid_ref[...])
    counted = d_normed * share
    rows_ref[1:2] = jnp.sum(counted * plain, 0, keepdims=True)
    rows_ref[2:3] = jnp.sum(counted, 0, keepdims=True)
    mid_grad_ref[...] = up_ref[...] + norm_pull(plain, scale, gain_two, d_normed)
    low_ref[...] = mid_grad_ref[...].astype(LOW)
    weighted = low_ref[...].astype(FULL) * share
    grad_refs[1][:, PACKED // 2 - WIDTH :] = weighted.astype(LOW)
    rows_ref[3:4] = jnp.sum(weighted, 0, keepdims=True)
    moves.flush(*grad_refs)
    up_row = up_row_ref[0:1]
    spots = [up_row[:, 24 * spot : 24 * (spot + 1)] for spot in range(128)]
    up_spot_ref[...] = jnp.concatenate(spots, 0)
    moves.wait(wout)

    def to_att(tile, carry):
        at = tile_at(tile, TILE)
        datt_ref[:, at] = nt(low_ref[...], wout[at, :]).astype(LOW)
        return carry

    lax.fori_loop(0, 3, to_att, 0, unroll=3)


def back_att_body(layer, moves, refs):
    r = iter(refs)
    nxt = lambda: next(r)
    first_ref, rows_in_ref, datt_ref = nxt(), nxt(), nxt()
    q_ref, k_ref, v_ref, lse_ref = nxt(), nxt(), nxt(), nxt()
    prompt_ref, vec_ref, query_seg_ref, key_ref = nxt(), nxt(), nxt(), nxt()
    if layer == 0:
        pick_ref, spot_ref, prompts_1, rows_1, up_0, up_1 = [nxt() for _ in range(6)]
    wqkv = nxt()
    dq_ref, qpart_ref, dkv_ref, pay_ref = nxt(), nxt(), nxt(), nxt()
    if layer == 0:
        small_refs = nxt(), nxt()
        dprompt_ref, rows_ref = nxt(), nxt()
    else:
        dprompt_ref, rows_ref = nxt(), nxt()
    mask_ref, dqf_ref, qt_ref, dat_ref, front_ref = [nxt() for _ in range(5)]

    moves.start(k_ref, v_ref, wqkv)
    gain_one = vec_ref[0:1]
    share = row_share(first_ref)
    seen_mask(key_ref, query_seg_ref, mask_ref)
    rows_ref[...] = rows_in_ref[...]

    def turn(tile, carry):
        at = tile_at(tile, TILE)
        dat_ref[at, :] = (datt_ref[:, at].astype(FULL) * share).T.astype(LOW)
        qt_ref[at, :] = (q_ref[:, at].astype(FULL) * share).T.astype(LOW)
        return carry

    lax.fori_loop(0, 3, turn, 0, unroll=3)
    lower = half_lanes(OWN)
    lane = lax.broadcasted_iota(jnp.int32, (OWN, 128), 1)
    moves.wait(k_ref)
    moves.wait(v_ref)

    def heads(pair, carry):
        at = tile_at(pair, 2 * HEAD)
        query, key, value, grad = q_ref[:, at], k_ref[:, at], v_ref[:, at], datt_ref[:, at]
        outs = []
        for side in range(2):
            mine = lower if side == 0 else ~lower
            head = 2 * pair + side
            log_total = jnp.sum(jnp.where(lane == head, lse_ref[...], 0.0), -1, keepdims=True)
            scores = nt(jnp.where(mine, query, jnp.zeros_like(query)), key) + mask_ref[...]
            probs = jnp.exp(scores - log_total)
            d_probs = nt(jnp.where(mine, grad, jnp.zeros_like(grad)), value)
            both = probs * d_probs
            across = jnp.sum(both, -1, keepdims=True)
            d_scores = (both - probs * across).astype(LOW)
            probs_low = probs.astype(LOW)
            outs.append(nn(d_scores, key))
            rows = tile_at(head, HEAD)
            dkv_ref[rows, :] = nn(qt_ref[rows, :], d_scores).astype(LOW)
            value_rows = pl.ds(pl.multiple_of(WIDTH + head * HEAD, HEAD), HEAD)
            dkv_ref[value_rows, :] = nn(dat_ref[rows, :], probs_low).astype(LOW)
        dqf_ref[:, at] = (jnp.where(lower, outs[0], outs[1]) * HEAD**-0.5).astype(LOW)
        return carry

    lax.fori_loop(0, HEADS // 2, heads, 0, unroll=2)
    moves.flush(dkv_ref)
    counted = dqf_ref[...].astype(FULL) * share
    dq_ref[...] = counted.astype(LOW)
    rows_ref[4:5] = jnp.sum(counted, 0, keepdims=True)
    moves.wait(wqkv)

    def to_normed(tile, carry):
        at = tile_at(tile, TILE)
        qpart_ref[:, at] = nt(dqf_ref[...], wqkv[at, 0:WIDTH])
        return carry

    lax.fori_loop(0, 3, to_normed, 0, unroll=3)

    front_ref[...] = nn(wqkv[:, WIDTH:], dkv_ref[:, CLS_AT:KEYS])
    shift = jnp.sum(front_ref[...], -1, keepdims=True)
    front = front_ref[...].T
    cls_rows = jnp.concatenate(
        [front[0:16, 128 * place : 128 * (place + 1)] for place in range(6)], 0
    )
    for block in range(0, BLOCKS, 2):
        part = nn(wqkv[:, WIDTH:], dkv_ref[:, block * PATCHES : (block + 2) * PATCHES])
        shift = shift + jnp.sum(part, -1, keepdims=True)
        for side in range(2):
            pay_ref[block + side, 0:WIDTH] = part[:, side * PATCHES : (side + 1) * PATCHES].astype(LOW)
            pay_ref[block + side, WIDTH:PAY] = cls_rows.astype(LOW)
    moves.flush(pay_ref)

    plain, scale = plain_norm(prompt_ref[...])
    d_prompt = norm_pull(plain, scale, gain_one, front[16:80])
    query_seg = query_seg_ref[0:PATCHES, 0:1]
    slots = jnp.sum((query_seg < CLS).astype(FULL), 0, keepdims=True)
    dprompt_ref[...] = d_prompt + (penalty_rate / 1024.0) * slots * prompt_ref[...]

    turned = jnp.broadcast_to(shift, (WIDTH, 128)).T
    rows_ref[6:7] = turned[0:1] + jnp.sum(qpart_ref[...] * share, 0, keepdims=True)
    totals = jnp.sum(dkv_ref[WIDTH : 2 * WIDTH].astype(FULL), -1, keepdims=True)
    rows_ref[5:6] = jnp.broadcast_to(totals, (WIDTH, 128)).T[0:1]
    if layer != 0:
        return
    joined = jnp.concatenate([dprompt_ref[0:56], prompts_1[0:56], rows_ref[...], rows_1[...]], 0)
    turned = nt(pick_ref[...], joined.astype(LOW))
    ups = [nn(spot_ref[...], up[...].astype(LOW)) for up in (up_0, up_1)]
    rows = jnp.concatenate([turned[128 * part : 128 * (part + 1)] for part in range(6)], 1)
    ups = jnp.concatenate([*ups, jnp.zeros((128, WIDTH - 48), FULL)], 1)
    for half in range(2):
        spots = slice(64 * half, 64 * (half + 1))
        small_refs[half][...] = jnp.concatenate([rows[spots], ups[spots]], 0).astype(LOW)


class Joined:
    def __init__(self, moves, last, *more):
        self.moves, self.last, self.more = moves, last, more
        self.wait, self.flush = moves.wait, moves.flush

    def start(self, *refs):
        self.moves.start(*refs)
        if any(ref is self.last for ref in refs):
            self.moves.start(*self.more)


class Started(Joined):
    def start(self, *refs):
        pass


def back_body(moves, refs):
    r = iter(refs)
    take = lambda count: [next(r) for _ in range(count)]
    start, first = take(5), next(r)
    mid, slope, q, k, v, lse, prompt, vec, query_seg, key = take(10)
    small, (wqkv, wout, wup, wdown) = take(6), take(4)
    grads, mid_grad, up_spot = take(2), next(r), next(r)
    dq, qpart, dkv, pay = take(4)
    small_out = take(2)
    datt, rows_in, up, low, hid, up_row, mask, dqf, qt, dat, front, dprompt, rows = take(13)
    back_mlp_body(
        False, Joined(moves, wup, k, v, wqkv),
        [*start, first, mid, slope, vec, wout, wup, wdown]
        + [*grads, datt, mid_grad, rows_in, up_spot, up, low, hid, up_row],
    )
    back_att_body(
        0, Started(moves, None),
        [first, rows_in, datt, q, k, v, lse, prompt, vec, query_seg, key, *small[:4], up_spot, small[5]]
        + [wqkv, dq, qpart, dkv, pay, *small_out, dprompt, rows, mask, dqf, qt, dat, front],
    )


def back_call(start, first_seq, saved, prompt, vec, query_seg, key_seg, small, weights):
    mid, slope, q, k, v, lse = saved
    operands = [*start, first_seq, mid, slope, q, k, v, lse, prompt, vec, query_seg, key_seg]
    operands += [*small, *weights]
    specs = [HERE] + [VM] * 4 + [SM, VM, Late(), VM, Late(), Late()] + [VM] * 11
    specs += [Late(0), Late(0), Late(0), Late(0, 4)]
    outs = [
        Early((OWN, PACKED // 2), LOW),
        Early((OWN, PACKED // 2), LOW),
        shape((OWN, WIDTH)),
        shape((128, 24)),
        shape((OWN, WIDTH), LOW),
        shape((OWN, WIDTH)),
        Early((2 * WIDTH, KEYS), LOW),
        Early((BLOCKS, PAY, 128), LOW),
        shape((128, WIDTH), LOW),
        shape((128, WIDTH), LOW),
    ]
    space = lambda *dims: pltpu.VMEM(dims, FULL)
    low = lambda *dims: pltpu.VMEM(dims, LOW)
    scratch = [low(OWN, WIDTH), space(8, WIDTH), space(OWN, WIDTH), low(OWN, WIDTH)]
    scratch += [low(OWN, HIDDEN), space(8, HIDDEN), space(OWN, KEYS), low(OWN, WIDTH)]
    scratch += [low(WIDTH, OWN), low(WIDTH, OWN), space(WIDTH, FRONT), space(64, WIDTH)]
    scratch += [space(8, WIDTH)]
    return run(back_body, operands, specs, outs, "backward_layer", ATT, scratch)


def turn_body(moves, refs):
    r = iter(refs)
    take = lambda count: [next(r) for _ in range(count)]
    x, come, own, prompt, vec, up_bias, query_seg, key = take(8)
    cots, first = take(2), next(r)
    wqkv, wout, wup, wdown = take(4)
    normed_all, att, nmid, active, out_patch, out_cls = take(6)
    grads, mid_grad, up_spot = take(2), next(r), next(r)
    dq, qpart, dkv, pay, dprompt, rows = take(6)
    q, k, v, lse, mid, slope, out, mask = take(8)
    datt, rows_in, up, low, hid, up_row = take(6)
    dqf, qt, dat, front = take(4)
    forward_body(
        1, True, moves,
        [x, come, own, prompt, vec, up_bias, query_seg, key, wqkv, wout, wup, wdown]
        + [q, k, v, normed_all, att, lse, mid, nmid, slope, active, out, out_patch, out_cls]
        + [mask],
    )
    still = moves.resident()
    back_mlp_body(
        True, still,
        [*cots, key, query_seg, first, mid, slope, vec, wout, wup, wdown]
        + [*grads, datt, mid_grad, rows_in, up_spot, up, low, hid, up_row],
    )
    back_att_body(
        1, still,
        [first, rows_in, datt, q, k, v, lse, prompt, vec, query_seg, key, wqkv]
        + [dq, qpart, dkv, pay, dprompt, rows, mask, dqf, qt, dat, front],
    )


def turn_call(x, come, own, prompt, vec, up_bias, query_seg, key_seg, cots, first_seq, weights):
    operands = [x, come, own, prompt, vec, up_bias, query_seg, key_seg, *cots, first_seq, *weights]
    specs = [VM, HERE] + [VM] * 8 + [SM, Late(1, 3, 1), Late(1), Late(1), Late(1)]
    outs = [
        Early((KEYS, WIDTH), LOW),
        shape((OWN, WIDTH), LOW),
        shape((OWN, WIDTH), LOW),
        Early((OWN, HIDDEN), LOW),
        shape((PATCHES, WIDTH)),
        shape((CLS, 1, WIDTH)),
        Early((OWN, PACKED // 2), LOW),
        Early((OWN, PACKED // 2), LOW),
        shape((OWN, WIDTH)),
        shape((128, 24)),
        shape((OWN, WIDTH), LOW),
        shape((OWN, WIDTH)),
        Early((2 * WIDTH, KEYS), LOW),
        Early((BLOCKS, PAY, 128), LOW),
        shape((64, WIDTH)),
        shape((8, WIDTH)),
    ]
    space = lambda *dims: pltpu.VMEM(dims, FULL)
    low = lambda *dims: pltpu.VMEM(dims, LOW)
    scratch = [low(OWN, WIDTH), low(KEYS, WIDTH), low(KEYS, WIDTH), space(OWN, 128)]
    scratch += [space(OWN, WIDTH), space(OWN, HIDDEN), space(OWN, WIDTH), space(OWN, KEYS)]
    scratch += [low(OWN, WIDTH), space(8, WIDTH), space(OWN, WIDTH), low(OWN, WIDTH)]
    scratch += [low(OWN, HIDDEN), space(8, HIDDEN), low(OWN, WIDTH), low(WIDTH, OWN)]
    scratch += [low(WIDTH, OWN), space(WIDTH, FRONT)]
    return run(turn_body, operands, specs, outs, "turn_layer", TURN, scratch)


def close_body(come_ref, qpart_ref, x_ref, mid_grad_ref, vec_ref, patch_ref, cls_ref):
    rows = gathered_pull(come_ref, qpart_ref, x_ref, vec_ref[0:1], mid_grad_ref)
    split_rows(rows, patch_ref, cls_ref)


def close_call(operands):
    outs = (shape((PATCHES, WIDTH)), shape((CLS, 1, WIDTH)))
    specs = [HERE] + [VM] * (len(operands) - 1)
    return run(lambda moves, refs: close_body(*refs), operands, specs, outs, "close_norm", 2)


def left_body(plan, moves, refs):
    order_ref, *refs = refs
    picks, (all_ref, att_ref, mid_ref, active_ref) = refs[0:2], refs[2:6]
    tall_refs, wide_refs = refs[6:8], refs[8:10]
    turned_ref, down_ref = refs[10:12]

    def turn(tile, carry):
        at = tile_at(tile, TILE)
        turned_ref[at, :] = active_ref[:, at].astype(FULL).T
        return carry

    def move(spot, carry):
        source = pl.ds(pl.multiple_of(order_ref[spot] * 24, 8), 24)
        target = pl.ds(pl.multiple_of(spot * 24, 8), 24)
        down_ref[target, :] = turned_ref[source, :]
        return carry

    moves.start(all_ref)
    lax.fori_loop(0, HIDDEN // TILE, turn, 0, unroll=3)
    lax.fori_loop(0, 128, move, 0, unroll=8)
    for half in range(2):
        rows = slice(half * 2 * WIDTH, (half + 1) * 2 * WIDTH)
        tall_refs[half][0 : 2 * WIDTH, 0:OWN] = down_ref[rows].astype(LOW)
    row = 2 * WIDTH
    for kind, ring_at in plan:
        source = {"mid": mid_ref, "att": att_ref}[kind][...]
        turned = nt(picks[ring_at][...], source).astype(LOW)
        for half in range(2):
            tall_refs[half][row : row + HALF, 0:OWN] = turned[half * HALF : (half + 1) * HALF]
        row += HALF
    moves.flush(*tall_refs)
    moves.wait(all_ref)
    for half in range(2):
        wide = nt(picks[1][half * HALF : (half + 1) * HALF], all_ref[...])
        wide_refs[half][...] = wide.astype(LOW)


def left_call(plan, order, picks, normed_all, att, nmid, active):
    tall = (2 * WIDTH + len(plan) * HALF, 256)
    outs = [Early(tall, LOW)] * 2 + [shape((HALF, KEYS), LOW)] * 2
    operands = (order, *picks, normed_all, att, nmid, active)
    scratch = [pltpu.VMEM((HIDDEN, OWN), FULL), pltpu.VMEM((HIDDEN, OWN), FULL)]
    body = lambda moves, refs: left_body(plan, moves, refs)
    return run(body, operands, [SM, VM, VM, Late(), VM, VM, VM], outs, "left_factors", LEFT, scratch)


def rights_of(grad_refs, kind, part, tile):
    at = {"down": 0, "up": WIDTH + part * WIDTH, "out": WIDTH + HIDDEN}[kind] + tile * TILE
    half, at = at // (PACKED // 2), at % (PACKED // 2)
    return [grad_refs[2 * side + half][:, at : at + TILE] for side in range(2)]


def piece_shapes(classes):
    outs = []
    for number, rows in classes:
        outs += [shape((4, rows, WIDTH), LOW)] if number == 0 else [shape((rows, WIDTH), LOW)] * 4
    return outs


def by_class(classes, arrays):
    found, at = {}, 0
    for number, _ in classes:
        if number == 0:
            found[0] = [arrays[at].at[way] for way in range(4)]
            at += 1
        else:
            found[number] = list(arrays[at : at + 4])
            at += 4
    return found


def deal(out, row, values, columns):
    size = values.shape[0] // 4
    for way in range(4):
        out[way][row : row + size, columns] = values[way * size : (way + 1) * size].astype(LOW)


def mlp_body(plan, classes, refs):
    tall_refs, grad_refs = refs[0:2], refs[2:6]
    outs = by_class(classes, refs[6:])
    for kind, part, left_row, out, out_row in plan:
        for tile in range(3):
            columns = slice(tile * TILE, (tile + 1) * TILE)
            rights = rights_of(grad_refs, kind, part, tile)
            for piece in range(4 if kind == "down" else 1):
                rows = slice(left_row + piece * HALF, left_row + (piece + 1) * HALF)
                lefts = [tall[rows, 0:OWN] for tall in tall_refs]
                values = nn(lefts[0], rights[0]) + nn(lefts[1], rights[1])
                if kind == "down":
                    outs[out][piece][out_row : out_row + HALF, columns] = values.astype(LOW)
                else:
                    deal(outs[out], out_row, values, columns)


def mlp_call(plan, classes, talls, grads, micros=MLP1):
    operands = (*talls, *grads)
    body = lambda moves, refs: mlp_body(plan, classes, refs)
    out = run(body, operands, [VM] * 6, piece_shapes(classes), "grad_mlp", micros)
    return by_class_values(classes, out)


def by_class_values(classes, arrays):
    found, at = {}, 0
    for number, _ in classes:
        found[number] = arrays[at] if number == 0 else list(arrays[at : at + 4])
        at += 1 if number == 0 else 4
    return found


def mixed_body(plan, classes, small, moves, refs):
    seq_ref, *refs = refs
    tall_refs, wide_refs, dq_refs, dkv_refs = [refs[2 * at : 2 * at + 2] for at in range(4)]
    grad_refs, small_refs = refs[8:12], refs[12:14]
    outs = by_class(classes, refs[14:] if small else refs[12:])
    moves.start(*wide_refs, *dkv_refs)
    for ref in (*wide_refs, *dkv_refs):
        moves.wait(ref)
    moves.start(*tall_refs, *grad_refs)
    brought = False
    if small:
        joined = small_refs[0][...].astype(FULL) + small_refs[1][...].astype(FULL)
        for way in range(4):
            spots = [joined[64 * part + 16 * way : 64 * part + 16 * (way + 1)] for part in range(2)]
            outs[1][way][3 * HALF // 4 : 3 * HALF // 4 + 32] = jnp.concatenate(spots, 0).astype(LOW)
    for kind, left_row, out, out_row in plan:
        for tile in range(3):
            columns = slice(tile * TILE, (tile + 1) * TILE)
            values = jnp.zeros((HALF, TILE), FULL)
            for side in range(2):
                if kind in ("k", "v"):
                    at = (0 if kind == "k" else WIDTH) + tile * TILE
                    values = values + nt(wide_refs[side][...], dkv_refs[side][at : at + TILE])
                    continue
                if kind == "q" and left_row is None:
                    wide = wide_refs[side]
                    mine = pl.ds(pl.multiple_of(seq_ref[0, 0] * PATCHES, PATCHES), PATCHES)
                    left = jnp.concatenate([wide[:, mine], wide[:, CLS_AT:PROMPT_AT]], 1)
                else:
                    if not brought:
                        brought = True
                        for ref in (*tall_refs, *grad_refs):
                            moves.wait(ref)
                    left = tall_refs[side][left_row : left_row + HALF, 0:OWN]
                if kind == "q":
                    right = dq_refs[side][:, columns]
                else:
                    name, part = ("out", 0) if kind == "out" else ("up", kind)
                    right = rights_of(grad_refs, name, part, tile)[side]
                values = values + nn(left, right)
            deal(outs[out], out_row, values, columns)


def mixed_call(plan, classes, seq, talls, wides, dqs, dkvs, grads, small=()):
    operands = (seq, *talls, *wides, *dqs, *dkvs, *grads, *small)
    body = lambda moves, refs: mixed_body(plan, classes, bool(small), moves, refs)
    specs = [SM] + [Late()] * 4 + [VM] * 2 + [Late()] * 6 + [VM] * len(small)
    out = run(body, operands, specs, piece_shapes(classes), "grad_mixed", MIX)
    return by_class_values(classes, out)


def fold_body(classes, refs):
    r = iter(refs)
    totals = []
    for _, groups in classes:
        totals.append([])
        for arrays, _ in groups:
            come = next(r)
            ways = [come.at[way] for way in range(4)] if len(come.shape) == 3 else [come]
            ways += [next(r) for _ in range(arrays - 1)]
            total = ways[0][...].astype(FULL)
            for way in ways[1:]:
                total = total + way[...].astype(FULL)
            totals[-1].append(total)
    for (ways, groups), sums in zip(classes, totals):
        joint = next(r) if ways == 16 else None
        for way in range(ways):
            out = joint.at[way] if ways == 16 else next(r)
            parts = []
            for total, (_, items) in zip(sums, groups):
                at = 0
                for rows in items:
                    size = rows // ways
                    parts.append(total[at + way * size : at + (way + 1) * size])
                    at += rows
            short = out.shape[0] - sum(part.shape[0] for part in parts)
            if short:
                parts.append(jnp.zeros((short, out.shape[1]), FULL))
            out[...] = jnp.concatenate(parts, 0).astype(LOW)


def fold_call(classes, micros=FOLD):
    operands = []
    for _, groups in classes:
        for come, _ in groups:
            operands += come if isinstance(come, list) else [come]
    number = lambda come: len(come) if isinstance(come, list) else 1
    counts = [(ways, [(number(come), items) for come, items in groups]) for ways, groups in classes]
    wide = 256
    outs = []
    for ways, groups in counts:
        size = -(-sum(sum(items) for _, items in groups) // (16 * ways)) * 16
        if ways == 16:
            outs.append(shape((16, size, WIDTH), LOW))
        else:
            outs += [shape((size, WIDTH), LOW)] * ways
    block = lambda *dims: pl.BlockSpec((*dims, wide), lambda i: (*[0] * len(dims), i))
    return list(
        pl.pallas_call(
            lambda *refs: fold_body(counts, refs),
            grid=(WIDTH // wide,),
            out_shape=tuple(outs),
            in_specs=[block(*come.shape[:-1]) for come in operands],
            out_specs=tuple(block(*out.shape[:-1]) for out in outs),
            compiler_params=params(63),
            cost_estimate=cost(micros),
            name="ring_fold",
        )(*operands)
    )


def final_body(layouts, refs):
    r = iter(refs)
    plane, ring = next(r), [next(r) for _ in range(4)]
    arrays = ([plane.at[way] for way in range(16)], ring)
    own_w_ref, own_vec_ref = next(r), next(r)
    qkv_ref, out_ref, up_ref, down_ref = next(r), next(r), next(r), next(r)
    prompt_ref, gain_ref, bias_ref, up_bias_ref = next(r), next(r), next(r), next(r)
    pieces = []
    for array, layout in zip(arrays, layouts):
        total = array[0][...].astype(FULL)
        for way in array[1:]:
            total = total + way[...].astype(FULL)
        at = 0
        for entry in layout:
            pieces.append((entry[:3], total[at : at + entry[3]]))
            at += entry[3]
    small = None
    wholes = [jnp.zeros((6, 1), FULL)] * 2
    for (kind, layer, part), piece in pieces:
        columns = slice(part * WIDTH, (part + 1) * WIDTH)
        if kind == "qkv":
            qkv_ref[:, layer, columns] = piece
            weight = own_w_ref[layer, :, columns].astype(FULL)
            wholes[layer] = wholes[layer] + jnp.sum(piece * weight, -1, keepdims=True)
        elif kind == "out":
            out_ref[:, layer, :] = piece
        elif kind == "up":
            up_ref[:, layer, columns] = piece
        elif kind == "down":
            down_ref[layer] = piece
        elif kind == "small":
            small = jnp.concatenate([piece[:, 128 * i : 128 * (i + 1)] for i in range(6)], 0)
        else:
            up_bias_ref[0:1] = piece[:, 0:24]
            up_bias_ref[1:2] = piece[:, 24:48]
    turn = lambda values: jnp.concatenate([values, jnp.zeros((2, 128), FULL)], 0).T
    rows = turn(small)
    for layer in range(2):
        prompt_ref[:, layer, :] = small[:, 56 * layer : 56 * layer + PROMPTS]
        at = 112 + 8 * layer
        part = rows[at : at + 8, 0:6]
        whole = turn(jnp.broadcast_to(wholes[layer], (6, 128)))[0:1, 0:6]
        gain, shift = own_vec_ref[layer, 0:1], own_vec_ref[layer, 1:2]
        gain_ref[layer, 0:1] = (whole - shift * part[6:7]) / gain
        gain_ref[layer, 1:2] = part[1:2]
        for place, source in enumerate((6, 4, 5, 3, 2, 0)):
            bias_ref[place, layer : layer + 1] = part[source : source + 1]


def final_call(arrays, layouts, own_w, own_vec):
    operands = [*arrays, own_w, own_vec]
    outs = (
        shape((6, 2, 3 * WIDTH)),
        shape((6, 2, WIDTH)),
        shape((6, 2, HIDDEN)),
        shape((2, 24, WIDTH)),
        shape((6, 2, PROMPTS)),
        shape((2, 2, 6)),
        shape((6, 2, 6)),
        shape((2, 24)),
    )
    body = lambda moves, refs: final_body(layouts, refs)
    return run(body, operands, [VM] * len(operands), outs, "final_fold", 3)


def per_device(
    patches,
    cls_tokens,
    segments,
    prompts,
    w_qkv,
    w_out,
    w_up,
    w_down,
    norm_gains,
    biases,
    up_bias,
    cot_patches,
    cot_cls,
):
    layers = 2
    weights = (w_qkv, w_out, w_up, w_down)
    first_seq = (lax.axis_index("seq") == 0).astype(FULL).reshape(1, 1)
    prompt_rows = jnp.pad(prompts.astype(FULL), ((0, 0), (0, 64 - PROMPTS), (0, 0)))
    vecs = []
    for layer in range(layers):
        following = min(layer + 1, layers - 1)
        vecs.append(
            jnp.concatenate(
                [
                    norm_gains[layer],
                    biases[layer],
                    norm_gains[following, 0:1],
                    biases[following, 0:1],
                    jnp.zeros((6, WIDTH), FULL),
                ],
                0,
            )
        )
    up_rows = [jnp.broadcast_to(up_bias[layer], (8, HIDDEN)) for layer in range(layers)]
    orders = [
        owner_order(RINGS[0]),
        owner_order(RINGS[1], RINGS[1]),
        owner_order(RINGS[0], RINGS[0][:1]),
    ]
    steps = jnp.arange(6, dtype=jnp.int32)
    one_hot = lambda wanted, size: (wanted[:, None] == jnp.arange(size)[None, :]).astype(LOW)
    picks = [one_hot((order[:, None] * 6 + steps).reshape(-1), WIDTH) for order in orders]
    small_pick = one_hot((orders[1][None, :] * 6 + steps[:, None]).reshape(-1), WIDTH)
    small_spot = one_hot(orders[1], 128)

    seq = lax.axis_index("seq").astype(jnp.int32).reshape(1, 1)
    here = lax.axis_index("dp") * 8 + lax.axis_index("seq")
    mine_of = lambda values, axis: lax.dynamic_slice_in_dim(values, here * 6, 6, axis)
    own_w = mine_of(w_qkv, 1)
    own_vec = jnp.stack([mine_of(norm_gains, 2)[:, 0], mine_of(biases, 2)[:, 0]], 1)
    prompt_rows = [prompt_rows[layer] for layer in range(layers)]
    x, payload, own, query_seg = open_call(patches, cls_tokens, segments, norm_gains, biases)
    key_seg = None
    kept = []
    lefts = []
    factors = []
    left_plans = (
        (("mid", 0), ("att", 0), ("mid", 1)),
        (("mid", 0), ("mid", 1), ("att", 1)),
    )
    def left_factors(layer, *behind):
        normed_all, att, nmid, active = factors[layer]
        tall, tall_other, wide, wide_other = left_call(
            left_plans[layer], orders[2 - 2 * layer], (picks[2 - 2 * layer], picks[1]), normed_all, att, after(nmid, *behind), active
        )
        return (tall, send(tall_other, "core", 1), wide, send(wide_other, "core", 1))

    come = swap_rows(payload)
    x, vecs, up_rows, prompt_rows, picks, small_pick, small_spot, own_w, own_vec = (
        lax.optimization_barrier(
            (x, vecs, up_rows, prompt_rows, picks, small_pick, small_spot, own_w, own_vec)
        )
    )
    out = forward_call(
        0, False, x, come, own, prompt_rows[0], vecs[0], up_rows[0], query_seg, None, weights
    )
    q, k, v, normed_all, att, lse, mid, nmid, slope, active, x_next, payload, own, key_seg = out
    kept.append((x, q, k, v, lse, mid, slope))
    factors.append((normed_all, att, nmid, active))
    lefts.append(left_factors(0))
    come = swap_rows(payload)
    x = after(x_next, lefts[0][0], lefts[0][2])
    kept.append((x,))
    cots = (cot_patches[0], cot_cls[0])
    out = turn_call(
        x, come, own, prompt_rows[1], vecs[1], up_rows[1], query_seg, key_seg, cots, first_seq, weights
    )
    factors.append(out[0:4])
    out_patch, out_cls = out[4:6]

    def both(values):
        return (values, send(values, "core", 1))

    def both_parts(parts):
        return (*parts, *[send(part, "core", 1) for part in parts])

    def give_back(layer, pays, qpart, mid_grad):
        return (swap_rows(pays), qpart, kept[layer][0], mid_grad, vecs[layer])

    arrived = [[], []]

    def start_ring(at, made, rows):
        pieces, ring_at = made[at], at % 2
        axis = RINGS[ring_at][0]
        if at == 0:
            come = deal_out(pieces, (axis,))
        else:
            come = [pieces[0]] + [send(pieces[step], axis, step) for step in (1, 3, 2)]
        arrived[ring_at].append((come, rows))

    tile = HALF // 4
    mid_at = 2 * WIDTH
    packed, (mid_grad, up_row_1, dq, qpart, dkv, pays, prompts_1, rows_1) = out[6:8], out[8:]
    grads = both_parts(packed)
    dqs, dkvs = both(dq), both(dkv)
    start = give_back(1, pays, qpart, mid_grad)
    lefts.append(left_factors(1, dkv, lefts[0][1], lefts[0][3], *grads[2:]))
    plan = [("down", 0, 0, 0, 0)]
    plan += [("up", part, mid_at, 0, HALF + part * tile) for part in range(3)]
    made = mlp_call(plan, ((0, HALF + 3 * tile),), lefts[1][0:2], grads)
    plan = [("q", None, 1, 0), ("k", None, 1, tile), ("v", None, 1, 2 * tile)]
    plan += [("out", mid_at + 2 * HALF, 1, 3 * tile), (3, mid_at + HALF, 1, 4 * tile)]
    talls = (after(lefts[1][0], made[0]), lefts[1][1])
    mixed = mixed_call(plan, ((1, 5 * tile),), seq, talls, lefts[1][2:], dqs, dkvs, grads)
    start_ring(0, made, (HALF,) + (tile,) * 3)
    start_ring(1, mixed, (tile,) * 5)

    start = (after(start[0], mixed[1][0]), *start[1:])
    x_in, q, k, v, lse, mid, slope = kept[0]
    small = (small_pick, small_spot, prompts_1, rows_1, up_row_1, up_row_1)
    out = back_call(
        start, first_seq, (mid, slope, q, k, v, lse), prompt_rows[0], vecs[0], query_seg, key_seg,
        small, weights,
    )
    packed, (mid_grad, _, dq, qpart, dkv, pays) = out[0:2], out[2:8]
    grads = both_parts(packed)
    plan = [("down", 0, 0, 2, 0), ("out", 0, mid_at + HALF, 2, HALF)]
    plan += [("up", part, mid_at, 2, HALF + (1 + part) * tile) for part in range(2)]
    talls = (after(lefts[0][0], dkv, arrived[0][0][0], *arrived[1][0][0]), lefts[0][1])
    made = mlp_call(plan, ((2, HALF + 3 * tile),), talls, grads, 60)
    second_steps = made[2]
    start = give_back(0, after(pays, arrived[0][0][0]), qpart, mid_grad)
    dqs, dkvs = both(dq), both(dkv)
    small = (out[8], send(out[9], "core", 1))
    plan = [("q", None, 1, 0), ("k", None, 1, tile), ("v", None, 1, 2 * tile)]
    plan += [(part, mid_at + 2 * HALF, 1, (1 + part) * tile + 32) for part in (2, 3)]
    talls = (after(lefts[0][0], second_steps[0]), lefts[0][1])
    mixed = mixed_call(
        plan, ((1, 5 * tile + 32),), seq, talls, lefts[0][2:], dqs, dkvs, grads, small
    )
    second_steps[2] = after(second_steps[2], mixed[1][0])
    start_ring(2, {2: second_steps}, (HALF,) + (tile,) * 3)
    start_ring(1, mixed, (tile,) * 3 + (16, 16) + (tile,) * 2)
    for group in arrived:
        come, rows = group[0]
        (total,) = fold_call([(1, [(come, rows)])])
        group[0] = ([total], rows)
    grad_patch, grad_cls = close_call((after(start[0], mixed[1][0]), *start[1:]))
    (come, rows), *others = arrived[0]
    (plane,) = fold_call([(16, [([after(come[0], arrived[1][0][0][0], grad_cls)], rows), *others])])
    (come, rows), *others = arrived[1]
    pieces = fold_call([(4, [([after(come[0], plane)], rows), *others])])
    plane = deal_out(plane, RINGS[0][1:])
    second = [pieces[0]] + [send(pieces[step], RINGS[1][1], step) for step in range(1, 4)]
    rows = tuple(row // 4 for _, items in arrived[1] for row in items)
    pieces = fold_call([(4, [(second, rows)])], LATE)
    third = [pieces[0]] + [send(pieces[step], RINGS[1][2], step) for step in range(1, 4)]
    lasts = [plane, *third]
    layouts = (
        [("down", 1, 0, 24)]
        + [("up", 1, part, 6) for part in range(3)]
        + [("down", 0, 0, 24), ("out", 0, 0, 6)]
        + [("up", 0, part, 6) for part in range(2)],
        [("qkv", 1, part, 6) for part in range(3)]
        + [("out", 1, 0, 6), ("up", 1, 3, 6)]
        + [("qkv", 0, part, 6) for part in range(3)]
        + [("small", 0, 0, 1), ("bias", 0, 0, 1), ("up", 0, 2, 6), ("up", 0, 3, 6)],
    )
    done = final_call(lasts, layouts, own_w, own_vec)
    swap = lambda values: jnp.transpose(values, (1, 0, 2))
    return (
        out_patch[None],
        swap(out_cls),
        grad_patch[None],
        swap(grad_cls),
        jnp.transpose(done[4], (1, 2, 0)),
        swap(done[0]),
        swap(done[1]),
        swap(done[2]),
        done[3],
        done[5],
        swap(done[6]),
        done[7],
    )


def solution(mesh):
    placed = (
        P("dp", "seq", None),
        P("dp", None, None),
        P("dp", "seq"),
        P(),
        P(),
        P(),
        P(),
        P(),
        P(),
        P(),
        P(),
        P("dp", "seq", None),
        P("dp", None, None),
    )
    return jax.shard_map(
        per_device,
        mesh=mesh,
        in_specs=placed,
        out_specs=(
            P("dp", "seq", None),
            P("dp", None, None),
            P("dp", "seq", None),
            P("dp", None, None),
            P(None, None, ("dp", "seq")),
            P(None, ("dp", "seq"), None),
            P(None, ("dp", "seq"), None),
            P(None, ("dp", "seq"), None),
            P(None, ("dp", "seq"), None),
            P(None, None, ("dp", "seq")),
            P(None, None, ("dp", "seq")),
            P(None, ("dp", "seq")),
        ),
        check_vma=False,
    )
```

```python
import functools

import jax
import jax.numpy as jnp
from jax import lax
from jax.experimental import pallas as pl
from jax.experimental.pallas import tpu as pltpu
from jax.sharding import PartitionSpec as P

HEADS = 12
HEAD = 64
WIDTH = 768
HIDDEN = 3072
PATCHES = 128
CLS = 10
PROMPTS = 50
OWN = 144
KEYS = 1152
CLS_AT = 1024
PROMPT_AT = 1040
FRONT = 128
BLOCKS = 8
PAY = 864
PACKED = 2 * WIDTH + HIDDEN
HALF = WIDTH // 2
TILE = 256
LOW = jnp.bfloat16
FULL = jnp.float32

eps_norm = 1e-06
penalty_rate = 2.0
big_negative = -1e30

AXES = ("dp", "seq")
SPAN = {"core": 2, "x": 4, "y": 4, "z": 4}
RINGS = (("y", "z", "x"), ("z", "y", "x"))
ANY = pl.BlockSpec(memory_space=pl.ANY)
VM = "whole"
HERE = pl.BlockSpec(memory_space=pltpu.VMEM)
SM = pl.BlockSpec(memory_space=pltpu.SMEM)


def place_of(device):
    dp, seq = device // 8, device % 8
    return {"core": dp % 2, "x": dp // 2 % 2 * 2 + seq // 4, "y": dp // 4, "z": seq % 4}


def device_of(place):
    dp = (place["y"] * 2 + place["x"] // 2) * 2 + place["core"]
    return dp * 8 + place["x"] % 2 * 4 + place["z"]


def moved(axis, step):
    pairs = []
    for device in range(128):
        place = place_of(device)
        place[axis] = (place[axis] + step) % SPAN[axis]
        pairs.append((device, device_of(place)))
    return pairs


def send(values, axis, step):
    return lax.ppermute(values, AXES, moved(axis, step))


def groups_of(axes):
    found = {}
    for device in range(128):
        place = place_of(device)
        rest = tuple(place[axis] for axis in SPAN if axis not in axes)
        found.setdefault(rest, []).append((tuple(place[axis] for axis in axes), device))
    return [[device for _, device in sorted(group)] for group in found.values()]


def deal_out(values, axes):
    return lax.all_to_all(
        values, AXES, 0, 0, tiled=True, axis_index_groups=groups_of(axes)
    )


def swap_rows(values):
    return lax.all_to_all(values, "seq", 0, 0, tiled=True)


def owner_order(axes, steps=()):
    here = place_of(lax.axis_index("dp") * 8 + lax.axis_index("seq"))
    rest = jnp.arange(128, dtype=jnp.int32)
    place = {}
    for axis in reversed(axes):
        place[axis] = rest % SPAN[axis]
        if axis in steps:
            place[axis] = (here[axis] + place[axis]) % SPAN[axis]
        rest = rest // SPAN[axis]
    place["core"] = (here["core"] + rest) % 2
    return device_of(place)


def nn(left, right):
    return lax.dot_general(left, right, (((1,), (0,)), ((), ())), preferred_element_type=FULL)


def nt(left, right):
    return lax.dot_general(left, right, (((1,), (1,)), ((), ())), preferred_element_type=FULL)


def plain_norm(values):
    centred = values - jnp.mean(values, -1, keepdims=True)
    scale = lax.rsqrt(jnp.mean(centred * centred, -1, keepdims=True) + eps_norm)
    return centred * scale, scale


def norm_pull(plain, scale, gain, upstream):
    inner = upstream * gain
    return scale * (
        inner
        - jnp.mean(inner, -1, keepdims=True)
        - plain * jnp.mean(inner * plain, -1, keepdims=True)
    )


def whole(dims):
    return pl.BlockSpec(dims, lambda i: (0,) * len(dims))


class Late:
    def __init__(self, index=None, cuts=1, axis=0):
        self.index, self.cuts, self.axis = index, cuts, axis


class Early:
    def __init__(self, dims, kind=FULL):
        self.shape, self.dtype = dims, kind


class Moves:
    def __init__(self):
        self.ins, self.outs, self.gone = {}, {}, []

    def start(self, *refs):
        for ref in refs:
            for copy in self.ins[id(ref)]:
                copy.start()

    def resident(self):
        part = Moves()
        part.start = part.wait = lambda *_: None
        part.flush = self.flush
        return part

    def wait(self, ref, piece=None):
        copies = self.ins[id(ref)]
        for copy in copies if piece is None else copies[piece : piece + 1]:
            copy.wait()

    def flush(self, *refs):
        for ref in refs:
            copy = self.outs.pop(id(ref), None)
            if copy is not None:
                copy.start()
                self.gone.append(copy)

    def close(self):
        for copy in self.outs.values():
            copy.start()
        for copy in [*self.gone, *self.outs.values()]:
            copy.wait()


def run(body, operands, specs, outs, name, micros, scratch=(), mib=63):
    late = [(at, spec) for at, spec in enumerate(specs) if isinstance(spec, Late)]
    early = [(at, out) for at, out in enumerate(outs) if isinstance(out, Early)]
    buffers, total = [], 0
    for at, spec in late:
        dims = operands[at].shape if spec.index is None else operands[at].shape[1:]
        buffers.append(pltpu.VMEM(dims, operands[at].dtype))
        total += spec.cuts
    buffers += [pltpu.VMEM(out.shape, out.dtype) for _, out in early]
    total += len(early)

    def kernel(*refs):
        refs = list(refs)
        first = len(operands) + len(outs) + len(scratch)
        space, sems = refs[first : first + len(buffers)], refs[-1]
        moves, sem = Moves(), 0
        for (at, spec), buffer in zip(late, space):
            source = refs[at] if spec.index is None else refs[at].at[spec.index]
            size = buffer.shape[spec.axis] // spec.cuts
            copies = []
            for piece in range(spec.cuts):
                part = pl.ds(piece * size, size)
                view = lambda ref: ref.at[part] if spec.axis == 0 else ref.at[:, part]
                pair = (source, buffer) if spec.cuts == 1 else (view(source), view(buffer))
                copies.append(pltpu.make_async_copy(*pair, sems.at[sem]))
                sem += 1
            moves.ins[id(buffer)] = copies
            refs[at] = buffer
        for (at, out), buffer in zip(early, space[len(late) :]):
            at += len(operands)
            moves.outs[id(buffer)] = pltpu.make_async_copy(buffer, refs[at], sems.at[sem])
            sem += 1
            refs[at] = buffer
        body(moves, refs[:first])
        moves.close()

    in_specs = []
    for operand, spec in zip(operands, specs):
        if isinstance(spec, Late):
            in_specs.append(ANY)
        else:
            in_specs.append(whole(operand.shape) if spec == "whole" else spec)
    return pl.pallas_call(
        kernel,
        grid=(1,),
        out_shape=tuple(shape(out.shape, out.dtype) for out in outs),
        in_specs=in_specs,
        out_specs=tuple(ANY if isinstance(out, Early) else whole(out.shape) for out in outs),
        scratch_shapes=[*scratch, *buffers, pltpu.SemaphoreType.DMA((max(total, 1),))],
        compiler_params=params(mib),
        cost_estimate=cost(micros),
        name=name,
    )(*operands)


def after(values, *others):
    return lax.optimization_barrier((values, others))[0]


def tile_at(index, size):
    return pl.ds(pl.multiple_of(index * size, size), size)


def params(mib=56):
    return pltpu.CompilerParams(vmem_limit_bytes=mib * 2**20)


SHARE = 1.0
ATT = 6
LEFT = 0.1
MIX = 0.1
TURN = 40
FOLD = 0.01
LATE = 12
MLP1 = 0.1


def cost(micros):
    return pl.CostEstimate(flops=int(micros * 1.1e9), bytes_accessed=1 << 20, transcendentals=0)


def shape(dims, kind=FULL):
    return jax.ShapeDtypeStruct(dims, kind)


def open_body(patch_ref, cls_ref, seg_ref, gain_ref, bias_ref, x_ref, pay_ref, own_ref, query_ref):
    x_ref[0:PATCHES] = patch_ref[0].astype(FULL)
    cls_rows = jnp.concatenate([cls_ref[0].astype(FULL), jnp.zeros((16 - CLS, WIDTH), FULL)], 0)
    x_ref[PATCHES:OWN] = cls_rows
    plain, _ = plain_norm(x_ref[...])
    normed = (plain * gain_ref[0, 0:1] + bias_ref[0, 0:1]).astype(LOW)
    own_ref[...] = normed
    segs = seg_ref[...].astype(FULL)
    last = jnp.broadcast_to(segs, (16, PATCHES)).astype(LOW)
    last = jnp.concatenate([last, jnp.zeros((16, WIDTH - PATCHES), LOW)], 1)
    for block in range(BLOCKS):
        pay_ref[block, 0:PATCHES] = normed[0:PATCHES]
        pay_ref[block, PATCHES:OWN] = last
    query_ref[0:PATCHES] = jnp.broadcast_to(segs, (PATCHES, PATCHES)).T
    row = lax.broadcasted_iota(jnp.int32, (16, 128), 0)
    query_ref[PATCHES:OWN] = jnp.where(row < CLS, row, -5).astype(FULL)


def open_call(patches, cls_tokens, segments, gains, biases):
    outs = (
        shape((OWN, WIDTH)),
        shape((BLOCKS, OWN, WIDTH), LOW),
        shape((OWN, WIDTH), LOW),
        shape((OWN, 128)),
    )
    operands = (patches, cls_tokens, segments, gains, biases)
    return run(lambda moves, refs: open_body(*refs), operands, [VM] * 5, outs, "open_norm", 2)


def seen_mask(key_ref, query_ref, mask_ref):
    keys = key_ref[0:1, :]
    seen = (keys == query_ref[:, 0:1]) | (keys == -1.0)
    mask_ref[...] = jnp.where(seen, 0.0, big_negative)


def half_lanes(rows):
    return lax.broadcasted_iota(jnp.int32, (rows, 2 * HEAD), 1) < HEAD


def split_rows(rows, patch_ref, cls_ref):
    patch_ref[...] = rows[0:PATCHES]
    for place in range(CLS):
        cls_ref[place] = rows[PATCHES + place : PATCHES + place + 1]


def forward_body(layer, last, moves, refs):
    first = layer == 0
    r = iter(refs)
    nxt = lambda: next(r)
    x_ref = nxt()
    come_ref = nxt()
    own_ref, prompt_ref, vec_ref, up_bias_ref, query_seg_ref = nxt(), nxt(), nxt(), nxt(), nxt()
    key_in_ref = None if first else nxt()
    wqkv, wout, wup, wdown = nxt(), nxt(), nxt(), nxt()
    q_ref, k_ref, v_ref, all_ref = nxt(), nxt(), nxt(), nxt()
    att_ref, lse_ref, mid_ref, nmid_ref = nxt(), nxt(), nxt(), nxt()
    slope_ref, active_ref, out_ref = nxt(), nxt(), nxt()
    next_ref, next_own_ref = nxt(), nxt()
    key_ref = nxt() if first else key_in_ref
    mask_ref = nxt()

    moves.start(wqkv)
    for block in range(BLOCKS):
        all_ref[block * PATCHES : (block + 1) * PATCHES] = come_ref[block, 0:PATCHES]

    gain_one, bias_one = vec_ref[0:1], vec_ref[2:3]
    gain_two, bias_two = vec_ref[1:2], vec_ref[6:7]

    plain, _ = plain_norm(prompt_ref[...])
    all_ref[CLS_AT:PROMPT_AT] = own_ref[PATCHES:OWN]
    all_ref[PROMPT_AT : PROMPT_AT + 64] = (plain * gain_one + bias_one).astype(LOW)
    all_ref[PROMPT_AT + 64 : KEYS] = jnp.zeros((KEYS - PROMPT_AT - 64, WIDTH), LOW)
    moves.flush(all_ref)
    if first:
        lane = lax.broadcasted_iota(jnp.int32, (8, FRONT), 1)
        front = jnp.where(
            lane < CLS, lane, jnp.where((lane >= 16) & (lane < 16 + PROMPTS), -1, -2)
        )
        for block in range(BLOCKS):
            segs = come_ref[block, PATCHES:OWN, 0:PATCHES].astype(FULL)
            key_ref[:, block * PATCHES : (block + 1) * PATCHES] = segs[0:8]
        key_ref[:, CLS_AT:KEYS] = front.astype(FULL)
    seen_mask(key_ref, query_seg_ref, mask_ref)

    def keys(tile, carry):
        at = tile_at(tile, TILE)
        rows = nn(all_ref[...], wqkv[:, pl.ds(pl.multiple_of(WIDTH + tile * TILE, TILE), TILE)])
        k_ref[:, at] = rows.astype(LOW)
        return carry

    def values(tile, carry):
        at = tile_at(tile, TILE)
        rows = nn(all_ref[...], wqkv[:, pl.ds(pl.multiple_of(2 * WIDTH + tile * TILE, TILE), TILE)])
        v_ref[:, at] = (rows + vec_ref[4:5, at]).astype(LOW)
        return carry

    def queries(tile, carry):
        at = tile_at(tile, TILE)
        rows = nn(own_ref[...], wqkv[:, at]) + vec_ref[3:4, at]
        q_ref[:, at] = (rows.astype(LOW).astype(FULL) * HEAD**-0.5).astype(LOW)
        return carry

    moves.wait(wqkv, 0)
    lax.fori_loop(0, 3, queries, 0, unroll=3)
    moves.wait(wqkv, 1)
    moves.start(wout, wup)
    lax.fori_loop(0, 3, keys, 0, unroll=3)
    moves.flush(k_ref)
    moves.wait(wqkv, 2)
    lax.fori_loop(0, 3, values, 0, unroll=3)
    moves.flush(v_ref)
    moves.start(wdown)

    lse_ref[...] = jnp.zeros((OWN, 128), FULL)
    lower = half_lanes(OWN)
    lane = lax.broadcasted_iota(jnp.int32, (OWN, 128), 1)

    def heads(pair, carry):
        at = tile_at(pair, 2 * HEAD)
        query, key, value = q_ref[:, at], k_ref[:, at], v_ref[:, at]
        outs = []
        for side in range(2):
            mine = lower if side == 0 else ~lower
            scores = nt(jnp.where(mine, query, jnp.zeros_like(query)), key) + mask_ref[...]
            top = jnp.max(scores, -1, keepdims=True)
            raised = jnp.exp(scores - top)
            total = jnp.sum(raised, -1, keepdims=True)
            outs.append(nn(raised.astype(LOW), value) / total)
            lane = lax.broadcasted_iota(jnp.int32, (OWN, 128), 1)
            lse_ref[...] = jnp.where(lane == 2 * pair + side, top + jnp.log(total), lse_ref[...])
        att_ref[:, at] = jnp.where(lower, outs[0], outs[1]).astype(LOW)
        return carry

    lax.fori_loop(0, HEADS // 2, heads, 0, unroll=2)

    moves.wait(wout)

    def project(tile, carry):
        at = tile_at(tile, TILE)
        mid_ref[:, at] = x_ref[:, at] + (nn(att_ref[...], wout[:, at]) + vec_ref[5:6, at])
        return carry

    lax.fori_loop(0, 3, project, 0, unroll=3)
    plain, _ = plain_norm(mid_ref[...])
    nmid_ref[...] = (plain * gain_two + bias_two).astype(LOW)
    moves.wait(wup)

    def rise(tile, carry):
        at = tile_at(tile, TILE)
        hidden = nn(nmid_ref[...], wup[:, at]) + up_bias_ref[0:1, at]
        share = 0.5 * (1.0 + lax.erf(hidden * 0.7071067811865476))
        active_ref[:, at] = (hidden * share).astype(LOW)
        slope_ref[:, at] = share + hidden * (0.3989422804014327 * jnp.exp(-0.5 * hidden * hidden))
        return carry

    lax.fori_loop(0, HIDDEN // TILE, rise, 0, unroll=4)
    moves.flush(slope_ref, active_ref)
    moves.wait(wdown)

    def lower_back(tile, carry):
        at = tile_at(tile, TILE)
        out_ref[:, at] = mid_ref[:, at] + (nn(active_ref[...], wdown[:, at]) + vec_ref[7:8, at])
        return carry

    lax.fori_loop(0, 3, lower_back, 0, unroll=3)
    if not last:
        plain, _ = plain_norm(out_ref[...])
        normed = (plain * vec_ref[8:9] + vec_ref[9:10]).astype(LOW)
        next_own_ref[...] = normed
        for block in range(BLOCKS):
            next_ref[block] = normed[0:PATCHES]
    else:
        split_rows(out_ref[...], next_ref, next_own_ref)


def forward_call(layer, last, x, come, own, prompt, vec, up_bias, query_seg, key_seg, weights):
    first = layer == 0
    outs = [
        shape((OWN, WIDTH), LOW),
        Early((KEYS, WIDTH), LOW),
        Early((KEYS, WIDTH), LOW),
        Early((KEYS, WIDTH), LOW),
        shape((OWN, WIDTH), LOW),
        shape((OWN, 128)),
        shape((OWN, WIDTH)),
        shape((OWN, WIDTH), LOW),
        Early((OWN, HIDDEN)),
        Early((OWN, HIDDEN), LOW),
        shape((OWN, WIDTH)),
    ]
    if last:
        outs += [shape((PATCHES, WIDTH)), shape((CLS, 1, WIDTH))]
    else:
        outs += [shape((BLOCKS, PATCHES, WIDTH), LOW), shape((OWN, WIDTH), LOW)]
    if first:
        outs += [shape((8, KEYS))]
    operands = [x, come, own, prompt, vec, up_bias, query_seg]
    specs = [VM, HERE] + [VM] * 5
    if not first:
        operands.append(key_seg)
        specs.append(VM)
    operands += weights
    specs += [Late(layer, 3, 1), Late(layer), Late(layer), Late(layer)]
    scratch = [pltpu.VMEM((OWN, KEYS), FULL)]
    body = lambda moves, refs: forward_body(layer, last, moves, refs)
    return run(body, operands, specs, outs, "forward_layer", 24 * SHARE, scratch)


def gathered_pull(come_ref, qpart_ref, x_ref, gain, mid_grad_ref):
    total = come_ref[0].astype(FULL)
    for block in range(1, BLOCKS):
        total = total + come_ref[block].astype(FULL)
    patch_part = total[0:WIDTH].T
    cls_part = jnp.concatenate(
        [total[WIDTH + 16 * lane : WIDTH + 16 * (lane + 1)] for lane in range(6)], 1
    )
    d_normed = jnp.concatenate([patch_part, cls_part], 0) + qpart_ref[...]
    plain, scale = plain_norm(x_ref[...])
    return mid_grad_ref[...] + norm_pull(plain, scale, gain, d_normed)


def row_share(first_ref):
    row = lax.broadcasted_iota(jnp.int32, (OWN, 1), 0)
    return jnp.where(row < PATCHES, 1.0, jnp.where(row < PATCHES + CLS, first_ref[0, 0], 0.0))


def back_mlp_body(last, moves, refs):
    r = iter(refs)
    nxt = lambda: next(r)
    if last:
        cot_ref, cot_cls_ref, key_ref, query_seg_ref = nxt(), nxt(), nxt(), nxt()
    else:
        come_ref = nxt()
        up_qpart_ref, up_x_ref, up_mid_grad_ref, up_vec_ref = nxt(), nxt(), nxt(), nxt()
    first_ref, mid_ref, slope_ref, vec_ref = nxt(), nxt(), nxt(), nxt()
    wout, wup, wdown = nxt(), nxt(), nxt()
    grad_refs = nxt(), nxt()
    datt_ref, mid_grad_ref = nxt(), nxt()
    rows_ref, up_spot_ref = nxt(), nxt()
    up_ref, low_ref, hid_ref, up_row_ref = nxt(), nxt(), nxt(), nxt()

    moves.start(wdown, slope_ref)
    gain_two = vec_ref[1:2]
    share = row_share(first_ref)
    if last:
        valid = ((query_seg_ref[...] < CLS) & (query_seg_ref[...] >= 0)).astype(FULL)
        up_ref[0:PATCHES] = cot_ref[...].astype(FULL) * valid[0:PATCHES, 0:1]
        hits = (key_ref[0:1, 0:CLS_AT] == query_seg_ref[PATCHES:OWN, 0:1]).astype(FULL)
        present = jnp.max(hits, -1, keepdims=True)
        cls_rows = [cot_cls_ref[...].astype(FULL), jnp.zeros((16 - CLS, WIDTH), FULL)]
        up_ref[PATCHES:OWN] = jnp.concatenate(cls_rows, 0) * present
    else:
        up_ref[...] = gathered_pull(
            come_ref, up_qpart_ref, up_x_ref, up_vec_ref[0:1], up_mid_grad_ref
        )
    low_ref[...] = up_ref[...].astype(LOW)
    weighted = low_ref[...].astype(FULL) * share
    grad_refs[0][:, 0:WIDTH] = weighted.astype(LOW)
    rows_ref[...] = jnp.zeros((8, WIDTH), FULL)
    rows_ref[0:1] = jnp.sum(weighted, 0, keepdims=True)
    moves.start(wup)

    def to_hidden(half, tile, carry):
        at = tile_at(tile, TILE)
        grad = (nt(low_ref[...], wdown[at, :]) * slope_ref[:, at]).astype(LOW)
        hid_ref[:, at] = grad
        counted = grad.astype(FULL) * share
        to = WIDTH + tile * TILE - half * (PACKED // 2)
        grad_refs[half][:, pl.ds(pl.multiple_of(to, TILE), TILE)] = counted.astype(LOW)
        up_row_ref[:, at] = jnp.broadcast_to(jnp.sum(counted, 0, keepdims=True), (8, TILE))
        return carry

    moves.wait(slope_ref)
    for piece in range(4):
        moves.wait(wdown, piece)
        body = functools.partial(to_hidden, piece // 2)
        lax.fori_loop(3 * piece, 3 * piece + 3, body, 0, unroll=3)
    moves.wait(wup)
    moves.start(wout)

    def to_mid(tile, carry):
        at = tile_at(tile, TILE)
        mid_grad_ref[:, at] = nt(hid_ref[...], wup[at, :])
        return carry

    lax.fori_loop(0, 3, to_mid, 0, unroll=3)
    d_normed = mid_grad_ref[...]
    plain, scale = plain_norm(mid_ref[...])
    counted = d_normed * share
    rows_ref[1:2] = jnp.sum(counted * plain, 0, keepdims=True)
    rows_ref[2:3] = jnp.sum(counted, 0, keepdims=True)
    mid_grad_ref[...] = up_ref[...] + norm_pull(plain, scale, gain_two, d_normed)
    low_ref[...] = mid_grad_ref[...].astype(LOW)
    weighted = low_ref[...].astype(FULL) * share
    grad_refs[1][:, PACKED // 2 - WIDTH :] = weighted.astype(LOW)
    rows_ref[3:4] = jnp.sum(weighted, 0, keepdims=True)
    moves.flush(*grad_refs)
    up_row = up_row_ref[0:1]
    spots = [up_row[:, 24 * spot : 24 * (spot + 1)] for spot in range(128)]
    up_spot_ref[...] = jnp.concatenate(spots, 0)
    moves.wait(wout)

    def to_att(tile, carry):
        at = tile_at(tile, TILE)
        datt_ref[:, at] = nt(low_ref[...], wout[at, :]).astype(LOW)
        return carry

    lax.fori_loop(0, 3, to_att, 0, unroll=3)


def back_att_body(layer, moves, refs):
    r = iter(refs)
    nxt = lambda: next(r)
    first_ref, rows_in_ref, datt_ref = nxt(), nxt(), nxt()
    q_ref, k_ref, v_ref, lse_ref = nxt(), nxt(), nxt(), nxt()
    prompt_ref, vec_ref, query_seg_ref, key_ref = nxt(), nxt(), nxt(), nxt()
    if layer == 0:
        pick_ref, spot_ref, prompts_1, rows_1, up_0, up_1 = [nxt() for _ in range(6)]
    wqkv = nxt()
    dq_ref, qpart_ref, dkv_ref, pay_ref = nxt(), nxt(), nxt(), nxt()
    if layer == 0:
        small_refs = nxt(), nxt()
        dprompt_ref, rows_ref = nxt(), nxt()
    else:
        dprompt_ref, rows_ref = nxt(), nxt()
    mask_ref, dqf_ref, qt_ref, dat_ref, front_ref = [nxt() for _ in range(5)]

    moves.start(k_ref, v_ref, wqkv)
    gain_one = vec_ref[0:1]
    share = row_share(first_ref)
    seen_mask(key_ref, query_seg_ref, mask_ref)
    rows_ref[...] = rows_in_ref[...]

    def turn(tile, carry):
        at = tile_at(tile, TILE)
        dat_ref[at, :] = (datt_ref[:, at].astype(FULL) * share).T.astype(LOW)
        qt_ref[at, :] = (q_ref[:, at].astype(FULL) * share).T.astype(LOW)
        return carry

    lax.fori_loop(0, 3, turn, 0, unroll=3)
    lower = half_lanes(OWN)
    lane = lax.broadcasted_iota(jnp.int32, (OWN, 128), 1)
    moves.wait(k_ref)
    moves.wait(v_ref)

    def heads(pair, carry):
        at = tile_at(pair, 2 * HEAD)
        query, key, value, grad = q_ref[:, at], k_ref[:, at], v_ref[:, at], datt_ref[:, at]
        outs = []
        for side in range(2):
            mine = lower if side == 0 else ~lower
            head = 2 * pair + side
            log_total = jnp.sum(jnp.where(lane == head, lse_ref[...], 0.0), -1, keepdims=True)
            scores = nt(jnp.where(mine, query, jnp.zeros_like(query)), key) + mask_ref[...]
            probs = jnp.exp(scores - log_total)
            d_probs = nt(jnp.where(mine, grad, jnp.zeros_like(grad)), value)
            both = probs * d_probs
            across = jnp.sum(both, -1, keepdims=True)
            d_scores = (both - probs * across).astype(LOW)
            probs_low = probs.astype(LOW)
            outs.append(nn(d_scores, key))
            rows = tile_at(head, HEAD)
            dkv_ref[rows, :] = nn(qt_ref[rows, :], d_scores).astype(LOW)
            value_rows = pl.ds(pl.multiple_of(WIDTH + head * HEAD, HEAD), HEAD)
            dkv_ref[value_rows, :] = nn(dat_ref[rows, :], probs_low).astype(LOW)
        dqf_ref[:, at] = (jnp.where(lower, outs[0], outs[1]) * HEAD**-0.5).astype(LOW)
        return carry

    lax.fori_loop(0, HEADS // 2, heads, 0, unroll=2)
    moves.flush(dkv_ref)
    counted = dqf_ref[...].astype(FULL) * share
    dq_ref[...] = counted.astype(LOW)
    rows_ref[4:5] = jnp.sum(counted, 0, keepdims=True)
    moves.wait(wqkv)

    def to_normed(tile, carry):
        at = tile_at(tile, TILE)
        qpart_ref[:, at] = nt(dqf_ref[...], wqkv[at, 0:WIDTH])
        return carry

    lax.fori_loop(0, 3, to_normed, 0, unroll=3)

    front_ref[...] = nn(wqkv[:, WIDTH:], dkv_ref[:, CLS_AT:KEYS])
    shift = jnp.sum(front_ref[...], -1, keepdims=True)
    front = front_ref[...].T
    cls_rows = jnp.concatenate(
        [front[0:16, 128 * place : 128 * (place + 1)] for place in range(6)], 0
    )
    for block in range(0, BLOCKS, 2):
        part = nn(wqkv[:, WIDTH:], dkv_ref[:, block * PATCHES : (block + 2) * PATCHES])
        shift = shift + jnp.sum(part, -1, keepdims=True)
        for side in range(2):
            pay_ref[block + side, 0:WIDTH] = part[:, side * PATCHES : (side + 1) * PATCHES].astype(LOW)
            pay_ref[block + side, WIDTH:PAY] = cls_rows.astype(LOW)
    moves.flush(pay_ref)

    plain, scale = plain_norm(prompt_ref[...])
    d_prompt = norm_pull(plain, scale, gain_one, front[16:80])
    query_seg = query_seg_ref[0:PATCHES, 0:1]
    slots = jnp.sum((query_seg < CLS).astype(FULL), 0, keepdims=True)
    dprompt_ref[...] = d_prompt + (penalty_rate / 1024.0) * slots * prompt_ref[...]

    turned = jnp.broadcast_to(shift, (WIDTH, 128)).T
    rows_ref[6:7] = turned[0:1] + jnp.sum(qpart_ref[...] * share, 0, keepdims=True)
    totals = jnp.sum(dkv_ref[WIDTH : 2 * WIDTH].astype(FULL), -1, keepdims=True)
    rows_ref[5:6] = jnp.broadcast_to(totals, (WIDTH, 128)).T[0:1]
    if layer != 0:
        return
    joined = jnp.concatenate([dprompt_ref[0:56], prompts_1[0:56], rows_ref[...], rows_1[...]], 0)
    turned = nt(pick_ref[...], joined.astype(LOW))
    ups = [nn(spot_ref[...], up[...].astype(LOW)) for up in (up_0, up_1)]
    rows = jnp.concatenate([turned[128 * part : 128 * (part + 1)] for part in range(6)], 1)
    ups = jnp.concatenate([*ups, jnp.zeros((128, WIDTH - 48), FULL)], 1)
    for half in range(2):
        spots = slice(64 * half, 64 * (half + 1))
        small_refs[half][...] = jnp.concatenate([rows[spots], ups[spots]], 0).astype(LOW)


class Joined:
    def __init__(self, moves, last, *more):
        self.moves, self.last, self.more = moves, last, more
        self.wait, self.flush = moves.wait, moves.flush

    def start(self, *refs):
        self.moves.start(*refs)
        if any(ref is self.last for ref in refs):
            self.moves.start(*self.more)


class Started(Joined):
    def start(self, *refs):
        pass


def back_body(moves, refs):
    r = iter(refs)
    take = lambda count: [next(r) for _ in range(count)]
    start, first = take(5), next(r)
    mid, slope, q, k, v, lse, prompt, vec, query_seg, key = take(10)
    small, (wqkv, wout, wup, wdown) = take(6), take(4)
    grads, mid_grad, up_spot = take(2), next(r), next(r)
    dq, qpart, dkv, pay = take(4)
    small_out = take(2)
    datt, rows_in, up, low, hid, up_row, mask, dqf, qt, dat, front, dprompt, rows = take(13)
    back_mlp_body(
        False, Joined(moves, wup, k, v, wqkv),
        [*start, first, mid, slope, vec, wout, wup, wdown]
        + [*grads, datt, mid_grad, rows_in, up_spot, up, low, hid, up_row],
    )
    back_att_body(
        0, Started(moves, None),
        [first, rows_in, datt, q, k, v, lse, prompt, vec, query_seg, key, *small[:4], up_spot, small[5]]
        + [wqkv, dq, qpart, dkv, pay, *small_out, dprompt, rows, mask, dqf, qt, dat, front],
    )


def back_call(start, first_seq, saved, prompt, vec, query_seg, key_seg, small, weights):
    mid, slope, q, k, v, lse = saved
    operands = [*start, first_seq, mid, slope, q, k, v, lse, prompt, vec, query_seg, key_seg]
    operands += [*small, *weights]
    specs = [HERE] + [VM] * 4 + [SM, VM, Late(), VM, Late(), Late()] + [VM] * 11
    specs += [Late(0), Late(0), Late(0), Late(0, 4)]
    outs = [
        Early((OWN, PACKED // 2), LOW),
        Early((OWN, PACKED // 2), LOW),
        shape((OWN, WIDTH)),
        shape((128, 24)),
        shape((OWN, WIDTH), LOW),
        shape((OWN, WIDTH)),
        Early((2 * WIDTH, KEYS), LOW),
        Early((BLOCKS, PAY, 128), LOW),
        shape((128, WIDTH), LOW),
        shape((128, WIDTH), LOW),
    ]
    space = lambda *dims: pltpu.VMEM(dims, FULL)
    low = lambda *dims: pltpu.VMEM(dims, LOW)
    scratch = [low(OWN, WIDTH), space(8, WIDTH), space(OWN, WIDTH), low(OWN, WIDTH)]
    scratch += [low(OWN, HIDDEN), space(8, HIDDEN), space(OWN, KEYS), low(OWN, WIDTH)]
    scratch += [low(WIDTH, OWN), low(WIDTH, OWN), space(WIDTH, FRONT), space(64, WIDTH)]
    scratch += [space(8, WIDTH)]
    return run(back_body, operands, specs, outs, "backward_layer", ATT, scratch)


def turn_body(moves, refs):
    r = iter(refs)
    take = lambda count: [next(r) for _ in range(count)]
    x, come, own, prompt, vec, up_bias, query_seg, key = take(8)
    cots, first = take(2), next(r)
    wqkv, wout, wup, wdown = take(4)
    normed_all, att, nmid, active, out_patch, out_cls = take(6)
    grads, mid_grad, up_spot = take(2), next(r), next(r)
    dq, qpart, dkv, pay, dprompt, rows = take(6)
    q, k, v, lse, mid, slope, out, mask = take(8)
    datt, rows_in, up, low, hid, up_row = take(6)
    dqf, qt, dat, front = take(4)
    forward_body(
        1, True, moves,
        [x, come, own, prompt, vec, up_bias, query_seg, key, wqkv, wout, wup, wdown]
        + [q, k, v, normed_all, att, lse, mid, nmid, slope, active, out, out_patch, out_cls]
        + [mask],
    )
    still = moves.resident()
    back_mlp_body(
        True, still,
        [*cots, key, query_seg, first, mid, slope, vec, wout, wup, wdown]
        + [*grads, datt, mid_grad, rows_in, up_spot, up, low, hid, up_row],
    )
    back_att_body(
        1, still,
        [first, rows_in, datt, q, k, v, lse, prompt, vec, query_seg, key, wqkv]
        + [dq, qpart, dkv, pay, dprompt, rows, mask, dqf, qt, dat, front],
    )


def turn_call(x, come, own, prompt, vec, up_bias, query_seg, key_seg, cots, first_seq, weights):
    operands = [x, come, own, prompt, vec, up_bias, query_seg, key_seg, *cots, first_seq, *weights]
    specs = [VM, HERE] + [VM] * 8 + [SM, Late(1, 3, 1), Late(1), Late(1), Late(1)]
    outs = [
        Early((KEYS, WIDTH), LOW),
        shape((OWN, WIDTH), LOW),
        shape((OWN, WIDTH), LOW),
        Early((OWN, HIDDEN), LOW),
        shape((PATCHES, WIDTH)),
        shape((CLS, 1, WIDTH)),
        Early((OWN, PACKED // 2), LOW),
        Early((OWN, PACKED // 2), LOW),
        shape((OWN, WIDTH)),
        shape((128, 24)),
        shape((OWN, WIDTH), LOW),
        shape((OWN, WIDTH)),
        Early((2 * WIDTH, KEYS), LOW),
        Early((BLOCKS, PAY, 128), LOW),
        shape((64, WIDTH)),
        shape((8, WIDTH)),
    ]
    space = lambda *dims: pltpu.VMEM(dims, FULL)
    low = lambda *dims: pltpu.VMEM(dims, LOW)
    scratch = [low(OWN, WIDTH), low(KEYS, WIDTH), low(KEYS, WIDTH), space(OWN, 128)]
    scratch += [space(OWN, WIDTH), space(OWN, HIDDEN), space(OWN, WIDTH), space(OWN, KEYS)]
    scratch += [low(OWN, WIDTH), space(8, WIDTH), space(OWN, WIDTH), low(OWN, WIDTH)]
    scratch += [low(OWN, HIDDEN), space(8, HIDDEN), low(OWN, WIDTH), low(WIDTH, OWN)]
    scratch += [low(WIDTH, OWN), space(WIDTH, FRONT)]
    return run(turn_body, operands, specs, outs, "turn_layer", TURN, scratch)


def close_body(come_ref, qpart_ref, x_ref, mid_grad_ref, vec_ref, patch_ref, cls_ref):
    rows = gathered_pull(come_ref, qpart_ref, x_ref, vec_ref[0:1], mid_grad_ref)
    split_rows(rows, patch_ref, cls_ref)


def close_call(operands):
    outs = (shape((PATCHES, WIDTH)), shape((CLS, 1, WIDTH)))
    specs = [HERE] + [VM] * (len(operands) - 1)
    return run(lambda moves, refs: close_body(*refs), operands, specs, outs, "close_norm", 2)


def left_body(plan, moves, refs):
    order_ref, *refs = refs
    picks, (all_ref, att_ref, mid_ref, active_ref) = refs[0:2], refs[2:6]
    tall_refs, wide_refs = refs[6:8], refs[8:10]
    turned_ref, down_ref = refs[10:12]

    def turn(tile, carry):
        at = tile_at(tile, TILE)
        turned_ref[at, :] = active_ref[:, at].astype(FULL).T
        return carry

    def move(spot, carry):
        source = pl.ds(pl.multiple_of(order_ref[spot] * 24, 8), 24)
        target = pl.ds(pl.multiple_of(spot * 24, 8), 24)
        down_ref[target, :] = turned_ref[source, :]
        return carry

    moves.start(all_ref)
    lax.fori_loop(0, HIDDEN // TILE, turn, 0, unroll=3)
    lax.fori_loop(0, 128, move, 0, unroll=8)
    for half in range(2):
        rows = slice(half * 2 * WIDTH, (half + 1) * 2 * WIDTH)
        tall_refs[half][0 : 2 * WIDTH, 0:OWN] = down_ref[rows].astype(LOW)
    row = 2 * WIDTH
    for kind, ring_at in plan:
        source = {"mid": mid_ref, "att": att_ref}[kind][...]
        turned = nt(picks[ring_at][...], source).astype(LOW)
        for half in range(2):
            tall_refs[half][row : row + HALF, 0:OWN] = turned[half * HALF : (half + 1) * HALF]
        row += HALF
    moves.flush(*tall_refs)
    moves.wait(all_ref)
    for half in range(2):
        wide = nt(picks[1][half * HALF : (half + 1) * HALF], all_ref[...])
        wide_refs[half][...] = wide.astype(LOW)


def left_call(plan, order, picks, normed_all, att, nmid, active):
    tall = (2 * WIDTH + len(plan) * HALF, 256)
    outs = [Early(tall, LOW)] * 2 + [shape((HALF, KEYS), LOW)] * 2
    operands = (order, *picks, normed_all, att, nmid, active)
    scratch = [pltpu.VMEM((HIDDEN, OWN), FULL), pltpu.VMEM((HIDDEN, OWN), FULL)]
    body = lambda moves, refs: left_body(plan, moves, refs)
    return run(body, operands, [SM, VM, VM, Late(), VM, VM, VM], outs, "left_factors", LEFT, scratch)


def rights_of(grad_refs, kind, part, tile):
    at = {"down": 0, "up": WIDTH + part * WIDTH, "out": WIDTH + HIDDEN}[kind] + tile * TILE
    half, at = at // (PACKED // 2), at % (PACKED // 2)
    return [grad_refs[2 * side + half][:, at : at + TILE] for side in range(2)]


def piece_shapes(classes):
    outs = []
    for number, rows in classes:
        outs += [shape((4, rows, WIDTH), LOW)] if number == 0 else [shape((rows, WIDTH), LOW)] * 4
    return outs


def by_class(classes, arrays):
    found, at = {}, 0
    for number, _ in classes:
        if number == 0:
            found[0] = [arrays[at].at[way] for way in range(4)]
            at += 1
        else:
            found[number] = list(arrays[at : at + 4])
            at += 4
    return found


def deal(out, row, values, columns):
    size = values.shape[0] // 4
    for way in range(4):
        out[way][row : row + size, columns] = values[way * size : (way + 1) * size].astype(LOW)


def mlp_body(plan, classes, refs):
    tall_refs, grad_refs = refs[0:2], refs[2:6]
    outs = by_class(classes, refs[6:])
    for kind, part, left_row, out, out_row in plan:
        for tile in range(3):
            columns = slice(tile * TILE, (tile + 1) * TILE)
            rights = rights_of(grad_refs, kind, part, tile)
            for piece in range(4 if kind == "down" else 1):
                rows = slice(left_row + piece * HALF, left_row + (piece + 1) * HALF)
                lefts = [tall[rows, 0:OWN] for tall in tall_refs]
                values = nn(lefts[0], rights[0]) + nn(lefts[1], rights[1])
                if kind == "down":
                    outs[out][piece][out_row : out_row + HALF, columns] = values.astype(LOW)
                else:
                    deal(outs[out], out_row, values, columns)


def mlp_call(plan, classes, talls, grads, micros=MLP1):
    operands = (*talls, *grads)
    body = lambda moves, refs: mlp_body(plan, classes, refs)
    out = run(body, operands, [VM] * 6, piece_shapes(classes), "grad_mlp", micros)
    return by_class_values(classes, out)


def by_class_values(classes, arrays):
    found, at = {}, 0
    for number, _ in classes:
        found[number] = arrays[at] if number == 0 else list(arrays[at : at + 4])
        at += 1 if number == 0 else 4
    return found


def mixed_body(plan, classes, small, moves, refs):
    seq_ref, *refs = refs
    tall_refs, wide_refs, dq_refs, dkv_refs = [refs[2 * at : 2 * at + 2] for at in range(4)]
    grad_refs, small_refs = refs[8:12], refs[12:14]
    outs = by_class(classes, refs[14:] if small else refs[12:])
    moves.start(*wide_refs, *dkv_refs)
    for ref in (*wide_refs, *dkv_refs):
        moves.wait(ref)
    moves.start(*tall_refs, *grad_refs)
    brought = False
    if small:
        joined = small_refs[0][...].astype(FULL) + small_refs[1][...].astype(FULL)
        for way in range(4):
            spots = [joined[64 * part + 16 * way : 64 * part + 16 * (way + 1)] for part in range(2)]
            outs[1][way][3 * HALF // 4 : 3 * HALF // 4 + 32] = jnp.concatenate(spots, 0).astype(LOW)
    for kind, left_row, out, out_row in plan:
        for tile in range(3):
            columns = slice(tile * TILE, (tile + 1) * TILE)
            values = jnp.zeros((HALF, TILE), FULL)
            for side in range(2):
                if kind in ("k", "v"):
                    at = (0 if kind == "k" else WIDTH) + tile * TILE
                    values = values + nt(wide_refs[side][...], dkv_refs[side][at : at + TILE])
                    continue
                if kind == "q" and left_row is None:
                    wide = wide_refs[side]
                    mine = pl.ds(pl.multiple_of(seq_ref[0, 0] * PATCHES, PATCHES), PATCHES)
                    left = jnp.concatenate([wide[:, mine], wide[:, CLS_AT:PROMPT_AT]], 1)
                else:
                    if not brought:
                        brought = True
                        for ref in (*tall_refs, *grad_refs):
                            moves.wait(ref)
                    left = tall_refs[side][left_row : left_row + HALF, 0:OWN]
                if kind == "q":
                    right = dq_refs[side][:, columns]
                else:
                    name, part = ("out", 0) if kind == "out" else ("up", kind)
                    right = rights_of(grad_refs, name, part, tile)[side]
                values = values + nn(left, right)
            deal(outs[out], out_row, values, columns)


def mixed_call(plan, classes, seq, talls, wides, dqs, dkvs, grads, small=()):
    operands = (seq, *talls, *wides, *dqs, *dkvs, *grads, *small)
    body = lambda moves, refs: mixed_body(plan, classes, bool(small), moves, refs)
    specs = [SM] + [Late()] * 4 + [VM] * 2 + [Late()] * 6 + [VM] * len(small)
    out = run(body, operands, specs, piece_shapes(classes), "grad_mixed", MIX)
    return by_class_values(classes, out)


def fold_body(classes, refs):
    r = iter(refs)
    totals = []
    for _, groups in classes:
        totals.append([])
        for arrays, _ in groups:
            come = next(r)
            ways = [come.at[way] for way in range(4)] if len(come.shape) == 3 else [come]
            ways += [next(r) for _ in range(arrays - 1)]
            total = ways[0][...].astype(FULL)
            for way in ways[1:]:
                total = total + way[...].astype(FULL)
            totals[-1].append(total)
    for (ways, groups), sums in zip(classes, totals):
        joint = next(r) if ways == 16 else None
        for way in range(ways):
            out = joint.at[way] if ways == 16 else next(r)
            parts = []
            for total, (_, items) in zip(sums, groups):
                at = 0
                for rows in items:
                    size = rows // ways
                    parts.append(total[at + way * size : at + (way + 1) * size])
                    at += rows
            short = out.shape[0] - sum(part.shape[0] for part in parts)
            if short:
                parts.append(jnp.zeros((short, out.shape[1]), FULL))
            out[...] = jnp.concatenate(parts, 0).astype(LOW)


def fold_call(classes, micros=FOLD):
    operands = []
    for _, groups in classes:
        for come, _ in groups:
            operands += come if isinstance(come, list) else [come]
    number = lambda come: len(come) if isinstance(come, list) else 1
    counts = [(ways, [(number(come), items) for come, items in groups]) for ways, groups in classes]
    wide = 256
    outs = []
    for ways, groups in counts:
        size = -(-sum(sum(items) for _, items in groups) // (16 * ways)) * 16
        if ways == 16:
            outs.append(shape((16, size, WIDTH), LOW))
        else:
            outs += [shape((size, WIDTH), LOW)] * ways
    block = lambda *dims: pl.BlockSpec((*dims, wide), lambda i: (*[0] * len(dims), i))
    return list(
        pl.pallas_call(
            lambda *refs: fold_body(counts, refs),
            grid=(WIDTH // wide,),
            out_shape=tuple(outs),
            in_specs=[block(*come.shape[:-1]) for come in operands],
            out_specs=tuple(block(*out.shape[:-1]) for out in outs),
            compiler_params=params(63),
            cost_estimate=cost(micros),
            name="ring_fold",
        )(*operands)
    )


def final_body(layouts, refs):
    r = iter(refs)
    plane, ring = next(r), [next(r) for _ in range(4)]
    arrays = ([plane.at[way] for way in range(16)], ring)
    own_w_ref, own_vec_ref = next(r), next(r)
    qkv_ref, out_ref, up_ref, down_ref = next(r), next(r), next(r), next(r)
    prompt_ref, gain_ref, bias_ref, up_bias_ref = next(r), next(r), next(r), next(r)
    pieces = []
    for array, layout in zip(arrays, layouts):
        total = array[0][...].astype(FULL)
        for way in array[1:]:
            total = total + way[...].astype(FULL)
        at = 0
        for entry in layout:
            pieces.append((entry[:3], total[at : at + entry[3]]))
            at += entry[3]
    small = None
    wholes = [jnp.zeros((6, 1), FULL)] * 2
    for (kind, layer, part), piece in pieces:
        columns = slice(part * WIDTH, (part + 1) * WIDTH)
        if kind == "qkv":
            qkv_ref[:, layer, columns] = piece
            weight = own_w_ref[layer, :, columns].astype(FULL)
            wholes[layer] = wholes[layer] + jnp.sum(piece * weight, -1, keepdims=True)
        elif kind == "out":
            out_ref[:, layer, :] = piece
        elif kind == "up":
            up_ref[:, layer, columns] = piece
        elif kind == "down":
            down_ref[layer] = piece
        elif kind == "small":
            small = jnp.concatenate([piece[:, 128 * i : 128 * (i + 1)] for i in range(6)], 0)
        else:
            up_bias_ref[0:1] = piece[:, 0:24]
            up_bias_ref[1:2] = piece[:, 24:48]
    turn = lambda values: jnp.concatenate([values, jnp.zeros((2, 128), FULL)], 0).T
    rows = turn(small)
    for layer in range(2):
        prompt_ref[:, layer, :] = small[:, 56 * layer : 56 * layer + PROMPTS]
        at = 112 + 8 * layer
        part = rows[at : at + 8, 0:6]
        whole = turn(jnp.broadcast_to(wholes[layer], (6, 128)))[0:1, 0:6]
        gain, shift = own_vec_ref[layer, 0:1], own_vec_ref[layer, 1:2]
        gain_ref[layer, 0:1] = (whole - shift * part[6:7]) / gain
        gain_ref[layer, 1:2] = part[1:2]
        for place, source in enumerate((6, 4, 5, 3, 2, 0)):
            bias_ref[place, layer : layer + 1] = part[source : source + 1]


def final_call(arrays, layouts, own_w, own_vec):
    operands = [*arrays, own_w, own_vec]
    outs = (
        shape((6, 2, 3 * WIDTH)),
        shape((6, 2, WIDTH)),
        shape((6, 2, HIDDEN)),
        shape((2, 24, WIDTH)),
        shape((6, 2, PROMPTS)),
        shape((2, 2, 6)),
        shape((6, 2, 6)),
        shape((2, 24)),
    )
    body = lambda moves, refs: final_body(layouts, refs)
    return run(body, operands, [VM] * len(operands), outs, "final_fold", 3)


def per_device(
    patches,
    cls_tokens,
    segments,
    prompts,
    w_qkv,
    w_out,
    w_up,
    w_down,
    norm_gains,
    biases,
    up_bias,
    cot_patches,
    cot_cls,
):
    layers = 2
    weights = (w_qkv, w_out, w_up, w_down)
    first_seq = (lax.axis_index("seq") == 0).astype(FULL).reshape(1, 1)
    prompt_rows = jnp.pad(prompts.astype(FULL), ((0, 0), (0, 64 - PROMPTS), (0, 0)))
    vecs = []
    for layer in range(layers):
        following = min(layer + 1, layers - 1)
        vecs.append(
            jnp.concatenate(
                [
                    norm_gains[layer],
                    biases[layer],
                    norm_gains[following, 0:1],
                    biases[following, 0:1],
                    jnp.zeros((6, WIDTH), FULL),
                ],
                0,
            )
        )
    up_rows = [jnp.broadcast_to(up_bias[layer], (8, HIDDEN)) for layer in range(layers)]
    orders = [
        owner_order(RINGS[0]),
        owner_order(RINGS[1], RINGS[1]),
        owner_order(RINGS[0], RINGS[0][:1]),
    ]
    steps = jnp.arange(6, dtype=jnp.int32)
    one_hot = lambda wanted, size: (wanted[:, None] == jnp.arange(size)[None, :]).astype(LOW)
    picks = [one_hot((order[:, None] * 6 + steps).reshape(-1), WIDTH) for order in orders]
    small_pick = one_hot((orders[1][None, :] * 6 + steps[:, None]).reshape(-1), WIDTH)
    small_spot = one_hot(orders[1], 128)

    seq = lax.axis_index("seq").astype(jnp.int32).reshape(1, 1)
    here = lax.axis_index("dp") * 8 + lax.axis_index("seq")
    mine_of = lambda values, axis: lax.dynamic_slice_in_dim(values, here * 6, 6, axis)
    own_w = mine_of(w_qkv, 1)
    own_vec = jnp.stack([mine_of(norm_gains, 2)[:, 0], mine_of(biases, 2)[:, 0]], 1)
    prompt_rows = [prompt_rows[layer] for layer in range(layers)]
    x, payload, own, query_seg = open_call(patches, cls_tokens, segments, norm_gains, biases)
    key_seg = None
    kept = []
    lefts = []
    factors = []
    left_plans = (
        (("mid", 0), ("att", 0), ("mid", 1)),
        (("mid", 0), ("mid", 1), ("att", 1)),
    )
    def left_factors(layer, *behind):
        normed_all, att, nmid, active = factors[layer]
        tall, tall_other, wide, wide_other = left_call(
            left_plans[layer], orders[2], (picks[2], picks[1]), normed_all, att, after(nmid, *behind), active
        )
        return (tall, send(tall_other, "core", 1), wide, send(wide_other, "core", 1))

    come = swap_rows(payload)
    x, vecs, up_rows, prompt_rows, picks, small_pick, small_spot, own_w, own_vec = (
        lax.optimization_barrier(
            (x, vecs, up_rows, prompt_rows, picks, small_pick, small_spot, own_w, own_vec)
        )
    )
    out = forward_call(
        0, False, x, come, own, prompt_rows[0], vecs[0], up_rows[0], query_seg, None, weights
    )
    q, k, v, normed_all, att, lse, mid, nmid, slope, active, x_next, payload, own, key_seg = out
    kept.append((x, q, k, v, lse, mid, slope))
    factors.append((normed_all, att, nmid, active))
    lefts.append(left_factors(0))
    come = swap_rows(payload)
    x = after(x_next, lefts[0][0], lefts[0][2])
    kept.append((x,))
    cots = (cot_patches[0], cot_cls[0])
    out = turn_call(
        x, come, own, prompt_rows[1], vecs[1], up_rows[1], query_seg, key_seg, cots, first_seq, weights
    )
    factors.append(out[0:4])
    out_patch, out_cls = out[4:6]

    def both(values):
        return (values, send(values, "core", 1))

    def both_parts(parts):
        return (*parts, *[send(part, "core", 1) for part in parts])

    def give_back(layer, pays, qpart, mid_grad):
        return (swap_rows(pays), qpart, kept[layer][0], mid_grad, vecs[layer])

    arrived = [[], []]

    def start_ring(at, made, rows):
        pieces, ring_at = made[at], at % 2
        axis = RINGS[ring_at][0]
        if at == 0:
            come = deal_out(pieces, (axis,))
        else:
            come = [pieces[0]] + [send(pieces[step], axis, step) for step in (1, 3, 2)]
        arrived[ring_at].append((come, rows))

    tile = HALF // 4
    mid_at = 2 * WIDTH
    packed, (mid_grad, up_row_1, dq, qpart, dkv, pays, prompts_1, rows_1) = out[6:8], out[8:]
    grads = both_parts(packed)
    dqs, dkvs = both(dq), both(dkv)
    start = give_back(1, pays, qpart, mid_grad)
    lefts.append(left_factors(1, dkv, lefts[0][1], lefts[0][3], *grads[2:]))
    plan = [("down", 0, 0, 2, 0)]
    plan += [("up", part, mid_at, 2, HALF + part * tile) for part in range(3)]
    made = mlp_call(plan, ((2, HALF + 3 * tile),), lefts[1][0:2], grads)
    steps = made[2]
    plan = [("q", None, 1, 0), ("k", None, 1, tile), ("v", None, 1, 2 * tile)]
    plan += [("out", mid_at + 2 * HALF, 1, 3 * tile), (3, mid_at + HALF, 1, 4 * tile)]
    talls = (after(lefts[1][0], steps[0]), lefts[1][1])
    mixed = mixed_call(plan, ((1, 5 * tile),), seq, talls, lefts[1][2:], dqs, dkvs, grads)
    axis = RINGS[0][0]
    near = [send(steps[step], axis, step) for step in (1, 3)]
    far = send(after(steps[2], mixed[1][0], *near), axis, 2)
    arrived[0].append(([steps[0], *near, far], (HALF,) + (tile,) * 3))
    start_ring(1, mixed, (tile,) * 5)

    start = (after(start[0], mixed[1][0]), *start[1:])
    x_in, q, k, v, lse, mid, slope = kept[0]
    small = (small_pick, small_spot, prompts_1, rows_1, up_row_1, up_row_1)
    out = back_call(
        start, first_seq, (mid, slope, q, k, v, lse), prompt_rows[0], vecs[0], query_seg, key_seg,
        small, weights,
    )
    packed, (mid_grad, _, dq, qpart, dkv, pays) = out[0:2], out[2:8]
    grads = both_parts(packed)
    plan = [("down", 0, 0, 2, 0), ("out", 0, mid_at + HALF, 2, HALF)]
    plan += [("up", part, mid_at, 2, HALF + (1 + part) * tile) for part in range(2)]
    talls = (after(lefts[0][0], dkv, *arrived[1][0][0]), lefts[0][1])
    made = mlp_call(plan, ((2, HALF + 3 * tile),), talls, grads, 60)
    second_steps = made[2]
    start = give_back(0, after(pays, far), qpart, mid_grad)
    dqs, dkvs = both(dq), both(dkv)
    small = (out[8], send(out[9], "core", 1))
    plan = [("q", None, 1, 0), ("k", None, 1, tile), ("v", None, 1, 2 * tile)]
    plan += [(part, mid_at + 2 * HALF, 1, (1 + part) * tile + 32) for part in (2, 3)]
    talls = (after(lefts[0][0], second_steps[0]), lefts[0][1])
    mixed = mixed_call(
        plan, ((1, 5 * tile + 32),), seq, talls, lefts[0][2:], dqs, dkvs, grads, small
    )
    second_steps[2] = after(second_steps[2], mixed[1][0])
    start_ring(2, {2: second_steps}, (HALF,) + (tile,) * 3)
    start_ring(1, mixed, (tile,) * 3 + (16, 16) + (tile,) * 2)
    for group in arrived:
        come, rows = group[0]
        (total,) = fold_call([(1, [(come, rows)])])
        group[0] = ([total], rows)
    grad_patch, grad_cls = close_call((after(start[0], mixed[1][0]), *start[1:]))
    (come, rows), *others = arrived[0]
    (plane,) = fold_call([(16, [([after(come[0], arrived[1][0][0][0], grad_cls)], rows), *others])])
    (come, rows), *others = arrived[1]
    pieces = fold_call([(4, [([after(come[0], plane)], rows), *others])])
    plane = deal_out(plane, RINGS[0][1:])
    second = [pieces[0]] + [send(pieces[step], RINGS[1][1], step) for step in range(1, 4)]
    rows = tuple(row // 4 for _, items in arrived[1] for row in items)
    pieces = fold_call([(4, [(second, rows)])], LATE)
    third = [pieces[0]] + [send(pieces[step], RINGS[1][2], step) for step in range(1, 4)]
    lasts = [plane, *third]
    layouts = (
        [("down", 1, 0, 24)]
        + [("up", 1, part, 6) for part in range(3)]
        + [("down", 0, 0, 24), ("out", 0, 0, 6)]
        + [("up", 0, part, 6) for part in range(2)],
        [("qkv", 1, part, 6) for part in range(3)]
        + [("out", 1, 0, 6), ("up", 1, 3, 6)]
        + [("qkv", 0, part, 6) for part in range(3)]
        + [("small", 0, 0, 1), ("bias", 0, 0, 1), ("up", 0, 2, 6), ("up", 0, 3, 6)],
    )
    done = final_call(lasts, layouts, own_w, own_vec)
    swap = lambda values: jnp.transpose(values, (1, 0, 2))
    return (
        out_patch[None],
        swap(out_cls),
        grad_patch[None],
        swap(grad_cls),
        jnp.transpose(done[4], (1, 2, 0)),
        swap(done[0]),
        swap(done[1]),
        swap(done[2]),
        done[3],
        done[5],
        swap(done[6]),
        done[7],
    )


def solution(mesh):
    placed = (
        P("dp", "seq", None),
        P("dp", None, None),
        P("dp", "seq"),
        P(),
        P(),
        P(),
        P(),
        P(),
        P(),
        P(),
        P(),
        P("dp", "seq", None),
        P("dp", None, None),
    )
    return jax.shard_map(
        per_device,
        mesh=mesh,
        in_specs=placed,
        out_specs=(
            P("dp", "seq", None),
            P("dp", None, None),
            P("dp", "seq", None),
            P("dp", None, None),
            P(None, None, ("dp", "seq")),
            P(None, ("dp", "seq"), None),
            P(None, ("dp", "seq"), None),
            P(None, ("dp", "seq"), None),
            P(None, ("dp", "seq"), None),
            P(None, None, ("dp", "seq")),
            P(None, None, ("dp", "seq")),
            P(None, ("dp", "seq")),
        ),
        check_vma=False,
    )
```

```python
import functools

import jax
import jax.numpy as jnp
from jax import lax
from jax.experimental import pallas as pl
from jax.experimental.pallas import tpu as pltpu
from jax.sharding import PartitionSpec as P

HEADS = 12
HEAD = 64
WIDTH = 768
HIDDEN = 3072
PATCHES = 128
CLS = 10
PROMPTS = 50
OWN = 144
KEYS = 1152
CLS_AT = 1024
PROMPT_AT = 1040
FRONT = 128
BLOCKS = 8
PAY = 864
PACKED = 2 * WIDTH + HIDDEN
HALF = WIDTH // 2
TILE = 256
LOW = jnp.bfloat16
FULL = jnp.float32

eps_norm = 1e-06
penalty_rate = 2.0
big_negative = -1e30

AXES = ("dp", "seq")
SPAN = {"core": 2, "x": 4, "y": 4, "z": 4}
RINGS = (("y", "z", "x"), ("z", "y", "x"))
ANY = pl.BlockSpec(memory_space=pl.ANY)
VM = "whole"
HERE = pl.BlockSpec(memory_space=pltpu.VMEM)
SM = pl.BlockSpec(memory_space=pltpu.SMEM)


def place_of(device):
    dp, seq = device // 8, device % 8
    return {"core": dp % 2, "x": dp // 2 % 2 * 2 + seq // 4, "y": dp // 4, "z": seq % 4}


def device_of(place):
    dp = (place["y"] * 2 + place["x"] // 2) * 2 + place["core"]
    return dp * 8 + place["x"] % 2 * 4 + place["z"]


def moved(axis, step):
    pairs = []
    for device in range(128):
        place = place_of(device)
        place[axis] = (place[axis] + step) % SPAN[axis]
        pairs.append((device, device_of(place)))
    return pairs


def send(values, axis, step):
    return lax.ppermute(values, AXES, moved(axis, step))


def groups_of(axes):
    found = {}
    for device in range(128):
        place = place_of(device)
        rest = tuple(place[axis] for axis in SPAN if axis not in axes)
        found.setdefault(rest, []).append((tuple(place[axis] for axis in axes), device))
    return [[device for _, device in sorted(group)] for group in found.values()]


def deal_out(values, axes):
    return lax.all_to_all(
        values, AXES, 0, 0, tiled=True, axis_index_groups=groups_of(axes)
    )


def swap_rows(values):
    return lax.all_to_all(values, "seq", 0, 0, tiled=True)


def owner_order(axes, steps=()):
    here = place_of(lax.axis_index("dp") * 8 + lax.axis_index("seq"))
    rest = jnp.arange(128, dtype=jnp.int32)
    place = {}
    for axis in reversed(axes):
        place[axis] = rest % SPAN[axis]
        if axis in steps:
            place[axis] = (here[axis] + place[axis]) % SPAN[axis]
        rest = rest // SPAN[axis]
    place["core"] = (here["core"] + rest) % 2
    return device_of(place)


def nn(left, right):
    return lax.dot_general(left, right, (((1,), (0,)), ((), ())), preferred_element_type=FULL)


def nt(left, right):
    return lax.dot_general(left, right, (((1,), (1,)), ((), ())), preferred_element_type=FULL)


def plain_norm(values):
    centred = values - jnp.mean(values, -1, keepdims=True)
    scale = lax.rsqrt(jnp.mean(centred * centred, -1, keepdims=True) + eps_norm)
    return centred * scale, scale


def norm_pull(plain, scale, gain, upstream):
    inner = upstream * gain
    return scale * (
        inner
        - jnp.mean(inner, -1, keepdims=True)
        - plain * jnp.mean(inner * plain, -1, keepdims=True)
    )


def whole(dims):
    return pl.BlockSpec(dims, lambda i: (0,) * len(dims))


class Late:
    def __init__(self, index=None, cuts=1, axis=0):
        self.index, self.cuts, self.axis = index, cuts, axis


class Early:
    def __init__(self, dims, kind=FULL):
        self.shape, self.dtype = dims, kind


class Moves:
    def __init__(self):
        self.ins, self.outs, self.gone = {}, {}, []

    def start(self, *refs):
        for ref in refs:
            for copy in self.ins[id(ref)]:
                copy.start()

    def resident(self):
        part = Moves()
        part.start = part.wait = lambda *_: None
        part.flush = self.flush
        return part

    def wait(self, ref, piece=None):
        copies = self.ins[id(ref)]
        for copy in copies if piece is None else copies[piece : piece + 1]:
            copy.wait()

    def flush(self, *refs):
        for ref in refs:
            copy = self.outs.pop(id(ref), None)
            if copy is not None:
                copy.start()
                self.gone.append(copy)

    def close(self):
        for copy in self.outs.values():
            copy.start()
        for copy in [*self.gone, *self.outs.values()]:
            copy.wait()


def run(body, operands, specs, outs, name, micros, scratch=(), mib=63):
    late = [(at, spec) for at, spec in enumerate(specs) if isinstance(spec, Late)]
    early = [(at, out) for at, out in enumerate(outs) if isinstance(out, Early)]
    buffers, total = [], 0
    for at, spec in late:
        dims = operands[at].shape if spec.index is None else operands[at].shape[1:]
        buffers.append(pltpu.VMEM(dims, operands[at].dtype))
        total += spec.cuts
    buffers += [pltpu.VMEM(out.shape, out.dtype) for _, out in early]
    total += len(early)

    def kernel(*refs):
        refs = list(refs)
        first = len(operands) + len(outs) + len(scratch)
        space, sems = refs[first : first + len(buffers)], refs[-1]
        moves, sem = Moves(), 0
        for (at, spec), buffer in zip(late, space):
            source = refs[at] if spec.index is None else refs[at].at[spec.index]
            size = buffer.shape[spec.axis] // spec.cuts
            copies = []
            for piece in range(spec.cuts):
                part = pl.ds(piece * size, size)
                view = lambda ref: ref.at[part] if spec.axis == 0 else ref.at[:, part]
                pair = (source, buffer) if spec.cuts == 1 else (view(source), view(buffer))
                copies.append(pltpu.make_async_copy(*pair, sems.at[sem]))
                sem += 1
            moves.ins[id(buffer)] = copies
            refs[at] = buffer
        for (at, out), buffer in zip(early, space[len(late) :]):
            at += len(operands)
            moves.outs[id(buffer)] = pltpu.make_async_copy(buffer, refs[at], sems.at[sem])
            sem += 1
            refs[at] = buffer
        body(moves, refs[:first])
        moves.close()

    in_specs = []
    for operand, spec in zip(operands, specs):
        if isinstance(spec, Late):
            in_specs.append(ANY)
        else:
            in_specs.append(whole(operand.shape) if spec == "whole" else spec)
    return pl.pallas_call(
        kernel,
        grid=(1,),
        out_shape=tuple(shape(out.shape, out.dtype) for out in outs),
        in_specs=in_specs,
        out_specs=tuple(ANY if isinstance(out, Early) else whole(out.shape) for out in outs),
        scratch_shapes=[*scratch, *buffers, pltpu.SemaphoreType.DMA((max(total, 1),))],
        compiler_params=params(mib),
        cost_estimate=cost(micros),
        name=name,
    )(*operands)


def after(values, *others):
    return lax.optimization_barrier((values, others))[0]


def tile_at(index, size):
    return pl.ds(pl.multiple_of(index * size, size), size)


def params(mib=56):
    return pltpu.CompilerParams(vmem_limit_bytes=mib * 2**20)


SHARE = 1.0
ATT = 6
LEFT = 0.1
MIX = 0.1
TURN = 40
FOLD = 0.01
LATE = 12
MLP1 = 0.1


def cost(micros):
    return pl.CostEstimate(flops=int(micros * 1.1e9), bytes_accessed=1 << 20, transcendentals=0)


def shape(dims, kind=FULL):
    return jax.ShapeDtypeStruct(dims, kind)


def open_body(patch_ref, cls_ref, seg_ref, gain_ref, bias_ref, x_ref, pay_ref, own_ref, query_ref):
    x_ref[0:PATCHES] = patch_ref[0].astype(FULL)
    cls_rows = jnp.concatenate([cls_ref[0].astype(FULL), jnp.zeros((16 - CLS, WIDTH), FULL)], 0)
    x_ref[PATCHES:OWN] = cls_rows
    plain, _ = plain_norm(x_ref[...])
    normed = (plain * gain_ref[0, 0:1] + bias_ref[0, 0:1]).astype(LOW)
    own_ref[...] = normed
    segs = seg_ref[...].astype(FULL)
    last = jnp.broadcast_to(segs, (16, PATCHES)).astype(LOW)
    last = jnp.concatenate([last, jnp.zeros((16, WIDTH - PATCHES), LOW)], 1)
    for block in range(BLOCKS):
        pay_ref[block, 0:PATCHES] = normed[0:PATCHES]
        pay_ref[block, PATCHES:OWN] = last
    query_ref[0:PATCHES] = jnp.broadcast_to(segs, (PATCHES, PATCHES)).T
    row = lax.broadcasted_iota(jnp.int32, (16, 128), 0)
    query_ref[PATCHES:OWN] = jnp.where(row < CLS, row, -5).astype(FULL)


def open_call(patches, cls_tokens, segments, gains, biases):
    outs = (
        shape((OWN, WIDTH)),
        shape((BLOCKS, OWN, WIDTH), LOW),
        shape((OWN, WIDTH), LOW),
        shape((OWN, 128)),
    )
    operands = (patches, cls_tokens, segments, gains, biases)
    return run(lambda moves, refs: open_body(*refs), operands, [VM] * 5, outs, "open_norm", 2)


def seen_mask(key_ref, query_ref, mask_ref):
    keys = key_ref[0:1, :]
    seen = (keys == query_ref[:, 0:1]) | (keys == -1.0)
    mask_ref[...] = jnp.where(seen, 0.0, big_negative)


def half_lanes(rows):
    return lax.broadcasted_iota(jnp.int32, (rows, 2 * HEAD), 1) < HEAD


def split_rows(rows, patch_ref, cls_ref):
    patch_ref[...] = rows[0:PATCHES]
    for place in range(CLS):
        cls_ref[place] = rows[PATCHES + place : PATCHES + place + 1]


def forward_body(layer, last, moves, refs):
    first = layer == 0
    r = iter(refs)
    nxt = lambda: next(r)
    x_ref = nxt()
    come_ref = nxt()
    own_ref, prompt_ref, vec_ref, up_bias_ref, query_seg_ref = nxt(), nxt(), nxt(), nxt(), nxt()
    key_in_ref = None if first else nxt()
    wqkv, wout, wup, wdown = nxt(), nxt(), nxt(), nxt()
    q_ref, k_ref, v_ref, all_ref = nxt(), nxt(), nxt(), nxt()
    att_ref, lse_ref, mid_ref, nmid_ref = nxt(), nxt(), nxt(), nxt()
    slope_ref, active_ref, out_ref = nxt(), nxt(), nxt()
    next_ref, next_own_ref = nxt(), nxt()
    key_ref = nxt() if first else key_in_ref
    mask_ref = nxt()

    moves.start(wqkv)
    for block in range(BLOCKS):
        all_ref[block * PATCHES : (block + 1) * PATCHES] = come_ref[block, 0:PATCHES]

    gain_one, bias_one = vec_ref[0:1], vec_ref[2:3]
    gain_two, bias_two = vec_ref[1:2], vec_ref[6:7]

    plain, _ = plain_norm(prompt_ref[...])
    all_ref[CLS_AT:PROMPT_AT] = own_ref[PATCHES:OWN]
    all_ref[PROMPT_AT : PROMPT_AT + 64] = (plain * gain_one + bias_one).astype(LOW)
    all_ref[PROMPT_AT + 64 : KEYS] = jnp.zeros((KEYS - PROMPT_AT - 64, WIDTH), LOW)
    moves.flush(all_ref)
    if first:
        lane = lax.broadcasted_iota(jnp.int32, (8, FRONT), 1)
        front = jnp.where(
            lane < CLS, lane, jnp.where((lane >= 16) & (lane < 16 + PROMPTS), -1, -2)
        )
        for block in range(BLOCKS):
            segs = come_ref[block, PATCHES:OWN, 0:PATCHES].astype(FULL)
            key_ref[:, block * PATCHES : (block + 1) * PATCHES] = segs[0:8]
        key_ref[:, CLS_AT:KEYS] = front.astype(FULL)
    seen_mask(key_ref, query_seg_ref, mask_ref)

    def keys(tile, carry):
        at = tile_at(tile, TILE)
        rows = nn(all_ref[...], wqkv[:, pl.ds(pl.multiple_of(WIDTH + tile * TILE, TILE), TILE)])
        k_ref[:, at] = rows.astype(LOW)
        return carry

    def values(tile, carry):
        at = tile_at(tile, TILE)
        rows = nn(all_ref[...], wqkv[:, pl.ds(pl.multiple_of(2 * WIDTH + tile * TILE, TILE), TILE)])
        v_ref[:, at] = (rows + vec_ref[4:5, at]).astype(LOW)
        return carry

    def queries(tile, carry):
        at = tile_at(tile, TILE)
        rows = nn(own_ref[...], wqkv[:, at]) + vec_ref[3:4, at]
        q_ref[:, at] = (rows.astype(LOW).astype(FULL) * HEAD**-0.5).astype(LOW)
        return carry

    moves.wait(wqkv, 0)
    lax.fori_loop(0, 3, queries, 0, unroll=3)
    moves.wait(wqkv, 1)
    moves.start(wout, wup)
    lax.fori_loop(0, 3, keys, 0, unroll=3)
    moves.flush(k_ref)
    moves.wait(wqkv, 2)
    lax.fori_loop(0, 3, values, 0, unroll=3)
    moves.flush(v_ref)
    moves.start(wdown)

    lse_ref[...] = jnp.zeros((OWN, 128), FULL)
    lower = half_lanes(OWN)
    lane = lax.broadcasted_iota(jnp.int32, (OWN, 128), 1)

    def heads(pair, carry):
        at = tile_at(pair, 2 * HEAD)
        query, key, value = q_ref[:, at], k_ref[:, at], v_ref[:, at]
        outs = []
        for side in range(2):
            mine = lower if side == 0 else ~lower
            scores = nt(jnp.where(mine, query, jnp.zeros_like(query)), key) + mask_ref[...]
            top = jnp.max(scores, -1, keepdims=True)
            raised = jnp.exp(scores - top)
            total = jnp.sum(raised, -1, keepdims=True)
            outs.append(nn(raised.astype(LOW), value) / total)
            lane = lax.broadcasted_iota(jnp.int32, (OWN, 128), 1)
            lse_ref[...] = jnp.where(lane == 2 * pair + side, top + jnp.log(total), lse_ref[...])
        att_ref[:, at] = jnp.where(lower, outs[0], outs[1]).astype(LOW)
        return carry

    lax.fori_loop(0, HEADS // 2, heads, 0, unroll=2)

    moves.wait(wout)

    def project(tile, carry):
        at = tile_at(tile, TILE)
        mid_ref[:, at] = x_ref[:, at] + (nn(att_ref[...], wout[:, at]) + vec_ref[5:6, at])
        return carry

    lax.fori_loop(0, 3, project, 0, unroll=3)
    plain, _ = plain_norm(mid_ref[...])
    nmid_ref[...] = (plain * gain_two + bias_two).astype(LOW)
    moves.wait(wup)

    def rise(tile, carry):
        at = tile_at(tile, TILE)
        hidden = nn(nmid_ref[...], wup[:, at]) + up_bias_ref[0:1, at]
        share = 0.5 * (1.0 + lax.erf(hidden * 0.7071067811865476))
        active_ref[:, at] = (hidden * share).astype(LOW)
        slope_ref[:, at] = share + hidden * (0.3989422804014327 * jnp.exp(-0.5 * hidden * hidden))
        return carry

    lax.fori_loop(0, HIDDEN // TILE, rise, 0, unroll=4)
    moves.flush(slope_ref, active_ref)
    moves.wait(wdown)

    def lower_back(tile, carry):
        at = tile_at(tile, TILE)
        out_ref[:, at] = mid_ref[:, at] + (nn(active_ref[...], wdown[:, at]) + vec_ref[7:8, at])
        return carry

    lax.fori_loop(0, 3, lower_back, 0, unroll=3)
    if not last:
        plain, _ = plain_norm(out_ref[...])
        normed = (plain * vec_ref[8:9] + vec_ref[9:10]).astype(LOW)
        next_own_ref[...] = normed
        for block in range(BLOCKS):
            next_ref[block] = normed[0:PATCHES]
    else:
        split_rows(out_ref[...], next_ref, next_own_ref)


def forward_call(layer, last, x, come, own, prompt, vec, up_bias, query_seg, key_seg, weights):
    first = layer == 0
    outs = [
        shape((OWN, WIDTH), LOW),
        Early((KEYS, WIDTH), LOW),
        Early((KEYS, WIDTH), LOW),
        Early((KEYS, WIDTH), LOW),
        shape((OWN, WIDTH), LOW),
        shape((OWN, 128)),
        shape((OWN, WIDTH)),
        shape((OWN, WIDTH), LOW),
        Early((OWN, HIDDEN)),
        Early((OWN, HIDDEN), LOW),
        shape((OWN, WIDTH)),
    ]
    if last:
        outs += [shape((PATCHES, WIDTH)), shape((CLS, 1, WIDTH))]
    else:
        outs += [shape((BLOCKS, PATCHES, WIDTH), LOW), shape((OWN, WIDTH), LOW)]
    if first:
        outs += [shape((8, KEYS))]
    operands = [x, come, own, prompt, vec, up_bias, query_seg]
    specs = [VM, HERE] + [VM] * 5
    if not first:
        operands.append(key_seg)
        specs.append(VM)
    operands += weights
    specs += [Late(layer, 3, 1), Late(layer), Late(layer), Late(layer)]
    scratch = [pltpu.VMEM((OWN, KEYS), FULL)]
    body = lambda moves, refs: forward_body(layer, last, moves, refs)
    return run(body, operands, specs, outs, "forward_layer", 24 * SHARE, scratch)


def gathered_pull(come_ref, qpart_ref, x_ref, gain, mid_grad_ref):
    total = come_ref[0].astype(FULL)
    for block in range(1, BLOCKS):
        total = total + come_ref[block].astype(FULL)
    patch_part = total[0:WIDTH].T
    cls_part = jnp.concatenate(
        [total[WIDTH + 16 * lane : WIDTH + 16 * (lane + 1)] for lane in range(6)], 1
    )
    d_normed = jnp.concatenate([patch_part, cls_part], 0) + qpart_ref[...]
    plain, scale = plain_norm(x_ref[...])
    return mid_grad_ref[...] + norm_pull(plain, scale, gain, d_normed)


def row_share(first_ref):
    row = lax.broadcasted_iota(jnp.int32, (OWN, 1), 0)
    return jnp.where(row < PATCHES, 1.0, jnp.where(row < PATCHES + CLS, first_ref[0, 0], 0.0))


def back_mlp_body(last, moves, refs):
    r = iter(refs)
    nxt = lambda: next(r)
    if last:
        cot_ref, cot_cls_ref, key_ref, query_seg_ref = nxt(), nxt(), nxt(), nxt()
    else:
        come_ref = nxt()
        up_qpart_ref, up_x_ref, up_mid_grad_ref, up_vec_ref = nxt(), nxt(), nxt(), nxt()
    first_ref, mid_ref, slope_ref, vec_ref = nxt(), nxt(), nxt(), nxt()
    wout, wup, wdown = nxt(), nxt(), nxt()
    grad_refs = nxt(), nxt()
    datt_ref, mid_grad_ref = nxt(), nxt()
    rows_ref, up_spot_ref = nxt(), nxt()
    up_ref, low_ref, hid_ref, up_row_ref = nxt(), nxt(), nxt(), nxt()

    moves.start(wdown, slope_ref)
    gain_two = vec_ref[1:2]
    share = row_share(first_ref)
    if last:
        valid = ((query_seg_ref[...] < CLS) & (query_seg_ref[...] >= 0)).astype(FULL)
        up_ref[0:PATCHES] = cot_ref[...].astype(FULL) * valid[0:PATCHES, 0:1]
        hits = (key_ref[0:1, 0:CLS_AT] == query_seg_ref[PATCHES:OWN, 0:1]).astype(FULL)
        present = jnp.max(hits, -1, keepdims=True)
        cls_rows = [cot_cls_ref[...].astype(FULL), jnp.zeros((16 - CLS, WIDTH), FULL)]
        up_ref[PATCHES:OWN] = jnp.concatenate(cls_rows, 0) * present
    else:
        up_ref[...] = gathered_pull(
            come_ref, up_qpart_ref, up_x_ref, up_vec_ref[0:1], up_mid_grad_ref
        )
    low_ref[...] = up_ref[...].astype(LOW)
    weighted = low_ref[...].astype(FULL) * share
    grad_refs[0][:, 0:WIDTH] = weighted.astype(LOW)
    rows_ref[...] = jnp.zeros((8, WIDTH), FULL)
    rows_ref[0:1] = jnp.sum(weighted, 0, keepdims=True)
    moves.start(wup)

    def to_hidden(half, tile, carry):
        at = tile_at(tile, TILE)
        grad = (nt(low_ref[...], wdown[at, :]) * slope_ref[:, at]).astype(LOW)
        hid_ref[:, at] = grad
        counted = grad.astype(FULL) * share
        to = WIDTH + tile * TILE - half * (PACKED // 2)
        grad_refs[half][:, pl.ds(pl.multiple_of(to, TILE), TILE)] = counted.astype(LOW)
        up_row_ref[:, at] = jnp.broadcast_to(jnp.sum(counted, 0, keepdims=True), (8, TILE))
        return carry

    moves.wait(slope_ref)
    for piece in range(4):
        moves.wait(wdown, piece)
        body = functools.partial(to_hidden, piece // 2)
        lax.fori_loop(3 * piece, 3 * piece + 3, body, 0, unroll=3)
    moves.wait(wup)
    moves.start(wout)

    def to_mid(tile, carry):
        at = tile_at(tile, TILE)
        mid_grad_ref[:, at] = nt(hid_ref[...], wup[at, :])
        return carry

    lax.fori_loop(0, 3, to_mid, 0, unroll=3)
    d_normed = mid_grad_ref[...]
    plain, scale = plain_norm(mid_ref[...])
    counted = d_normed * share
    rows_ref[1:2] = jnp.sum(counted * plain, 0, keepdims=True)
    rows_ref[2:3] = jnp.sum(counted, 0, keepdims=True)
    mid_grad_ref[...] = up_ref[...] + norm_pull(plain, scale, gain_two, d_normed)
    low_ref[...] = mid_grad_ref[...].astype(LOW)
    weighted = low_ref[...].astype(FULL) * share
    grad_refs[1][:, PACKED // 2 - WIDTH :] = weighted.astype(LOW)
    rows_ref[3:4] = jnp.sum(weighted, 0, keepdims=True)
    moves.flush(*grad_refs)
    up_row = up_row_ref[0:1]
    spots = [up_row[:, 24 * spot : 24 * (spot + 1)] for spot in range(128)]
    up_spot_ref[...] = jnp.concatenate(spots, 0)
    moves.wait(wout)

    def to_att(tile, carry):
        at = tile_at(tile, TILE)
        datt_ref[:, at] = nt(low_ref[...], wout[at, :]).astype(LOW)
        return carry

    lax.fori_loop(0, 3, to_att, 0, unroll=3)


def back_att_body(layer, moves, refs):
    r = iter(refs)
    nxt = lambda: next(r)
    first_ref, rows_in_ref, datt_ref = nxt(), nxt(), nxt()
    q_ref, k_ref, v_ref, lse_ref = nxt(), nxt(), nxt(), nxt()
    prompt_ref, vec_ref, query_seg_ref, key_ref = nxt(), nxt(), nxt(), nxt()
    if layer == 0:
        pick_ref, spot_ref, prompts_1, rows_1, up_0, up_1 = [nxt() for _ in range(6)]
    wqkv = nxt()
    dq_ref, qpart_ref, dkv_ref, pay_ref = nxt(), nxt(), nxt(), nxt()
    if layer == 0:
        small_refs = nxt(), nxt()
        dprompt_ref, rows_ref = nxt(), nxt()
    else:
        dprompt_ref, rows_ref = nxt(), nxt()
    mask_ref, dqf_ref, qt_ref, dat_ref, front_ref = [nxt() for _ in range(5)]

    moves.start(k_ref, v_ref, wqkv)
    gain_one = vec_ref[0:1]
    share = row_share(first_ref)
    seen_mask(key_ref, query_seg_ref, mask_ref)
    rows_ref[...] = rows_in_ref[...]

    def turn(tile, carry):
        at = tile_at(tile, TILE)
        dat_ref[at, :] = (datt_ref[:, at].astype(FULL) * share).T.astype(LOW)
        qt_ref[at, :] = (q_ref[:, at].astype(FULL) * share).T.astype(LOW)
        return carry

    lax.fori_loop(0, 3, turn, 0, unroll=3)
    lower = half_lanes(OWN)
    lane = lax.broadcasted_iota(jnp.int32, (OWN, 128), 1)
    moves.wait(k_ref)
    moves.wait(v_ref)

    def heads(pair, carry):
        at = tile_at(pair, 2 * HEAD)
        query, key, value, grad = q_ref[:, at], k_ref[:, at], v_ref[:, at], datt_ref[:, at]
        outs = []
        for side in range(2):
            mine = lower if side == 0 else ~lower
            head = 2 * pair + side
            log_total = jnp.sum(jnp.where(lane == head, lse_ref[...], 0.0), -1, keepdims=True)
            scores = nt(jnp.where(mine, query, jnp.zeros_like(query)), key) + mask_ref[...]
            probs = jnp.exp(scores - log_total)
            d_probs = nt(jnp.where(mine, grad, jnp.zeros_like(grad)), value)
            both = probs * d_probs
            across = jnp.sum(both, -1, keepdims=True)
            d_scores = (both - probs * across).astype(LOW)
            probs_low = probs.astype(LOW)
            outs.append(nn(d_scores, key))
            rows = tile_at(head, HEAD)
            dkv_ref[rows, :] = nn(qt_ref[rows, :], d_scores).astype(LOW)
            value_rows = pl.ds(pl.multiple_of(WIDTH + head * HEAD, HEAD), HEAD)
            dkv_ref[value_rows, :] = nn(dat_ref[rows, :], probs_low).astype(LOW)
        dqf_ref[:, at] = (jnp.where(lower, outs[0], outs[1]) * HEAD**-0.5).astype(LOW)
        return carry

    lax.fori_loop(0, HEADS // 2, heads, 0, unroll=2)
    moves.flush(dkv_ref)
    counted = dqf_ref[...].astype(FULL) * share
    dq_ref[...] = counted.astype(LOW)
    rows_ref[4:5] = jnp.sum(counted, 0, keepdims=True)
    moves.wait(wqkv)

    def to_normed(tile, carry):
        at = tile_at(tile, TILE)
        qpart_ref[:, at] = nt(dqf_ref[...], wqkv[at, 0:WIDTH])
        return carry

    lax.fori_loop(0, 3, to_normed, 0, unroll=3)

    front_ref[...] = nn(wqkv[:, WIDTH:], dkv_ref[:, CLS_AT:KEYS])
    shift = jnp.sum(front_ref[...], -1, keepdims=True)
    front = front_ref[...].T
    cls_rows = jnp.concatenate(
        [front[0:16, 128 * place : 128 * (place + 1)] for place in range(6)], 0
    )
    for block in range(0, BLOCKS, 2):
        part = nn(wqkv[:, WIDTH:], dkv_ref[:, block * PATCHES : (block + 2) * PATCHES])
        shift = shift + jnp.sum(part, -1, keepdims=True)
        for side in range(2):
            pay_ref[block + side, 0:WIDTH] = part[:, side * PATCHES : (side + 1) * PATCHES].astype(LOW)
            pay_ref[block + side, WIDTH:PAY] = cls_rows.astype(LOW)
    moves.flush(pay_ref)

    plain, scale = plain_norm(prompt_ref[...])
    d_prompt = norm_pull(plain, scale, gain_one, front[16:80])
    query_seg = query_seg_ref[0:PATCHES, 0:1]
    slots = jnp.sum((query_seg < CLS).astype(FULL), 0, keepdims=True)
    dprompt_ref[...] = d_prompt + (penalty_rate / 1024.0) * slots * prompt_ref[...]

    turned = jnp.broadcast_to(shift, (WIDTH, 128)).T
    rows_ref[6:7] = turned[0:1] + jnp.sum(qpart_ref[...] * share, 0, keepdims=True)
    totals = jnp.sum(dkv_ref[WIDTH : 2 * WIDTH].astype(FULL), -1, keepdims=True)
    rows_ref[5:6] = jnp.broadcast_to(totals, (WIDTH, 128)).T[0:1]
    if layer != 0:
        return
    joined = jnp.concatenate([dprompt_ref[0:56], prompts_1[0:56], rows_ref[...], rows_1[...]], 0)
    turned = nt(pick_ref[...], joined.astype(LOW))
    ups = [nn(spot_ref[...], up[...].astype(LOW)) for up in (up_0, up_1)]
    rows = jnp.concatenate([turned[128 * part : 128 * (part + 1)] for part in range(6)], 1)
    ups = jnp.concatenate([*ups, jnp.zeros((128, WIDTH - 48), FULL)], 1)
    for half in range(2):
        spots = slice(64 * half, 64 * (half + 1))
        small_refs[half][...] = jnp.concatenate([rows[spots], ups[spots]], 0).astype(LOW)


class Joined:
    def __init__(self, moves, last, *more):
        self.moves, self.last, self.more = moves, last, more
        self.wait, self.flush = moves.wait, moves.flush

    def start(self, *refs):
        self.moves.start(*refs)
        if any(ref is self.last for ref in refs):
            self.moves.start(*self.more)


class Started(Joined):
    def start(self, *refs):
        pass


def back_body(moves, refs):
    r = iter(refs)
    take = lambda count: [next(r) for _ in range(count)]
    start, first = take(5), next(r)
    mid, slope, q, k, v, lse, prompt, vec, query_seg, key = take(10)
    small, (wqkv, wout, wup, wdown) = take(6), take(4)
    grads, mid_grad, up_spot = take(2), next(r), next(r)
    dq, qpart, dkv, pay = take(4)
    small_out = take(2)
    datt, rows_in, up, low, hid, up_row, mask, dqf, qt, dat, front, dprompt, rows = take(13)
    back_mlp_body(
        False, Joined(moves, wup, k, v, wqkv),
        [*start, first, mid, slope, vec, wout, wup, wdown]
        + [*grads, datt, mid_grad, rows_in, up_spot, up, low, hid, up_row],
    )
    back_att_body(
        0, Started(moves, None),
        [first, rows_in, datt, q, k, v, lse, prompt, vec, query_seg, key, *small[:4], up_spot, small[5]]
        + [wqkv, dq, qpart, dkv, pay, *small_out, dprompt, rows, mask, dqf, qt, dat, front],
    )


def back_call(start, first_seq, saved, prompt, vec, query_seg, key_seg, small, weights):
    mid, slope, q, k, v, lse = saved
    operands = [*start, first_seq, mid, slope, q, k, v, lse, prompt, vec, query_seg, key_seg]
    operands += [*small, *weights]
    specs = [HERE] + [VM] * 4 + [SM, VM, Late(), VM, Late(), Late()] + [VM] * 11
    specs += [Late(0), Late(0), Late(0), Late(0, 4)]
    outs = [
        Early((OWN, PACKED // 2), LOW),
        Early((OWN, PACKED // 2), LOW),
        shape((OWN, WIDTH)),
        shape((128, 24)),
        shape((OWN, WIDTH), LOW),
        shape((OWN, WIDTH)),
        Early((2 * WIDTH, KEYS), LOW),
        Early((BLOCKS, PAY, 128), LOW),
        shape((128, WIDTH), LOW),
        shape((128, WIDTH), LOW),
    ]
    space = lambda *dims: pltpu.VMEM(dims, FULL)
    low = lambda *dims: pltpu.VMEM(dims, LOW)
    scratch = [low(OWN, WIDTH), space(8, WIDTH), space(OWN, WIDTH), low(OWN, WIDTH)]
    scratch += [low(OWN, HIDDEN), space(8, HIDDEN), space(OWN, KEYS), low(OWN, WIDTH)]
    scratch += [low(WIDTH, OWN), low(WIDTH, OWN), space(WIDTH, FRONT), space(64, WIDTH)]
    scratch += [space(8, WIDTH)]
    return run(back_body, operands, specs, outs, "backward_layer", ATT, scratch)


def turn_body(moves, refs):
    r = iter(refs)
    take = lambda count: [next(r) for _ in range(count)]
    x, come, own, prompt, vec, up_bias, query_seg, key = take(8)
    cots, first = take(2), next(r)
    wqkv, wout, wup, wdown = take(4)
    normed_all, att, nmid, active, out_patch, out_cls = take(6)
    grads, mid_grad, up_spot = take(2), next(r), next(r)
    dq, qpart, dkv, pay, dprompt, rows = take(6)
    q, k, v, lse, mid, slope, out, mask = take(8)
    datt, rows_in, up, low, hid, up_row = take(6)
    dqf, qt, dat, front = take(4)
    forward_body(
        1, True, moves,
        [x, come, own, prompt, vec, up_bias, query_seg, key, wqkv, wout, wup, wdown]
        + [q, k, v, normed_all, att, lse, mid, nmid, slope, active, out, out_patch, out_cls]
        + [mask],
    )
    still = moves.resident()
    back_mlp_body(
        True, still,
        [*cots, key, query_seg, first, mid, slope, vec, wout, wup, wdown]
        + [*grads, datt, mid_grad, rows_in, up_spot, up, low, hid, up_row],
    )
    back_att_body(
        1, still,
        [first, rows_in, datt, q, k, v, lse, prompt, vec, query_seg, key, wqkv]
        + [dq, qpart, dkv, pay, dprompt, rows, mask, dqf, qt, dat, front],
    )


def turn_call(x, come, own, prompt, vec, up_bias, query_seg, key_seg, cots, first_seq, weights):
    operands = [x, come, own, prompt, vec, up_bias, query_seg, key_seg, *cots, first_seq, *weights]
    specs = [VM, HERE] + [VM] * 8 + [SM, Late(1, 3, 1), Late(1), Late(1), Late(1)]
    outs = [
        Early((KEYS, WIDTH), LOW),
        shape((OWN, WIDTH), LOW),
        shape((OWN, WIDTH), LOW),
        Early((OWN, HIDDEN), LOW),
        shape((PATCHES, WIDTH)),
        shape((CLS, 1, WIDTH)),
        Early((OWN, PACKED // 2), LOW),
        Early((OWN, PACKED // 2), LOW),
        shape((OWN, WIDTH)),
        shape((128, 24)),
        shape((OWN, WIDTH), LOW),
        shape((OWN, WIDTH)),
        Early((2 * WIDTH, KEYS), LOW),
        Early((BLOCKS, PAY, 128), LOW),
        shape((64, WIDTH)),
        shape((8, WIDTH)),
    ]
    space = lambda *dims: pltpu.VMEM(dims, FULL)
    low = lambda *dims: pltpu.VMEM(dims, LOW)
    scratch = [low(OWN, WIDTH), low(KEYS, WIDTH), low(KEYS, WIDTH), space(OWN, 128)]
    scratch += [space(OWN, WIDTH), space(OWN, HIDDEN), space(OWN, WIDTH), space(OWN, KEYS)]
    scratch += [low(OWN, WIDTH), space(8, WIDTH), space(OWN, WIDTH), low(OWN, WIDTH)]
    scratch += [low(OWN, HIDDEN), space(8, HIDDEN), low(OWN, WIDTH), low(WIDTH, OWN)]
    scratch += [low(WIDTH, OWN), space(WIDTH, FRONT)]
    return run(turn_body, operands, specs, outs, "turn_layer", TURN, scratch)


def close_body(come_ref, qpart_ref, x_ref, mid_grad_ref, vec_ref, patch_ref, cls_ref):
    rows = gathered_pull(come_ref, qpart_ref, x_ref, vec_ref[0:1], mid_grad_ref)
    split_rows(rows, patch_ref, cls_ref)


def close_call(operands):
    outs = (shape((PATCHES, WIDTH)), shape((CLS, 1, WIDTH)))
    specs = [HERE] + [VM] * (len(operands) - 1)
    return run(lambda moves, refs: close_body(*refs), operands, specs, outs, "close_norm", 2)


def left_body(plan, moves, refs):
    order_ref, *refs = refs
    picks, (all_ref, att_ref, mid_ref, active_ref) = refs[0:2], refs[2:6]
    tall_refs, wide_refs = refs[6:8], refs[8:10]
    turned_ref, down_ref = refs[10:12]

    def turn(tile, carry):
        at = tile_at(tile, TILE)
        turned_ref[at, :] = active_ref[:, at].astype(FULL).T
        return carry

    def move(spot, carry):
        source = pl.ds(pl.multiple_of(order_ref[spot] * 24, 8), 24)
        target = pl.ds(pl.multiple_of(spot * 24, 8), 24)
        down_ref[target, :] = turned_ref[source, :]
        return carry

    moves.start(all_ref)
    lax.fori_loop(0, HIDDEN // TILE, turn, 0, unroll=3)
    lax.fori_loop(0, 128, move, 0, unroll=8)
    for half in range(2):
        rows = slice(half * 2 * WIDTH, (half + 1) * 2 * WIDTH)
        tall_refs[half][0 : 2 * WIDTH, 0:OWN] = down_ref[rows].astype(LOW)
    row = 2 * WIDTH
    for kind, ring_at in plan:
        source = {"mid": mid_ref, "att": att_ref}[kind][...]
        turned = nt(picks[ring_at][...], source).astype(LOW)
        for half in range(2):
            tall_refs[half][row : row + HALF, 0:OWN] = turned[half * HALF : (half + 1) * HALF]
        row += HALF
    moves.flush(*tall_refs)
    moves.wait(all_ref)
    for half in range(2):
        wide = nt(picks[1][half * HALF : (half + 1) * HALF], all_ref[...])
        wide_refs[half][...] = wide.astype(LOW)


def left_call(plan, order, picks, normed_all, att, nmid, active):
    tall = (2 * WIDTH + len(plan) * HALF, 256)
    outs = [Early(tall, LOW)] * 2 + [shape((HALF, KEYS), LOW)] * 2
    operands = (order, *picks, normed_all, att, nmid, active)
    scratch = [pltpu.VMEM((HIDDEN, OWN), FULL), pltpu.VMEM((HIDDEN, OWN), FULL)]
    body = lambda moves, refs: left_body(plan, moves, refs)
    return run(body, operands, [SM, VM, VM, Late(), VM, VM, VM], outs, "left_factors", LEFT, scratch)


def rights_of(grad_refs, kind, part, tile):
    at = {"down": 0, "up": WIDTH + part * WIDTH, "out": WIDTH + HIDDEN}[kind] + tile * TILE
    half, at = at // (PACKED // 2), at % (PACKED // 2)
    return [grad_refs[2 * side + half][:, at : at + TILE] for side in range(2)]


def piece_shapes(classes):
    outs = []
    for number, rows in classes:
        outs += [shape((4, rows, WIDTH), LOW)] if number == 0 else [shape((rows, WIDTH), LOW)] * 4
    return outs


def by_class(classes, arrays):
    found, at = {}, 0
    for number, _ in classes:
        if number == 0:
            found[0] = [arrays[at].at[way] for way in range(4)]
            at += 1
        else:
            found[number] = list(arrays[at : at + 4])
            at += 4
    return found


def deal(out, row, values, columns):
    size = values.shape[0] // 4
    for way in range(4):
        out[way][row : row + size, columns] = values[way * size : (way + 1) * size].astype(LOW)


def mlp_body(plan, classes, refs):
    tall_refs, grad_refs = refs[0:2], refs[2:6]
    outs = by_class(classes, refs[6:])
    for kind, part, left_row, out, out_row in plan:
        for tile in range(3):
            columns = slice(tile * TILE, (tile + 1) * TILE)
            rights = rights_of(grad_refs, kind, part, tile)
            for piece in range(4 if kind == "down" else 1):
                rows = slice(left_row + piece * HALF, left_row + (piece + 1) * HALF)
                lefts = [tall[rows, 0:OWN] for tall in tall_refs]
                values = nn(lefts[0], rights[0]) + nn(lefts[1], rights[1])
                if kind == "down":
                    outs[out][piece][out_row : out_row + HALF, columns] = values.astype(LOW)
                else:
                    deal(outs[out], out_row, values, columns)


def mlp_call(plan, classes, talls, grads, micros=MLP1):
    operands = (*talls, *grads)
    body = lambda moves, refs: mlp_body(plan, classes, refs)
    out = run(body, operands, [VM] * 6, piece_shapes(classes), "grad_mlp", micros)
    return by_class_values(classes, out)


def by_class_values(classes, arrays):
    found, at = {}, 0
    for number, _ in classes:
        found[number] = arrays[at] if number == 0 else list(arrays[at : at + 4])
        at += 1 if number == 0 else 4
    return found


def mixed_body(plan, classes, small, moves, refs):
    seq_ref, *refs = refs
    tall_refs, wide_refs, dq_refs, dkv_refs = [refs[2 * at : 2 * at + 2] for at in range(4)]
    grad_refs, small_refs = refs[8:12], refs[12:14]
    outs = by_class(classes, refs[14:] if small else refs[12:])
    moves.start(*wide_refs, *dkv_refs)
    for ref in (*wide_refs, *dkv_refs):
        moves.wait(ref)
    moves.start(*tall_refs, *grad_refs)
    brought = False
    if small:
        joined = small_refs[0][...].astype(FULL) + small_refs[1][...].astype(FULL)
        for way in range(4):
            spots = [joined[64 * part + 16 * way : 64 * part + 16 * (way + 1)] for part in range(2)]
            outs[1][way][3 * HALF // 4 : 3 * HALF // 4 + 32] = jnp.concatenate(spots, 0).astype(LOW)
    for kind, left_row, out, out_row in plan:
        for tile in range(3):
            columns = slice(tile * TILE, (tile + 1) * TILE)
            values = jnp.zeros((HALF, TILE), FULL)
            for side in range(2):
                if kind in ("k", "v"):
                    at = (0 if kind == "k" else WIDTH) + tile * TILE
                    values = values + nt(wide_refs[side][...], dkv_refs[side][at : at + TILE])
                    continue
                if kind == "q" and left_row is None:
                    wide = wide_refs[side]
                    mine = pl.ds(pl.multiple_of(seq_ref[0, 0] * PATCHES, PATCHES), PATCHES)
                    left = jnp.concatenate([wide[:, mine], wide[:, CLS_AT:PROMPT_AT]], 1)
                else:
                    if not brought:
                        brought = True
                        for ref in (*tall_refs, *grad_refs):
                            moves.wait(ref)
                    left = tall_refs[side][left_row : left_row + HALF, 0:OWN]
                if kind == "q":
                    right = dq_refs[side][:, columns]
                else:
                    name, part = ("out", 0) if kind == "out" else ("up", kind)
                    right = rights_of(grad_refs, name, part, tile)[side]
                values = values + nn(left, right)
            deal(outs[out], out_row, values, columns)


def mixed_call(plan, classes, seq, talls, wides, dqs, dkvs, grads, small=()):
    operands = (seq, *talls, *wides, *dqs, *dkvs, *grads, *small)
    body = lambda moves, refs: mixed_body(plan, classes, bool(small), moves, refs)
    specs = [SM] + [Late()] * 4 + [VM] * 2 + [Late()] * 6 + [VM] * len(small)
    out = run(body, operands, specs, piece_shapes(classes), "grad_mixed", MIX)
    return by_class_values(classes, out)


def fold_body(classes, refs):
    r = iter(refs)
    totals = []
    for _, groups in classes:
        totals.append([])
        for arrays, _ in groups:
            come = next(r)
            ways = [come.at[way] for way in range(4)] if len(come.shape) == 3 else [come]
            ways += [next(r) for _ in range(arrays - 1)]
            total = ways[0][...].astype(FULL)
            for way in ways[1:]:
                total = total + way[...].astype(FULL)
            totals[-1].append(total)
    for (ways, groups), sums in zip(classes, totals):
        joint = next(r) if ways == 16 else None
        for way in range(ways):
            out = joint.at[way] if ways == 16 else next(r)
            parts = []
            for total, (_, items) in zip(sums, groups):
                at = 0
                for rows in items:
                    size = rows // ways
                    parts.append(total[at + way * size : at + (way + 1) * size])
                    at += rows
            short = out.shape[0] - sum(part.shape[0] for part in parts)
            if short:
                parts.append(jnp.zeros((short, out.shape[1]), FULL))
            out[...] = jnp.concatenate(parts, 0).astype(LOW)


def fold_call(classes, micros=FOLD):
    operands = []
    for _, groups in classes:
        for come, _ in groups:
            operands += come if isinstance(come, list) else [come]
    number = lambda come: len(come) if isinstance(come, list) else 1
    counts = [(ways, [(number(come), items) for come, items in groups]) for ways, groups in classes]
    wide = 256
    outs = []
    for ways, groups in counts:
        size = -(-sum(sum(items) for _, items in groups) // (16 * ways)) * 16
        if ways == 16:
            outs.append(shape((16, size, WIDTH), LOW))
        else:
            outs += [shape((size, WIDTH), LOW)] * ways
    block = lambda *dims: pl.BlockSpec((*dims, wide), lambda i: (*[0] * len(dims), i))
    return list(
        pl.pallas_call(
            lambda *refs: fold_body(counts, refs),
            grid=(WIDTH // wide,),
            out_shape=tuple(outs),
            in_specs=[block(*come.shape[:-1]) for come in operands],
            out_specs=tuple(block(*out.shape[:-1]) for out in outs),
            compiler_params=params(63),
            cost_estimate=cost(micros),
            name="ring_fold",
        )(*operands)
    )


def final_body(layouts, refs):
    r = iter(refs)
    plane, ring = next(r), [next(r) for _ in range(4)]
    arrays = ([plane.at[way] for way in range(16)], ring)
    own_w_ref, own_vec_ref = next(r), next(r)
    qkv_ref, out_ref, up_ref, down_ref = next(r), next(r), next(r), next(r)
    prompt_ref, gain_ref, bias_ref, up_bias_ref = next(r), next(r), next(r), next(r)
    pieces = []
    for array, layout in zip(arrays, layouts):
        total = array[0][...].astype(FULL)
        for way in array[1:]:
            total = total + way[...].astype(FULL)
        at = 0
        for entry in layout:
            pieces.append((entry[:3], total[at : at + entry[3]]))
            at += entry[3]
    small = None
    wholes = [jnp.zeros((6, 1), FULL)] * 2
    for (kind, layer, part), piece in pieces:
        columns = slice(part * WIDTH, (part + 1) * WIDTH)
        if kind == "qkv":
            qkv_ref[:, layer, columns] = piece
            weight = own_w_ref[layer, :, columns].astype(FULL)
            wholes[layer] = wholes[layer] + jnp.sum(piece * weight, -1, keepdims=True)
        elif kind == "out":
            out_ref[:, layer, :] = piece
        elif kind == "up":
            up_ref[:, layer, columns] = piece
        elif kind == "down":
            down_ref[layer] = piece
        elif kind == "small":
            small = jnp.concatenate([piece[:, 128 * i : 128 * (i + 1)] for i in range(6)], 0)
        else:
            up_bias_ref[0:1] = piece[:, 0:24]
            up_bias_ref[1:2] = piece[:, 24:48]
    turn = lambda values: jnp.concatenate([values, jnp.zeros((2, 128), FULL)], 0).T
    rows = turn(small)
    for layer in range(2):
        prompt_ref[:, layer, :] = small[:, 56 * layer : 56 * layer + PROMPTS]
        at = 112 + 8 * layer
        part = rows[at : at + 8, 0:6]
        whole = turn(jnp.broadcast_to(wholes[layer], (6, 128)))[0:1, 0:6]
        gain, shift = own_vec_ref[layer, 0:1], own_vec_ref[layer, 1:2]
        gain_ref[layer, 0:1] = (whole - shift * part[6:7]) / gain
        gain_ref[layer, 1:2] = part[1:2]
        for place, source in enumerate((6, 4, 5, 3, 2, 0)):
            bias_ref[place, layer : layer + 1] = part[source : source + 1]


def final_call(arrays, layouts, own_w, own_vec):
    operands = [*arrays, own_w, own_vec]
    outs = (
        shape((6, 2, 3 * WIDTH)),
        shape((6, 2, WIDTH)),
        shape((6, 2, HIDDEN)),
        shape((2, 24, WIDTH)),
        shape((6, 2, PROMPTS)),
        shape((2, 2, 6)),
        shape((6, 2, 6)),
        shape((2, 24)),
    )
    body = lambda moves, refs: final_body(layouts, refs)
    return run(body, operands, [VM] * len(operands), outs, "final_fold", 3)


def per_device(
    patches,
    cls_tokens,
    segments,
    prompts,
    w_qkv,
    w_out,
    w_up,
    w_down,
    norm_gains,
    biases,
    up_bias,
    cot_patches,
    cot_cls,
):
    layers = 2
    weights = (w_qkv, w_out, w_up, w_down)
    first_seq = (lax.axis_index("seq") == 0).astype(FULL).reshape(1, 1)
    prompt_rows = jnp.pad(prompts.astype(FULL), ((0, 0), (0, 64 - PROMPTS), (0, 0)))
    vecs = []
    for layer in range(layers):
        following = min(layer + 1, layers - 1)
        vecs.append(
            jnp.concatenate(
                [
                    norm_gains[layer],
                    biases[layer],
                    norm_gains[following, 0:1],
                    biases[following, 0:1],
                    jnp.zeros((6, WIDTH), FULL),
                ],
                0,
            )
        )
    up_rows = [jnp.broadcast_to(up_bias[layer], (8, HIDDEN)) for layer in range(layers)]
    orders = [
        owner_order(RINGS[0]),
        owner_order(RINGS[1], RINGS[1]),
        owner_order(RINGS[0], RINGS[0][:1]),
    ]
    steps = jnp.arange(6, dtype=jnp.int32)
    one_hot = lambda wanted, size: (wanted[:, None] == jnp.arange(size)[None, :]).astype(LOW)
    picks = [one_hot((order[:, None] * 6 + steps).reshape(-1), WIDTH) for order in orders]
    small_pick = one_hot((orders[1][None, :] * 6 + steps[:, None]).reshape(-1), WIDTH)
    small_spot = one_hot(orders[1], 128)

    seq = lax.axis_index("seq").astype(jnp.int32).reshape(1, 1)
    here = lax.axis_index("dp") * 8 + lax.axis_index("seq")
    mine_of = lambda values, axis: lax.dynamic_slice_in_dim(values, here * 6, 6, axis)
    own_w = mine_of(w_qkv, 1)
    own_vec = jnp.stack([mine_of(norm_gains, 2)[:, 0], mine_of(biases, 2)[:, 0]], 1)
    prompt_rows = [prompt_rows[layer] for layer in range(layers)]
    x, payload, own, query_seg = open_call(patches, cls_tokens, segments, norm_gains, biases)
    key_seg = None
    kept = []
    lefts = []
    factors = []
    left_plans = (
        (("mid", 0), ("att", 0), ("mid", 1)),
        (("mid", 0), ("mid", 1), ("att", 1)),
    )
    def left_factors(layer, *behind):
        normed_all, att, nmid, active = factors[layer]
        tall, tall_other, wide, wide_other = left_call(
            left_plans[layer], orders[2 - 2 * layer], (picks[2 - 2 * layer], picks[1]), normed_all, att, after(nmid, *behind), active
        )
        return (tall, send(tall_other, "core", 1), wide, send(wide_other, "core", 1))

    come = swap_rows(payload)
    x, vecs, up_rows, prompt_rows, picks, small_pick, small_spot, own_w, own_vec = (
        lax.optimization_barrier(
            (x, vecs, up_rows, prompt_rows, picks, small_pick, small_spot, own_w, own_vec)
        )
    )
    out = forward_call(
        0, False, x, come, own, prompt_rows[0], vecs[0], up_rows[0], query_seg, None, weights
    )
    q, k, v, normed_all, att, lse, mid, nmid, slope, active, x_next, payload, own, key_seg = out
    kept.append((x, q, k, v, lse, mid, slope))
    factors.append((normed_all, att, nmid, active))
    lefts.append(left_factors(0))
    come = swap_rows(payload)
    x = after(x_next, lefts[0][0], lefts[0][2])
    kept.append((x,))
    cots = (cot_patches[0], cot_cls[0])
    out = turn_call(
        x, come, own, prompt_rows[1], vecs[1], up_rows[1], query_seg, key_seg, cots, first_seq, weights
    )
    factors.append(out[0:4])
    out_patch, out_cls = out[4:6]

    def both(values):
        return (values, send(values, "core", 1))

    def both_parts(parts):
        return (*parts, *[send(part, "core", 1) for part in parts])

    def give_back(layer, pays, qpart, mid_grad):
        return (swap_rows(pays), qpart, kept[layer][0], mid_grad, vecs[layer])

    arrived = [[], []]

    def start_ring(at, made, rows):
        pieces, ring_at = made[at], at % 2
        axis = RINGS[ring_at][0]
        if at == 0:
            come = deal_out(pieces, (axis,))
        else:
            come = [pieces[0]] + [send(pieces[step], axis, step) for step in (1, 3, 2)]
        arrived[ring_at].append((come, rows))

    tile = HALF // 4
    mid_at = 2 * WIDTH
    packed, (mid_grad, up_row_1, dq, qpart, dkv, pays, prompts_1, rows_1) = out[6:8], out[8:]
    grads = both_parts(packed)
    dqs, dkvs = both(dq), both(dkv)
    start = give_back(1, pays, qpart, mid_grad)
    lefts.append(left_factors(1, dkv, lefts[0][1], lefts[0][3], *grads[2:]))
    plan = [("down", 0, 0, 0, 0)]
    plan += [("up", part, mid_at, 0, HALF + part * tile) for part in range(3)]
    made = mlp_call(plan, ((0, HALF + 3 * tile),), lefts[1][0:2], grads)
    plan = [("q", None, 1, 0), ("k", None, 1, tile), ("v", None, 1, 2 * tile)]
    plan += [("out", mid_at + 2 * HALF, 1, 3 * tile), (3, mid_at + HALF, 1, 4 * tile)]
    talls = (after(lefts[1][0], made[0]), lefts[1][1])
    mixed = mixed_call(plan, ((1, 5 * tile),), seq, talls, lefts[1][2:], dqs, dkvs, grads)
    start_ring(0, made, (HALF,) + (tile,) * 3)
    start_ring(1, mixed, (tile,) * 5)

    start = (after(start[0], mixed[1][0]), *start[1:])
    x_in, q, k, v, lse, mid, slope = kept[0]
    small = (small_pick, small_spot, prompts_1, rows_1, up_row_1, up_row_1)
    out = back_call(
        start, first_seq, (mid, slope, q, k, v, lse), prompt_rows[0], vecs[0], query_seg, key_seg,
        small, weights,
    )
    packed, (mid_grad, _, dq, qpart, dkv, pays) = out[0:2], out[2:8]
    grads = both_parts(packed)
    plan = [("down", 0, 0, 2, 0), ("out", 0, mid_at + HALF, 2, HALF)]
    plan += [("up", part, mid_at, 2, HALF + (1 + part) * tile) for part in range(2)]
    talls = (after(lefts[0][0], dkv, arrived[0][0][0], *arrived[1][0][0]), lefts[0][1])
    made = mlp_call(plan, ((2, HALF + 3 * tile),), talls, grads, 60)
    second_steps = made[2]
    start = give_back(0, after(pays, arrived[0][0][0]), qpart, mid_grad)
    dqs, dkvs = both(dq), both(dkv)
    small = (out[8], send(out[9], "core", 1))
    plan = [("q", None, 1, 0), ("k", None, 1, tile), ("v", None, 1, 2 * tile)]
    plan += [(part, mid_at + 2 * HALF, 1, (1 + part) * tile + 32) for part in (2, 3)]
    talls = (after(lefts[0][0], second_steps[0]), lefts[0][1])
    mixed = mixed_call(
        plan, ((1, 5 * tile + 32),), seq, talls, lefts[0][2:], dqs, dkvs, grads, small
    )
    second_steps[2] = after(second_steps[2], mixed[1][0])
    start_ring(2, {2: second_steps}, (HALF,) + (tile,) * 3)
    start_ring(1, mixed, (tile,) * 3 + (16, 16) + (tile,) * 2)
    for group in arrived:
        come, rows = group[0]
        (total,) = fold_call([(1, [(come, rows)])])
        group[0] = ([total], rows)
    grad_patch, grad_cls = close_call((after(start[0], mixed[1][0]), *start[1:]))
    (come, rows), *others = arrived[0]
    (plane,) = fold_call([(16, [([after(come[0], arrived[1][0][0][0], grad_cls)], rows), *others])])
    (come, rows), *others = arrived[1]
    pieces = fold_call([(4, [([after(come[0], plane)], rows), *others])])
    plane = deal_out(plane, RINGS[0][1:])
    second = [pieces[0]] + [send(pieces[step], RINGS[1][1], step) for step in (1, 3, 2)]
    rows = tuple(row // 4 for _, items in arrived[1] for row in items)
    pieces = fold_call([(4, [(second, rows)])], LATE)
    third = [pieces[0]] + [send(pieces[step], RINGS[1][2], step) for step in (1, 3, 2)]
    lasts = [plane, *third]
    layouts = (
        [("down", 1, 0, 24)]
        + [("up", 1, part, 6) for part in range(3)]
        + [("down", 0, 0, 24), ("out", 0, 0, 6)]
        + [("up", 0, part, 6) for part in range(2)],
        [("qkv", 1, part, 6) for part in range(3)]
        + [("out", 1, 0, 6), ("up", 1, 3, 6)]
        + [("qkv", 0, part, 6) for part in range(3)]
        + [("small", 0, 0, 1), ("bias", 0, 0, 1), ("up", 0, 2, 6), ("up", 0, 3, 6)],
    )
    done = final_call(lasts, layouts, own_w, own_vec)
    swap = lambda values: jnp.transpose(values, (1, 0, 2))
    return (
        out_patch[None],
        swap(out_cls),
        grad_patch[None],
        swap(grad_cls),
        jnp.transpose(done[4], (1, 2, 0)),
        swap(done[0]),
        swap(done[1]),
        swap(done[2]),
        done[3],
        done[5],
        swap(done[6]),
        done[7],
    )


def solution(mesh):
    placed = (
        P("dp", "seq", None),
        P("dp", None, None),
        P("dp", "seq"),
        P(),
        P(),
        P(),
        P(),
        P(),
        P(),
        P(),
        P(),
        P("dp", "seq", None),
        P("dp", None, None),
    )
    return jax.shard_map(
        per_device,
        mesh=mesh,
        in_specs=placed,
        out_specs=(
            P("dp", "seq", None),
            P("dp", None, None),
            P("dp", "seq", None),
            P("dp", None, None),
            P(None, None, ("dp", "seq")),
            P(None, ("dp", "seq"), None),
            P(None, ("dp", "seq"), None),
            P(None, ("dp", "seq"), None),
            P(None, ("dp", "seq"), None),
            P(None, None, ("dp", "seq")),
            P(None, None, ("dp", "seq")),
            P(None, ("dp", "seq")),
        ),
        check_vma=False,
    )
```
